32 devices in a mesh: px: 4 (over y, core), py: 8 (over z, x).
Axes of the slice: x: 2, y: 2, z: 4, core: 2. Of those that a mesh axis runs over, the one named last changes fastest.
Arguments:
- control_start: float32 [2, 8, 64, 2048], P(None, 'py', None, 'px'), may hold values from -12 to 12
- coef_x: float32 [8, 64, 2048], P('py', None, 'px'), may hold values from 0.1 to 0.45
- coef_y: float32 [8, 64, 2048], P('py', 'px'), may hold values from 0.1 to 0.45
- innovation: float32 [32768, 128], P(('px', 'py')), may hold values from -6 to 6
- obs_weight: float32 [32768, 128], P(('px', 'py')), may hold values from 0.25 to 4
- interp: float32 [32768], P(('px', 'py')), may hold values from 0 to 1
- obs_owner: int32 [32768, 1], P(('px', 'py')), may hold values from 0 to 7; in each aligned block of 1024 rows (0 to 1023, 1024 to 2047, ...) at most 384 rows name the same one
- cell_key: int32 [32768], P(('px', 'py')), may hold values from 0 to 31
- stencil: int32 [32768], P(('px', 'py')), may hold values from 0 to 14
Outputs:
- control: float32 [2, 8, 64, 2048], P(None, 'py', None, 'px')
- residual: float32 [2, 8, 64, 2048], P(None, 'py', None, 'px')
The draws below stay inside these ranges and needn't reach their ends.
Inputs may be any that keep to these rules, and one draw needn't show every extreme that they name: `obs_owner`: at most 384 of the observation rows of one device name the same owner, and exactly 384 do for some owner on some device.
All inputs are finite; a program needn't handle non-finite values.
Results may differ from the reference program's by a relative error of at most 0.00023.
Values sent between devices are 32-bit elements; how exact they have to be, the bound alone decides.
No kernel may reach another device: no remote copies, remote signals or barrier semaphores. Data moves between devices by JAX's collectives and lax.ppermute only.
A program may use at most 64 MiB of HBM per device.

```python
import math
import jax
import jax.numpy as jnp
import numpy as np
from jax import lax

F = 2
SEG = 128
M = 4
ITERS = 2
LZ = 1
LX = 16
NY = 2048
OBS_DEV = 1024
NX = 64
NZ = 8
NB = 16
CAP = 384
PX_ROWS = 8192
OBS = 32768
N_PY = 8


def draw_control_start(key, part):
    y_frac = jnp.arange(NY, dtype=jnp.float32) / NY
    z_frac = jnp.arange(NZ, dtype=jnp.float32) / NZ
    random_part = jnp.clip(jax.random.normal(key, (F, NZ, NX, NY), jnp.float32), -4.0, 4.0)
    row_scale = (0.5 + y_frac)[None, None, None, :] * (1.0 + z_frac)[None, :, None, None]
    return random_part * row_scale


def set_ends(values, stream_key, smallest, high):
    index_at = [jax.random.randint(jax.random.fold_in(stream_key, axis), (), 0, length) for axis, length in enumerate(values.shape)]
    main_axis = values.shape.index(max(values.shape))
    beside = index_at[:main_axis] + [(index_at[main_axis] + 1) % values.shape[main_axis]] + index_at[main_axis + 1:]
    return values.at[tuple(index_at)].set(smallest).at[tuple(beside)].set(high)


def level_of(stream_key, dims, pieces, low, high):
    def one(position, blocks):
        draws = jax.random.uniform(jax.random.fold_in(jax.random.fold_in(stream_key, 6), position), (blocks,), jnp.float32, low / len(pieces), high / len(pieces))
        return jnp.repeat(jnp.exp(draws), dims[position] // blocks).reshape((-1,) + (1,) * (len(dims) - position - 1))

    factor_of = one(*pieces[0])
    for cut in pieces[1:]:
        factor_of = factor_of * one(*cut)
    return factor_of


def deal_out(own_key, own, number, rows, count, top, most, skew):
    sequence = jax.random.permutation(own_key, count)
    heavy_load, ordinary = load_shares(count, rows * top, most, skew, True), load_shares(count, rows * top, most, skew, False)
    places = jnp.arange(count)

    def named(tallies, rotation):
        used = int((tallies > 0).sum())
        fixed = max(1, used // 4)
        passed = fixed + (places - fixed + rotation * (used - fixed)) % max(1, count - fixed)
        return jnp.zeros((count,), jnp.int32).at[sequence[jnp.where(places < fixed, places, passed)]].set(jnp.asarray(tallies, jnp.int32))

    tallies = jnp.where(number % 4 == 0, named(heavy_load, number // 4), named(ordinary, number - number // 4 - 1))
    mixed = jax.random.permutation(jax.random.fold_in(own, 3), count)
    source_of, taker = mixed[0:count // 2 * 2:2], mixed[1:count // 2 * 2:2]
    margin = jnp.minimum(tallies[source_of] - 1, most - tallies[taker]) // 2
    margin = jnp.where((source_of == sequence[0]) | (taker == sequence[0]) | (tallies[taker] == 0), 0, jnp.maximum(margin, 0))
    passed = jax.random.randint(jax.random.fold_in(own, 4), (count // 2,), 0, 1 << 20) % (margin + 1)
    tallies = tallies.at[source_of].add(-passed).at[taker].add(passed)
    labels = jnp.searchsorted(jnp.cumsum(tallies), jnp.arange(rows * top), side="right").astype(jnp.int32)
    listing = labels.reshape(top, rows).T
    listing = listing[jax.random.permutation(jax.random.fold_in(own, 1), rows)]
    rotation = jax.random.randint(jax.random.fold_in(own, 2), (rows, 1), 0, top)
    return jnp.take_along_axis(listing, (jnp.arange(top)[None, :] + rotation) % top, axis=1)


def load_shares(count, total, reach, lean, full):
    weights = [(1 << 20) // math.isqrt(rank ** lean) + 1 for rank in range(1, count + 1)]
    largest = reach if full else min(reach, max(-(-total // count), total * weights[0] // sum(weights)))
    least = 1 if total - largest >= count - 1 else 0
    counts, rest = [largest] + [least] * (count - 1), total - largest - least * (count - 1)
    while rest > 0:
        free = [i for i in range(1, count) if counts[i] < largest] or [i for i in range(1, count) if counts[i] < reach]
        pool, budget = sum([weights[i] for i in free]), rest
        for i in free:
            more = min(reach - counts[i], max(1, budget * weights[i] // pool), rest)
            counts[i] = counts[i] + more
            rest = rest - more
    return np.array(counts)


def normal_values(key, dims, deviation, most, pieces=(), kind=jnp.bfloat16):
    factor_of = level_of(key, dims, pieces, -0.22, 0.18) if pieces else 1.0
    values = jax.random.normal(key, dims, jnp.float32) * deviation * factor_of
    return jnp.minimum(jnp.maximum(values, -most), most).astype(kind)


def setup_inputs(seed: int = 0) -> dict:
    key_list = jax.random.split(jax.random.key(seed), 10)
    control_start = draw_control_start(jax.random.fold_in(key_list[9], 71), 0)
    coef_x = jnp.clip(jnp.exp(math.log(0.45) - 1.50407736 * jax.random.uniform(key_list[1], (NZ, NX, NY), jnp.float32) ** level_of(key_list[1], (NZ, NX, NY), ((0, 8), (2, 4)), -0.2, 0.2)), 0.1, 0.45)
    coef_y = jnp.clip(jnp.exp(math.log(0.45) - 1.50407736 * jax.random.uniform(key_list[2], (NZ, NX, NY), jnp.float32) ** level_of(key_list[2], (NZ, NX, NY), ((0, 8), (1, 4)), -0.2, 0.2)), 0.1, 0.45)
    innovation = normal_values(key_list[3], (OBS, SEG), 1.0, 6.0, ((0, 32),), jnp.float32)
    obs_weight = jnp.clip(jnp.exp(math.log(4.0) - 2.7725887 * jax.random.uniform(key_list[4], (OBS, SEG), jnp.float32) ** level_of(key_list[4], (OBS, SEG), ((0, 32),), -0.2, 0.2)), 0.25, 4.0)
    interp = jnp.clip(1.0 * jax.random.uniform(key_list[5], (OBS,), jnp.float32) ** level_of(key_list[5], (OBS,), ((0, 32),), -0.2, 0.2), 0.0, 1.0)
    obs_owner_keys = jax.random.split(jax.random.fold_in(key_list[6], 1), OBS // OBS_DEV)
    obs_owner_turns = jax.random.permutation(jax.random.fold_in(key_list[6], 3), OBS // OBS_DEV)
    obs_owner = jax.vmap(lambda own, number: deal_out(jax.random.fold_in(key_list[6], 2), own, number, OBS_DEV, N_PY, 1, CAP, 2))(obs_owner_keys, obs_owner_turns).reshape((OBS, 1))
    cell_key = set_ends(jax.random.randint(key_list[7], (OBS,), 0, F * LZ * NB), jax.random.fold_in(key_list[7], 1), 0, (F * LZ * NB) - 1).astype(jnp.int32)
    stencil = set_ends(jax.random.randint(key_list[8], (OBS,), 0, LX - 1), jax.random.fold_in(key_list[8], 1), 0, (LX - 1) - 1).astype(jnp.int32)
    return dict(control_start=control_start, coef_x=coef_x, coef_y=coef_y, innovation=innovation, obs_weight=obs_weight, interp=interp, obs_owner=obs_owner, cell_key=cell_key, stencil=stencil)


def diffuse(values, coeffs, axis_dim):
    length = values.shape[axis_dim]
    face_coef = lax.slice_in_dim(coeffs[None], 0, length - 1, axis=axis_dim)
    pad_after = [(0, 0)] * values.ndim
    pad_before = [(0, 0)] * values.ndim
    pad_after[axis_dim] = (0, 1)
    pad_before[axis_dim] = (1, 0)
    for repeat in range(M):
        next_cell = lax.slice_in_dim(values, 1, length, axis=axis_dim)
        this_cell = lax.slice_in_dim(values, 0, length - 1, axis=axis_dim)
        flux_face = face_coef * (next_cell - this_cell)
        values = values + jnp.pad(flux_face, pad_after) - jnp.pad(flux_face, pad_before)
    return values


def misfit(state_in, observed, weights, shares_in, row_index):
    flat_field = state_in.reshape(-1, SEG)
    lower_rows = flat_field[row_index]
    upper_rows = flat_field[row_index + NB]
    shares = shares_in[:, None]
    modelled = (1.0 - shares) * lower_rows + shares * upper_rows
    weighted = weights * (observed - modelled)
    result = jnp.zeros_like(flat_field).at[row_index].add((1.0 - shares) * weighted)
    result = result.at[row_index + NB].add(shares * weighted)
    return result.reshape(state_in.shape)


def reference(control_start, coef_x, coef_y, innovation, obs_weight, interp, obs_owner, cell_key, stencil):
    coef_x = coef_x.at[:, -1, :].set(0.0)
    coef_y = coef_y.at[:, :, -1].set(0.0)
    rows_all = jnp.arange(OBS, dtype=jnp.int32)
    px_index = rows_all // PX_ROWS
    level_z = obs_owner[:, 0] * LZ + (cell_key // NB) % LZ
    field_id = cell_key // (LZ * NB)
    x_cell = px_index * LX + stencil
    row_index = (((field_id * NZ + level_z) * NX + x_cell) * NB + cell_key % NB).astype(jnp.int32)

    def forward(values_in):
        return diffuse(diffuse(values_in, coef_x, 2), coef_y, 3)

    def adjoint(values_in):
        return diffuse(diffuse(values_in, coef_y, 3), coef_x, 2)

    no_data = jnp.zeros_like(innovation)
    residual = adjoint(misfit(forward(control_start), innovation, obs_weight, interp, row_index)) - control_start
    control = control_start
    direction = residual
    norm_now = jnp.sum(residual * residual)
    for repeat in range(ITERS):
        applied = direction - adjoint(misfit(forward(direction), no_data, obs_weight, interp, row_index))
        step_size = norm_now / jnp.sum(direction * applied)
        control = control + step_size * direction
        residual = residual - step_size * applied
        norm_next = jnp.sum(residual * residual)
        direction = residual + (norm_next / norm_now) * direction
        norm_now = norm_next
    return control, residual
```

```python
import functools

import jax
import jax.numpy as jnp
from jax import lax
from jax.experimental import pallas as pl
from jax.experimental.pallas import tpu as pltpu
from jax.sharding import PartitionSpec as P

F = 2
SEG = 128
M = 4
NB = 16
LX = 16
ROWS = F * NB * LX
HALF = SEG // 2
VMEM_BYTES = 32 * 1024 * 1024


def iota(shape, axis):
    return lax.broadcasted_iota(jnp.int32, shape, axis)


def flag(condition, kind=jnp.bfloat16):
    return jnp.where(condition, 1.0, 0.0).astype(kind)


def mxu(left, right):
    return jnp.dot(left, right, preferred_element_type=jnp.float32)


def split_parts(values, count):
    parts = []
    for _ in range(count):
        part = values.astype(jnp.bfloat16)
        parts.append(part)
        values = values - part.astype(jnp.float32)
    return parts


def ends_tile(before, after):
    return jnp.where(iota(after.shape, after.ndim - 1) < HALF, after, before)


def sweep(values, coeffs, axis):
    size = values.shape[axis]
    for _ in range(M):
        flux = coeffs * (pltpu.roll(values, size - 1, axis) - values)
        values = values + flux - pltpu.roll(flux, 1, axis)
    return values


def pack_kernel(groups, cap, blk, block_rows, own_ref, key_ref, sten_ref, itp_ref, w_ref, d_ref,
                cy_ref, out_ref, cy_out, slot_v, slot_s, sem):
    chunks = own_ref.shape[0]
    nb = cap // blk
    own = own_ref[...]
    high = groups * chunks
    shift = chunks.bit_length() - 1
    masks = [flag(own == o, jnp.float32) for o in range(groups)]
    hits = jnp.concatenate(masks, axis=0).astype(jnp.bfloat16)
    square = (SEG, SEG)
    within = mxu(hits, flag(iota(square, 0) < iota(square, 1)))
    tallies = mxu(hits, jnp.ones(square, jnp.bfloat16)).astype(jnp.bfloat16)
    line, column = iota((high, high), 0), iota((high, high), 1)
    same = (line >> shift) == (column >> shift)
    ranks = within + mxu(flag(same & (column < line)), tallies)
    totals = mxu(flag(same), tallies)
    rank = sum(masks[o] * ranks[o * chunks:(o + 1) * chunks] for o in range(groups))
    rank = rank.astype(jnp.int32)
    slot_v[...] = own * block_rows + rank
    copy = pltpu.make_async_copy(slot_v, slot_s, sem)
    copy.start()

    def clear(o, carry):
        start = pl.multiple_of(o * block_rows, 8)
        out_ref[pl.ds(start, block_rows), :] = jnp.zeros((block_rows, SEG), jnp.float32)
        return carry

    lax.fori_loop(0, groups, clear, 0)

    width = cy_out.shape[2] - SEG
    columns = cy_ref.shape[1]
    cy = cy_ref[...]
    cy = jnp.where(iota(cy.shape, 1) == columns - 1, 0.0, cy)
    empty = jnp.zeros((cy.shape[0], SEG), jnp.float32)
    for q in range(columns // width):
        low, top = q * width, (q + 1) * width
        cy_out[q, :, :width] = cy[:, low:top]
        before = cy[:, low - SEG:low] if low > 0 else empty
        after = cy[:, top:top + SEG] if top < columns else empty
        cy_out[q, :, width:] = ends_tile(before, after)

    log = blk.bit_length() - 1
    place = own * nb + (rank >> log)
    lane = rank & (blk - 1)
    key, sten, itp = key_ref[...], sten_ref[...], itp_ref[...]
    tall = groups * nb
    meta = jnp.zeros((5 * tall, SEG), jnp.float32)
    for i in range(chunks):
        chosen = iota((tall, SEG), 0) == place[i:i + 1]
        parts = split_parts(itp[i:i + 1], 3)
        parts += [key[i:i + 1].astype(jnp.bfloat16), sten[i:i + 1].astype(jnp.bfloat16)]
        left = [jnp.where(chosen, part.astype(jnp.float32), 0.0) for part in parts]
        right = flag(iota(square, 0) == lane[i:i + 1])
        meta = meta + lax.dot_general(
            jnp.concatenate(left, axis=0).astype(jnp.bfloat16), right,
            (((1,), (1,)), ((), ())), preferred_element_type=jnp.float32)
    shares = meta[:tall] + meta[tall:2 * tall] + meta[2 * tall:3 * tall]
    targets = meta[3 * tall:4 * tall] * LX + meta[4 * tall:]
    for o in range(groups):
        base = o * block_rows + 2 * cap
        out_ref[base:base + nb, :] = shares[o * nb:(o + 1) * nb]
        out_ref[base + nb:base + 2 * nb, :] = targets[o * nb:(o + 1) * nb]
        out_ref[base + 2 * nb:base + 2 * nb + 1, :] = totals[o * chunks:o * chunks + 1]

    copy.wait()

    def place_rows(g, carry):
        start = pl.multiple_of(g * 8, 8)
        weights = w_ref[pl.ds(start, 8), :]
        products = weights * d_ref[pl.ds(start, 8), :]
        for i in range(8):
            slot = slot_s[g // 16, (g % 16) * 8 + i]
            out_ref[pl.ds(slot, 1), :] = weights[i:i + 1]
            out_ref[pl.ds(slot + cap, 1), :] = products[i:i + 1]
        return carry

    lax.fori_loop(0, w_ref.shape[0] // 8, place_rows, 0)


def gather_kernel(groups, cap, blk, block_rows, in_ref, out_ref, acc_ref):
    nb = cap // blk
    acc_ref[...] = jnp.zeros_like(acc_ref)

    def block(index, carry):
        source, part = index // nb, index % nb
        base = pl.multiple_of(source * block_rows, 8)
        count = in_ref[pl.ds(base + 2 * cap + 2 * nb, 1), :][0, 0]

        @pl.when(count > (part * blk).astype(jnp.float32))
        def _():
            share = in_ref[pl.ds(base + 2 * cap + part, 1), :]
            target = in_ref[pl.ds(base + 2 * cap + nb + part, 1), :][:, :blk]
            upper = jnp.broadcast_to(share, (SEG, SEG)).T[:blk]
            lower = 1.0 - upper
            start = pl.multiple_of(base + part * blk, 8)
            weights = in_ref[pl.ds(start, blk), :]
            start = pl.multiple_of(base + cap + part * blk, 8)
            products = in_ref[pl.ds(start, blk), :]
            lower_w, upper_w = lower * weights, upper * weights
            values = jnp.concatenate(
                [lower * lower_w, upper * lower_w, upper * upper_w,
                 lower * products, upper * products], axis=1)
            hit = flag(iota((ROWS, blk), 0).astype(jnp.float32) == target)
            acc_ref[...] += mxu(
                jnp.concatenate([hit, hit], axis=1),
                jnp.concatenate(split_parts(values, 2), axis=0))

        return carry

    lax.fori_loop(0, groups * nb, block, 0)

    width = out_ref.shape[3] - SEG
    per = width // SEG
    empty = jnp.zeros((LX, SEG), jnp.float32)
    fields = (
        acc_ref[:, :SEG] + pltpu.roll(acc_ref[:, 2 * SEG:3 * SEG], 1, 0),
        acc_ref[:, SEG:2 * SEG],
        acc_ref[:, 3 * SEG:4 * SEG] + pltpu.roll(acc_ref[:, 4 * SEG:], 1, 0),
    )
    for channel, values in enumerate(fields):
        for f in range(F):
            tiles = [values[(f * NB + b) * LX:(f * NB + b + 1) * LX] for b in range(NB)]
            for q in range(NB // per):
                for j in range(per):
                    out_ref[q, channel * F + f, :, j * SEG:(j + 1) * SEG] = tiles[q * per + j]
                before = tiles[q * per - 1] if q > 0 else empty
                after = tiles[(q + 1) * per] if (q + 1) * per < NB else empty
                out_ref[q, channel * F + f, :, width:] = ends_tile(before, after)


def sweep_x_into(to_ref, from_ref, cx_ref, plus_ref=None, sign=1.0):
    for low in range(0, cx_ref.shape[1], SEG):
        tile = slice(low, low + SEG)
        values = sweep(from_ref[:, tile], cx_ref[:, tile], 0)
        if plus_ref is not None:
            values = values + sign * plus_ref[:, tile]
        to_ref[:, tile] = values


def sweep_y_into(to_ref, from_ref, cy_ref):
    for low in range(0, cy_ref.shape[0], 8):
        lines = slice(low, low + 8)
        to_ref[lines, :] = sweep(from_ref[lines, :], cy_ref[lines, :], 1)


def start_kernel(c0_ref, cx_ref, prev_ref, next_ref, cy_ref, c0_out, cx_out, cy_out, u_out):
    width = c0_ref.shape[2]
    for p in range(cy_ref.shape[0]):
        cy_out[p * LX:(p + 1) * LX, :] = cy_ref[p]
    last = cx_ref.shape[0] - 1
    cx_out[:, :width] = cx_ref[...]
    cx_out[:, width:] = ends_tile(prev_ref[F], next_ref[F])
    cx_out[last:, :] = jnp.zeros((1, width + SEG), jnp.float32)
    for f in range(F):
        c0_out[f, :, :width] = c0_ref[f]
        c0_out[f, :, width:] = ends_tile(prev_ref[f], next_ref[f])
        sweep_x_into(u_out.at[f], c0_out.at[f], cx_out)
        sweep_y_into(u_out.at[f], u_out.at[f], cy_out)


def solve_kernel(obs_ref, c0_ref, cx_ref, cy_ref, u_ref, r_out, q_out, qq_out, dots_out,
                 vec, coef, work):
    width = r_out.shape[2]
    parts = obs_ref.shape[0]
    for p in range(parts):
        for channel in range(3 * F):
            coef[channel, p * LX:(p + 1) * LX, :] = obs_ref[p, channel]

    def normal(f, values, tile):
        size = values.shape[0]
        side = coef[F + f, :, tile]
        return (coef[f, :, tile] * values + side * pltpu.roll(values, size - 1, 0)
                + pltpu.roll(side * values, 1, 0))

    tiles = [slice(low, low + SEG) for low in range(0, width + SEG, SEG)]

    def first(f, carry):
        for tile in tiles:
            work[:, tile] = coef[2 * F + f, :, tile] - normal(f, u_ref[f, :, tile], tile)
        sweep_y_into(work, work, cy_ref)
        sweep_x_into(vec.at[0, f], work, cx_ref, c0_ref.at[f], -1.0)
        return carry

    lax.fori_loop(0, F, first, 0)

    def apply(index, carry):
        step, f = index // F, index % F
        sweep_x_into(work, vec.at[step, f], cx_ref)
        sweep_y_into(work, work, cy_ref)
        for tile in tiles:
            work[:, tile] = normal(f, work[:, tile], tile)
        sweep_y_into(work, work, cy_ref)
        sweep_x_into(vec.at[step + 1, f], work, cx_ref, vec.at[step, f])
        return carry

    lax.fori_loop(0, 2 * F, apply, 0)

    sums = [jnp.zeros((8, SEG), jnp.float32) for _ in range(5)]
    for f in range(F):
        r_out[f] = vec[0, f, :, :width]
        q_out[f] = vec[1, f, :, :width]
        qq_out[f] = vec[2, f, :, :width]
        for low in range(0, vec.shape[2], 8):
            for tile in tiles[:-1]:
                r = vec[0, f, low:low + 8, tile]
                q = vec[1, f, low:low + 8, tile]
                qq = vec[2, f, low:low + 8, tile]
                for i, product in enumerate((r * r, r * q, q * q, r * qq, q * qq)):
                    sums[i] = sums[i] + product
    lines = [jnp.sum(s, axis=0, keepdims=True) for s in sums]
    dots = jnp.concatenate(lines + [jnp.zeros((3, SEG), jnp.float32)], axis=0)
    for device in range(dots_out.shape[0]):
        dots_out[device] = dots


def finish_kernel(dots_ref, c0_ref, r_ref, q_ref, qq_ref, control_out, residual_out):
    dots = jnp.sum(dots_ref[...], axis=0)
    rr, rq, qq2, rqq, qqq = (dots[i:i + 1] for i in range(5))

    def total(line):
        return jnp.sum(line, axis=1, keepdims=True)

    rr_sum = total(rr)
    alpha = rr_sum / total(rq)
    new_sum = total(rr - 2.0 * alpha * rq + alpha * alpha * qq2)
    more = 1.0 + new_sum / rr_sum
    curve = total(more * more * rq - more * alpha * (rqq + qq2) + alpha * alpha * qqq)
    second = new_sum / curve
    first_weight = alpha + second * more
    both = alpha * second
    for f in range(F):
        r, q = r_ref[f], q_ref[f]
        control_out[f] = c0_ref[f] + first_weight * r - both * q
        residual_out[f] = r - first_weight * q + both * qq_ref[f]


def call(kernel, out_shape, scratch=(), in_specs=None):
    params = {} if in_specs is None else {"in_specs": in_specs}
    return pl.pallas_call(
        kernel,
        out_shape=out_shape,
        scratch_shapes=list(scratch),
        compiler_params=pltpu.CompilerParams(vmem_limit_bytes=VMEM_BYTES),
        **params,
    )


def f32(*shape):
    return jax.ShapeDtypeStruct(shape, jnp.float32)


def shards(
    control_start, coef_x, coef_y, innovation, obs_weight, interp, obs_owner, cell_key, stencil
):
    groups, spans = lax.axis_size("py"), lax.axis_size("px")
    rows = innovation.shape[0]
    cap = 3 * rows // groups
    blk = SEG if cap % SEG == 0 else HALF
    nb = cap // blk
    block_rows = 2 * cap + -(-(2 * nb + 1) // 8) * 8
    chunks = rows // SEG
    nx, width = control_start.shape[2], control_start.shape[3]
    ext = width + SEG
    c0, cx = control_start[:, 0], coef_x[0]

    packed, cy_parts = call(
        functools.partial(pack_kernel, groups, cap, blk, block_rows),
        (f32(groups * block_rows, SEG), f32(spans, LX, ext)),
        [pltpu.VMEM((chunks, SEG), jnp.int32), pltpu.SMEM((chunks, SEG), jnp.int32),
         pltpu.SemaphoreType.DMA],
    )(
        obs_owner.reshape(chunks, SEG), cell_key.reshape(chunks, SEG),
        stencil.reshape(chunks, SEG), interp.reshape(chunks, SEG),
        obs_weight, innovation, coef_y[0],
    )
    arrived = lax.all_to_all(packed, "py", split_axis=0, concat_axis=0, tiled=True)

    cy_lines = lax.all_to_all(cy_parts, "px", split_axis=0, concat_axis=0, tiled=True)
    fields = jnp.concatenate([c0, cx[None]], axis=0)
    steps = [(i, i + 1) for i in range(spans - 1)]
    from_prev = lax.ppermute(fields[:, :, -SEG:], "px", steps)
    from_next = lax.ppermute(fields[:, :, :SEG], "px", [(j, i) for i, j in steps])
    c0_ext, cx_ext, cy_ext, u_ext = call(
        start_kernel,
        (f32(F, nx, ext), f32(nx, ext), f32(nx, ext), f32(F, nx, ext)),
    )(c0, cx, from_prev, from_next, cy_lines)

    obs_parts = call(
        functools.partial(gather_kernel, groups, cap, blk, block_rows),
        f32(spans, 3 * F, LX, ext),
        [pltpu.VMEM((ROWS, 5 * SEG), jnp.float32)],
    )(arrived)
    obs_fields = lax.all_to_all(obs_parts, "px", split_axis=0, concat_axis=0, tiled=True)

    r, q, qq, dots = call(
        solve_kernel,
        (f32(F, nx, width),) * 3 + (f32(groups * spans, 8, SEG),),
        [pltpu.VMEM((3, F, nx, ext), jnp.float32), pltpu.VMEM((3 * F, nx, ext), jnp.float32),
         pltpu.VMEM((nx, ext), jnp.float32)],
    )(obs_fields, c0_ext, cx_ext, cy_ext, u_ext)
    dots = lax.all_to_all(dots, ("px", "py"), split_axis=0, concat_axis=0, tiled=True)
    control, residual = call(finish_kernel, (f32(F, nx, width),) * 2)(dots, c0, r, q, qq)
    return control[:, None], residual[:, None]


def solution(mesh):
    return jax.shard_map(
        shards,
        mesh=mesh,
        in_specs=(
            P(None, "py", None, "px"),
            P("py", None, "px"),
            P("py", "px", None),
            P(("px", "py"), None),
            P(("px", "py"), None),
            P(("px", "py")),
            P(("px", "py"), None),
            P(("px", "py")),
            P(("px", "py")),
        ),
        out_specs=(P(None, "py", None, "px"), P(None, "py", None, "px")),
        check_vma=False,
    )
```

```python
import functools

import jax
import jax.numpy as jnp
from jax import lax
from jax.experimental import pallas as pl
from jax.experimental.pallas import tpu as pltpu
from jax.sharding import PartitionSpec as P

F = 2
SEG = 128
M = 4
NB = 16
LX = 16
ROWS = F * NB * LX
HALF = SEG // 2
VMEM_BYTES = 32 * 1024 * 1024
PACK_BYTES = 60 * 1024 * 1024


def iota(shape, axis):
    return lax.broadcasted_iota(jnp.int32, shape, axis)


def flag(condition, kind=jnp.bfloat16):
    return jnp.where(condition, 1.0, 0.0).astype(kind)


def mxu(left, right):
    return jnp.dot(left, right, preferred_element_type=jnp.float32)


def split_parts(values, count):
    parts = []
    for _ in range(count):
        part = values.astype(jnp.bfloat16)
        parts.append(part)
        values = values - part.astype(jnp.float32)
    return parts


def ends_tile(before, after):
    return jnp.where(iota(after.shape, after.ndim - 1) < HALF, after, before)


def sweep(values, coeffs, axis):
    size = values.shape[axis]
    for _ in range(M):
        flux = coeffs * (pltpu.roll(values, size - 1, axis) - values)
        values = values + flux - pltpu.roll(flux, 1, axis)
    return values


def pack_kernel(groups, cap, blk, block_rows, own_hbm, key_hbm, sten_hbm, itp_hbm, w_hbm, d_hbm,
                cy_hbm, c0_hbm, cx_hbm, w_out, v_out, first_out, last_out, *rest):
    cy_outs, rest = rest[:-11], rest[-11:]
    own_ref, key_ref, sten_ref, itp_ref, w_ref, d_ref, cy_ref, slot_v, slot_s, sems, sem = rest
    width = c0_hbm.shape[2]
    pairs = [
        (own_hbm, own_ref), (key_hbm, key_ref), (sten_hbm, sten_ref), (itp_hbm, itp_ref),
        (w_hbm, w_ref), (d_hbm, d_ref), (cy_hbm, cy_ref),
        (c0_hbm.at[:, :, pl.ds(0, SEG)], first_out.at[pl.ds(0, F)]),
        (cx_hbm.at[:, pl.ds(0, SEG)], first_out.at[F]),
        (c0_hbm.at[:, :, pl.ds(width - SEG, SEG)], last_out.at[pl.ds(0, F)]),
        (cx_hbm.at[:, pl.ds(width - SEG, SEG)], last_out.at[F]),
    ]
    loads = [pltpu.make_async_copy(*pair, sems.at[i]) for i, pair in enumerate(pairs)]
    for load in loads:
        load.start()

    def clear(o, carry):
        start = pl.multiple_of(o * block_rows, 8)
        w_out[pl.ds(start, block_rows), :] = jnp.zeros((block_rows, SEG), jnp.float32)
        start = pl.multiple_of(o * cap, 8)
        v_out[pl.ds(start, cap), :] = jnp.zeros((cap, SEG), jnp.float32)
        return carry

    lax.fori_loop(0, groups, clear, 0)

    for load in loads[:4]:
        load.wait()
    chunks = own_ref.shape[0]
    nb = cap // blk
    own = own_ref[...]
    high = groups * chunks
    shift = chunks.bit_length() - 1
    masks = [flag(own == o, jnp.float32) for o in range(groups)]
    hits = jnp.concatenate(masks, axis=0).astype(jnp.bfloat16)
    square = (SEG, SEG)
    within = mxu(hits, flag(iota(square, 0) < iota(square, 1)))
    tallies = mxu(hits, jnp.ones(square, jnp.bfloat16)).astype(jnp.bfloat16)
    line, column = iota((high, high), 0), iota((high, high), 1)
    same = (line >> shift) == (column >> shift)
    ranks = within + mxu(flag(same & (column < line)), tallies)
    totals = mxu(flag(same), tallies)
    rank = sum(masks[o] * ranks[o * chunks:(o + 1) * chunks] for o in range(groups))
    rank = rank.astype(jnp.int32)
    slot_v[:chunks] = own * block_rows + rank
    slot_v[chunks:] = own * cap + rank
    copy = pltpu.make_async_copy(slot_v, slot_s, sem)
    copy.start()

    log = blk.bit_length() - 1
    place = own * nb + (rank >> log)
    lane = rank & (blk - 1)
    key, sten, itp = key_ref[...], sten_ref[...], itp_ref[...]
    tall = groups * nb
    meta = jnp.zeros((5 * tall, SEG), jnp.float32)
    for i in range(chunks):
        chosen = iota((tall, SEG), 0) == place[i:i + 1]
        parts = split_parts(itp[i:i + 1], 3)
        parts += [key[i:i + 1].astype(jnp.bfloat16), sten[i:i + 1].astype(jnp.bfloat16)]
        left = [jnp.where(chosen, part.astype(jnp.float32), 0.0) for part in parts]
        right = flag(iota(square, 0) == lane[i:i + 1])
        meta = meta + lax.dot_general(
            jnp.concatenate(left, axis=0).astype(jnp.bfloat16), right,
            (((1,), (1,)), ((), ())), preferred_element_type=jnp.float32)
    shares = meta[:tall] + meta[tall:2 * tall] + meta[2 * tall:3 * tall]
    targets = meta[3 * tall:4 * tall] * LX + meta[4 * tall:]
    for o in range(groups):
        base = o * block_rows + cap
        w_out[base:base + nb, :] = shares[o * nb:(o + 1) * nb]
        w_out[base + nb:base + 2 * nb, :] = targets[o * nb:(o + 1) * nb]
        w_out[base + 2 * nb:base + 2 * nb + 1, :] = totals[o * chunks:o * chunks + 1]

    for load in loads[4:]:
        load.wait()
    columns = cy_ref.shape[1]
    cy = cy_ref[...]
    cy_ref[...] = jnp.where(iota(cy.shape, 1) == columns - 1, 0.0, cy)
    me = lax.axis_index("px")
    for k, cy_out in enumerate(cy_outs):
        q = me ^ k
        low = pl.multiple_of(q * width, SEG)
        cy_out[:, :width] = cy_ref[:, pl.ds(low, width)]
        before = cy_ref[:, pl.ds(pl.multiple_of(jnp.maximum(low - SEG, 0), SEG), SEG)]
        after = cy_ref[:, pl.ds(pl.multiple_of(jnp.minimum(low + width, columns - SEG), SEG), SEG)]
        cy_out[:, width:] = ends_tile(jnp.where(q > 0, before, 0.0),
                                      jnp.where(q < len(cy_outs) - 1, after, 0.0))

    copy.wait()

    def place_rows(g, carry):
        start = pl.multiple_of(g * 8, 8)
        weights = w_ref[pl.ds(start, 8), :]
        products = weights * d_ref[pl.ds(start, 8), :]
        line, lane = g // 16, (g % 16) * 8
        for i in range(8):
            w_out[pl.ds(slot_s[line, lane + i], 1), :] = weights[i:i + 1]
            v_out[pl.ds(slot_s[chunks + line, lane + i], 1), :] = products[i:i + 1]
        return carry

    lax.fori_loop(0, w_ref.shape[0] // 8, place_rows, 0)


def sum_rows(groups, cap, blk, block_rows, w_ref, acc_ref, terms):
    nb = cap // blk
    acc_ref[...] = jnp.zeros_like(acc_ref)

    def block(index, carry):
        source, part = index // nb, index % nb
        base = pl.multiple_of(source * block_rows, 8)
        count = w_ref[pl.ds(base + cap + 2 * nb, 1), :][0, 0]

        @pl.when(count > (part * blk).astype(jnp.float32))
        def _():
            share = w_ref[pl.ds(base + cap + part, 1), :]
            target = w_ref[pl.ds(base + cap + nb + part, 1), :][:, :blk]
            upper = jnp.broadcast_to(share, (SEG, SEG)).T[:blk]
            values = jnp.concatenate(terms(source, part, upper), axis=1)
            hit = flag(iota((ROWS, blk), 0).astype(jnp.float32) == target)
            acc_ref[...] += mxu(
                jnp.concatenate([hit, hit], axis=1),
                jnp.concatenate(split_parts(values, 2), axis=0))

        return carry

    lax.fori_loop(0, groups * nb, block, 0)


def cut_parts(stage_ref, outs):
    width = outs[0].shape[2] - SEG
    per = width // SEG
    me = lax.axis_index("px")
    for k, out in enumerate(outs):
        q = me ^ k
        for channel in range(stage_ref.shape[0]):
            for f in range(F):
                def tile(b):
                    start = pl.multiple_of((f * NB + b) * LX, LX)
                    return stage_ref[channel, pl.ds(start, LX), :]

                to = out.at[channel * F + f]
                for j in range(per):
                    to[:, j * SEG:(j + 1) * SEG] = tile(q * per + j)
                before = tile(jnp.maximum(q * per - 1, 0))
                after = tile(jnp.minimum(q * per + per, NB - 1))
                to[:, width:] = ends_tile(jnp.where(q > 0, before, 0.0),
                                          jnp.where(q < len(outs) - 1, after, 0.0))


def weights_kernel(groups, cap, blk, block_rows, w_ref, tie_ref, *rest):
    outs, acc_ref, stage_ref = rest[:-2], rest[-2], rest[-1]

    def terms(source, part, upper):
        lower = 1.0 - upper
        start = pl.multiple_of(source * block_rows + part * blk, 8)
        weights = w_ref[pl.ds(start, blk), :]
        lower_w, upper_w = lower * weights, upper * weights
        return [lower * lower_w, upper * lower_w, upper * upper_w]

    sum_rows(groups, cap, blk, block_rows, w_ref, acc_ref, terms)
    stage_ref[0] = acc_ref[:, :SEG] + pltpu.roll(acc_ref[:, 2 * SEG:], 1, 0)
    stage_ref[1] = acc_ref[:, SEG:2 * SEG]
    cut_parts(stage_ref, outs)


def products_kernel(groups, cap, blk, block_rows, w_ref, v_ref, tie_ref, *rest):
    outs, acc_ref, stage_ref = rest[:-2], rest[-2], rest[-1]

    def terms(source, part, upper):
        start = pl.multiple_of(source * cap + part * blk, 8)
        products = v_ref[pl.ds(start, blk), :]
        return [(1.0 - upper) * products, upper * products]

    sum_rows(groups, cap, blk, block_rows, w_ref, acc_ref, terms)
    stage_ref[0] = acc_ref[:, :SEG] + pltpu.roll(acc_ref[:, SEG:], 1, 0)
    cut_parts(stage_ref, outs)


def sweep_x_into(to_ref, from_ref, cx_ref, plus_ref=None, sign=1.0):
    for low in range(0, cx_ref.shape[1], SEG):
        tile = slice(low, low + SEG)
        values = sweep(from_ref[:, tile], cx_ref[:, tile], 0)
        if plus_ref is not None:
            values = values + sign * plus_ref[:, tile]
        to_ref[:, tile] = values


def sweep_y_into(to_ref, from_ref, cy_ref):
    for low in range(0, cy_ref.shape[0], 8):
        lines = slice(low, low + 8)
        to_ref[lines, :] = sweep(from_ref[lines, :], cy_ref[lines, :], 1)


def start_kernel(c0_ref, cx_ref, prev_ref, next_ref, *rest):
    cy_refs, (c0_out, cx_out, cy_out, u_out) = rest[:-4], rest[-4:]
    width = c0_ref.shape[2]
    me = lax.axis_index("px")
    for k, cy_ref in enumerate(cy_refs):
        cy_out[pl.ds(pl.multiple_of((me ^ k) * LX, LX), LX), :] = cy_ref[...]
    last = cx_ref.shape[0] - 1
    cx_out[:, :width] = cx_ref[...]
    cx_out[:, width:] = ends_tile(prev_ref[F], next_ref[F])
    cx_out[last:, :] = jnp.zeros((1, width + SEG), jnp.float32)
    for f in range(F):
        c0_out[f, :, :width] = c0_ref[f]
        c0_out[f, :, width:] = ends_tile(prev_ref[f], next_ref[f])
        sweep_x_into(u_out.at[f], c0_out.at[f], cx_out)
        sweep_y_into(u_out.at[f], u_out.at[f], cy_out)


def solve_kernel(spans, c0_ref, cx_ref, cy_ref, u_ref, *rest):
    side_refs, sum_refs = rest[:spans], rest[spans:2 * spans]
    r_out, q_out, qq_out, dots_out, vec, coef, work = rest[2 * spans:]
    width = r_out.shape[2]
    me = lax.axis_index("px")
    for k in range(spans):
        rows = pl.ds(pl.multiple_of((me ^ k) * LX, LX), LX)
        for channel in range(2 * F):
            coef[channel, rows, :] = side_refs[k][channel]
        for f in range(F):
            coef[2 * F + f, rows, :] = sum_refs[k][f]

    def normal(f, values, tile):
        size = values.shape[0]
        side = coef[F + f, :, tile]
        return (coef[f, :, tile] * values + side * pltpu.roll(values, size - 1, 0)
                + pltpu.roll(side * values, 1, 0))

    tiles = [slice(low, low + SEG) for low in range(0, width + SEG, SEG)]

    def first(f, carry):
        for tile in tiles:
            work[:, tile] = coef[2 * F + f, :, tile] - normal(f, u_ref[f, :, tile], tile)
        sweep_y_into(work, work, cy_ref)
        sweep_x_into(vec.at[0, f], work, cx_ref, c0_ref.at[f], -1.0)
        return carry

    lax.fori_loop(0, F, first, 0)

    def apply(index, carry):
        step, f = index // F, index % F
        sweep_x_into(work, vec.at[step, f], cx_ref)
        sweep_y_into(work, work, cy_ref)
        for tile in tiles:
            work[:, tile] = normal(f, work[:, tile], tile)
        sweep_y_into(work, work, cy_ref)
        sweep_x_into(vec.at[step + 1, f], work, cx_ref, vec.at[step, f])
        return carry

    lax.fori_loop(0, 2 * F, apply, 0)

    sums = [jnp.zeros((8, SEG), jnp.float32) for _ in range(5)]
    for f in range(F):
        r_out[f] = vec[0, f, :, :width]
        q_out[f] = vec[1, f, :, :width]
        qq_out[f] = vec[2, f, :, :width]
        for low in range(0, vec.shape[2], 8):
            for tile in tiles[:-1]:
                r = vec[0, f, low:low + 8, tile]
                q = vec[1, f, low:low + 8, tile]
                qq = vec[2, f, low:low + 8, tile]
                for i, product in enumerate((r * r, r * q, q * q, r * qq, q * qq)):
                    sums[i] = sums[i] + product
    lines = [jnp.sum(s, axis=0, keepdims=True) for s in sums]
    dots = jnp.concatenate(lines + [jnp.zeros((3, SEG), jnp.float32)], axis=0)
    for device in range(dots_out.shape[0]):
        dots_out[device] = dots


def finish_kernel(dots_ref, c0_ref, r_ref, q_ref, qq_ref, control_out, residual_out):
    dots = jnp.sum(dots_ref[...], axis=0)
    rr, rq, qq2, rqq, qqq = (dots[i:i + 1] for i in range(5))

    def total(line):
        return jnp.sum(line, axis=1, keepdims=True)

    rr_sum = total(rr)
    alpha = rr_sum / total(rq)
    new_sum = total(rr - 2.0 * alpha * rq + alpha * alpha * qq2)
    more = 1.0 + new_sum / rr_sum
    curve = total(more * more * rq - more * alpha * (rqq + qq2) + alpha * alpha * qqq)
    second = new_sum / curve
    first_weight = alpha + second * more
    both = alpha * second
    for f in range(F):
        r, q = r_ref[f], q_ref[f]
        control_out[f] = c0_ref[f] + first_weight * r - both * q
        residual_out[f] = r - first_weight * q + both * qq_ref[f]


def call(kernel, out_shape, scratch=(), in_specs=None, work=0, limit=VMEM_BYTES):
    params = {} if in_specs is None else {"in_specs": in_specs}
    return pl.pallas_call(
        kernel,
        out_shape=out_shape,
        scratch_shapes=list(scratch),
        compiler_params=pltpu.CompilerParams(vmem_limit_bytes=limit),
        cost_estimate=pl.CostEstimate(flops=work, bytes_accessed=work, transcendentals=0),
        **params,
    )


def f32(*shape):
    return jax.ShapeDtypeStruct(shape, jnp.float32)


def vmem(*shape, kind=jnp.float32):
    return pltpu.VMEM(shape, kind)


def shards(
    control_start, coef_x, coef_y, innovation, obs_weight, interp, obs_owner, cell_key, stencil
):
    groups, spans = lax.axis_size("py"), lax.axis_size("px")
    rows = innovation.shape[0]
    cap = 3 * rows // groups
    blk = SEG if cap % SEG == 0 else HALF
    nb = cap // blk
    block_rows = cap + -(-(2 * nb + 1) // 8) * 8
    chunks = rows // SEG
    nx, width = control_start.shape[2], control_start.shape[3]
    ext = width + SEG
    c0, cx = control_start[:, 0], coef_x[0]
    hbm, any_space, local = (pl.BlockSpec(memory_space=s) for s in (pltpu.HBM, pl.ANY, pltpu.VMEM))
    layout = (groups, cap, blk, block_rows)
    ints = vmem(chunks, SEG, kind=jnp.int32)

    def partners(parts):
        moves = [[(i, i ^ k) for i in range(spans)] for k in range(spans)]
        return [parts[0]] + [lax.ppermute(parts[k], "px", moves[k]) for k in range(1, spans)]

    w_packed, v_packed, first, last, *cy_parts = call(
        functools.partial(pack_kernel, *layout),
        (f32(groups * block_rows, SEG), f32(groups * cap, SEG), f32(F + 1, nx, SEG),
         f32(F + 1, nx, SEG)) + (f32(LX, ext),) * spans,
        [ints, ints, ints, vmem(chunks, SEG), vmem(rows, SEG), vmem(rows, SEG),
         vmem(*coef_y.shape[1:]), vmem(2 * chunks, SEG, kind=jnp.int32),
         pltpu.SMEM((2 * chunks, SEG), jnp.int32), pltpu.SemaphoreType.DMA((11,)),
         pltpu.SemaphoreType.DMA],
        [hbm] * 9,
        limit=PACK_BYTES,
    )(
        obs_owner.reshape(chunks, SEG), cell_key.reshape(chunks, SEG),
        stencil.reshape(chunks, SEG), interp.reshape(chunks, SEG),
        obs_weight, innovation, coef_y[0], c0, cx,
    )
    w_arrived = lax.all_to_all(w_packed, "py", split_axis=0, concat_axis=0, tiled=True)

    steps = [(i, i + 1) for i in range(spans - 1)]
    from_prev = lax.ppermute(last, "px", steps)
    from_next = lax.ppermute(first, "px", [(j, i) for i, j in steps])
    c0_ext, cx_ext, cy_ext, u_ext = call(
        start_kernel,
        (f32(F, nx, ext), f32(nx, ext), f32(nx, ext), f32(F, nx, ext)),
        work=10_000_000,
    )(c0, cx, from_prev, from_next, *partners(cy_parts))

    w_arrived, v_packed = lax.optimization_barrier((w_arrived, v_packed))
    v_arrived = lax.all_to_all(v_packed, "py", split_axis=0, concat_axis=0, tiled=True)
    side_parts = call(
        functools.partial(weights_kernel, *layout),
        (f32(2 * F, LX, ext),) * spans,
        [vmem(ROWS, 3 * SEG), vmem(2, ROWS, SEG)],
        [local, any_space],
        work=20_000_000,
    )(w_arrived, cx_ext)
    side_parts = partners(side_parts)
    sum_parts = call(
        functools.partial(products_kernel, *layout),
        (f32(F, LX, ext),) * spans,
        [vmem(ROWS, 2 * SEG), vmem(1, ROWS, SEG)],
        [local, local, any_space],
        work=10_000_000,
    )(w_arrived, v_arrived, side_parts[0])
    sum_parts = partners(sum_parts)

    r, q, qq, dots = call(
        functools.partial(solve_kernel, spans),
        (f32(F, nx, width),) * 3 + (f32(spans, 8, SEG),),
        [vmem(3, F, nx, ext), vmem(3 * F, nx, ext), vmem(nx, ext)],
        work=20_000_000,
    )(c0_ext, cx_ext, cy_ext, u_ext, *side_parts, *sum_parts)
    dots = lax.all_to_all(dots, "px", split_axis=0, concat_axis=0, tiled=True)
    dots = jnp.broadcast_to(jnp.sum(dots, axis=0), (groups, 8, SEG))
    dots = lax.all_to_all(dots, "py", split_axis=0, concat_axis=0, tiled=True)
    control, residual = call(finish_kernel, (f32(F, nx, width),) * 2)(dots, c0, r, q, qq)
    return control[:, None], residual[:, None]


def solution(mesh):
    return jax.shard_map(
        shards,
        mesh=mesh,
        in_specs=(
            P(None, "py", None, "px"),
            P("py", None, "px"),
            P("py", "px", None),
            P(("px", "py"), None),
            P(("px", "py"), None),
            P(("px", "py")),
            P(("px", "py"), None),
            P(("px", "py")),
            P(("px", "py")),
        ),
        out_specs=(P(None, "py", None, "px"), P(None, "py", None, "px")),
        check_vma=False,
    )
```

```python
import functools

import jax
import jax.numpy as jnp
from jax import lax
from jax.experimental import pallas as pl
from jax.experimental.pallas import tpu as pltpu
from jax.sharding import PartitionSpec as P

F = 2
SEG = 128
M = 4
NB = 16
LX = 16
ROWS = F * NB * LX
HALF = SEG // 2
SPLIT = 16
X_WIDTH = 256
Y_LINES = 16
VMEM_BYTES = 32 * 1024 * 1024
PACK_BYTES = 60 * 1024 * 1024


def iota(shape, axis):
    return lax.broadcasted_iota(jnp.int32, shape, axis)


def flag(condition, kind=jnp.bfloat16):
    return jnp.where(condition, 1.0, 0.0).astype(kind)


def mxu(left, right):
    return jnp.dot(left, right, preferred_element_type=jnp.float32)


def split_parts(values, count):
    parts = []
    for _ in range(count):
        part = values.astype(jnp.bfloat16)
        parts.append(part)
        values = values - part.astype(jnp.float32)
    return parts


def ends_tile(before, after):
    return jnp.where(iota(after.shape, after.ndim - 1) < HALF, after, before)


def sweep(values, coeffs, axis):
    size = values.shape[axis]
    for _ in range(M):
        flux = coeffs * (pltpu.roll(values, size - 1, axis) - values)
        values = values + flux - pltpu.roll(flux, 1, axis)
    return values


def start_copies(pairs, sems):
    copies = [pltpu.make_async_copy(*pair, sems.at[i]) for i, pair in enumerate(pairs)]
    for copy in copies:
        copy.start()
    return copies


def pack_weights_kernel(groups, cap, blk, block_rows, own_hbm, key_hbm, sten_hbm, itp_hbm, w_hbm,
                        w_out, slot_out, own_ref, key_ref, sten_ref, itp_ref, w_ref, slot_v,
                        slot_s, sems, sem):
    loads = start_copies([(own_hbm, own_ref), (key_hbm, key_ref), (sten_hbm, sten_ref),
                          (itp_hbm, itp_ref), (w_hbm, w_ref)], sems)

    def clear(o, carry):
        start = pl.multiple_of(o * block_rows, 8)
        w_out[pl.ds(start, block_rows), :] = jnp.zeros((block_rows, SEG), jnp.float32)
        return carry

    lax.fori_loop(0, groups, clear, 0)

    for load in loads[:4]:
        load.wait()
    chunks = own_ref.shape[0]
    nb = cap // blk
    own = own_ref[...]
    high = groups * chunks
    shift = chunks.bit_length() - 1
    masks = [flag(own == o, jnp.float32) for o in range(groups)]
    hits = jnp.concatenate(masks, axis=0).astype(jnp.bfloat16)
    square = (SEG, SEG)
    within = mxu(hits, flag(iota(square, 0) < iota(square, 1)))
    tallies = mxu(hits, jnp.ones(square, jnp.bfloat16)).astype(jnp.bfloat16)
    line, column = iota((high, high), 0), iota((high, high), 1)
    same = (line >> shift) == (column >> shift)
    ranks = within + mxu(flag(same & (column < line)), tallies)
    rank = sum(masks[o] * ranks[o * chunks:(o + 1) * chunks] for o in range(groups))
    rank = rank.astype(jnp.int32)
    slot_v[...] = own * block_rows + rank
    slot_out[...] = own * cap + rank
    copy = pltpu.make_async_copy(slot_v, slot_s, sem)
    copy.start()

    log = blk.bit_length() - 1
    place = own * nb + (rank >> log)
    lane = rank & (blk - 1)
    key, sten, itp = key_ref[...], sten_ref[...], itp_ref[...]
    tall = groups * nb
    meta = jnp.zeros((5 * tall, SEG), jnp.float32)
    for i in range(chunks):
        chosen = iota((tall, SEG), 0) == place[i:i + 1]
        parts = split_parts(itp[i:i + 1], 3)
        parts += [key[i:i + 1].astype(jnp.bfloat16), (sten[i:i + 1] + 1).astype(jnp.bfloat16)]
        left = [jnp.where(chosen, part.astype(jnp.float32), 0.0) for part in parts]
        right = flag(iota(square, 0) == lane[i:i + 1])
        meta = meta + lax.dot_general(
            jnp.concatenate(left, axis=0).astype(jnp.bfloat16), right,
            (((1,), (1,)), ((), ())), preferred_element_type=jnp.float32)
    shares = meta[:tall] + meta[tall:2 * tall] + meta[2 * tall:3 * tall]
    targets = meta[3 * tall:4 * tall] * LX + meta[4 * tall:]
    for o in range(groups):
        base = o * block_rows + cap
        w_out[base:base + nb, :] = shares[o * nb:(o + 1) * nb]
        w_out[base + nb:base + 2 * nb, :] = targets[o * nb:(o + 1) * nb]

    copy.wait()
    loads[4].wait()

    def place_rows(g, carry):
        weights = w_ref[pl.ds(pl.multiple_of(g * 8, 8), 8), :]
        line, lane = g // 16, (g % 16) * 8
        for i in range(8):
            w_out[pl.ds(slot_s[line, lane + i], 1), :] = weights[i:i + 1]
        return carry

    lax.fori_loop(0, w_ref.shape[0] // 8, place_rows, 0)


def pack_products_kernel(groups, cap, slot_ref, w_hbm, d_hbm, cy_hbm, c0_hbm, cx_hbm, v_out,
                         first_out, last_out, *rest):
    cy_outs, (w_ref, d_ref, cy_ref, sems) = rest[:-4], rest[-4:]
    width = c0_hbm.shape[2]
    loads = start_copies([
        (w_hbm, w_ref), (d_hbm, d_ref), (cy_hbm, cy_ref),
        (c0_hbm.at[:, :, pl.ds(0, SEG)], first_out.at[pl.ds(0, F)]),
        (cx_hbm.at[:, pl.ds(0, SEG)], first_out.at[F]),
        (c0_hbm.at[:, :, pl.ds(width - SEG, SEG)], last_out.at[pl.ds(0, F)]),
        (cx_hbm.at[:, pl.ds(width - SEG, SEG)], last_out.at[F]),
    ], sems)

    def clear(o, carry):
        start = pl.multiple_of(o * cap, 8)
        v_out[pl.ds(start, cap), :] = jnp.zeros((cap, SEG), jnp.float32)
        return carry

    lax.fori_loop(0, groups, clear, 0)

    for load in loads:
        load.wait()
    columns = cy_ref.shape[1]
    cy = cy_ref[...]
    cy_ref[...] = jnp.where(iota(cy.shape, 1) == columns - 1, 0.0, cy)
    me = lax.axis_index("px")
    for k, cy_out in enumerate(cy_outs):
        q = me ^ k
        low = pl.multiple_of(q * width, SEG)
        cy_out[:, :width] = cy_ref[:, pl.ds(low, width)]
        before = cy_ref[:, pl.ds(pl.multiple_of(jnp.maximum(low - SEG, 0), SEG), SEG)]
        after = cy_ref[:, pl.ds(pl.multiple_of(jnp.minimum(low + width, columns - SEG), SEG), SEG)]
        cy_out[:, width:] = ends_tile(jnp.where(q > 0, before, 0.0),
                                      jnp.where(q < len(cy_outs) - 1, after, 0.0))

    def place_rows(g, carry):
        start = pl.multiple_of(g * 8, 8)
        products = w_ref[pl.ds(start, 8), :] * d_ref[pl.ds(start, 8), :]
        line, lane = g // 16, (g % 16) * 8
        for i in range(8):
            v_out[pl.ds(slot_ref[line, lane + i], 1), :] = products[i:i + 1]
        return carry

    lax.fori_loop(0, w_ref.shape[0] // 8, place_rows, 0)


def sum_rows(groups, cap, blk, block_rows, w_ref, acc_ref, terms):
    nb = cap // blk
    acc_ref[...] = jnp.zeros_like(acc_ref)
    numbers = 1.0 + iota((ROWS, cap), 0).astype(jnp.float32)

    def source_rows(source, carry):
        start = pl.multiple_of(source * block_rows + cap, 8)
        meta = w_ref[pl.ds(start, 8), :]
        upper = jnp.concatenate(
            [jnp.broadcast_to(meta[i:i + 1], (SEG, SEG)).T[:blk] for i in range(nb)], axis=0)
        target = jnp.concatenate([meta[nb + i:nb + i + 1, :blk] for i in range(nb)], axis=1)
        hit = flag(numbers == target)
        values = jnp.concatenate(terms(source, upper), axis=1)
        acc_ref[...] += mxu(
            jnp.concatenate([hit, hit], axis=1),
            jnp.concatenate(split_parts(values, 2), axis=0))
        return carry

    lax.fori_loop(0, groups, source_rows, 0, unroll=2)


def cut_parts(stage_ref, outs):
    width = outs[0].shape[2] - SEG
    per = width // SEG
    me = lax.axis_index("px")
    for k, out in enumerate(outs):
        q = me ^ k
        for channel in range(stage_ref.shape[0]):
            for f in range(F):
                def tile(b):
                    start = pl.multiple_of((f * NB + b) * LX, LX)
                    return stage_ref[channel, pl.ds(start, LX), :]

                to = out.at[channel * F + f]
                for j in range(per):
                    to[:, j * SEG:(j + 1) * SEG] = tile(q * per + j)
                before = tile(jnp.maximum(q * per - 1, 0))
                after = tile(jnp.minimum(q * per + per, NB - 1))
                to[:, width:] = ends_tile(jnp.where(q > 0, before, 0.0),
                                          jnp.where(q < len(outs) - 1, after, 0.0))


def weights_kernel(groups, cap, blk, block_rows, w_ref, tie_ref, *rest):
    outs, acc_ref, stage_ref = rest[:-2], rest[-2], rest[-1]

    def terms(source, upper):
        lower = 1.0 - upper
        weights = w_ref[pl.ds(pl.multiple_of(source * block_rows, 8), cap), :]
        lower_w, upper_w = lower * weights, upper * weights
        return [lower * lower_w, upper * lower_w, upper * upper_w]

    sum_rows(groups, cap, blk, block_rows, w_ref, acc_ref, terms)
    stage_ref[0] = acc_ref[:, :SEG] + pltpu.roll(acc_ref[:, 2 * SEG:], 1, 0)
    stage_ref[1] = acc_ref[:, SEG:2 * SEG]
    cut_parts(stage_ref, outs)


def products_kernel(groups, cap, blk, block_rows, w_ref, v_ref, *rest):
    outs, acc_ref, stage_ref = rest[:-2], rest[-2], rest[-1]

    def terms(source, upper):
        products = v_ref[pl.ds(pl.multiple_of(source * cap, 8), cap), :]
        return [(1.0 - upper) * products, upper * products]

    sum_rows(groups, cap, blk, block_rows, w_ref, acc_ref, terms)
    stage_ref[0] = acc_ref[:, :SEG] + pltpu.roll(acc_ref[:, SEG:], 1, 0)
    cut_parts(stage_ref, outs)


def sweep_x_into(to_ref, from_ref, cx_ref, plus_ref=None, sign=1.0):
    size = cx_ref.shape[1]
    for low in range(0, size, X_WIDTH):
        tile = slice(low, min(low + X_WIDTH, size))
        values = sweep(from_ref[:, tile], cx_ref[:, tile], 0)
        if plus_ref is not None:
            values = values + sign * plus_ref[:, tile]
        to_ref[:, tile] = values


def sweep_y_into(to_ref, from_ref, cy_ref):
    for low in range(0, cy_ref.shape[0], Y_LINES):
        lines = slice(low, low + Y_LINES)
        to_ref[lines, :] = sweep(from_ref[lines, :], cy_ref[lines, :], 1)


def start_kernel(c0_ref, cx_ref, prev_ref, next_ref, *rest):
    cy_refs, (c0_out, cx_out, cy_out, u_out) = rest[:-4], rest[-4:]
    width = c0_ref.shape[2]
    me = lax.axis_index("px")
    for k, cy_ref in enumerate(cy_refs):
        cy_out[pl.ds(pl.multiple_of((me ^ k) * LX, LX), LX), :] = cy_ref[...]
    last = cx_ref.shape[0] - 1
    cx_out[:, :width] = cx_ref[...]
    cx_out[:, width:] = ends_tile(prev_ref[F], next_ref[F])
    cx_out[last:, :] = jnp.zeros((1, width + SEG), jnp.float32)
    for f in range(F):
        c0_out[f, :, :width] = c0_ref[f]
        c0_out[f, :, width:] = ends_tile(prev_ref[f], next_ref[f])
        sweep_x_into(u_out.at[f], c0_out.at[f], cx_out)
        sweep_y_into(u_out.at[f], u_out.at[f], cy_out)


def solve_kernel(spans, c0_ref, cx_ref, cy_ref, u_ref, *rest):
    side_refs, sum_refs = rest[:spans], rest[spans:2 * spans]
    r_out, q_out, qq_out, dots_out, vec, coef, work = rest[2 * spans:]
    width = r_out.shape[2]
    me = lax.axis_index("px")
    for k in range(spans):
        rows = pl.ds(pl.multiple_of((me ^ k) * LX, LX), LX)
        for channel in range(2 * F):
            coef[channel, rows, :] = side_refs[k][channel]
        for f in range(F):
            coef[2 * F + f, rows, :] = sum_refs[k][f]

    def normal(f, values, tile):
        size = values.shape[0]
        side = coef[F + f, :, tile]
        return (coef[f, :, tile] * values + side * pltpu.roll(values, size - 1, 0)
                + pltpu.roll(side * values, 1, 0))

    tiles = [slice(low, low + SEG) for low in range(0, width + SEG, SEG)]

    def first(f, carry):
        for tile in tiles:
            work[:, tile] = coef[2 * F + f, :, tile] - normal(f, u_ref[f, :, tile], tile)
        sweep_y_into(work, work, cy_ref)
        sweep_x_into(vec.at[0, f], work, cx_ref, c0_ref.at[f], -1.0)
        return carry

    lax.fori_loop(0, F, first, 0)

    def apply(index, carry):
        step, f = index // F, index % F
        sweep_x_into(work, vec.at[step, f], cx_ref)
        sweep_y_into(work, work, cy_ref)
        for tile in tiles:
            work[:, tile] = normal(f, work[:, tile], tile)
        sweep_y_into(work, work, cy_ref)
        sweep_x_into(vec.at[step + 1, f], work, cx_ref, vec.at[step, f])
        return carry

    lax.fori_loop(0, 2 * F, apply, 0)

    sums = [jnp.zeros((8, SEG), jnp.float32) for _ in range(5)]
    for f in range(F):
        r_out[f] = vec[0, f, :, :width]
        q_out[f] = vec[1, f, :, :width]
        qq_out[f] = vec[2, f, :, :width]
        for low in range(0, vec.shape[2], 8):
            for tile in tiles[:-1]:
                r = vec[0, f, low:low + 8, tile]
                q = vec[1, f, low:low + 8, tile]
                qq = vec[2, f, low:low + 8, tile]
                for i, product in enumerate((r * r, r * q, q * q, r * qq, q * qq)):
                    sums[i] = sums[i] + product
    dots = jnp.zeros((1, SEG), jnp.float32)
    for i, total in enumerate(sums):
        line = jnp.sum(total, axis=0, keepdims=True)
        for distance in (64, 32, 16):
            line = line + pltpu.roll(line, distance, 1)
        dots = jnp.where(iota((1, SEG), 1) // SPLIT == i, line, dots)
    dots_out[...] = jnp.broadcast_to(dots, dots_out.shape)


def finish_kernel(dots_ref, c0_ref, r_ref, q_ref, qq_ref, control_out, residual_out):
    dots = jnp.sum(dots_ref[...], axis=0)
    lane = iota((1, SEG), 1)
    rr, rq, qq2, rqq, qqq = (pltpu.roll(dots, (SEG - i * SPLIT) % SEG, 1) for i in range(5))

    def total(line):
        return jnp.sum(jnp.where(lane < SPLIT, line, 0.0), axis=1, keepdims=True)

    rr_sum = total(rr)
    alpha = rr_sum / total(rq)
    new_sum = total(rr - 2.0 * alpha * rq + alpha * alpha * qq2)
    more = 1.0 + new_sum / rr_sum
    curve = total(more * more * rq - more * alpha * (rqq + qq2) + alpha * alpha * qqq)
    second = new_sum / curve
    first_weight = alpha + second * more
    both = alpha * second
    for f in range(F):
        r, q = r_ref[f], q_ref[f]
        control_out[f] = c0_ref[f] + first_weight * r - both * q
        residual_out[f] = r - first_weight * q + both * qq_ref[f]


def call(kernel, out_shape, scratch=(), in_specs=None, work=0, limit=VMEM_BYTES):
    params = {} if in_specs is None else {"in_specs": in_specs}
    return pl.pallas_call(
        kernel,
        out_shape=out_shape,
        scratch_shapes=list(scratch),
        compiler_params=pltpu.CompilerParams(vmem_limit_bytes=limit),
        cost_estimate=pl.CostEstimate(flops=work, bytes_accessed=work, transcendentals=0),
        **params,
    )


def f32(*shape):
    return jax.ShapeDtypeStruct(shape, jnp.float32)


def vmem(*shape, kind=jnp.float32):
    return pltpu.VMEM(shape, kind)


def shards(
    control_start, coef_x, coef_y, innovation, obs_weight, interp, obs_owner, cell_key, stencil
):
    groups, spans = lax.axis_size("py"), lax.axis_size("px")
    rows = innovation.shape[0]
    cap = 3 * rows // groups
    blk = SEG if cap % SEG == 0 else HALF
    nb = cap // blk
    block_rows = cap + -(-2 * nb // 8) * 8
    chunks = rows // SEG
    nx, width = control_start.shape[2], control_start.shape[3]
    ext = width + SEG
    c0, cx = control_start[:, 0], coef_x[0]
    hbm, any_space, local, scalars = (
        pl.BlockSpec(memory_space=s) for s in (pltpu.HBM, pl.ANY, pltpu.VMEM, pltpu.SMEM))
    layout = (groups, cap, blk, block_rows)
    ints = vmem(chunks, SEG, kind=jnp.int32)

    def partners(parts):
        moves = [[(i, i ^ k) for i in range(spans)] for k in range(spans)]
        return [parts[0]] + [lax.ppermute(parts[k], "px", moves[k]) for k in range(1, spans)]

    w_packed, slots = call(
        functools.partial(pack_weights_kernel, *layout),
        (f32(groups * block_rows, SEG), jax.ShapeDtypeStruct((chunks, SEG), jnp.int32)),
        [ints, ints, ints, vmem(chunks, SEG), vmem(rows, SEG), ints,
         pltpu.SMEM((chunks, SEG), jnp.int32), pltpu.SemaphoreType.DMA((5,)),
         pltpu.SemaphoreType.DMA],
        [hbm] * 5,
        limit=PACK_BYTES,
    )(
        obs_owner.reshape(chunks, SEG), cell_key.reshape(chunks, SEG),
        stencil.reshape(chunks, SEG), interp.reshape(chunks, SEG), obs_weight,
    )
    v_packed, first, last, *cy_parts = call(
        functools.partial(pack_products_kernel, groups, cap),
        (f32(groups * cap, SEG), f32(F + 1, nx, SEG), f32(F + 1, nx, SEG))
        + (f32(LX, ext),) * spans,
        [vmem(rows, SEG), vmem(rows, SEG), vmem(*coef_y.shape[1:]),
         pltpu.SemaphoreType.DMA((7,))],
        [scalars] + [hbm] * 5,
        work=20_000_000,
        limit=PACK_BYTES,
    )(slots, obs_weight, innovation, coef_y[0], c0, cx)
    w_arrived = lax.all_to_all(w_packed, "py", split_axis=0, concat_axis=0, tiled=True)

    steps = [(i, i + 1) for i in range(spans - 1)]
    from_prev = lax.ppermute(last, "px", steps)
    from_next = lax.ppermute(first, "px", [(j, i) for i, j in steps])
    c0_ext, cx_ext, cy_ext, u_ext = call(
        start_kernel,
        (f32(F, nx, ext), f32(nx, ext), f32(nx, ext), f32(F, nx, ext)),
        work=10_000_000,
    )(c0, cx, from_prev, from_next, *partners(cy_parts))

    w_arrived, v_packed = lax.optimization_barrier((w_arrived, v_packed))
    v_arrived = lax.all_to_all(v_packed, "py", split_axis=0, concat_axis=0, tiled=True)
    side_parts = call(
        functools.partial(weights_kernel, *layout),
        (f32(2 * F, LX, ext),) * spans,
        [vmem(ROWS, 3 * SEG), vmem(2, ROWS, SEG)],
        [local, any_space],
        work=20_000_000,
    )(w_arrived, cx_ext)
    side_parts = partners(side_parts)
    sum_parts = call(
        functools.partial(products_kernel, *layout),
        (f32(F, LX, ext),) * spans,
        [vmem(ROWS, 2 * SEG), vmem(1, ROWS, SEG)],
        work=10_000_000,
    )(w_arrived, v_arrived)
    sum_parts = partners(sum_parts)

    r, q, qq, dots = call(
        functools.partial(solve_kernel, spans),
        (f32(F, nx, width),) * 3 + (f32(groups * spans, 1, SEG),),
        [vmem(3, F, nx, ext), vmem(3 * F, nx, ext), vmem(nx, ext)],
        work=20_000_000,
    )(c0_ext, cx_ext, cy_ext, u_ext, *side_parts, *sum_parts)
    dots = lax.all_to_all(dots, ("px", "py"), split_axis=0, concat_axis=0, tiled=True)
    control, residual = call(finish_kernel, (f32(F, nx, width),) * 2)(dots, c0, r, q, qq)
    return control[:, None], residual[:, None]


def solution(mesh):
    return jax.shard_map(
        shards,
        mesh=mesh,
        in_specs=(
            P(None, "py", None, "px"),
            P("py", None, "px"),
            P("py", "px", None),
            P(("px", "py"), None),
            P(("px", "py"), None),
            P(("px", "py")),
            P(("px", "py"), None),
            P(("px", "py")),
            P(("px", "py")),
        ),
        out_specs=(P(None, "py", None, "px"), P(None, "py", None, "px")),
        check_vma=False,
    )
```

```python
import functools

import jax
import jax.numpy as jnp
from jax import lax
from jax.experimental import pallas as pl
from jax.experimental.pallas import tpu as pltpu
from jax.sharding import PartitionSpec as P

F = 2
SEG = 128
M = 4
NB = 16
LX = 16
ROWS = F * NB * LX
HALF = SEG // 2
SPLIT = 16
X_WIDTH = 256
Y_LINES = 16
VMEM_BYTES = 32 * 1024 * 1024
PACK_BYTES = 60 * 1024 * 1024


def iota(shape, axis):
    return lax.broadcasted_iota(jnp.int32, shape, axis)


def flag(condition, kind=jnp.bfloat16):
    return jnp.where(condition, 1.0, 0.0).astype(kind)


def mxu(left, right):
    return jnp.dot(left, right, preferred_element_type=jnp.float32)


def split_parts(values, count):
    parts = []
    for _ in range(count):
        part = values.astype(jnp.bfloat16)
        parts.append(part)
        values = values - part.astype(jnp.float32)
    return parts


def ends_tile(before, after):
    return jnp.where(iota(after.shape, after.ndim - 1) < HALF, after, before)


def sweep(values, coeffs, axis):
    size = values.shape[axis]
    for _ in range(M):
        flux = coeffs * (pltpu.roll(values, size - 1, axis) - values)
        values = values + flux - pltpu.roll(flux, 1, axis)
    return values


def start_copies(pairs, sems):
    copies = [pltpu.make_async_copy(*pair, sems.at[i]) for i, pair in enumerate(pairs)]
    for copy in copies:
        copy.start()
    return copies


def pack_weights_kernel(groups, cap, blk, block_rows, own_hbm, key_hbm, sten_hbm, itp_hbm, w_hbm,
                        *rest):
    half = groups // 2
    outs, rest = rest[:half], rest[half:]
    (slot_out, own_ref, key_ref, sten_ref, itp_ref, w_ref, buffer, slot_v, slot_s, sems, out_sems,
     sem) = rest
    loads = start_copies([(own_hbm, own_ref), (key_hbm, key_ref), (sten_hbm, sten_ref),
                          (itp_hbm, itp_ref), (w_hbm, w_ref)], sems)

    def clear(k, carry):
        start = pl.multiple_of(k * block_rows, 8)
        buffer[pl.ds(start, block_rows), :] = jnp.zeros((block_rows, SEG), jnp.float32)
        return carry

    lax.fori_loop(0, half, clear, 0)

    for load in loads[:4]:
        load.wait()
    chunks = own_ref.shape[0]
    nb = cap // blk
    own = own_ref[...]
    high = groups * chunks
    shift = chunks.bit_length() - 1
    masks = [flag(own == o, jnp.float32) for o in range(groups)]
    hits = jnp.concatenate(masks, axis=0).astype(jnp.bfloat16)
    square = (SEG, SEG)
    within = mxu(hits, flag(iota(square, 0) < iota(square, 1)))
    tallies = mxu(hits, jnp.ones(square, jnp.bfloat16)).astype(jnp.bfloat16)
    line, column = iota((high, high), 0), iota((high, high), 1)
    same = (line >> shift) == (column >> shift)
    ranks = within + mxu(flag(same & (column < line)), tallies)
    rank = sum(masks[o] * ranks[o * chunks:(o + 1) * chunks] for o in range(groups))
    rank = rank.astype(jnp.int32)
    relative = own ^ lax.axis_index("py")
    block, across = relative & (half - 1), relative >> (half.bit_length() - 1)
    slot_v[...] = block * block_rows + across * cap + rank
    slot_out[...] = (block * 2 + across) * cap + rank
    copy = pltpu.make_async_copy(slot_v, slot_s, sem)
    copy.start()

    log = blk.bit_length() - 1
    place = relative * nb + (rank >> log)
    lane = rank & (blk - 1)
    key, sten, itp = key_ref[...], sten_ref[...], itp_ref[...]
    tall = groups * nb
    meta = jnp.zeros((5 * tall, SEG), jnp.float32)
    for i in range(chunks):
        chosen = iota((tall, SEG), 0) == place[i:i + 1]
        parts = split_parts(itp[i:i + 1], 3)
        parts += [key[i:i + 1].astype(jnp.bfloat16), (sten[i:i + 1] + 1).astype(jnp.bfloat16)]
        left = [jnp.where(chosen, part.astype(jnp.float32), 0.0) for part in parts]
        right = flag(iota(square, 0) == lane[i:i + 1])
        meta = meta + lax.dot_general(
            jnp.concatenate(left, axis=0).astype(jnp.bfloat16), right,
            (((1,), (1,)), ((), ())), preferred_element_type=jnp.float32)
    shares = meta[:tall] + meta[tall:2 * tall] + meta[2 * tall:3 * tall]
    targets = meta[3 * tall:4 * tall] * LX + meta[4 * tall:]
    for v in range(groups):
        base = (v % half) * block_rows + 2 * cap + (v // half) * 2 * nb
        buffer[base:base + nb, :] = shares[v * nb:(v + 1) * nb]
        buffer[base + nb:base + 2 * nb, :] = targets[v * nb:(v + 1) * nb]

    copy.wait()
    loads[4].wait()

    def place_rows(g, carry):
        weights = w_ref[pl.ds(pl.multiple_of(g * 8, 8), 8), :]
        line, lane = g // 16, (g % 16) * 8
        for i in range(8):
            buffer[pl.ds(slot_s[line, lane + i], 1), :] = weights[i:i + 1]
        return carry

    lax.fori_loop(0, w_ref.shape[0] // 8, place_rows, 0)
    for store in start_copies([(buffer.at[pl.ds(k * block_rows, block_rows)], out)
                               for k, out in enumerate(outs)], out_sems):
        store.wait()


def pack_products_kernel(groups, cap, slot_ref, w_hbm, d_hbm, cy_hbm, c0_hbm, cx_hbm, *rest):
    half = groups // 2
    outs, (swap_out, w_ref, d_ref, cy_ref, first, last, buffer, sems, out_sems) = (
        rest[:half], rest[half:])
    width = c0_hbm.shape[2]
    loads = start_copies([
        (w_hbm, w_ref), (d_hbm, d_ref), (cy_hbm, cy_ref),
        (c0_hbm.at[:, :, pl.ds(0, SEG)], first.at[pl.ds(0, F)]),
        (cx_hbm.at[:, pl.ds(0, SEG)], first.at[F]),
        (c0_hbm.at[:, :, pl.ds(width - SEG, SEG)], last.at[pl.ds(0, F)]),
        (cx_hbm.at[:, pl.ds(width - SEG, SEG)], last.at[F]),
    ], sems)

    def clear(o, carry):
        start = pl.multiple_of(o * cap, 8)
        buffer[pl.ds(start, cap), :] = jnp.zeros((cap, SEG), jnp.float32)
        return carry

    lax.fori_loop(0, groups, clear, 0)

    for load in loads:
        load.wait()

    def place_rows(g, carry):
        start = pl.multiple_of(g * 8, 8)
        products = w_ref[pl.ds(start, 8), :] * d_ref[pl.ds(start, 8), :]
        line, lane = g // 16, (g % 16) * 8
        for i in range(8):
            buffer[pl.ds(slot_ref[line, lane + i], 1), :] = products[i:i + 1]
        return carry

    lax.fori_loop(0, w_ref.shape[0] // 8, place_rows, 0)
    stores = start_copies([(buffer.at[pl.ds(k * 2 * cap, 2 * cap)], out)
                           for k, out in enumerate(outs)], out_sems)
    columns = cy_ref.shape[1]
    cy = cy_ref[...]
    cy = jnp.where(iota(cy.shape, 1) == columns - 1, 0.0, cy)
    empty = jnp.zeros((LX, SEG), jnp.float32)
    me = lax.axis_index("px")
    nx = first.shape[1]
    for q in range(columns // width):
        low, top = q * width, (q + 1) * width
        tiles = [cy[:, t:t + SEG] for t in range(low, top, SEG)]
        before = cy[:, low - SEG:low] if low > 0 else empty
        after = cy[:, top:top + SEG] if top < columns else empty
        tiles.append(ends_tile(before, after))
        for t, tile in enumerate(tiles):
            swap_out[q, t * LX:(t + 1) * LX, :] = tile
        base = len(tiles) * LX
        for i in range(F + 1):
            swap_out[q, base + i * nx:base + (i + 1) * nx, :] = jnp.where(
                q < me, first[i], last[i])
    for store in stores:
        store.wait()


def sum_rows(cap, blk, metas, acc_ref, terms):
    nb = cap // blk
    numbers = 1.0 + iota((ROWS, cap), 0).astype(jnp.float32)
    for source, meta in enumerate(metas):
        upper = jnp.concatenate(
            [jnp.broadcast_to(meta[i:i + 1], (SEG, SEG)).T[:blk] for i in range(nb)], axis=0)
        target = jnp.concatenate([meta[nb + i:nb + i + 1, :blk] for i in range(nb)], axis=1)
        hit = flag(numbers == target)
        values = jnp.concatenate(terms(source, upper), axis=1)
        part = mxu(jnp.concatenate([hit, hit], axis=1),
                   jnp.concatenate(split_parts(values, 2), axis=0))
        if source:
            acc_ref[...] += part
        else:
            acc_ref[...] = part


def cut_part(rows_ref, to, f, q, spans):
    width = to.shape[1] - SEG
    per = width // SEG

    def tile(b):
        start = pl.multiple_of((f * NB + b) * LX, LX)
        return rows_ref[pl.ds(start, LX), :]

    for j in range(per):
        to[:, j * SEG:(j + 1) * SEG] = tile(q * per + j)
    before = tile(jnp.maximum(q * per - 1, 0))
    after = tile(jnp.minimum(q * per + per, NB - 1))
    to[:, width:] = ends_tile(jnp.where(q > 0, before, 0.0),
                              jnp.where(q < spans - 1, after, 0.0))


def weights_kernel(half, cap, blk, across, *rest):
    w_refs, (_, meta_out, out, acc_ref) = rest[:half], rest[half:]
    nb = cap // blk
    for k, w_ref in enumerate(w_refs):
        meta_out[k] = w_ref[2 * cap:, :]
    rows = slice(across * cap, (across + 1) * cap)

    def terms(source, upper):
        lower = 1.0 - upper
        weights = w_refs[source][rows, :]
        lower_w, upper_w = lower * weights, upper * weights
        return [lower * lower_w, upper * lower_w, upper * upper_w]

    low = 2 * cap + across * 2 * nb
    sum_rows(cap, blk, [w_ref[low:low + 2 * nb, :] for w_ref in w_refs], acc_ref, terms)
    out[0] = acc_ref[:, :SEG] + pltpu.roll(acc_ref[:, 2 * SEG:], 1, 0)
    out[1] = acc_ref[:, SEG:2 * SEG]


def sum_products(half, cap, blk, across, meta_ref, v_refs, acc_ref, sums_ref):
    nb = cap // blk
    rows = slice(across * cap, (across + 1) * cap)

    def terms(source, upper):
        products = v_refs[source][rows, :]
        return [(1.0 - upper) * products, upper * products]

    low = across * 2 * nb
    sum_rows(cap, blk, [meta_ref[k, low:low + 2 * nb, :] for k in range(half)], acc_ref, terms)
    sums_ref[...] = acc_ref[:, :SEG] + pltpu.roll(acc_ref[:, SEG:], 1, 0)


def products_across_kernel(half, cap, blk, meta_ref, *rest):
    v_refs, (*outs, acc_ref, sums_ref) = rest[:half], rest[half:]
    sum_products(half, cap, blk, 1, meta_ref, v_refs, acc_ref, sums_ref)
    me = lax.axis_index("px")
    for k, out in enumerate(outs):
        for f in range(F):
            cut_part(sums_ref, out.at[f], f, me ^ k, len(outs))


def products_kernel(half, cap, blk, meta_ref, side_ref, other_ref, *rest):
    v_refs, (out, acc_ref, sums_ref, side) = rest[:half], rest[half:]
    spans = out.shape[0]
    sum_products(half, cap, blk, 0, meta_ref, v_refs, acc_ref, sums_ref)
    side[...] = side_ref[...] + other_ref[...]
    for q in range(spans):
        for channel, rows_ref in enumerate((side.at[0], side.at[1], sums_ref)):
            for f in range(F):
                cut_part(rows_ref, out.at[q, channel * F + f], f, q, spans)


def sweep_x_into(to_ref, from_ref, cx_ref, plus_ref=None, sign=1.0):
    size = cx_ref.shape[1]
    for low in range(0, size, X_WIDTH):
        tile = slice(low, min(low + X_WIDTH, size))
        values = sweep(from_ref[:, tile], cx_ref[:, tile], 0)
        if plus_ref is not None:
            values = values + sign * plus_ref[:, tile]
        to_ref[:, tile] = values


def sweep_y_into(to_ref, from_ref, cy_ref):
    for low in range(0, cy_ref.shape[0], Y_LINES):
        lines = slice(low, low + Y_LINES)
        to_ref[lines, :] = sweep(from_ref[lines, :], cy_ref[lines, :], 1)


def start_kernel(c0_ref, cx_ref, swap_ref, c0_out, cx_out, cy_out, u_out):
    width = c0_ref.shape[2]
    nx = cx_ref.shape[0]
    spans, count = swap_ref.shape[0], cy_out.shape[1] // SEG
    me = lax.axis_index("px")
    for p in range(spans):
        for t in range(count):
            cy_out[p * LX:(p + 1) * LX, t * SEG:(t + 1) * SEG] = (
                swap_ref[p, t * LX:(t + 1) * LX, :])

    def beside(i):
        lines = slice(count * LX + i * nx, count * LX + (i + 1) * nx)
        before = swap_ref[jnp.maximum(me - 1, 0), lines, :]
        after = swap_ref[jnp.minimum(me + 1, spans - 1), lines, :]
        return ends_tile(jnp.where(me > 0, before, 0.0), jnp.where(me < spans - 1, after, 0.0))

    last = cx_ref.shape[0] - 1
    cx_out[:, :width] = cx_ref[...]
    cx_out[:, width:] = beside(F)
    cx_out[last:, :] = jnp.zeros((1, width + SEG), jnp.float32)
    for f in range(F):
        c0_out[f, :, :width] = c0_ref[f]
        c0_out[f, :, width:] = beside(f)
        sweep_x_into(u_out.at[f], c0_out.at[f], cx_out)
        sweep_y_into(u_out.at[f], u_out.at[f], cy_out)


def solve_kernel(spans, c0_ref, cx_ref, cy_ref, u_ref, obs_ref, *rest):
    sum_refs, (r_out, q_out, h_out, dots_out, vec, coef, work) = rest[:spans], rest[spans:]
    width = r_out.shape[2]
    for p in range(spans):
        for channel in range(3 * F):
            coef[channel, p * LX:(p + 1) * LX, :] = obs_ref[p, channel]
    me = lax.axis_index("px")
    for k in range(spans):
        rows = pl.ds(pl.multiple_of((me ^ k) * LX, LX), LX)
        for f in range(F):
            coef[2 * F + f, rows, :] += sum_refs[k][f]

    def normal(f, values, tile):
        size = values.shape[0]
        side = coef[F + f, :, tile]
        return (coef[f, :, tile] * values + side * pltpu.roll(values, size - 1, 0)
                + pltpu.roll(side * values, 1, 0))

    tiles = [slice(low, low + SEG) for low in range(0, width + SEG, SEG)]

    def first(f, carry):
        for tile in tiles:
            work[:, tile] = coef[2 * F + f, :, tile] - normal(f, u_ref[f, :, tile], tile)
        sweep_y_into(work, work, cy_ref)
        sweep_x_into(vec.at[0, f], work, cx_ref, c0_ref.at[f], -1.0)
        return carry

    lax.fori_loop(0, F, first, 0)

    def apply(f, carry):
        sweep_x_into(work, vec.at[0, f], cx_ref)
        sweep_y_into(work, work, cy_ref)
        for tile in tiles:
            work[:, tile] = normal(f, work[:, tile], tile)
        sweep_y_into(work, work, cy_ref)
        sweep_x_into(vec.at[1, f], work, cx_ref, vec.at[0, f])
        sweep_x_into(vec.at[2, f], vec.at[1, f], cx_ref)
        sweep_y_into(vec.at[2, f], vec.at[2, f], cy_ref)
        for tile in tiles:
            h_out[f, :, tile] = normal(f, vec[2, f, :, tile], tile)
        return carry

    lax.fori_loop(0, F, apply, 0)

    sums = [jnp.zeros((8, SEG), jnp.float32) for _ in range(4)]
    for f in range(F):
        r_out[f] = vec[0, f, :, :width]
        q_out[f] = vec[1, f, :, :width]
        for low in range(0, vec.shape[2], 8):
            for tile in tiles[:-1]:
                r = vec[0, f, low:low + 8, tile]
                q = vec[1, f, low:low + 8, tile]
                s = vec[2, f, low:low + 8, tile]
                for i, product in enumerate((r * r, r * q, q * q, s * h_out[f, low:low + 8, tile])):
                    sums[i] = sums[i] + product
    dots = jnp.zeros((1, SEG), jnp.float32)
    for i, total in enumerate(sums):
        line = jnp.sum(total, axis=0, keepdims=True)
        for distance in (64, 32, 16):
            line = line + pltpu.roll(line, distance, 1)
        dots = jnp.where(iota((1, SEG), 1) // SPLIT == i, line, dots)
    dots_out[...] = jnp.broadcast_to(dots, dots_out.shape)


def last_kernel(h_ref, q_ref, cx_ref, cy_ref, qq_out, work, other):
    width = qq_out.shape[2]

    def apply(f, carry):
        sweep_y_into(work, h_ref.at[f], cy_ref)
        sweep_x_into(other, work, cx_ref)
        qq_out[f] = q_ref[f] + other[:, :width]
        return carry

    lax.fori_loop(0, F, apply, 0)


def finish_kernel(dots_ref, c0_ref, r_ref, q_ref, qq_ref, control_out, residual_out):
    dots = jnp.sum(dots_ref[...], axis=0)
    lane = iota((1, SEG), 1)
    rr, rq, qq2, energy = (pltpu.roll(dots, (SEG - i * SPLIT) % SEG, 1) for i in range(4))

    def total(line):
        return jnp.sum(jnp.where(lane < SPLIT, line, 0.0), axis=1, keepdims=True)

    rr_sum = total(rr)
    alpha = rr_sum / total(rq)
    new_sum = total(rr - 2.0 * alpha * rq + alpha * alpha * qq2)
    more = 1.0 + new_sum / rr_sum
    curve = total(more * more * rq - 2.0 * more * alpha * qq2 + alpha * alpha * (qq2 + energy))
    second = new_sum / curve
    first_weight = alpha + second * more
    both = alpha * second
    for f in range(F):
        r, q = r_ref[f], q_ref[f]
        control_out[f] = c0_ref[f] + first_weight * r - both * q
        residual_out[f] = r - first_weight * q + both * qq_ref[f]


def call(kernel, out_shape, scratch=(), in_specs=None, out_specs=None, limit=VMEM_BYTES):
    params = {"in_specs": in_specs, "out_specs": out_specs}
    return pl.pallas_call(
        kernel,
        out_shape=out_shape,
        scratch_shapes=list(scratch),
        compiler_params=pltpu.CompilerParams(vmem_limit_bytes=limit),
        **{name: value for name, value in params.items() if value is not None},
    )


def f32(*shape):
    return jax.ShapeDtypeStruct(shape, jnp.float32)


def vmem(*shape, kind=jnp.float32):
    return pltpu.VMEM(shape, kind)


def shards(
    control_start, coef_x, coef_y, innovation, obs_weight, interp, obs_owner, cell_key, stencil
):
    groups, spans = lax.axis_size("py"), lax.axis_size("px")
    half = groups // 2
    rows = innovation.shape[0]
    cap = 3 * rows // groups
    blk = SEG if cap % SEG == 0 else HALF
    meta_rows = -(-4 * (cap // blk) // 8) * 8
    block_rows = 2 * cap + meta_rows
    chunks = rows // SEG
    nx, width = control_start.shape[2], control_start.shape[3]
    ext = width + SEG
    c0, cx = control_start[:, 0], coef_x[0]
    hbm, any_space, local, scalars = (
        pl.BlockSpec(memory_space=s) for s in (pltpu.HBM, pl.ANY, pltpu.VMEM, pltpu.SMEM))
    ints = vmem(chunks, SEG, kind=jnp.int32)
    dma = pltpu.SemaphoreType.DMA

    def to_half(block, k):
        return lax.ppermute(block, "py", [(i, i ^ k) for i in range(groups)])

    def across(parts):
        return [
            lax.ppermute(parts[k], ("px", "py"), [
                (i * groups + j, (i ^ k) * groups + (j ^ half))
                for i in range(spans) for j in range(groups)])
            for k in range(spans)]

    *w_blocks, slots = call(
        functools.partial(pack_weights_kernel, groups, cap, blk, block_rows),
        (f32(block_rows, SEG),) * half + (jax.ShapeDtypeStruct((chunks, SEG), jnp.int32),),
        [ints, ints, ints, vmem(chunks, SEG), vmem(rows, SEG), vmem(half * block_rows, SEG), ints,
         pltpu.SMEM((chunks, SEG), jnp.int32), dma((5,)), dma((half,)), dma],
        [hbm] * 5,
        (hbm,) * half + (local,),
        limit=PACK_BYTES,
    )(
        obs_owner.reshape(chunks, SEG), cell_key.reshape(chunks, SEG),
        stencil.reshape(chunks, SEG), interp.reshape(chunks, SEG), obs_weight,
    )
    *v_blocks, swap = call(
        functools.partial(pack_products_kernel, groups, cap),
        (f32(2 * cap, SEG),) * half + (f32(spans, LX * ext // SEG + (F + 1) * nx, SEG),),
        [vmem(rows, SEG), vmem(rows, SEG), vmem(*coef_y.shape[1:]), vmem(F + 1, nx, SEG),
         vmem(F + 1, nx, SEG), vmem(groups * cap, SEG), dma((7,)), dma((half,))],
        [scalars] + [hbm] * 5,
        (hbm,) * half + (local,),
        limit=PACK_BYTES,
    )(slots, obs_weight, innovation, coef_y[0], c0, cx)
    for k in range(1, half):
        w_blocks[k], v_blocks[k] = lax.optimization_barrier((to_half(w_blocks[k], k), v_blocks[k]))
        v_blocks[k] = to_half(v_blocks[k], k)

    swap = lax.all_to_all(swap, "px", split_axis=0, concat_axis=0, tiled=True)
    c0_ext, cx_ext, cy_ext, u_ext = call(
        start_kernel,
        (f32(F, nx, ext), f32(nx, ext), f32(nx, ext), f32(F, nx, ext)),
    )(c0, cx, swap)

    def sum_weights(side, tie):
        return call(
            functools.partial(weights_kernel, half, cap, blk, side),
            (f32(half, meta_rows, SEG), f32(2, ROWS, SEG)),
            [vmem(ROWS, 3 * SEG)],
            [local] * half + [any_space],
        )(*w_blocks, tie)

    meta, side_across = sum_weights(1, slots)
    side_across = to_half(side_across, half)
    _, side = sum_weights(0, cx_ext)
    sums_across = across(call(
        functools.partial(products_across_kernel, half, cap, blk),
        (f32(F, LX, ext),) * spans,
        [vmem(ROWS, 2 * SEG), vmem(ROWS, SEG)],
    )(meta, *v_blocks))
    parts = call(
        functools.partial(products_kernel, half, cap, blk),
        f32(spans, 3 * F, LX, ext),
        [vmem(ROWS, 2 * SEG), vmem(ROWS, SEG), vmem(2, ROWS, SEG)],
    )(meta, side, side_across, *v_blocks)
    parts = lax.all_to_all(parts, "px", split_axis=0, concat_axis=0, tiled=True)

    r, q, h, dots = call(
        functools.partial(solve_kernel, spans),
        (f32(F, nx, width),) * 2 + (f32(F, nx, ext), f32(groups * spans, 1, SEG)),
        [vmem(3, F, nx, ext), vmem(3 * F, nx, ext), vmem(nx, ext)],
    )(c0_ext, cx_ext, cy_ext, u_ext, parts, *sums_across)
    dots = lax.all_to_all(dots, ("px", "py"), split_axis=0, concat_axis=0, tiled=True)
    qq = call(last_kernel, f32(F, nx, width), [vmem(nx, ext)] * 2)(h, q, cx_ext, cy_ext)
    control, residual = call(finish_kernel, (f32(F, nx, width),) * 2)(dots, c0, r, q, qq)
    return control[:, None], residual[:, None]


def solution(mesh):
    return jax.shard_map(
        shards,
        mesh=mesh,
        in_specs=(
            P(None, "py", None, "px"),
            P("py", None, "px"),
            P("py", "px", None),
            P(("px", "py"), None),
            P(("px", "py"), None),
            P(("px", "py")),
            P(("px", "py"), None),
            P(("px", "py")),
            P(("px", "py")),
        ),
        out_specs=(P(None, "py", None, "px"), P(None, "py", None, "px")),
        check_vma=False,
    )
```

```python
import functools

import jax
import jax.numpy as jnp
from jax import lax
from jax.experimental import pallas as pl
from jax.experimental.pallas import tpu as pltpu
from jax.sharding import PartitionSpec as P

F = 2
SEG = 128
M = 4
NB = 16
LX = 16
ROWS = F * NB * LX
HALF = SEG // 2
SPLIT = 16
X_WIDTH = 256
Y_LINES = 16
VMEM_BYTES = 32 * 1024 * 1024
PACK_BYTES = 60 * 1024 * 1024


def iota(shape, axis):
    return lax.broadcasted_iota(jnp.int32, shape, axis)


def flag(condition, kind=jnp.bfloat16):
    return jnp.where(condition, 1.0, 0.0).astype(kind)


def mxu(left, right):
    return jnp.dot(left, right, preferred_element_type=jnp.float32)


def split_parts(values, count):
    parts = []
    for _ in range(count):
        part = values.astype(jnp.bfloat16)
        parts.append(part)
        values = values - part.astype(jnp.float32)
    return parts


def ends_tile(before, after):
    return jnp.where(iota(after.shape, after.ndim - 1) < HALF, after, before)


def sweep(values, coeffs, axis):
    size = values.shape[axis]
    for _ in range(M):
        flux = coeffs * (pltpu.roll(values, size - 1, axis) - values)
        values = values + flux - pltpu.roll(flux, 1, axis)
    return values


def start_copies(pairs, sems):
    copies = [pltpu.make_async_copy(*pair, sems.at[i]) for i, pair in enumerate(pairs)]
    for copy in copies:
        copy.start()
    return copies


def pack_weights_kernel(groups, cap, blk, block_rows, own_hbm, key_hbm, sten_hbm, itp_hbm, w_hbm,
                        *rest):
    half = groups // 2
    outs, rest = rest[:half], rest[half:]
    (slot_out, own_ref, key_ref, sten_ref, itp_ref, w_ref, buffer, slot_v, slot_s, sems, out_sems,
     sem) = rest
    loads = start_copies([(own_hbm, own_ref), (key_hbm, key_ref), (sten_hbm, sten_ref),
                          (itp_hbm, itp_ref), (w_hbm, w_ref)], sems)

    def clear(k, carry):
        start = pl.multiple_of(k * block_rows, 8)
        buffer[pl.ds(start, block_rows), :] = jnp.zeros((block_rows, SEG), jnp.float32)
        return carry

    lax.fori_loop(0, half, clear, 0)

    for load in loads[:4]:
        load.wait()
    chunks = own_ref.shape[0]
    nb = cap // blk
    own = own_ref[...]
    high = groups * chunks
    shift = chunks.bit_length() - 1
    masks = [flag(own == o, jnp.float32) for o in range(groups)]
    hits = jnp.concatenate(masks, axis=0).astype(jnp.bfloat16)
    square = (SEG, SEG)
    within = mxu(hits, flag(iota(square, 0) < iota(square, 1)))
    tallies = mxu(hits, jnp.ones(square, jnp.bfloat16)).astype(jnp.bfloat16)
    line, column = iota((high, high), 0), iota((high, high), 1)
    same = (line >> shift) == (column >> shift)
    ranks = within + mxu(flag(same & (column < line)), tallies)
    rank = sum(masks[o] * ranks[o * chunks:(o + 1) * chunks] for o in range(groups))
    rank = rank.astype(jnp.int32)
    relative = own ^ lax.axis_index("py")
    block, across = relative & (half - 1), relative >> (half.bit_length() - 1)
    slot_v[...] = block * block_rows + across * cap + rank
    slot_out[...] = (block * 2 + across) * cap + rank
    copy = pltpu.make_async_copy(slot_v, slot_s, sem)
    copy.start()

    log = blk.bit_length() - 1
    place = relative * nb + (rank >> log)
    lane = rank & (blk - 1)
    key, sten, itp = key_ref[...], sten_ref[...], itp_ref[...]
    tall = groups * nb
    meta = jnp.zeros((5 * tall, SEG), jnp.float32)
    for i in range(chunks):
        chosen = iota((tall, SEG), 0) == place[i:i + 1]
        parts = split_parts(itp[i:i + 1], 3)
        parts += [key[i:i + 1].astype(jnp.bfloat16), (sten[i:i + 1] + 1).astype(jnp.bfloat16)]
        left = [jnp.where(chosen, part.astype(jnp.float32), 0.0) for part in parts]
        right = flag(iota(square, 0) == lane[i:i + 1])
        meta = meta + lax.dot_general(
            jnp.concatenate(left, axis=0).astype(jnp.bfloat16), right,
            (((1,), (1,)), ((), ())), preferred_element_type=jnp.float32)
    shares = meta[:tall] + meta[tall:2 * tall] + meta[2 * tall:3 * tall]
    targets = meta[3 * tall:4 * tall] * LX + meta[4 * tall:]
    for v in range(groups):
        base = (v % half) * block_rows + 2 * cap + (v // half) * 2 * nb
        buffer[base:base + nb, :] = shares[v * nb:(v + 1) * nb]
        buffer[base + nb:base + 2 * nb, :] = targets[v * nb:(v + 1) * nb]

    copy.wait()
    loads[4].wait()

    def place_rows(g, carry):
        weights = w_ref[pl.ds(pl.multiple_of(g * 8, 8), 8), :]
        line, lane = g // 16, (g % 16) * 8
        for i in range(8):
            buffer[pl.ds(slot_s[line, lane + i], 1), :] = weights[i:i + 1]
        return carry

    lax.fori_loop(0, w_ref.shape[0] // 8, place_rows, 0)
    for store in start_copies([(buffer.at[pl.ds(k * block_rows, block_rows)], out)
                               for k, out in enumerate(outs)], out_sems):
        store.wait()


def pack_products_kernel(groups, cap, slot_ref, w_hbm, d_hbm, cy_hbm, c0_hbm, cx_hbm, *rest):
    half = groups // 2
    outs, (swap_out, w_ref, d_ref, cy_ref, first, last, buffer, sems, out_sems) = (
        rest[:half], rest[half:])
    width = c0_hbm.shape[2]
    loads = start_copies([
        (w_hbm, w_ref), (d_hbm, d_ref), (cy_hbm, cy_ref),
        (c0_hbm.at[:, :, pl.ds(0, SEG)], first.at[pl.ds(0, F)]),
        (cx_hbm.at[:, pl.ds(0, SEG)], first.at[F]),
        (c0_hbm.at[:, :, pl.ds(width - SEG, SEG)], last.at[pl.ds(0, F)]),
        (cx_hbm.at[:, pl.ds(width - SEG, SEG)], last.at[F]),
    ], sems)

    def clear(o, carry):
        start = pl.multiple_of(o * cap, 8)
        buffer[pl.ds(start, cap), :] = jnp.zeros((cap, SEG), jnp.float32)
        return carry

    lax.fori_loop(0, groups, clear, 0)

    for load in loads:
        load.wait()

    def place_rows(g, carry):
        start = pl.multiple_of(g * 8, 8)
        products = w_ref[pl.ds(start, 8), :] * d_ref[pl.ds(start, 8), :]
        line, lane = g // 16, (g % 16) * 8
        for i in range(8):
            buffer[pl.ds(slot_ref[line, lane + i], 1), :] = products[i:i + 1]
        return carry

    lax.fori_loop(0, w_ref.shape[0] // 8, place_rows, 0)
    stores = start_copies([(buffer.at[pl.ds(k * 2 * cap, 2 * cap)], out)
                           for k, out in enumerate(outs)], out_sems)
    columns = cy_ref.shape[1]
    cy = cy_ref[...]
    cy = jnp.where(iota(cy.shape, 1) == columns - 1, 0.0, cy)
    empty = jnp.zeros((LX, SEG), jnp.float32)
    me = lax.axis_index("px")
    nx = first.shape[1]
    for q in range(columns // width):
        low, top = q * width, (q + 1) * width
        tiles = [cy[:, t:t + SEG] for t in range(low, top, SEG)]
        before = cy[:, low - SEG:low] if low > 0 else empty
        after = cy[:, top:top + SEG] if top < columns else empty
        tiles.append(ends_tile(before, after))
        for t, tile in enumerate(tiles):
            swap_out[q, t * LX:(t + 1) * LX, :] = tile
        base = len(tiles) * LX
        for i in range(F + 1):
            swap_out[q, base + i * nx:base + (i + 1) * nx, :] = jnp.where(
                q < me, first[i], last[i])
    for store in stores:
        store.wait()


def sum_rows(cap, blk, metas, acc_ref, terms):
    nb = cap // blk
    numbers = 1.0 + iota((ROWS, cap), 0).astype(jnp.float32)
    for source, meta in enumerate(metas):
        upper = jnp.concatenate(
            [jnp.broadcast_to(meta[i:i + 1], (SEG, SEG)).T[:blk] for i in range(nb)], axis=0)
        target = jnp.concatenate([meta[nb + i:nb + i + 1, :blk] for i in range(nb)], axis=1)
        hit = flag(numbers == target)
        values = jnp.concatenate(terms(source, upper), axis=1)
        part = mxu(jnp.concatenate([hit, hit], axis=1),
                   jnp.concatenate(split_parts(values, 2), axis=0))
        if source:
            acc_ref[...] += part
        else:
            acc_ref[...] = part


def cut_part(rows_ref, to, f, q, spans):
    width = to.shape[1] - SEG
    per = width // SEG

    def tile(b):
        start = pl.multiple_of((f * NB + b) * LX, LX)
        return rows_ref[pl.ds(start, LX), :]

    for j in range(per):
        to[:, j * SEG:(j + 1) * SEG] = tile(q * per + j)
    before = tile(jnp.maximum(q * per - 1, 0))
    after = tile(jnp.minimum(q * per + per, NB - 1))
    to[:, width:] = ends_tile(jnp.where(q > 0, before, 0.0),
                              jnp.where(q < spans - 1, after, 0.0))


def weights_kernel(half, cap, blk, across, *rest):
    w_refs, (_, meta_out, diagonal_out, side_out, acc_ref) = rest[:half], rest[half:]
    nb = cap // blk
    for k, w_ref in enumerate(w_refs):
        meta_out[k] = w_ref[2 * cap:, :]
    rows = slice(across * cap, (across + 1) * cap)

    def terms(source, upper):
        lower = 1.0 - upper
        weights = w_refs[source][rows, :]
        lower_w, upper_w = lower * weights, upper * weights
        return [lower * lower_w, upper * lower_w, upper * upper_w]

    low = 2 * cap + across * 2 * nb
    sum_rows(cap, blk, [w_ref[low:low + 2 * nb, :] for w_ref in w_refs], acc_ref, terms)
    diagonal_out[...] = acc_ref[:, :SEG] + pltpu.roll(acc_ref[:, 2 * SEG:], 1, 0)
    side_out[...] = acc_ref[:, SEG:2 * SEG]


def sum_products(half, cap, blk, across, meta_ref, v_refs, acc_ref, sums_ref):
    nb = cap // blk
    rows = slice(across * cap, (across + 1) * cap)

    def terms(source, upper):
        products = v_refs[source][rows, :]
        return [(1.0 - upper) * products, upper * products]

    low = across * 2 * nb
    sum_rows(cap, blk, [meta_ref[k, low:low + 2 * nb, :] for k in range(half)], acc_ref, terms)
    sums_ref[...] = acc_ref[:, :SEG] + pltpu.roll(acc_ref[:, SEG:], 1, 0)


def products_across_kernel(half, cap, blk, meta_ref, *rest):
    v_refs, (meta_out, *outs, acc_ref, sums_ref) = rest[:half], rest[half:]
    meta_out[...] = meta_ref[...]
    sum_products(half, cap, blk, 1, meta_ref, v_refs, acc_ref, sums_ref)
    me = lax.axis_index("px")
    for k, out in enumerate(outs):
        for f in range(F):
            cut_part(sums_ref, out.at[f], f, me ^ k, len(outs))


def products_kernel(half, cap, blk, meta_ref, d_ref, e_ref, far_d_ref, far_e_ref, *rest):
    v_refs, (out, acc_ref, sums_ref, side) = rest[:half], rest[half:]
    spans = out.shape[0]
    sum_products(half, cap, blk, 0, meta_ref, v_refs, acc_ref, sums_ref)
    side[0] = d_ref[...] + far_d_ref[...]
    side[1] = e_ref[...] + far_e_ref[...]
    for q in range(spans):
        for channel, rows_ref in enumerate((side.at[0], side.at[1], sums_ref)):
            for f in range(F):
                cut_part(rows_ref, out.at[q, channel * F + f], f, q, spans)


def sweep_x_into(to_ref, from_ref, cx_ref, plus_ref=None, sign=1.0):
    size = cx_ref.shape[1]
    for low in range(0, size, X_WIDTH):
        tile = slice(low, min(low + X_WIDTH, size))
        values = sweep(from_ref[:, tile], cx_ref[:, tile], 0)
        if plus_ref is not None:
            values = values + sign * plus_ref[:, tile]
        to_ref[:, tile] = values


def sweep_y_into(to_ref, from_ref, cy_ref):
    for low in range(0, cy_ref.shape[0], Y_LINES):
        lines = slice(low, low + Y_LINES)
        to_ref[lines, :] = sweep(from_ref[lines, :], cy_ref[lines, :], 1)


def start_kernel(c0_ref, cx_ref, swap_ref, c0_out, cx_out, cy_out, u_out, token_out):
    token_out[...] = jnp.zeros_like(token_out)
    width = c0_ref.shape[2]
    nx = cx_ref.shape[0]
    spans, count = swap_ref.shape[0], cy_out.shape[1] // SEG
    me = lax.axis_index("px")
    for p in range(spans):
        for t in range(count):
            cy_out[p * LX:(p + 1) * LX, t * SEG:(t + 1) * SEG] = (
                swap_ref[p, t * LX:(t + 1) * LX, :])

    def beside(i):
        lines = slice(count * LX + i * nx, count * LX + (i + 1) * nx)
        before = swap_ref[jnp.maximum(me - 1, 0), lines, :]
        after = swap_ref[jnp.minimum(me + 1, spans - 1), lines, :]
        return ends_tile(jnp.where(me > 0, before, 0.0), jnp.where(me < spans - 1, after, 0.0))

    last = cx_ref.shape[0] - 1
    cx_out[:, :width] = cx_ref[...]
    cx_out[:, width:] = beside(F)
    cx_out[last:, :] = jnp.zeros((1, width + SEG), jnp.float32)
    for f in range(F):
        c0_out[f, :, :width] = c0_ref[f]
        c0_out[f, :, width:] = beside(f)
        sweep_x_into(u_out.at[f], c0_out.at[f], cx_out)
        sweep_y_into(u_out.at[f], u_out.at[f], cy_out)


def solve_kernel(spans, c0_ref, cx_ref, cy_ref, u_ref, obs_ref, *rest):
    sum_refs, (r_out, q_out, h_out, dots_out, vec, coef, work) = rest[:spans], rest[spans:]
    width = r_out.shape[2]
    for p in range(spans):
        for channel in range(3 * F):
            coef[channel, p * LX:(p + 1) * LX, :] = obs_ref[p, channel]
    me = lax.axis_index("px")
    for k in range(spans):
        rows = pl.ds(pl.multiple_of((me ^ k) * LX, LX), LX)
        for f in range(F):
            coef[2 * F + f, rows, :] += sum_refs[k][f]

    def normal(f, values, tile):
        size = values.shape[0]
        side = coef[F + f, :, tile]
        return (coef[f, :, tile] * values + side * pltpu.roll(values, size - 1, 0)
                + pltpu.roll(side * values, 1, 0))

    tiles = [slice(low, low + SEG) for low in range(0, width + SEG, SEG)]

    def first(f, carry):
        for tile in tiles:
            work[:, tile] = coef[2 * F + f, :, tile] - normal(f, u_ref[f, :, tile], tile)
        sweep_y_into(work, work, cy_ref)
        sweep_x_into(vec.at[0, f], work, cx_ref, c0_ref.at[f], -1.0)
        return carry

    lax.fori_loop(0, F, first, 0)

    def apply(f, carry):
        sweep_x_into(work, vec.at[0, f], cx_ref)
        sweep_y_into(work, work, cy_ref)
        for tile in tiles:
            work[:, tile] = normal(f, work[:, tile], tile)
        sweep_y_into(work, work, cy_ref)
        sweep_x_into(vec.at[1, f], work, cx_ref, vec.at[0, f])
        sweep_x_into(vec.at[2, f], vec.at[1, f], cx_ref)
        sweep_y_into(vec.at[2, f], vec.at[2, f], cy_ref)
        for tile in tiles:
            h_out[f, :, tile] = normal(f, vec[2, f, :, tile], tile)
        return carry

    lax.fori_loop(0, F, apply, 0)

    sums = [jnp.zeros((8, SEG), jnp.float32) for _ in range(4)]
    for f in range(F):
        r_out[f] = vec[0, f, :, :width]
        q_out[f] = vec[1, f, :, :width]
        for low in range(0, vec.shape[2], 8):
            for tile in tiles[:-1]:
                r = vec[0, f, low:low + 8, tile]
                q = vec[1, f, low:low + 8, tile]
                s = vec[2, f, low:low + 8, tile]
                for i, product in enumerate((r * r, r * q, q * q, s * h_out[f, low:low + 8, tile])):
                    sums[i] = sums[i] + product
    dots = jnp.zeros((1, SEG), jnp.float32)
    for i, total in enumerate(sums):
        line = jnp.sum(total, axis=0, keepdims=True)
        for distance in (64, 32, 16):
            line = line + pltpu.roll(line, distance, 1)
        dots = jnp.where(iota((1, SEG), 1) // SPLIT == i, line, dots)
    dots_out[...] = jnp.broadcast_to(dots, dots_out.shape)


def last_kernel(h_ref, q_ref, cx_ref, cy_ref, qq_out, work, other):
    width = qq_out.shape[2]

    def apply(f, carry):
        sweep_y_into(work, h_ref.at[f], cy_ref)
        sweep_x_into(other, work, cx_ref)
        qq_out[f] = q_ref[f] + other[:, :width]
        return carry

    lax.fori_loop(0, F, apply, 0)


def finish_kernel(dots_ref, c0_ref, r_ref, q_ref, qq_ref, control_out, residual_out):
    dots = jnp.sum(dots_ref[...], axis=0)
    lane = iota((1, SEG), 1)
    rr, rq, qq2, energy = (pltpu.roll(dots, (SEG - i * SPLIT) % SEG, 1) for i in range(4))

    def total(line):
        return jnp.sum(jnp.where(lane < SPLIT, line, 0.0), axis=1, keepdims=True)

    rr_sum = total(rr)
    alpha = rr_sum / total(rq)
    new_sum = total(rr - 2.0 * alpha * rq + alpha * alpha * qq2)
    more = 1.0 + new_sum / rr_sum
    curve = total(more * more * rq - 2.0 * more * alpha * qq2 + alpha * alpha * (qq2 + energy))
    second = new_sum / curve
    first_weight = alpha + second * more
    both = alpha * second
    for f in range(F):
        r, q = r_ref[f], q_ref[f]
        control_out[f] = c0_ref[f] + first_weight * r - both * q
        residual_out[f] = r - first_weight * q + both * qq_ref[f]


def call(kernel, out_shape, scratch=(), in_specs=None, out_specs=None, limit=VMEM_BYTES):
    params = {"in_specs": in_specs, "out_specs": out_specs}
    return pl.pallas_call(
        kernel,
        out_shape=out_shape,
        scratch_shapes=list(scratch),
        compiler_params=pltpu.CompilerParams(vmem_limit_bytes=limit),
        **{name: value for name, value in params.items() if value is not None},
    )


def f32(*shape):
    return jax.ShapeDtypeStruct(shape, jnp.float32)


def vmem(*shape, kind=jnp.float32):
    return pltpu.VMEM(shape, kind)


def shards(
    control_start, coef_x, coef_y, innovation, obs_weight, interp, obs_owner, cell_key, stencil
):
    groups, spans = lax.axis_size("py"), lax.axis_size("px")
    half = groups // 2
    rows = innovation.shape[0]
    cap = 3 * rows // groups
    blk = SEG if cap % SEG == 0 else HALF
    meta_rows = -(-4 * (cap // blk) // 8) * 8
    block_rows = 2 * cap + meta_rows
    chunks = rows // SEG
    nx, width = control_start.shape[2], control_start.shape[3]
    ext = width + SEG
    c0, cx = control_start[:, 0], coef_x[0]
    hbm, local, scalars = (
        pl.BlockSpec(memory_space=s) for s in (pltpu.HBM, pltpu.VMEM, pltpu.SMEM))
    ints = vmem(chunks, SEG, kind=jnp.int32)
    dma = pltpu.SemaphoreType.DMA

    def to_half(block, k):
        return lax.ppermute(block, "py", [(i, i ^ k) for i in range(groups)])

    def across(parts):
        return [
            lax.ppermute(parts[k], ("px", "py"), [
                (i * groups + j, (i ^ k) * groups + (j ^ half))
                for i in range(spans) for j in range(groups)])
            for k in range(spans)]

    *w_blocks, slots = call(
        functools.partial(pack_weights_kernel, groups, cap, blk, block_rows),
        (f32(block_rows, SEG),) * half + (jax.ShapeDtypeStruct((chunks, SEG), jnp.int32),),
        [ints, ints, ints, vmem(chunks, SEG), vmem(rows, SEG), vmem(half * block_rows, SEG), ints,
         pltpu.SMEM((chunks, SEG), jnp.int32), dma((5,)), dma((half,)), dma],
        [hbm] * 5,
        (hbm,) * half + (local,),
        limit=PACK_BYTES,
    )(
        obs_owner.reshape(chunks, SEG), cell_key.reshape(chunks, SEG),
        stencil.reshape(chunks, SEG), interp.reshape(chunks, SEG), obs_weight,
    )
    *v_blocks, swap = call(
        functools.partial(pack_products_kernel, groups, cap),
        (f32(2 * cap, SEG),) * half + (f32(spans, LX * ext // SEG + (F + 1) * nx, SEG),),
        [vmem(rows, SEG), vmem(rows, SEG), vmem(*coef_y.shape[1:]), vmem(F + 1, nx, SEG),
         vmem(F + 1, nx, SEG), vmem(groups * cap, SEG), dma((7,)), dma((half,))],
        [scalars] + [hbm] * 5,
        (hbm,) * half + (local,),
        limit=PACK_BYTES,
    )(slots, obs_weight, innovation, coef_y[0], c0, cx)
    w_blocks[1:] = [to_half(w_blocks[k], k) for k in range(1, half)]
    w_blocks[1], *v_blocks[1:] = lax.optimization_barrier((w_blocks[1], *v_blocks[1:]))
    v_blocks[1:] = [to_half(v_blocks[k], k) for k in range(1, half)]

    swap = lax.all_to_all(swap, "px", split_axis=0, concat_axis=0, tiled=True)
    c0_ext, cx_ext, cy_ext, u_ext, token = call(
        start_kernel,
        (f32(F, nx, ext), f32(nx, ext), f32(nx, ext), f32(F, nx, ext), f32(8, SEG)),
    )(c0, cx, swap)

    def sum_weights(side, token):
        return call(
            functools.partial(weights_kernel, half, cap, blk, side),
            (f32(half, meta_rows, SEG),) + (f32(ROWS, SEG),) * 2,
            [vmem(ROWS, 3 * SEG)],
        )(*w_blocks, token)

    meta, *side_across = sum_weights(1, token)
    side_across = [to_half(values, half) for values in side_across]
    meta, *side = sum_weights(0, meta)
    meta, *sums_across = call(
        functools.partial(products_across_kernel, half, cap, blk),
        (f32(half, meta_rows, SEG),) + (f32(F, LX, ext),) * spans,
        [vmem(ROWS, 2 * SEG), vmem(ROWS, SEG)],
    )(meta, *v_blocks)
    sums_across = across(sums_across)
    parts = call(
        functools.partial(products_kernel, half, cap, blk),
        f32(spans, 3 * F, LX, ext),
        [vmem(ROWS, 2 * SEG), vmem(ROWS, SEG), vmem(2, ROWS, SEG)],
    )(meta, *side, *side_across, *v_blocks)
    parts = lax.all_to_all(parts, "px", split_axis=0, concat_axis=0, tiled=True)

    r, q, h, dots = call(
        functools.partial(solve_kernel, spans),
        (f32(F, nx, width),) * 2 + (f32(F, nx, ext), f32(groups * spans, 1, SEG)),
        [vmem(3, F, nx, ext), vmem(3 * F, nx, ext), vmem(nx, ext)],
    )(c0_ext, cx_ext, cy_ext, u_ext, parts, *sums_across)
    dots = lax.all_to_all(dots, ("px", "py"), split_axis=0, concat_axis=0, tiled=True)
    qq = call(last_kernel, f32(F, nx, width), [vmem(nx, ext)] * 2)(h, q, cx_ext, cy_ext)
    control, residual = call(finish_kernel, (f32(F, nx, width),) * 2)(dots, c0, r, q, qq)
    return control[:, None], residual[:, None]


def solution(mesh):
    return jax.shard_map(
        shards,
        mesh=mesh,
        in_specs=(
            P(None, "py", None, "px"),
            P("py", None, "px"),
            P("py", "px", None),
            P(("px", "py"), None),
            P(("px", "py"), None),
            P(("px", "py")),
            P(("px", "py"), None),
            P(("px", "py")),
            P(("px", "py")),
        ),
        out_specs=(P(None, "py", None, "px"), P(None, "py", None, "px")),
        check_vma=False,
    )
```

```python
import functools

import jax
import jax.numpy as jnp
from jax import lax
from jax.experimental import pallas as pl
from jax.experimental.pallas import tpu as pltpu
from jax.sharding import PartitionSpec as P

F = 2
SEG = 128
M = 4
NB = 16
LX = 16
ROWS = F * NB * LX
HALF = SEG // 2
SPLIT = 16
X_WIDTH = 256
Y_LINES = 16
VMEM_BYTES = 32 * 1024 * 1024
PACK_BYTES = 60 * 1024 * 1024


def iota(shape, axis):
    return lax.broadcasted_iota(jnp.int32, shape, axis)


def flag(condition, kind=jnp.bfloat16):
    return jnp.where(condition, 1.0, 0.0).astype(kind)


def mxu(left, right):
    return jnp.dot(left, right, preferred_element_type=jnp.float32)


def split_parts(values, count):
    parts = []
    for _ in range(count):
        part = values.astype(jnp.bfloat16)
        parts.append(part)
        values = values - part.astype(jnp.float32)
    return parts


def ends_tile(before, after):
    return jnp.where(iota(after.shape, after.ndim - 1) < HALF, after, before)


def sweep(values, coeffs, axis):
    size = values.shape[axis]
    for _ in range(M):
        flux = coeffs * (pltpu.roll(values, size - 1, axis) - values)
        values = values + flux - pltpu.roll(flux, 1, axis)
    return values


def start_copies(pairs, sems):
    copies = [pltpu.make_async_copy(*pair, sems.at[i]) for i, pair in enumerate(pairs)]
    for copy in copies:
        copy.start()
    return copies


def pack_weights_kernel(groups, cap, blk, block_rows, own_hbm, key_hbm, sten_hbm, itp_hbm, w_hbm,
                        *rest):
    half = groups // 2
    outs, rest = rest[:half], rest[half:]
    (slot_out, own_ref, key_ref, sten_ref, itp_ref, w_ref, buffer, slot_v, slot_s, sems, out_sems,
     sem) = rest
    loads = start_copies([(own_hbm, own_ref), (key_hbm, key_ref), (sten_hbm, sten_ref),
                          (itp_hbm, itp_ref), (w_hbm, w_ref)], sems)

    def clear(k, carry):
        start = pl.multiple_of(k * block_rows, 8)
        buffer[pl.ds(start, block_rows), :] = jnp.zeros((block_rows, SEG), jnp.float32)
        return carry

    lax.fori_loop(0, half, clear, 0)

    for load in loads[:4]:
        load.wait()
    chunks = own_ref.shape[0]
    nb = cap // blk
    own = own_ref[...]
    high = groups * chunks
    shift = chunks.bit_length() - 1
    masks = [flag(own == o, jnp.float32) for o in range(groups)]
    hits = jnp.concatenate(masks, axis=0).astype(jnp.bfloat16)
    square = (SEG, SEG)
    within = mxu(hits, flag(iota(square, 0) < iota(square, 1)))
    tallies = mxu(hits, jnp.ones(square, jnp.bfloat16)).astype(jnp.bfloat16)
    line, column = iota((high, high), 0), iota((high, high), 1)
    same = (line >> shift) == (column >> shift)
    ranks = within + mxu(flag(same & (column < line)), tallies)
    rank = sum(masks[o] * ranks[o * chunks:(o + 1) * chunks] for o in range(groups))
    rank = rank.astype(jnp.int32)
    relative = own ^ lax.axis_index("py")
    block, across = relative & (half - 1), relative >> (half.bit_length() - 1)
    slot_v[...] = block * block_rows + across * cap + rank
    slot_out[...] = (block * 2 + across) * cap + rank
    copy = pltpu.make_async_copy(slot_v, slot_s, sem)
    copy.start()

    log = blk.bit_length() - 1
    place = relative * nb + (rank >> log)
    lane = rank & (blk - 1)
    key, sten, itp = key_ref[...], sten_ref[...], itp_ref[...]
    tall = groups * nb
    meta = jnp.zeros((5 * tall, SEG), jnp.float32)
    for i in range(chunks):
        chosen = iota((tall, SEG), 0) == place[i:i + 1]
        parts = split_parts(itp[i:i + 1], 3)
        parts += [key[i:i + 1].astype(jnp.bfloat16), (sten[i:i + 1] + 1).astype(jnp.bfloat16)]
        left = [jnp.where(chosen, part.astype(jnp.float32), 0.0) for part in parts]
        right = flag(iota(square, 0) == lane[i:i + 1])
        meta = meta + lax.dot_general(
            jnp.concatenate(left, axis=0).astype(jnp.bfloat16), right,
            (((1,), (1,)), ((), ())), preferred_element_type=jnp.float32)
    shares = meta[:tall] + meta[tall:2 * tall] + meta[2 * tall:3 * tall]
    targets = meta[3 * tall:4 * tall] * LX + meta[4 * tall:]
    for v in range(groups):
        base = (v % half) * block_rows + 2 * cap + (v // half) * 2 * nb
        buffer[base:base + nb, :] = shares[v * nb:(v + 1) * nb]
        buffer[base + nb:base + 2 * nb, :] = targets[v * nb:(v + 1) * nb]

    copy.wait()
    loads[4].wait()

    def place_rows(g, carry):
        weights = w_ref[pl.ds(pl.multiple_of(g * 8, 8), 8), :]
        line, lane = g // 16, (g % 16) * 8
        for i in range(8):
            buffer[pl.ds(slot_s[line, lane + i], 1), :] = weights[i:i + 1]
        return carry

    lax.fori_loop(0, w_ref.shape[0] // 8, place_rows, 0)
    for store in start_copies([(buffer.at[pl.ds(k * block_rows, block_rows)], out)
                               for k, out in enumerate(outs)], out_sems):
        store.wait()


def pack_products_kernel(groups, cap, slot_ref, w_hbm, d_hbm, cy_hbm, c0_hbm, cx_hbm, *rest):
    half = groups // 2
    outs, (swap_out, w_ref, d_ref, cy_ref, first, last, buffer, sems, out_sems) = (
        rest[:half], rest[half:])
    width = c0_hbm.shape[2]
    loads = start_copies([
        (w_hbm, w_ref), (d_hbm, d_ref), (cy_hbm, cy_ref),
        (c0_hbm.at[:, :, pl.ds(0, SEG)], first.at[pl.ds(0, F)]),
        (cx_hbm.at[:, pl.ds(0, SEG)], first.at[F]),
        (c0_hbm.at[:, :, pl.ds(width - SEG, SEG)], last.at[pl.ds(0, F)]),
        (cx_hbm.at[:, pl.ds(width - SEG, SEG)], last.at[F]),
    ], sems)

    def clear(o, carry):
        start = pl.multiple_of(o * cap, 8)
        buffer[pl.ds(start, cap), :] = jnp.zeros((cap, SEG), jnp.float32)
        return carry

    lax.fori_loop(0, groups, clear, 0)

    for load in loads:
        load.wait()

    def place_rows(g, carry):
        start = pl.multiple_of(g * 8, 8)
        products = w_ref[pl.ds(start, 8), :] * d_ref[pl.ds(start, 8), :]
        line, lane = g // 16, (g % 16) * 8
        for i in range(8):
            buffer[pl.ds(slot_ref[line, lane + i], 1), :] = products[i:i + 1]
        return carry

    lax.fori_loop(0, w_ref.shape[0] // 8, place_rows, 0)
    stores = start_copies([(buffer.at[pl.ds(k * 2 * cap, 2 * cap)], out)
                           for k, out in enumerate(outs)], out_sems)
    columns = cy_ref.shape[1]
    cy = cy_ref[...]
    cy = jnp.where(iota(cy.shape, 1) == columns - 1, 0.0, cy)
    empty = jnp.zeros((LX, SEG), jnp.float32)
    me = lax.axis_index("px")
    nx = first.shape[1]
    for q in range(columns // width):
        low, top = q * width, (q + 1) * width
        tiles = [cy[:, t:t + SEG] for t in range(low, top, SEG)]
        before = cy[:, low - SEG:low] if low > 0 else empty
        after = cy[:, top:top + SEG] if top < columns else empty
        tiles.append(ends_tile(before, after))
        for t, tile in enumerate(tiles):
            swap_out[q, t * LX:(t + 1) * LX, :] = tile
        base = len(tiles) * LX
        for i in range(F + 1):
            swap_out[q, base + i * nx:base + (i + 1) * nx, :] = jnp.where(
                q < me, first[i], last[i])
    for store in stores:
        store.wait()


def sum_rows(cap, blk, metas, acc_ref, terms):
    nb = cap // blk
    numbers = 1.0 + iota((ROWS, cap), 0).astype(jnp.float32)
    for source, meta in enumerate(metas):
        upper = jnp.concatenate(
            [jnp.broadcast_to(meta[i:i + 1], (SEG, SEG)).T[:blk] for i in range(nb)], axis=0)
        target = jnp.concatenate([meta[nb + i:nb + i + 1, :blk] for i in range(nb)], axis=1)
        hit = flag(numbers == target)
        values = jnp.concatenate(terms(source, upper), axis=1)
        part = mxu(jnp.concatenate([hit, hit], axis=1),
                   jnp.concatenate(split_parts(values, 2), axis=0))
        if source:
            acc_ref[...] += part
        else:
            acc_ref[...] = part


def cut_part(rows_ref, to, f, q, spans):
    width = to.shape[1] - SEG
    per = width // SEG

    def tile(b):
        start = pl.multiple_of((f * NB + b) * LX, LX)
        return rows_ref[pl.ds(start, LX), :]

    for j in range(per):
        to[:, j * SEG:(j + 1) * SEG] = tile(q * per + j)
    before = tile(jnp.maximum(q * per - 1, 0))
    after = tile(jnp.minimum(q * per + per, NB - 1))
    to[:, width:] = ends_tile(jnp.where(q > 0, before, 0.0),
                              jnp.where(q < spans - 1, after, 0.0))


def weights_kernel(half, cap, blk, across, *rest):
    w_refs, (_, meta_out, diagonal_out, side_out, acc_ref) = rest[:half], rest[half:]
    nb = cap // blk
    for k, w_ref in enumerate(w_refs):
        meta_out[k] = w_ref[2 * cap:, :]
    rows = slice(across * cap, (across + 1) * cap)

    def terms(source, upper):
        lower = 1.0 - upper
        weights = w_refs[source][rows, :]
        lower_w, upper_w = lower * weights, upper * weights
        return [lower * lower_w, upper * lower_w, upper * upper_w]

    low = 2 * cap + across * 2 * nb
    sum_rows(cap, blk, [w_ref[low:low + 2 * nb, :] for w_ref in w_refs], acc_ref, terms)
    diagonal_out[...] = acc_ref[:, :SEG] + pltpu.roll(acc_ref[:, 2 * SEG:], 1, 0)
    side_out[...] = acc_ref[:, SEG:2 * SEG]


def sum_products(half, cap, blk, across, meta_ref, v_refs, acc_ref, sums_ref):
    nb = cap // blk
    rows = slice(across * cap, (across + 1) * cap)

    def terms(source, upper):
        products = v_refs[source][rows, :]
        return [(1.0 - upper) * products, upper * products]

    low = across * 2 * nb
    sum_rows(cap, blk, [meta_ref[k, low:low + 2 * nb, :] for k in range(half)], acc_ref, terms)
    sums_ref[...] = acc_ref[:, :SEG] + pltpu.roll(acc_ref[:, SEG:], 1, 0)


def products_across_kernel(half, cap, blk, meta_ref, *rest):
    v_refs, (meta_out, *outs, acc_ref, sums_ref) = rest[:half], rest[half:]
    meta_out[...] = meta_ref[...]
    sum_products(half, cap, blk, 1, meta_ref, v_refs, acc_ref, sums_ref)
    me = lax.axis_index("px")
    for k, out in enumerate(outs):
        for f in range(F):
            cut_part(sums_ref, out.at[f], f, me ^ k, len(outs))


def products_kernel(half, cap, blk, meta_ref, d_ref, e_ref, far_d_ref, far_e_ref, *rest):
    v_refs, (out, acc_ref, sums_ref, side) = rest[:half], rest[half:]
    spans = out.shape[0]
    sum_products(half, cap, blk, 0, meta_ref, v_refs, acc_ref, sums_ref)
    side[0] = d_ref[...] + far_d_ref[...]
    side[1] = e_ref[...] + far_e_ref[...]
    for q in range(spans):
        for channel, rows_ref in enumerate((side.at[0], side.at[1], sums_ref)):
            for f in range(F):
                cut_part(rows_ref, out.at[q, channel * F + f], f, q, spans)


def sweep_x_into(to_ref, from_ref, cx_ref, plus_ref=None, sign=1.0):
    size = cx_ref.shape[1]
    for low in range(0, size, X_WIDTH):
        tile = slice(low, min(low + X_WIDTH, size))
        values = sweep(from_ref[:, tile], cx_ref[:, tile], 0)
        if plus_ref is not None:
            values = values + sign * plus_ref[:, tile]
        to_ref[:, tile] = values


def sweep_y_into(to_ref, from_ref, cy_ref):
    for low in range(0, cy_ref.shape[0], Y_LINES):
        lines = slice(low, low + Y_LINES)
        to_ref[lines, :] = sweep(from_ref[lines, :], cy_ref[lines, :], 1)


def start_kernel(c0_ref, cx_ref, swap_ref, c0_out, cx_out, cy_out, u_out, token_out):
    token_out[...] = jnp.zeros_like(token_out)
    width = c0_ref.shape[2]
    nx = cx_ref.shape[0]
    spans, count = swap_ref.shape[0], cy_out.shape[1] // SEG
    me = lax.axis_index("px")
    for p in range(spans):
        for t in range(count):
            cy_out[p * LX:(p + 1) * LX, t * SEG:(t + 1) * SEG] = (
                swap_ref[p, t * LX:(t + 1) * LX, :])

    def beside(i):
        lines = slice(count * LX + i * nx, count * LX + (i + 1) * nx)
        before = swap_ref[jnp.maximum(me - 1, 0), lines, :]
        after = swap_ref[jnp.minimum(me + 1, spans - 1), lines, :]
        return ends_tile(jnp.where(me > 0, before, 0.0), jnp.where(me < spans - 1, after, 0.0))

    last = cx_ref.shape[0] - 1
    cx_out[:, :width] = cx_ref[...]
    cx_out[:, width:] = beside(F)
    cx_out[last:, :] = jnp.zeros((1, width + SEG), jnp.float32)
    for f in range(F):
        c0_out[f, :, :width] = c0_ref[f]
        c0_out[f, :, width:] = beside(f)
        sweep_x_into(u_out.at[f], c0_out.at[f], cx_out)
        sweep_y_into(u_out.at[f], u_out.at[f], cy_out)


def solve_kernel(spans, c0_ref, cx_ref, cy_ref, u_ref, obs_ref, *rest):
    sum_refs, (r_out, q_out, h_out, dots_out, vec, coef, work) = rest[:spans], rest[spans:]
    width = r_out.shape[2]
    for p in range(spans):
        for channel in range(3 * F):
            coef[channel, p * LX:(p + 1) * LX, :] = obs_ref[p, channel]
    me = lax.axis_index("px")
    for k in range(spans):
        rows = pl.ds(pl.multiple_of((me ^ k) * LX, LX), LX)
        for f in range(F):
            coef[2 * F + f, rows, :] += sum_refs[k][f]

    def normal(f, values, tile):
        size = values.shape[0]
        side = coef[F + f, :, tile]
        return (coef[f, :, tile] * values + side * pltpu.roll(values, size - 1, 0)
                + pltpu.roll(side * values, 1, 0))

    tiles = [slice(low, low + SEG) for low in range(0, width + SEG, SEG)]

    def first(f, carry):
        for tile in tiles:
            work[:, tile] = coef[2 * F + f, :, tile] - normal(f, u_ref[f, :, tile], tile)
        sweep_y_into(work, work, cy_ref)
        sweep_x_into(vec.at[0, f], work, cx_ref, c0_ref.at[f], -1.0)
        return carry

    lax.fori_loop(0, F, first, 0)

    def apply(f, carry):
        sweep_x_into(work, vec.at[0, f], cx_ref)
        sweep_y_into(work, work, cy_ref)
        for tile in tiles:
            work[:, tile] = normal(f, work[:, tile], tile)
        sweep_y_into(work, work, cy_ref)
        sweep_x_into(vec.at[1, f], work, cx_ref, vec.at[0, f])
        sweep_x_into(vec.at[2, f], vec.at[1, f], cx_ref)
        sweep_y_into(vec.at[2, f], vec.at[2, f], cy_ref)
        for tile in tiles:
            h_out[f, :, tile] = normal(f, vec[2, f, :, tile], tile)
        return carry

    lax.fori_loop(0, F, apply, 0)

    sums = [jnp.zeros((8, SEG), jnp.float32) for _ in range(4)]
    for f in range(F):
        r_out[f] = vec[0, f, :, :width]
        q_out[f] = vec[1, f, :, :width]
        for low in range(0, vec.shape[2], 8):
            for tile in tiles[:-1]:
                r = vec[0, f, low:low + 8, tile]
                q = vec[1, f, low:low + 8, tile]
                s = vec[2, f, low:low + 8, tile]
                for i, product in enumerate((r * r, r * q, q * q, s * h_out[f, low:low + 8, tile])):
                    sums[i] = sums[i] + product
    dots = jnp.zeros((1, SEG), jnp.float32)
    for i, total in enumerate(sums):
        line = jnp.sum(total, axis=0, keepdims=True)
        for distance in (64, 32, 16):
            line = line + pltpu.roll(line, distance, 1)
        dots = jnp.where(iota((1, SEG), 1) // SPLIT == i, line, dots)
    dots_out[...] = jnp.broadcast_to(dots, dots_out.shape)


def last_kernel(h_ref, q_ref, cx_ref, cy_ref, qq_out, work, other):
    width = qq_out.shape[2]

    def apply(f, carry):
        sweep_y_into(work, h_ref.at[f], cy_ref)
        sweep_x_into(other, work, cx_ref)
        qq_out[f] = q_ref[f] + other[:, :width]
        return carry

    lax.fori_loop(0, F, apply, 0)


def finish_kernel(dots_ref, c0_ref, r_ref, q_ref, qq_ref, control_out, residual_out):
    dots = jnp.sum(dots_ref[...], axis=0)
    lane = iota((1, SEG), 1)
    rr, rq, qq2, energy = (pltpu.roll(dots, (SEG - i * SPLIT) % SEG, 1) for i in range(4))

    def total(line):
        return jnp.sum(jnp.where(lane < SPLIT, line, 0.0), axis=1, keepdims=True)

    rr_sum = total(rr)
    alpha = rr_sum / total(rq)
    new_sum = total(rr - 2.0 * alpha * rq + alpha * alpha * qq2)
    more = 1.0 + new_sum / rr_sum
    curve = total(more * more * rq - 2.0 * more * alpha * qq2 + alpha * alpha * (qq2 + energy))
    second = new_sum / curve
    first_weight = alpha + second * more
    both = alpha * second
    for f in range(F):
        r, q = r_ref[f], q_ref[f]
        control_out[f] = c0_ref[f] + first_weight * r - both * q
        residual_out[f] = r - first_weight * q + both * qq_ref[f]


def call(kernel, out_shape, scratch=(), in_specs=None, out_specs=None, limit=VMEM_BYTES):
    params = {"in_specs": in_specs, "out_specs": out_specs}
    return pl.pallas_call(
        kernel,
        out_shape=out_shape,
        scratch_shapes=list(scratch),
        compiler_params=pltpu.CompilerParams(vmem_limit_bytes=limit),
        cost_estimate=pl.CostEstimate(flops=1, bytes_accessed=1, transcendentals=0),
        **{name: value for name, value in params.items() if value is not None},
    )


def f32(*shape):
    return jax.ShapeDtypeStruct(shape, jnp.float32)


def vmem(*shape, kind=jnp.float32):
    return pltpu.VMEM(shape, kind)


def shards(
    control_start, coef_x, coef_y, innovation, obs_weight, interp, obs_owner, cell_key, stencil
):
    groups, spans = lax.axis_size("py"), lax.axis_size("px")
    half = groups // 2
    rows = innovation.shape[0]
    cap = 3 * rows // groups
    blk = SEG if cap % SEG == 0 else HALF
    meta_rows = -(-4 * (cap // blk) // 8) * 8
    block_rows = 2 * cap + meta_rows
    chunks = rows // SEG
    nx, width = control_start.shape[2], control_start.shape[3]
    ext = width + SEG
    c0, cx = control_start[:, 0], coef_x[0]
    hbm, local, scalars = (
        pl.BlockSpec(memory_space=s) for s in (pltpu.HBM, pltpu.VMEM, pltpu.SMEM))
    ints = vmem(chunks, SEG, kind=jnp.int32)
    dma = pltpu.SemaphoreType.DMA

    def to_half(block, k):
        return lax.ppermute(block, "py", [(i, i ^ k) for i in range(groups)])

    def across(parts):
        return [
            lax.ppermute(parts[k], ("px", "py"), [
                (i * groups + j, (i ^ k) * groups + (j ^ half))
                for i in range(spans) for j in range(groups)])
            for k in range(spans)]

    *w_blocks, slots = call(
        functools.partial(pack_weights_kernel, groups, cap, blk, block_rows),
        (f32(block_rows, SEG),) * half + (jax.ShapeDtypeStruct((chunks, SEG), jnp.int32),),
        [ints, ints, ints, vmem(chunks, SEG), vmem(rows, SEG), vmem(half * block_rows, SEG), ints,
         pltpu.SMEM((chunks, SEG), jnp.int32), dma((5,)), dma((half,)), dma],
        [hbm] * 5,
        (hbm,) * half + (local,),
        limit=PACK_BYTES,
    )(
        obs_owner.reshape(chunks, SEG), cell_key.reshape(chunks, SEG),
        stencil.reshape(chunks, SEG), interp.reshape(chunks, SEG), obs_weight,
    )
    *v_blocks, swap = call(
        functools.partial(pack_products_kernel, groups, cap),
        (f32(2 * cap, SEG),) * half + (f32(spans, LX * ext // SEG + (F + 1) * nx, SEG),),
        [vmem(rows, SEG), vmem(rows, SEG), vmem(*coef_y.shape[1:]), vmem(F + 1, nx, SEG),
         vmem(F + 1, nx, SEG), vmem(groups * cap, SEG), dma((7,)), dma((half,))],
        [scalars] + [hbm] * 5,
        (hbm,) * half + (local,),
        limit=PACK_BYTES,
    )(slots, obs_weight, innovation, coef_y[0], c0, cx)
    w_blocks[1:] = [to_half(w_blocks[k], k) for k in range(1, half)]
    w_blocks[1], *v_blocks[1:] = lax.optimization_barrier((w_blocks[1], *v_blocks[1:]))
    v_blocks[1:] = [to_half(v_blocks[k], k) for k in range(1, half)]

    swap = lax.all_to_all(swap, "px", split_axis=0, concat_axis=0, tiled=True)
    c0_ext, cx_ext, cy_ext, u_ext, token = call(
        start_kernel,
        (f32(F, nx, ext), f32(nx, ext), f32(nx, ext), f32(F, nx, ext), f32(8, SEG)),
    )(c0, cx, swap)

    def sum_weights(side, token):
        return call(
            functools.partial(weights_kernel, half, cap, blk, side),
            (f32(half, meta_rows, SEG),) + (f32(ROWS, SEG),) * 2,
            [vmem(ROWS, 3 * SEG)],
        )(*w_blocks, token)

    meta, *side_across = sum_weights(1, token)
    side_across = [to_half(values, half) for values in side_across]
    meta, *side = sum_weights(0, meta)
    meta, *sums_across = call(
        functools.partial(products_across_kernel, half, cap, blk),
        (f32(half, meta_rows, SEG),) + (f32(F, LX, ext),) * spans,
        [vmem(ROWS, 2 * SEG), vmem(ROWS, SEG)],
    )(meta, *v_blocks)
    sums_across = across(sums_across)
    parts = call(
        functools.partial(products_kernel, half, cap, blk),
        f32(spans, 3 * F, LX, ext),
        [vmem(ROWS, 2 * SEG), vmem(ROWS, SEG), vmem(2, ROWS, SEG)],
    )(meta, *side, *side_across, *v_blocks)
    parts = lax.all_to_all(parts, "px", split_axis=0, concat_axis=0, tiled=True)

    r, q, h, dots = call(
        functools.partial(solve_kernel, spans),
        (f32(F, nx, width),) * 2 + (f32(F, nx, ext), f32(groups * spans, 1, SEG)),
        [vmem(3, F, nx, ext), vmem(3 * F, nx, ext), vmem(nx, ext)],
    )(c0_ext, cx_ext, cy_ext, u_ext, parts, *sums_across)
    dots = lax.all_to_all(dots, ("px", "py"), split_axis=0, concat_axis=0, tiled=True)
    qq = call(last_kernel, f32(F, nx, width), [vmem(nx, ext)] * 2)(h, q, cx_ext, cy_ext)
    control, residual = call(finish_kernel, (f32(F, nx, width),) * 2)(dots, c0, r, q, qq)
    return control[:, None], residual[:, None]


def solution(mesh):
    return jax.shard_map(
        shards,
        mesh=mesh,
        in_specs=(
            P(None, "py", None, "px"),
            P("py", None, "px"),
            P("py", "px", None),
            P(("px", "py"), None),
            P(("px", "py"), None),
            P(("px", "py")),
            P(("px", "py"), None),
            P(("px", "py")),
            P(("px", "py")),
        ),
        out_specs=(P(None, "py", None, "px"), P(None, "py", None, "px")),
        check_vma=False,
    )
```

```python
import functools

import jax
import jax.numpy as jnp
from jax import lax
from jax.experimental import pallas as pl
from jax.experimental.pallas import tpu as pltpu
from jax.sharding import PartitionSpec as P

F = 2
SEG = 128
M = 4
NB = 16
LX = 16
ROWS = F * NB * LX
HALF = SEG // 2
SPLIT = 16
X_WIDTH = 256
Y_LINES = 16
VMEM_BYTES = 32 * 1024 * 1024
PACK_BYTES = 60 * 1024 * 1024
FIRST = 100_000_000
JOIN = 100_000_000


def iota(shape, axis):
    return lax.broadcasted_iota(jnp.int32, shape, axis)


def flag(condition, kind=jnp.bfloat16):
    return jnp.where(condition, 1.0, 0.0).astype(kind)


def mxu(left, right):
    return jnp.dot(left, right, preferred_element_type=jnp.float32)


def split_parts(values, count):
    parts = []
    for _ in range(count):
        part = values.astype(jnp.bfloat16)
        parts.append(part)
        values = values - part.astype(jnp.float32)
    return parts


def ends_tile(before, after):
    return jnp.where(iota(after.shape, after.ndim - 1) < HALF, after, before)


def sweep(values, coeffs, axis):
    size = values.shape[axis]
    for _ in range(M):
        flux = coeffs * (pltpu.roll(values, size - 1, axis) - values)
        values = values + flux - pltpu.roll(flux, 1, axis)
    return values


def start_copies(pairs, sems):
    copies = [pltpu.make_async_copy(*pair, sems.at[i]) for i, pair in enumerate(pairs)]
    for copy in copies:
        copy.start()
    return copies


def pack_weights_kernel(groups, cap, blk, block_rows, own_hbm, key_hbm, sten_hbm, itp_hbm, w_hbm,
                        *rest):
    half = groups // 2
    outs, rest = rest[:half], rest[half:]
    (slot_out, own_ref, key_ref, sten_ref, itp_ref, w_ref, buffer, slot_v, slot_s, sems, out_sems,
     sem) = rest
    loads = start_copies([(own_hbm, own_ref), (key_hbm, key_ref), (sten_hbm, sten_ref),
                          (itp_hbm, itp_ref), (w_hbm, w_ref)], sems)

    def clear(k, carry):
        start = pl.multiple_of(k * block_rows, 8)
        buffer[pl.ds(start, block_rows), :] = jnp.zeros((block_rows, SEG), jnp.float32)
        return carry

    lax.fori_loop(0, half, clear, 0)

    for load in loads[:4]:
        load.wait()
    chunks = own_ref.shape[0]
    nb = cap // blk
    own = own_ref[...]
    high = groups * chunks
    shift = chunks.bit_length() - 1
    masks = [flag(own == o, jnp.float32) for o in range(groups)]
    hits = jnp.concatenate(masks, axis=0).astype(jnp.bfloat16)
    square = (SEG, SEG)
    within = mxu(hits, flag(iota(square, 0) < iota(square, 1)))
    tallies = mxu(hits, jnp.ones(square, jnp.bfloat16)).astype(jnp.bfloat16)
    line, column = iota((high, high), 0), iota((high, high), 1)
    same = (line >> shift) == (column >> shift)
    ranks = within + mxu(flag(same & (column < line)), tallies)
    rank = sum(masks[o] * ranks[o * chunks:(o + 1) * chunks] for o in range(groups))
    rank = rank.astype(jnp.int32)
    relative = own ^ lax.axis_index("py")
    block, across = relative & (half - 1), relative >> (half.bit_length() - 1)
    slot_v[...] = block * block_rows + across * cap + rank
    slot_out[...] = (block * 2 + across) * cap + rank
    copy = pltpu.make_async_copy(slot_v, slot_s, sem)
    copy.start()

    log = blk.bit_length() - 1
    place = relative * nb + (rank >> log)
    lane = rank & (blk - 1)
    key, sten, itp = key_ref[...], sten_ref[...], itp_ref[...]
    tall = groups * nb
    meta = jnp.zeros((5 * tall, SEG), jnp.float32)
    for i in range(chunks):
        chosen = iota((tall, SEG), 0) == place[i:i + 1]
        parts = split_parts(itp[i:i + 1], 3)
        parts += [key[i:i + 1].astype(jnp.bfloat16), (sten[i:i + 1] + 1).astype(jnp.bfloat16)]
        left = [jnp.where(chosen, part.astype(jnp.float32), 0.0) for part in parts]
        right = flag(iota(square, 0) == lane[i:i + 1])
        meta = meta + lax.dot_general(
            jnp.concatenate(left, axis=0).astype(jnp.bfloat16), right,
            (((1,), (1,)), ((), ())), preferred_element_type=jnp.float32)
    shares = meta[:tall] + meta[tall:2 * tall] + meta[2 * tall:3 * tall]
    targets = meta[3 * tall:4 * tall] * LX + meta[4 * tall:]
    for v in range(groups):
        base = (v % half) * block_rows + 2 * cap + (v // half) * 2 * nb
        buffer[base:base + nb, :] = shares[v * nb:(v + 1) * nb]
        buffer[base + nb:base + 2 * nb, :] = targets[v * nb:(v + 1) * nb]

    copy.wait()
    loads[4].wait()

    def place_rows(g, carry):
        weights = w_ref[pl.ds(pl.multiple_of(g * 8, 8), 8), :]
        line, lane = g // 16, (g % 16) * 8
        for i in range(8):
            buffer[pl.ds(slot_s[line, lane + i], 1), :] = weights[i:i + 1]
        return carry

    lax.fori_loop(0, w_ref.shape[0] // 8, place_rows, 0)
    for store in start_copies([(buffer.at[pl.ds(k * block_rows, block_rows)], out)
                               for k, out in enumerate(outs)], out_sems):
        store.wait()


def pack_products_kernel(groups, cap, slot_ref, w_hbm, d_hbm, cy_hbm, c0_hbm, cx_hbm, *rest):
    half = groups // 2
    outs, (swap_out, w_ref, d_ref, cy_ref, first, last, buffer, sems, out_sems) = (
        rest[:half], rest[half:])
    width = c0_hbm.shape[2]
    loads = start_copies([
        (w_hbm, w_ref), (d_hbm, d_ref), (cy_hbm, cy_ref),
        (c0_hbm.at[:, :, pl.ds(0, SEG)], first.at[pl.ds(0, F)]),
        (cx_hbm.at[:, pl.ds(0, SEG)], first.at[F]),
        (c0_hbm.at[:, :, pl.ds(width - SEG, SEG)], last.at[pl.ds(0, F)]),
        (cx_hbm.at[:, pl.ds(width - SEG, SEG)], last.at[F]),
    ], sems)

    def clear(o, carry):
        start = pl.multiple_of(o * cap, 8)
        buffer[pl.ds(start, cap), :] = jnp.zeros((cap, SEG), jnp.float32)
        return carry

    lax.fori_loop(0, groups, clear, 0)

    for load in loads:
        load.wait()

    def place_rows(g, carry):
        start = pl.multiple_of(g * 8, 8)
        products = w_ref[pl.ds(start, 8), :] * d_ref[pl.ds(start, 8), :]
        line, lane = g // 16, (g % 16) * 8
        for i in range(8):
            buffer[pl.ds(slot_ref[line, lane + i], 1), :] = products[i:i + 1]
        return carry

    lax.fori_loop(0, w_ref.shape[0] // 8, place_rows, 0)
    stores = start_copies([(buffer.at[pl.ds(k * 2 * cap, 2 * cap)], out)
                           for k, out in enumerate(outs)], out_sems)
    columns = cy_ref.shape[1]
    cy = cy_ref[...]
    cy = jnp.where(iota(cy.shape, 1) == columns - 1, 0.0, cy)
    empty = jnp.zeros((LX, SEG), jnp.float32)
    me = lax.axis_index("px")
    nx = first.shape[1]
    for q in range(columns // width):
        low, top = q * width, (q + 1) * width
        tiles = [cy[:, t:t + SEG] for t in range(low, top, SEG)]
        before = cy[:, low - SEG:low] if low > 0 else empty
        after = cy[:, top:top + SEG] if top < columns else empty
        tiles.append(ends_tile(before, after))
        for t, tile in enumerate(tiles):
            swap_out[q, t * LX:(t + 1) * LX, :] = tile
        base = len(tiles) * LX
        for i in range(F + 1):
            swap_out[q, base + i * nx:base + (i + 1) * nx, :] = jnp.where(
                q < me, first[i], last[i])
    for store in stores:
        store.wait()


def sum_rows(cap, blk, metas, acc_ref, terms):
    nb = cap // blk
    numbers = 1.0 + iota((ROWS, cap), 0).astype(jnp.float32)
    for source, meta in enumerate(metas):
        upper = jnp.concatenate(
            [jnp.broadcast_to(meta[i:i + 1], (SEG, SEG)).T[:blk] for i in range(nb)], axis=0)
        target = jnp.concatenate([meta[nb + i:nb + i + 1, :blk] for i in range(nb)], axis=1)
        hit = flag(numbers == target)
        values = jnp.concatenate(terms(source, upper), axis=1)
        part = mxu(jnp.concatenate([hit, hit], axis=1),
                   jnp.concatenate(split_parts(values, 2), axis=0))
        if source:
            acc_ref[...] += part
        else:
            acc_ref[...] = part


def cut_part(rows_ref, to, f, q, spans):
    width = to.shape[1] - SEG
    per = width // SEG

    def tile(b):
        start = pl.multiple_of((f * NB + b) * LX, LX)
        return rows_ref[pl.ds(start, LX), :]

    for j in range(per):
        to[:, j * SEG:(j + 1) * SEG] = tile(q * per + j)
    before = tile(jnp.maximum(q * per - 1, 0))
    after = tile(jnp.minimum(q * per + per, NB - 1))
    to[:, width:] = ends_tile(jnp.where(q > 0, before, 0.0),
                              jnp.where(q < spans - 1, after, 0.0))


def weights_kernel(half, cap, blk, across, *rest):
    w_refs, (_, meta_out, diagonal_out, side_out, acc_ref) = rest[:half], rest[half:]
    nb = cap // blk
    for k, w_ref in enumerate(w_refs):
        meta_out[k] = w_ref[2 * cap:, :]
    rows = slice(across * cap, (across + 1) * cap)

    def terms(source, upper):
        lower = 1.0 - upper
        weights = w_refs[source][rows, :]
        lower_w, upper_w = lower * weights, upper * weights
        return [lower * lower_w, upper * lower_w, upper * upper_w]

    low = 2 * cap + across * 2 * nb
    sum_rows(cap, blk, [w_ref[low:low + 2 * nb, :] for w_ref in w_refs], acc_ref, terms)
    diagonal_out[...] = acc_ref[:, :SEG] + pltpu.roll(acc_ref[:, 2 * SEG:], 1, 0)
    side_out[...] = acc_ref[:, SEG:2 * SEG]


def sum_products(half, cap, blk, across, meta_ref, v_refs, acc_ref, sums_ref):
    nb = cap // blk
    rows = slice(across * cap, (across + 1) * cap)

    def terms(source, upper):
        products = v_refs[source][rows, :]
        return [(1.0 - upper) * products, upper * products]

    low = across * 2 * nb
    sum_rows(cap, blk, [meta_ref[k, low:low + 2 * nb, :] for k in range(half)], acc_ref, terms)
    sums_ref[...] = acc_ref[:, :SEG] + pltpu.roll(acc_ref[:, SEG:], 1, 0)


def products_across_kernel(half, cap, blk, meta_ref, *rest):
    v_refs, (meta_out, *outs, acc_ref, sums_ref) = rest[:half], rest[half:]
    meta_out[...] = meta_ref[...]
    sum_products(half, cap, blk, 1, meta_ref, v_refs, acc_ref, sums_ref)
    me = lax.axis_index("px")
    for k, out in enumerate(outs):
        for f in range(F):
            cut_part(sums_ref, out.at[f], f, me ^ k, len(outs))


def products_kernel(half, cap, blk, meta_ref, d_ref, e_ref, far_d_ref, far_e_ref, *rest):
    v_refs, (out, acc_ref, sums_ref, side) = rest[:half], rest[half:]
    spans = out.shape[0]
    sum_products(half, cap, blk, 0, meta_ref, v_refs, acc_ref, sums_ref)
    side[0] = d_ref[...] + far_d_ref[...]
    side[1] = e_ref[...] + far_e_ref[...]
    for q in range(spans):
        for channel, rows_ref in enumerate((side.at[0], side.at[1], sums_ref)):
            for f in range(F):
                cut_part(rows_ref, out.at[q, channel * F + f], f, q, spans)


def sweep_x_into(to_ref, from_ref, cx_ref, plus_ref=None, sign=1.0):
    size = cx_ref.shape[1]
    for low in range(0, size, X_WIDTH):
        tile = slice(low, min(low + X_WIDTH, size))
        values = sweep(from_ref[:, tile], cx_ref[:, tile], 0)
        if plus_ref is not None:
            values = values + sign * plus_ref[:, tile]
        to_ref[:, tile] = values


def sweep_y_into(to_ref, from_ref, cy_ref):
    for low in range(0, cy_ref.shape[0], Y_LINES):
        lines = slice(low, low + Y_LINES)
        to_ref[lines, :] = sweep(from_ref[lines, :], cy_ref[lines, :], 1)


def start_kernel(c0_ref, cx_ref, swap_ref, c0_out, cx_out, cy_out, u_out, token_out):
    token_out[...] = jnp.zeros_like(token_out)
    width = c0_ref.shape[2]
    nx = cx_ref.shape[0]
    spans, count = swap_ref.shape[0], cy_out.shape[1] // SEG
    me = lax.axis_index("px")
    for p in range(spans):
        for t in range(count):
            cy_out[p * LX:(p + 1) * LX, t * SEG:(t + 1) * SEG] = (
                swap_ref[p, t * LX:(t + 1) * LX, :])

    def beside(i):
        lines = slice(count * LX + i * nx, count * LX + (i + 1) * nx)
        before = swap_ref[jnp.maximum(me - 1, 0), lines, :]
        after = swap_ref[jnp.minimum(me + 1, spans - 1), lines, :]
        return ends_tile(jnp.where(me > 0, before, 0.0), jnp.where(me < spans - 1, after, 0.0))

    last = cx_ref.shape[0] - 1
    cx_out[:, :width] = cx_ref[...]
    cx_out[:, width:] = beside(F)
    cx_out[last:, :] = jnp.zeros((1, width + SEG), jnp.float32)
    for f in range(F):
        c0_out[f, :, :width] = c0_ref[f]
        c0_out[f, :, width:] = beside(f)
        sweep_x_into(u_out.at[f], c0_out.at[f], cx_out)
        sweep_y_into(u_out.at[f], u_out.at[f], cy_out)


def join_kernel(spans, *rest):
    parts, out = rest[:spans], rest[spans]
    me = lax.axis_index("px")
    for k, part in enumerate(parts):
        for f in range(F):
            out[f, pl.ds(pl.multiple_of((me ^ k) * LX, LX), LX), :] = part[f]


def solve_kernel(c0_ref, cx_ref, cy_ref, u_ref, obs_ref, far_ref, r_out, q_out, h_out, dots_out,
                 vec, coef, work):
    width = r_out.shape[2]
    for p in range(obs_ref.shape[0]):
        rows = slice(p * LX, (p + 1) * LX)
        for channel in range(2 * F):
            coef[channel, rows, :] = obs_ref[p, channel]
        for f in range(F):
            coef[2 * F + f, rows, :] = obs_ref[p, 2 * F + f] + far_ref[f, rows, :]

    def normal(f, values, tile):
        size = values.shape[0]
        side = coef[F + f, :, tile]
        return (coef[f, :, tile] * values + side * pltpu.roll(values, size - 1, 0)
                + pltpu.roll(side * values, 1, 0))

    tiles = [slice(low, low + SEG) for low in range(0, width + SEG, SEG)]

    def first(f, carry):
        for tile in tiles:
            work[:, tile] = coef[2 * F + f, :, tile] - normal(f, u_ref[f, :, tile], tile)
        sweep_y_into(work, work, cy_ref)
        sweep_x_into(vec.at[0, f], work, cx_ref, c0_ref.at[f], -1.0)
        return carry

    lax.fori_loop(0, F, first, 0)

    def apply(f, carry):
        sweep_x_into(work, vec.at[0, f], cx_ref)
        sweep_y_into(work, work, cy_ref)
        for tile in tiles:
            work[:, tile] = normal(f, work[:, tile], tile)
        sweep_y_into(work, work, cy_ref)
        sweep_x_into(vec.at[1, f], work, cx_ref, vec.at[0, f])
        sweep_x_into(vec.at[2, f], vec.at[1, f], cx_ref)
        sweep_y_into(vec.at[2, f], vec.at[2, f], cy_ref)
        for tile in tiles:
            h_out[f, :, tile] = normal(f, vec[2, f, :, tile], tile)
        return carry

    lax.fori_loop(0, F, apply, 0)

    sums = [jnp.zeros((8, SEG), jnp.float32) for _ in range(4)]
    for f in range(F):
        r_out[f] = vec[0, f, :, :width]
        q_out[f] = vec[1, f, :, :width]
        for low in range(0, vec.shape[2], 8):
            for tile in tiles[:-1]:
                r = vec[0, f, low:low + 8, tile]
                q = vec[1, f, low:low + 8, tile]
                s = vec[2, f, low:low + 8, tile]
                for i, product in enumerate((r * r, r * q, q * q, s * h_out[f, low:low + 8, tile])):
                    sums[i] = sums[i] + product
    dots = jnp.zeros((1, SEG), jnp.float32)
    for i, total in enumerate(sums):
        line = jnp.sum(total, axis=0, keepdims=True)
        for distance in (64, 32, 16):
            line = line + pltpu.roll(line, distance, 1)
        dots = jnp.where(iota((1, SEG), 1) // SPLIT == i, line, dots)
    dots_out[...] = jnp.broadcast_to(dots, dots_out.shape)


def last_kernel(h_ref, q_ref, cx_ref, cy_ref, qq_out, work, other):
    width = qq_out.shape[2]

    def apply(f, carry):
        sweep_y_into(work, h_ref.at[f], cy_ref)
        sweep_x_into(other, work, cx_ref)
        qq_out[f] = q_ref[f] + other[:, :width]
        return carry

    lax.fori_loop(0, F, apply, 0)


def finish_kernel(dots_ref, c0_ref, r_ref, q_ref, qq_ref, control_out, residual_out):
    dots = jnp.sum(dots_ref[...], axis=0)
    lane = iota((1, SEG), 1)
    rr, rq, qq2, energy = (pltpu.roll(dots, (SEG - i * SPLIT) % SEG, 1) for i in range(4))

    def total(line):
        return jnp.sum(jnp.where(lane < SPLIT, line, 0.0), axis=1, keepdims=True)

    rr_sum = total(rr)
    alpha = rr_sum / total(rq)
    new_sum = total(rr - 2.0 * alpha * rq + alpha * alpha * qq2)
    more = 1.0 + new_sum / rr_sum
    curve = total(more * more * rq - 2.0 * more * alpha * qq2 + alpha * alpha * (qq2 + energy))
    second = new_sum / curve
    first_weight = alpha + second * more
    both = alpha * second
    for f in range(F):
        r, q = r_ref[f], q_ref[f]
        control_out[f] = c0_ref[f] + first_weight * r - both * q
        residual_out[f] = r - first_weight * q + both * qq_ref[f]


def call(kernel, out_shape, scratch=(), in_specs=None, out_specs=None, limit=VMEM_BYTES,
         weight=1):
    params = {"in_specs": in_specs, "out_specs": out_specs}
    return pl.pallas_call(
        kernel,
        out_shape=out_shape,
        scratch_shapes=list(scratch),
        compiler_params=pltpu.CompilerParams(vmem_limit_bytes=limit),
        cost_estimate=pl.CostEstimate(flops=weight, bytes_accessed=weight, transcendentals=0),
        **{name: value for name, value in params.items() if value is not None},
    )


def f32(*shape):
    return jax.ShapeDtypeStruct(shape, jnp.float32)


def vmem(*shape, kind=jnp.float32):
    return pltpu.VMEM(shape, kind)


def shards(
    control_start, coef_x, coef_y, innovation, obs_weight, interp, obs_owner, cell_key, stencil
):
    groups, spans = lax.axis_size("py"), lax.axis_size("px")
    half = groups // 2
    rows = innovation.shape[0]
    cap = 3 * rows // groups
    blk = SEG if cap % SEG == 0 else HALF
    meta_rows = -(-4 * (cap // blk) // 8) * 8
    block_rows = 2 * cap + meta_rows
    chunks = rows // SEG
    nx, width = control_start.shape[2], control_start.shape[3]
    ext = width + SEG
    c0, cx = control_start[:, 0], coef_x[0]
    hbm, local, scalars = (
        pl.BlockSpec(memory_space=s) for s in (pltpu.HBM, pltpu.VMEM, pltpu.SMEM))
    ints = vmem(chunks, SEG, kind=jnp.int32)
    dma = pltpu.SemaphoreType.DMA

    def to_half(block, k):
        return lax.ppermute(block, "py", [(i, i ^ k) for i in range(groups)])

    def across(parts):
        return [
            lax.ppermute(parts[k], ("px", "py"), [
                (i * groups + j, (i ^ k) * groups + (j ^ half))
                for i in range(spans) for j in range(groups)])
            for k in range(spans)]

    *w_blocks, slots = call(
        functools.partial(pack_weights_kernel, groups, cap, blk, block_rows),
        (f32(block_rows, SEG),) * half + (jax.ShapeDtypeStruct((chunks, SEG), jnp.int32),),
        [ints, ints, ints, vmem(chunks, SEG), vmem(rows, SEG), vmem(half * block_rows, SEG), ints,
         pltpu.SMEM((chunks, SEG), jnp.int32), dma((5,)), dma((half,)), dma],
        [hbm] * 5,
        (hbm,) * half + (local,),
        limit=PACK_BYTES,
    )(
        obs_owner.reshape(chunks, SEG), cell_key.reshape(chunks, SEG),
        stencil.reshape(chunks, SEG), interp.reshape(chunks, SEG), obs_weight,
    )
    *v_blocks, swap = call(
        functools.partial(pack_products_kernel, groups, cap),
        (f32(2 * cap, SEG),) * half + (f32(spans, LX * ext // SEG + (F + 1) * nx, SEG),),
        [vmem(rows, SEG), vmem(rows, SEG), vmem(*coef_y.shape[1:]), vmem(F + 1, nx, SEG),
         vmem(F + 1, nx, SEG), vmem(groups * cap, SEG), dma((7,)), dma((half,))],
        [scalars] + [hbm] * 5,
        (hbm,) * half + (local,),
        limit=PACK_BYTES,
    )(slots, obs_weight, innovation, coef_y[0], c0, cx)
    for k in range(1, half):
        w_blocks[k], v_blocks[k] = lax.optimization_barrier((to_half(w_blocks[k], k), v_blocks[k]))
        v_blocks[k] = to_half(v_blocks[k], k)

    swap = lax.all_to_all(swap, "px", split_axis=0, concat_axis=0, tiled=True)
    c0_ext, cx_ext, cy_ext, u_ext, token = call(
        start_kernel,
        (f32(F, nx, ext), f32(nx, ext), f32(nx, ext), f32(F, nx, ext), f32(8, SEG)),
    )(c0, cx, swap)

    def sum_weights(side, token, weight):
        return call(
            functools.partial(weights_kernel, half, cap, blk, side),
            (f32(half, meta_rows, SEG),) + (f32(ROWS, SEG),) * 2,
            [vmem(ROWS, 3 * SEG)],
            weight=weight,
        )(*w_blocks, token)

    meta, *side_across = sum_weights(1, w_blocks[0], FIRST)
    side_across = [to_half(values, half) for values in side_across]
    meta, *side = sum_weights(0, token, 1)
    meta, *sums_across = call(
        functools.partial(products_across_kernel, half, cap, blk),
        (f32(half, meta_rows, SEG),) + (f32(F, LX, ext),) * spans,
        [vmem(ROWS, 2 * SEG), vmem(ROWS, SEG)],
    )(meta, *v_blocks)
    far_sums = call(
        functools.partial(join_kernel, spans), f32(F, nx, ext), weight=JOIN,
    )(*across(sums_across))
    parts = call(
        functools.partial(products_kernel, half, cap, blk),
        f32(spans, 3 * F, LX, ext),
        [vmem(ROWS, 2 * SEG), vmem(ROWS, SEG), vmem(2, ROWS, SEG)],
    )(meta, *side, *side_across, *v_blocks)
    parts = lax.all_to_all(parts, "px", split_axis=0, concat_axis=0, tiled=True)

    r, q, h, dots = call(
        solve_kernel,
        (f32(F, nx, width),) * 2 + (f32(F, nx, ext), f32(groups * spans, 1, SEG)),
        [vmem(3, F, nx, ext), vmem(3 * F, nx, ext), vmem(nx, ext)],
    )(c0_ext, cx_ext, cy_ext, u_ext, parts, far_sums)
    dots = lax.all_to_all(dots, ("px", "py"), split_axis=0, concat_axis=0, tiled=True)
    qq = call(last_kernel, f32(F, nx, width), [vmem(nx, ext)] * 2)(h, q, cx_ext, cy_ext)
    control, residual = call(finish_kernel, (f32(F, nx, width),) * 2)(dots, c0, r, q, qq)
    return control[:, None], residual[:, None]


def solution(mesh):
    return jax.shard_map(
        shards,
        mesh=mesh,
        in_specs=(
            P(None, "py", None, "px"),
            P("py", None, "px"),
            P("py", "px", None),
            P(("px", "py"), None),
            P(("px", "py"), None),
            P(("px", "py")),
            P(("px", "py"), None),
            P(("px", "py")),
            P(("px", "py")),
        ),
        out_specs=(P(None, "py", None, "px"), P(None, "py", None, "px")),
        check_vma=False,
    )
```

```python
import functools

import jax
import jax.numpy as jnp
from jax import lax
from jax.experimental import pallas as pl
from jax.experimental.pallas import tpu as pltpu
from jax.sharding import PartitionSpec as P

F = 2
SEG = 128
M = 4
NB = 16
LX = 16
ROWS = F * NB * LX
HALF = SEG // 2
SPLIT = 16
X_WIDTH = 256
Y_LINES = 16
VMEM_BYTES = 32 * 1024 * 1024
PACK_BYTES = 60 * 1024 * 1024
FIRST = 100_000_000
JOIN = 400_000_000


def iota(shape, axis):
    return lax.broadcasted_iota(jnp.int32, shape, axis)


def flag(condition, kind=jnp.bfloat16):
    return jnp.where(condition, 1.0, 0.0).astype(kind)


def mxu(left, right):
    return jnp.dot(left, right, preferred_element_type=jnp.float32)


def split_parts(values, count):
    parts = []
    for _ in range(count):
        part = values.astype(jnp.bfloat16)
        parts.append(part)
        values = values - part.astype(jnp.float32)
    return parts


def ends_tile(before, after):
    return jnp.where(iota(after.shape, after.ndim - 1) < HALF, after, before)


def sweep(values, coeffs, axis):
    size = values.shape[axis]
    for _ in range(M):
        flux = coeffs * (pltpu.roll(values, size - 1, axis) - values)
        values = values + flux - pltpu.roll(flux, 1, axis)
    return values


def start_copies(pairs, sems):
    copies = [pltpu.make_async_copy(*pair, sems.at[i]) for i, pair in enumerate(pairs)]
    for copy in copies:
        copy.start()
    return copies


def pack_weights_kernel(groups, cap, blk, block_rows, own_hbm, key_hbm, sten_hbm, itp_hbm, w_hbm,
                        *rest):
    half = groups // 2
    outs, rest = rest[:half], rest[half:]
    (slot_out, own_ref, key_ref, sten_ref, itp_ref, w_ref, buffer, slot_v, slot_s, sems, out_sems,
     sem) = rest
    loads = start_copies([(own_hbm, own_ref), (key_hbm, key_ref), (sten_hbm, sten_ref),
                          (itp_hbm, itp_ref), (w_hbm, w_ref)], sems)

    def clear(k, carry):
        start = pl.multiple_of(k * block_rows, 8)
        buffer[pl.ds(start, block_rows), :] = jnp.zeros((block_rows, SEG), jnp.float32)
        return carry

    lax.fori_loop(0, half, clear, 0)

    for load in loads[:4]:
        load.wait()
    chunks = own_ref.shape[0]
    nb = cap // blk
    own = own_ref[...]
    high = groups * chunks
    shift = chunks.bit_length() - 1
    masks = [flag(own == o, jnp.float32) for o in range(groups)]
    hits = jnp.concatenate(masks, axis=0).astype(jnp.bfloat16)
    square = (SEG, SEG)
    within = mxu(hits, flag(iota(square, 0) < iota(square, 1)))
    tallies = mxu(hits, jnp.ones(square, jnp.bfloat16)).astype(jnp.bfloat16)
    line, column = iota((high, high), 0), iota((high, high), 1)
    same = (line >> shift) == (column >> shift)
    ranks = within + mxu(flag(same & (column < line)), tallies)
    rank = sum(masks[o] * ranks[o * chunks:(o + 1) * chunks] for o in range(groups))
    rank = rank.astype(jnp.int32)
    relative = own ^ lax.axis_index("py")
    block, across = relative & (half - 1), relative >> (half.bit_length() - 1)
    slot_v[...] = block * block_rows + across * cap + rank
    slot_out[...] = (block * 2 + across) * cap + rank
    copy = pltpu.make_async_copy(slot_v, slot_s, sem)
    copy.start()

    log = blk.bit_length() - 1
    place = relative * nb + (rank >> log)
    lane = rank & (blk - 1)
    key, sten, itp = key_ref[...], sten_ref[...], itp_ref[...]
    tall = groups * nb
    meta = jnp.zeros((5 * tall, SEG), jnp.float32)
    for i in range(chunks):
        chosen = iota((tall, SEG), 0) == place[i:i + 1]
        parts = split_parts(itp[i:i + 1], 3)
        parts += [key[i:i + 1].astype(jnp.bfloat16), (sten[i:i + 1] + 1).astype(jnp.bfloat16)]
        left = [jnp.where(chosen, part.astype(jnp.float32), 0.0) for part in parts]
        right = flag(iota(square, 0) == lane[i:i + 1])
        meta = meta + lax.dot_general(
            jnp.concatenate(left, axis=0).astype(jnp.bfloat16), right,
            (((1,), (1,)), ((), ())), preferred_element_type=jnp.float32)
    shares = meta[:tall] + meta[tall:2 * tall] + meta[2 * tall:3 * tall]
    targets = meta[3 * tall:4 * tall] * LX + meta[4 * tall:]
    for v in range(groups):
        base = (v % half) * block_rows + 2 * cap + (v // half) * 2 * nb
        buffer[base:base + nb, :] = shares[v * nb:(v + 1) * nb]
        buffer[base + nb:base + 2 * nb, :] = targets[v * nb:(v + 1) * nb]

    copy.wait()
    loads[4].wait()

    def place_rows(g, carry):
        weights = w_ref[pl.ds(pl.multiple_of(g * 8, 8), 8), :]
        line, lane = g // 16, (g % 16) * 8
        for i in range(8):
            buffer[pl.ds(slot_s[line, lane + i], 1), :] = weights[i:i + 1]
        return carry

    lax.fori_loop(0, w_ref.shape[0] // 8, place_rows, 0)
    for store in start_copies([(buffer.at[pl.ds(k * block_rows, block_rows)], out)
                               for k, out in enumerate(outs)], out_sems):
        store.wait()


def pack_products_kernel(groups, cap, slot_ref, w_hbm, d_hbm, cy_hbm, c0_hbm, cx_hbm, *rest):
    half = groups // 2
    outs, (swap_out, w_ref, d_ref, cy_ref, first, last, buffer, sems, out_sems) = (
        rest[:half], rest[half:])
    width = c0_hbm.shape[2]
    loads = start_copies([
        (w_hbm, w_ref), (d_hbm, d_ref), (cy_hbm, cy_ref),
        (c0_hbm.at[:, :, pl.ds(0, SEG)], first.at[pl.ds(0, F)]),
        (cx_hbm.at[:, pl.ds(0, SEG)], first.at[F]),
        (c0_hbm.at[:, :, pl.ds(width - SEG, SEG)], last.at[pl.ds(0, F)]),
        (cx_hbm.at[:, pl.ds(width - SEG, SEG)], last.at[F]),
    ], sems)

    def clear(o, carry):
        start = pl.multiple_of(o * cap, 8)
        buffer[pl.ds(start, cap), :] = jnp.zeros((cap, SEG), jnp.float32)
        return carry

    lax.fori_loop(0, groups, clear, 0)

    for load in loads:
        load.wait()

    def place_rows(g, carry):
        start = pl.multiple_of(g * 8, 8)
        products = w_ref[pl.ds(start, 8), :] * d_ref[pl.ds(start, 8), :]
        line, lane = g // 16, (g % 16) * 8
        for i in range(8):
            buffer[pl.ds(slot_ref[line, lane + i], 1), :] = products[i:i + 1]
        return carry

    lax.fori_loop(0, w_ref.shape[0] // 8, place_rows, 0)
    stores = start_copies([(buffer.at[pl.ds(k * 2 * cap, 2 * cap)], out)
                           for k, out in enumerate(outs)], out_sems)
    columns = cy_ref.shape[1]
    cy = cy_ref[...]
    cy = jnp.where(iota(cy.shape, 1) == columns - 1, 0.0, cy)
    empty = jnp.zeros((LX, SEG), jnp.float32)
    me = lax.axis_index("px")
    nx = first.shape[1]
    for q in range(columns // width):
        low, top = q * width, (q + 1) * width
        tiles = [cy[:, t:t + SEG] for t in range(low, top, SEG)]
        before = cy[:, low - SEG:low] if low > 0 else empty
        after = cy[:, top:top + SEG] if top < columns else empty
        tiles.append(ends_tile(before, after))
        for t, tile in enumerate(tiles):
            swap_out[q, t * LX:(t + 1) * LX, :] = tile
        base = len(tiles) * LX
        for i in range(F + 1):
            swap_out[q, base + i * nx:base + (i + 1) * nx, :] = jnp.where(
                q < me, first[i], last[i])
    for store in stores:
        store.wait()


def sum_rows(cap, blk, metas, acc_ref, terms):
    nb = cap // blk
    numbers = 1.0 + iota((ROWS, cap), 0).astype(jnp.float32)
    for source, meta in enumerate(metas):
        upper = jnp.concatenate(
            [jnp.broadcast_to(meta[i:i + 1], (SEG, SEG)).T[:blk] for i in range(nb)], axis=0)
        target = jnp.concatenate([meta[nb + i:nb + i + 1, :blk] for i in range(nb)], axis=1)
        hit = flag(numbers == target)
        values = jnp.concatenate(terms(source, upper), axis=1)
        part = mxu(jnp.concatenate([hit, hit], axis=1),
                   jnp.concatenate(split_parts(values, 2), axis=0))
        if source:
            acc_ref[...] += part
        else:
            acc_ref[...] = part


def cut_part(rows_ref, to, f, q, spans):
    width = to.shape[1] - SEG
    per = width // SEG

    def tile(b):
        start = pl.multiple_of((f * NB + b) * LX, LX)
        return rows_ref[pl.ds(start, LX), :]

    for j in range(per):
        to[:, j * SEG:(j + 1) * SEG] = tile(q * per + j)
    before = tile(jnp.maximum(q * per - 1, 0))
    after = tile(jnp.minimum(q * per + per, NB - 1))
    to[:, width:] = ends_tile(jnp.where(q > 0, before, 0.0),
                              jnp.where(q < spans - 1, after, 0.0))


def weights_kernel(half, cap, blk, across, *rest):
    w_refs, (_, meta_out, out, acc_ref) = rest[:half], rest[half:]
    nb = cap // blk
    for k, w_ref in enumerate(w_refs):
        meta_out[k] = w_ref[2 * cap:, :]
    rows = slice(across * cap, (across + 1) * cap)

    def terms(source, upper):
        lower = 1.0 - upper
        weights = w_refs[source][rows, :]
        lower_w, upper_w = lower * weights, upper * weights
        return [lower * lower_w, upper * lower_w, upper * upper_w]

    low = 2 * cap + across * 2 * nb
    sum_rows(cap, blk, [w_ref[low:low + 2 * nb, :] for w_ref in w_refs], acc_ref, terms)
    out[0] = acc_ref[:, :SEG] + pltpu.roll(acc_ref[:, 2 * SEG:], 1, 0)
    out[1] = acc_ref[:, SEG:2 * SEG]


def sum_products(half, cap, blk, across, meta_ref, v_refs, acc_ref, sums_ref):
    nb = cap // blk
    rows = slice(across * cap, (across + 1) * cap)

    def terms(source, upper):
        products = v_refs[source][rows, :]
        return [(1.0 - upper) * products, upper * products]

    low = across * 2 * nb
    sum_rows(cap, blk, [meta_ref[k, low:low + 2 * nb, :] for k in range(half)], acc_ref, terms)
    sums_ref[...] = acc_ref[:, :SEG] + pltpu.roll(acc_ref[:, SEG:], 1, 0)


def products_across_kernel(half, cap, blk, meta_ref, *rest):
    v_refs, (meta_out, *outs, acc_ref, sums_ref) = rest[:half], rest[half:]
    meta_out[...] = meta_ref[...]
    sum_products(half, cap, blk, 1, meta_ref, v_refs, acc_ref, sums_ref)
    me = lax.axis_index("px")
    for k, out in enumerate(outs):
        for f in range(F):
            cut_part(sums_ref, out.at[f], f, me ^ k, len(outs))


def products_kernel(half, cap, blk, meta_ref, side_ref, far_ref, *rest):
    v_refs, (out, acc_ref, sums_ref, side) = rest[:half], rest[half:]
    spans = out.shape[0]
    sum_products(half, cap, blk, 0, meta_ref, v_refs, acc_ref, sums_ref)
    side[...] = side_ref[...] + far_ref[...]
    for q in range(spans):
        for channel, rows_ref in enumerate((side.at[0], side.at[1], sums_ref)):
            for f in range(F):
                cut_part(rows_ref, out.at[q, channel * F + f], f, q, spans)


def sweep_x_into(to_ref, from_ref, cx_ref, plus_ref=None, sign=1.0):
    size = cx_ref.shape[1]
    for low in range(0, size, X_WIDTH):
        tile = slice(low, min(low + X_WIDTH, size))
        values = sweep(from_ref[:, tile], cx_ref[:, tile], 0)
        if plus_ref is not None:
            values = values + sign * plus_ref[:, tile]
        to_ref[:, tile] = values


def sweep_y_into(to_ref, from_ref, cy_ref):
    for low in range(0, cy_ref.shape[0], Y_LINES):
        lines = slice(low, low + Y_LINES)
        to_ref[lines, :] = sweep(from_ref[lines, :], cy_ref[lines, :], 1)


def start_kernel(c0_ref, cx_ref, swap_ref, c0_out, cx_out, cy_out, u_out, token_out):
    token_out[...] = jnp.zeros_like(token_out)
    width = c0_ref.shape[2]
    nx = cx_ref.shape[0]
    spans, count = swap_ref.shape[0], cy_out.shape[1] // SEG
    me = lax.axis_index("px")
    for p in range(spans):
        for t in range(count):
            cy_out[p * LX:(p + 1) * LX, t * SEG:(t + 1) * SEG] = (
                swap_ref[p, t * LX:(t + 1) * LX, :])

    def beside(i):
        lines = slice(count * LX + i * nx, count * LX + (i + 1) * nx)
        before = swap_ref[jnp.maximum(me - 1, 0), lines, :]
        after = swap_ref[jnp.minimum(me + 1, spans - 1), lines, :]
        return ends_tile(jnp.where(me > 0, before, 0.0), jnp.where(me < spans - 1, after, 0.0))

    last = cx_ref.shape[0] - 1
    cx_out[:, :width] = cx_ref[...]
    cx_out[:, width:] = beside(F)
    cx_out[last:, :] = jnp.zeros((1, width + SEG), jnp.float32)
    for f in range(F):
        c0_out[f, :, :width] = c0_ref[f]
        c0_out[f, :, width:] = beside(f)
        sweep_x_into(u_out.at[f], c0_out.at[f], cx_out)
        sweep_y_into(u_out.at[f], u_out.at[f], cy_out)


def join_kernel(spans, *rest):
    parts, out = rest[:spans], rest[spans]
    me = lax.axis_index("px")
    for k, part in enumerate(parts):
        for f in range(F):
            out[f, pl.ds(pl.multiple_of((me ^ k) * LX, LX), LX), :] = part[f]


def solve_kernel(c0_ref, cx_ref, cy_ref, u_ref, obs_ref, far_ref, r_out, q_out, h_out, dots_out,
                 vec, coef, work):
    width = r_out.shape[2]
    for p in range(obs_ref.shape[0]):
        rows = slice(p * LX, (p + 1) * LX)
        for channel in range(2 * F):
            coef[channel, rows, :] = obs_ref[p, channel]
        for f in range(F):
            coef[2 * F + f, rows, :] = obs_ref[p, 2 * F + f] + far_ref[f, rows, :]

    def normal(f, values, tile):
        size = values.shape[0]
        side = coef[F + f, :, tile]
        return (coef[f, :, tile] * values + side * pltpu.roll(values, size - 1, 0)
                + pltpu.roll(side * values, 1, 0))

    tiles = [slice(low, low + SEG) for low in range(0, width + SEG, SEG)]

    def first(f, carry):
        for tile in tiles:
            work[:, tile] = coef[2 * F + f, :, tile] - normal(f, u_ref[f, :, tile], tile)
        sweep_y_into(work, work, cy_ref)
        sweep_x_into(vec.at[0, f], work, cx_ref, c0_ref.at[f], -1.0)
        return carry

    lax.fori_loop(0, F, first, 0)

    def apply(f, carry):
        sweep_x_into(work, vec.at[0, f], cx_ref)
        sweep_y_into(work, work, cy_ref)
        for tile in tiles:
            work[:, tile] = normal(f, work[:, tile], tile)
        sweep_y_into(work, work, cy_ref)
        sweep_x_into(vec.at[1, f], work, cx_ref, vec.at[0, f])
        sweep_x_into(vec.at[2, f], vec.at[1, f], cx_ref)
        sweep_y_into(vec.at[2, f], vec.at[2, f], cy_ref)
        for tile in tiles:
            h_out[f, :, tile] = normal(f, vec[2, f, :, tile], tile)
        return carry

    lax.fori_loop(0, F, apply, 0)

    sums = [jnp.zeros((8, SEG), jnp.float32) for _ in range(4)]
    for f in range(F):
        r_out[f] = vec[0, f, :, :width]
        q_out[f] = vec[1, f, :, :width]
        for low in range(0, vec.shape[2], 8):
            for tile in tiles[:-1]:
                r = vec[0, f, low:low + 8, tile]
                q = vec[1, f, low:low + 8, tile]
                s = vec[2, f, low:low + 8, tile]
                for i, product in enumerate((r * r, r * q, q * q, s * h_out[f, low:low + 8, tile])):
                    sums[i] = sums[i] + product
    dots = jnp.zeros((1, SEG), jnp.float32)
    for i, total in enumerate(sums):
        line = jnp.sum(total, axis=0, keepdims=True)
        for distance in (64, 32, 16):
            line = line + pltpu.roll(line, distance, 1)
        dots = jnp.where(iota((1, SEG), 1) // SPLIT == i, line, dots)
    dots_out[...] = jnp.broadcast_to(dots, dots_out.shape)


def last_kernel(h_ref, q_ref, cx_ref, cy_ref, qq_out, work, other):
    width = qq_out.shape[2]

    def apply(f, carry):
        sweep_y_into(work, h_ref.at[f], cy_ref)
        sweep_x_into(other, work, cx_ref)
        qq_out[f] = q_ref[f] + other[:, :width]
        return carry

    lax.fori_loop(0, F, apply, 0)


def finish_kernel(dots_ref, c0_ref, r_ref, q_ref, qq_ref, control_out, residual_out):
    dots = jnp.sum(dots_ref[...], axis=0)
    lane = iota((1, SEG), 1)
    rr, rq, qq2, energy = (pltpu.roll(dots, (SEG - i * SPLIT) % SEG, 1) for i in range(4))

    def total(line):
        return jnp.sum(jnp.where(lane < SPLIT, line, 0.0), axis=1, keepdims=True)

    rr_sum = total(rr)
    alpha = rr_sum / total(rq)
    new_sum = total(rr - 2.0 * alpha * rq + alpha * alpha * qq2)
    more = 1.0 + new_sum / rr_sum
    curve = total(more * more * rq - 2.0 * more * alpha * qq2 + alpha * alpha * (qq2 + energy))
    second = new_sum / curve
    first_weight = alpha + second * more
    both = alpha * second
    for f in range(F):
        r, q = r_ref[f], q_ref[f]
        control_out[f] = c0_ref[f] + first_weight * r - both * q
        residual_out[f] = r - first_weight * q + both * qq_ref[f]


def call(kernel, out_shape, scratch=(), in_specs=None, out_specs=None, limit=VMEM_BYTES,
         weight=1):
    params = {"in_specs": in_specs, "out_specs": out_specs}
    return pl.pallas_call(
        kernel,
        out_shape=out_shape,
        scratch_shapes=list(scratch),
        compiler_params=pltpu.CompilerParams(vmem_limit_bytes=limit),
        cost_estimate=pl.CostEstimate(flops=weight, bytes_accessed=weight, transcendentals=0),
        **{name: value for name, value in params.items() if value is not None},
    )


def f32(*shape):
    return jax.ShapeDtypeStruct(shape, jnp.float32)


def vmem(*shape, kind=jnp.float32):
    return pltpu.VMEM(shape, kind)


def shards(
    control_start, coef_x, coef_y, innovation, obs_weight, interp, obs_owner, cell_key, stencil
):
    groups, spans = lax.axis_size("py"), lax.axis_size("px")
    half = groups // 2
    rows = innovation.shape[0]
    cap = 3 * rows // groups
    blk = SEG if cap % SEG == 0 else HALF
    meta_rows = -(-4 * (cap // blk) // 8) * 8
    block_rows = 2 * cap + meta_rows
    chunks = rows // SEG
    nx, width = control_start.shape[2], control_start.shape[3]
    ext = width + SEG
    c0, cx = control_start[:, 0], coef_x[0]
    hbm, local, scalars = (
        pl.BlockSpec(memory_space=s) for s in (pltpu.HBM, pltpu.VMEM, pltpu.SMEM))
    ints = vmem(chunks, SEG, kind=jnp.int32)
    dma = pltpu.SemaphoreType.DMA

    def to_half(block, k):
        return lax.ppermute(block, "py", [(i, i ^ k) for i in range(groups)])

    def across(parts):
        return [
            lax.ppermute(parts[k], ("px", "py"), [
                (i * groups + j, (i ^ k) * groups + (j ^ half))
                for i in range(spans) for j in range(groups)])
            for k in range(spans)]

    *w_blocks, slots = call(
        functools.partial(pack_weights_kernel, groups, cap, blk, block_rows),
        (f32(block_rows, SEG),) * half + (jax.ShapeDtypeStruct((chunks, SEG), jnp.int32),),
        [ints, ints, ints, vmem(chunks, SEG), vmem(rows, SEG), vmem(half * block_rows, SEG), ints,
         pltpu.SMEM((chunks, SEG), jnp.int32), dma((5,)), dma((half,)), dma],
        [hbm] * 5,
        (hbm,) * half + (local,),
        limit=PACK_BYTES,
    )(
        obs_owner.reshape(chunks, SEG), cell_key.reshape(chunks, SEG),
        stencil.reshape(chunks, SEG), interp.reshape(chunks, SEG), obs_weight,
    )
    *v_blocks, swap = call(
        functools.partial(pack_products_kernel, groups, cap),
        (f32(2 * cap, SEG),) * half + (f32(spans, LX * ext // SEG + (F + 1) * nx, SEG),),
        [vmem(rows, SEG), vmem(rows, SEG), vmem(*coef_y.shape[1:]), vmem(F + 1, nx, SEG),
         vmem(F + 1, nx, SEG), vmem(groups * cap, SEG), dma((7,)), dma((half,))],
        [scalars] + [hbm] * 5,
        (hbm,) * half + (local,),
        limit=PACK_BYTES,
    )(slots, obs_weight, innovation, coef_y[0], c0, cx)
    for k in range(1, half):
        w_blocks[k], v_blocks[k] = lax.optimization_barrier((to_half(w_blocks[k], k), v_blocks[k]))
        v_blocks[k] = to_half(v_blocks[k], k)

    swap = lax.all_to_all(swap, "px", split_axis=0, concat_axis=0, tiled=True)
    c0_ext, cx_ext, cy_ext, u_ext, token = call(
        start_kernel,
        (f32(F, nx, ext), f32(nx, ext), f32(nx, ext), f32(F, nx, ext), f32(8, SEG)),
    )(c0, cx, swap)

    def sum_weights(side, token, weight):
        return call(
            functools.partial(weights_kernel, half, cap, blk, side),
            (f32(half, meta_rows, SEG), f32(2, ROWS, SEG)),
            [vmem(ROWS, 3 * SEG)],
            weight=weight,
        )(*w_blocks, token)

    meta, far_side = sum_weights(1, w_blocks[0], FIRST)
    far_side = to_half(far_side, half)
    meta, side = sum_weights(0, token, 1)
    meta, *sums_across = call(
        functools.partial(products_across_kernel, half, cap, blk),
        (f32(half, meta_rows, SEG),) + (f32(F, LX, ext),) * spans,
        [vmem(ROWS, 2 * SEG), vmem(ROWS, SEG)],
    )(meta, *v_blocks)
    far_sums = call(
        functools.partial(join_kernel, spans), f32(F, nx, ext), weight=JOIN,
    )(*across(sums_across))
    parts = call(
        functools.partial(products_kernel, half, cap, blk),
        f32(spans, 3 * F, LX, ext),
        [vmem(ROWS, 2 * SEG), vmem(ROWS, SEG), vmem(2, ROWS, SEG)],
    )(meta, side, far_side, *v_blocks)
    parts = lax.all_to_all(parts, "px", split_axis=0, concat_axis=0, tiled=True)

    r, q, h, dots = call(
        solve_kernel,
        (f32(F, nx, width),) * 2 + (f32(F, nx, ext), f32(groups * spans, 1, SEG)),
        [vmem(3, F, nx, ext), vmem(3 * F, nx, ext), vmem(nx, ext)],
    )(c0_ext, cx_ext, cy_ext, u_ext, parts, far_sums)
    dots = lax.all_to_all(dots, ("px", "py"), split_axis=0, concat_axis=0, tiled=True)
    qq = call(last_kernel, f32(F, nx, width), [vmem(nx, ext)] * 2)(h, q, cx_ext, cy_ext)
    control, residual = call(finish_kernel, (f32(F, nx, width),) * 2)(dots, c0, r, q, qq)
    return control[:, None], residual[:, None]


def solution(mesh):
    return jax.shard_map(
        shards,
        mesh=mesh,
        in_specs=(
            P(None, "py", None, "px"),
            P("py", None, "px"),
            P("py", "px", None),
            P(("px", "py"), None),
            P(("px", "py"), None),
            P(("px", "py")),
            P(("px", "py"), None),
            P(("px", "py")),
            P(("px", "py")),
        ),
        out_specs=(P(None, "py", None, "px"), P(None, "py", None, "px")),
        check_vma=False,
    )
```

```python
import functools

import jax
import jax.numpy as jnp
from jax import lax
from jax.experimental import pallas as pl
from jax.experimental.pallas import tpu as pltpu
from jax.sharding import PartitionSpec as P

F = 2
SEG = 128
M = 4
NB = 16
LX = 16
ROWS = F * NB * LX
HALF = SEG // 2
SPLIT = 16
X_WIDTH = 256
Y_LINES = 16
VMEM_BYTES = 32 * 1024 * 1024
PACK_BYTES = 60 * 1024 * 1024
FIRST = 100_000_000
JOIN = 100_000_000


def iota(shape, axis):
    return lax.broadcasted_iota(jnp.int32, shape, axis)


def flag(condition, kind=jnp.bfloat16):
    return jnp.where(condition, 1.0, 0.0).astype(kind)


def mxu(left, right):
    return jnp.dot(left, right, preferred_element_type=jnp.float32)


def split_parts(values, count):
    parts = []
    for _ in range(count):
        part = values.astype(jnp.bfloat16)
        parts.append(part)
        values = values - part.astype(jnp.float32)
    return parts


def ends_tile(before, after):
    return jnp.where(iota(after.shape, after.ndim - 1) < HALF, after, before)


def sweep(values, coeffs, axis):
    size = values.shape[axis]
    for _ in range(M):
        flux = coeffs * (pltpu.roll(values, size - 1, axis) - values)
        values = values + flux - pltpu.roll(flux, 1, axis)
    return values


def start_copies(pairs, sems):
    copies = [pltpu.make_async_copy(*pair, sems.at[i]) for i, pair in enumerate(pairs)]
    for copy in copies:
        copy.start()
    return copies


def pack_weights_kernel(groups, cap, blk, block_rows, own_hbm, key_hbm, sten_hbm, itp_hbm, w_hbm,
                        *rest):
    half = groups // 2
    outs, rest = rest[:half], rest[half:]
    (slot_out, own_ref, key_ref, sten_ref, itp_ref, w_ref, buffer, slot_v, slot_s, sems, out_sems,
     sem) = rest
    loads = start_copies([(own_hbm, own_ref), (key_hbm, key_ref), (sten_hbm, sten_ref),
                          (itp_hbm, itp_ref), (w_hbm, w_ref)], sems)

    def clear(k, carry):
        start = pl.multiple_of(k * block_rows, 8)
        buffer[pl.ds(start, block_rows), :] = jnp.zeros((block_rows, SEG), jnp.float32)
        return carry

    lax.fori_loop(0, half, clear, 0)

    for load in loads[:4]:
        load.wait()
    chunks = own_ref.shape[0]
    nb = cap // blk
    own = own_ref[...]
    high = groups * chunks
    shift = chunks.bit_length() - 1
    masks = [flag(own == o, jnp.float32) for o in range(groups)]
    hits = jnp.concatenate(masks, axis=0).astype(jnp.bfloat16)
    square = (SEG, SEG)
    within = mxu(hits, flag(iota(square, 0) < iota(square, 1)))
    tallies = mxu(hits, jnp.ones(square, jnp.bfloat16)).astype(jnp.bfloat16)
    line, column = iota((high, high), 0), iota((high, high), 1)
    same = (line >> shift) == (column >> shift)
    ranks = within + mxu(flag(same & (column < line)), tallies)
    rank = sum(masks[o] * ranks[o * chunks:(o + 1) * chunks] for o in range(groups))
    rank = rank.astype(jnp.int32)
    relative = own ^ lax.axis_index("py")
    block, across = relative & (half - 1), relative >> (half.bit_length() - 1)
    slot_v[...] = block * block_rows + across * cap + rank
    slot_out[...] = (block * 2 + across) * cap + rank
    copy = pltpu.make_async_copy(slot_v, slot_s, sem)
    copy.start()

    log = blk.bit_length() - 1
    place = relative * nb + (rank >> log)
    lane = rank & (blk - 1)
    key, sten, itp = key_ref[...], sten_ref[...], itp_ref[...]
    tall = groups * nb
    meta = jnp.zeros((5 * tall, SEG), jnp.float32)
    for i in range(chunks):
        chosen = iota((tall, SEG), 0) == place[i:i + 1]
        parts = split_parts(itp[i:i + 1], 3)
        parts += [key[i:i + 1].astype(jnp.bfloat16), (sten[i:i + 1] + 1).astype(jnp.bfloat16)]
        left = [jnp.where(chosen, part.astype(jnp.float32), 0.0) for part in parts]
        right = flag(iota(square, 0) == lane[i:i + 1])
        meta = meta + lax.dot_general(
            jnp.concatenate(left, axis=0).astype(jnp.bfloat16), right,
            (((1,), (1,)), ((), ())), preferred_element_type=jnp.float32)
    shares = meta[:tall] + meta[tall:2 * tall] + meta[2 * tall:3 * tall]
    targets = meta[3 * tall:4 * tall] * LX + meta[4 * tall:]
    for v in range(groups):
        base = (v % half) * block_rows + 2 * cap + (v // half) * 2 * nb
        buffer[base:base + nb, :] = shares[v * nb:(v + 1) * nb]
        buffer[base + nb:base + 2 * nb, :] = targets[v * nb:(v + 1) * nb]

    copy.wait()
    loads[4].wait()

    def place_rows(g, carry):
        weights = w_ref[pl.ds(pl.multiple_of(g * 8, 8), 8), :]
        line, lane = g // 16, (g % 16) * 8
        for i in range(8):
            buffer[pl.ds(slot_s[line, lane + i], 1), :] = weights[i:i + 1]
        return carry

    lax.fori_loop(0, w_ref.shape[0] // 8, place_rows, 0)
    for store in start_copies([(buffer.at[pl.ds(k * block_rows, block_rows)], out)
                               for k, out in enumerate(outs)], out_sems):
        store.wait()


def pack_products_kernel(groups, cap, slot_ref, w_hbm, d_hbm, *rest):
    half = groups // 2
    outs, (w_ref, d_ref, buffer, sems, out_sems) = rest[:half], rest[half:]
    loads = start_copies([(w_hbm, w_ref), (d_hbm, d_ref)], sems)

    def clear(o, carry):
        start = pl.multiple_of(o * cap, 8)
        buffer[pl.ds(start, cap), :] = jnp.zeros((cap, SEG), jnp.float32)
        return carry

    lax.fori_loop(0, groups, clear, 0)

    for load in loads:
        load.wait()

    def place_rows(g, carry):
        start = pl.multiple_of(g * 8, 8)
        products = w_ref[pl.ds(start, 8), :] * d_ref[pl.ds(start, 8), :]
        line, lane = g // 16, (g % 16) * 8
        for i in range(8):
            buffer[pl.ds(slot_ref[line, lane + i], 1), :] = products[i:i + 1]
        return carry

    lax.fori_loop(0, w_ref.shape[0] // 8, place_rows, 0)
    for store in start_copies([(buffer.at[pl.ds(k * 2 * cap, 2 * cap)], out)
                               for k, out in enumerate(outs)], out_sems):
        store.wait()


def pack_swap_kernel(_, cy_hbm, c0_hbm, cx_hbm, swap_out, cy_ref, first, last, sems):
    width = c0_hbm.shape[2]
    for load in start_copies([
        (cy_hbm, cy_ref),
        (c0_hbm.at[:, :, pl.ds(0, SEG)], first.at[pl.ds(0, F)]),
        (cx_hbm.at[:, pl.ds(0, SEG)], first.at[F]),
        (c0_hbm.at[:, :, pl.ds(width - SEG, SEG)], last.at[pl.ds(0, F)]),
        (cx_hbm.at[:, pl.ds(width - SEG, SEG)], last.at[F]),
    ], sems):
        load.wait()
    columns = cy_ref.shape[1]
    cy = cy_ref[...]
    cy = jnp.where(iota(cy.shape, 1) == columns - 1, 0.0, cy)
    empty = jnp.zeros((LX, SEG), jnp.float32)
    me = lax.axis_index("px")
    nx = first.shape[1]
    for q in range(columns // width):
        low, top = q * width, (q + 1) * width
        tiles = [cy[:, t:t + SEG] for t in range(low, top, SEG)]
        before = cy[:, low - SEG:low] if low > 0 else empty
        after = cy[:, top:top + SEG] if top < columns else empty
        tiles.append(ends_tile(before, after))
        for t, tile in enumerate(tiles):
            swap_out[q, t * LX:(t + 1) * LX, :] = tile
        base = len(tiles) * LX
        for i in range(F + 1):
            swap_out[q, base + i * nx:base + (i + 1) * nx, :] = jnp.where(
                q < me, first[i], last[i])


def sum_rows(cap, blk, metas, acc_ref, terms):
    nb = cap // blk
    numbers = 1.0 + iota((ROWS, cap), 0).astype(jnp.float32)
    for source, meta in enumerate(metas):
        upper = jnp.concatenate(
            [jnp.broadcast_to(meta[i:i + 1], (SEG, SEG)).T[:blk] for i in range(nb)], axis=0)
        target = jnp.concatenate([meta[nb + i:nb + i + 1, :blk] for i in range(nb)], axis=1)
        hit = flag(numbers == target)
        values = jnp.concatenate(terms(source, upper), axis=1)
        part = mxu(jnp.concatenate([hit, hit], axis=1),
                   jnp.concatenate(split_parts(values, 2), axis=0))
        if source:
            acc_ref[...] += part
        else:
            acc_ref[...] = part


def cut_part(rows_ref, to, f, q, spans):
    width = to.shape[1] - SEG
    per = width // SEG

    def tile(b):
        start = pl.multiple_of((f * NB + b) * LX, LX)
        return rows_ref[pl.ds(start, LX), :]

    for j in range(per):
        to[:, j * SEG:(j + 1) * SEG] = tile(q * per + j)
    before = tile(jnp.maximum(q * per - 1, 0))
    after = tile(jnp.minimum(q * per + per, NB - 1))
    to[:, width:] = ends_tile(jnp.where(q > 0, before, 0.0),
                              jnp.where(q < spans - 1, after, 0.0))


def weights_kernel(half, cap, blk, across, *rest):
    w_refs, (_, meta_out, diagonal_out, side_out, acc_ref) = rest[:half], rest[half:]
    nb = cap // blk
    for k, w_ref in enumerate(w_refs):
        meta_out[k] = w_ref[2 * cap:, :]
    rows = slice(across * cap, (across + 1) * cap)

    def terms(source, upper):
        lower = 1.0 - upper
        weights = w_refs[source][rows, :]
        lower_w, upper_w = lower * weights, upper * weights
        return [lower * lower_w, upper * lower_w, upper * upper_w]

    low = 2 * cap + across * 2 * nb
    sum_rows(cap, blk, [w_ref[low:low + 2 * nb, :] for w_ref in w_refs], acc_ref, terms)
    diagonal_out[...] = acc_ref[:, :SEG] + pltpu.roll(acc_ref[:, 2 * SEG:], 1, 0)
    side_out[...] = acc_ref[:, SEG:2 * SEG]


def sum_products(half, cap, blk, across, meta_ref, v_refs, acc_ref, sums_ref):
    nb = cap // blk
    rows = slice(across * cap, (across + 1) * cap)

    def terms(source, upper):
        products = v_refs[source][rows, :]
        return [(1.0 - upper) * products, upper * products]

    low = across * 2 * nb
    sum_rows(cap, blk, [meta_ref[k, low:low + 2 * nb, :] for k in range(half)], acc_ref, terms)
    sums_ref[...] = acc_ref[:, :SEG] + pltpu.roll(acc_ref[:, SEG:], 1, 0)


def products_across_kernel(half, cap, blk, meta_ref, *rest):
    v_refs, (meta_out, *outs, acc_ref, sums_ref) = rest[:half], rest[half:]
    meta_out[...] = meta_ref[...]
    sum_products(half, cap, blk, 1, meta_ref, v_refs, acc_ref, sums_ref)
    me = lax.axis_index("px")
    for k, out in enumerate(outs):
        for f in range(F):
            cut_part(sums_ref, out.at[f], f, me ^ k, len(outs))


def products_kernel(half, cap, blk, meta_ref, d_ref, e_ref, far_d_ref, far_e_ref, *rest):
    v_refs, (out, acc_ref, sums_ref, side) = rest[:half], rest[half:]
    spans = out.shape[0]
    sum_products(half, cap, blk, 0, meta_ref, v_refs, acc_ref, sums_ref)
    side[0] = d_ref[...] + far_d_ref[...]
    side[1] = e_ref[...] + far_e_ref[...]
    for q in range(spans):
        for channel, rows_ref in enumerate((side.at[0], side.at[1], sums_ref)):
            for f in range(F):
                cut_part(rows_ref, out.at[q, channel * F + f], f, q, spans)


def sweep_x_into(to_ref, from_ref, cx_ref, plus_ref=None, sign=1.0):
    size = cx_ref.shape[1]
    for low in range(0, size, X_WIDTH):
        tile = slice(low, min(low + X_WIDTH, size))
        values = sweep(from_ref[:, tile], cx_ref[:, tile], 0)
        if plus_ref is not None:
            values = values + sign * plus_ref[:, tile]
        to_ref[:, tile] = values


def sweep_y_into(to_ref, from_ref, cy_ref):
    for low in range(0, cy_ref.shape[0], Y_LINES):
        lines = slice(low, low + Y_LINES)
        to_ref[lines, :] = sweep(from_ref[lines, :], cy_ref[lines, :], 1)


def start_kernel(c0_ref, cx_ref, swap_ref, c0_out, cx_out, cy_out, u_out, token_out):
    token_out[...] = jnp.zeros_like(token_out)
    width = c0_ref.shape[2]
    nx = cx_ref.shape[0]
    spans, count = swap_ref.shape[0], cy_out.shape[1] // SEG
    me = lax.axis_index("px")
    for p in range(spans):
        for t in range(count):
            cy_out[p * LX:(p + 1) * LX, t * SEG:(t + 1) * SEG] = (
                swap_ref[p, t * LX:(t + 1) * LX, :])

    def beside(i):
        lines = slice(count * LX + i * nx, count * LX + (i + 1) * nx)
        before = swap_ref[jnp.maximum(me - 1, 0), lines, :]
        after = swap_ref[jnp.minimum(me + 1, spans - 1), lines, :]
        return ends_tile(jnp.where(me > 0, before, 0.0), jnp.where(me < spans - 1, after, 0.0))

    last = cx_ref.shape[0] - 1
    cx_out[:, :width] = cx_ref[...]
    cx_out[:, width:] = beside(F)
    cx_out[last:, :] = jnp.zeros((1, width + SEG), jnp.float32)
    for f in range(F):
        c0_out[f, :, :width] = c0_ref[f]
        c0_out[f, :, width:] = beside(f)
        sweep_x_into(u_out.at[f], c0_out.at[f], cx_out)
        sweep_y_into(u_out.at[f], u_out.at[f], cy_out)


def join_kernel(spans, *rest):
    parts, out = rest[:spans], rest[spans]
    me = lax.axis_index("px")
    for k, part in enumerate(parts):
        for f in range(F):
            out[f, pl.ds(pl.multiple_of((me ^ k) * LX, LX), LX), :] = part[f]


def solve_kernel(c0_ref, cx_ref, cy_ref, u_ref, obs_ref, far_ref, r_out, q_out, h_out, dots_out,
                 vec, coef, work):
    width = r_out.shape[2]
    for p in range(obs_ref.shape[0]):
        rows = slice(p * LX, (p + 1) * LX)
        for channel in range(2 * F):
            coef[channel, rows, :] = obs_ref[p, channel]
        for f in range(F):
            coef[2 * F + f, rows, :] = obs_ref[p, 2 * F + f] + far_ref[f, rows, :]

    def normal(f, values, tile):
        size = values.shape[0]
        side = coef[F + f, :, tile]
        return (coef[f, :, tile] * values + side * pltpu.roll(values, size - 1, 0)
                + pltpu.roll(side * values, 1, 0))

    tiles = [slice(low, low + SEG) for low in range(0, width + SEG, SEG)]

    def first(f, carry):
        for tile in tiles:
            work[:, tile] = coef[2 * F + f, :, tile] - normal(f, u_ref[f, :, tile], tile)
        sweep_y_into(work, work, cy_ref)
        sweep_x_into(vec.at[0, f], work, cx_ref, c0_ref.at[f], -1.0)
        return carry

    lax.fori_loop(0, F, first, 0)

    def apply(f, carry):
        sweep_x_into(work, vec.at[0, f], cx_ref)
        sweep_y_into(work, work, cy_ref)
        for tile in tiles:
            work[:, tile] = normal(f, work[:, tile], tile)
        sweep_y_into(work, work, cy_ref)
        sweep_x_into(vec.at[1, f], work, cx_ref, vec.at[0, f])
        sweep_x_into(vec.at[2, f], vec.at[1, f], cx_ref)
        sweep_y_into(vec.at[2, f], vec.at[2, f], cy_ref)
        for tile in tiles:
            h_out[f, :, tile] = normal(f, vec[2, f, :, tile], tile)
        return carry

    lax.fori_loop(0, F, apply, 0)

    sums = [jnp.zeros((8, SEG), jnp.float32) for _ in range(4)]
    for f in range(F):
        r_out[f] = vec[0, f, :, :width]
        q_out[f] = vec[1, f, :, :width]
        for low in range(0, vec.shape[2], 8):
            for tile in tiles[:-1]:
                r = vec[0, f, low:low + 8, tile]
                q = vec[1, f, low:low + 8, tile]
                s = vec[2, f, low:low + 8, tile]
                for i, product in enumerate((r * r, r * q, q * q, s * h_out[f, low:low + 8, tile])):
                    sums[i] = sums[i] + product
    dots = jnp.zeros((1, SEG), jnp.float32)
    for i, total in enumerate(sums):
        line = jnp.sum(total, axis=0, keepdims=True)
        for distance in (64, 32, 16):
            line = line + pltpu.roll(line, distance, 1)
        dots = jnp.where(iota((1, SEG), 1) // SPLIT == i, line, dots)
    dots_out[...] = jnp.broadcast_to(dots, dots_out.shape)


def last_kernel(h_ref, q_ref, cx_ref, cy_ref, qq_out, work, other):
    width = qq_out.shape[2]

    def apply(f, carry):
        sweep_y_into(work, h_ref.at[f], cy_ref)
        sweep_x_into(other, work, cx_ref)
        qq_out[f] = q_ref[f] + other[:, :width]
        return carry

    lax.fori_loop(0, F, apply, 0)


def finish_kernel(dots_ref, c0_ref, r_ref, q_ref, qq_ref, control_out, residual_out):
    dots = jnp.sum(dots_ref[...], axis=0)
    lane = iota((1, SEG), 1)
    rr, rq, qq2, energy = (pltpu.roll(dots, (SEG - i * SPLIT) % SEG, 1) for i in range(4))

    def total(line):
        return jnp.sum(jnp.where(lane < SPLIT, line, 0.0), axis=1, keepdims=True)

    rr_sum = total(rr)
    alpha = rr_sum / total(rq)
    new_sum = total(rr - 2.0 * alpha * rq + alpha * alpha * qq2)
    more = 1.0 + new_sum / rr_sum
    curve = total(more * more * rq - 2.0 * more * alpha * qq2 + alpha * alpha * (qq2 + energy))
    second = new_sum / curve
    first_weight = alpha + second * more
    both = alpha * second
    for f in range(F):
        r, q = r_ref[f], q_ref[f]
        control_out[f] = c0_ref[f] + first_weight * r - both * q
        residual_out[f] = r - first_weight * q + both * qq_ref[f]


def call(kernel, out_shape, scratch=(), in_specs=None, out_specs=None, limit=VMEM_BYTES,
         weight=1):
    params = {"in_specs": in_specs, "out_specs": out_specs}
    return pl.pallas_call(
        kernel,
        out_shape=out_shape,
        scratch_shapes=list(scratch),
        compiler_params=pltpu.CompilerParams(vmem_limit_bytes=limit),
        cost_estimate=pl.CostEstimate(flops=weight, bytes_accessed=weight, transcendentals=0),
        **{name: value for name, value in params.items() if value is not None},
    )


def f32(*shape):
    return jax.ShapeDtypeStruct(shape, jnp.float32)


def vmem(*shape, kind=jnp.float32):
    return pltpu.VMEM(shape, kind)


def shards(
    control_start, coef_x, coef_y, innovation, obs_weight, interp, obs_owner, cell_key, stencil
):
    groups, spans = lax.axis_size("py"), lax.axis_size("px")
    half = groups // 2
    rows = innovation.shape[0]
    cap = 3 * rows // groups
    blk = SEG if cap % SEG == 0 else HALF
    meta_rows = -(-4 * (cap // blk) // 8) * 8
    block_rows = 2 * cap + meta_rows
    chunks = rows // SEG
    nx, width = control_start.shape[2], control_start.shape[3]
    ext = width + SEG
    c0, cx = control_start[:, 0], coef_x[0]
    hbm, local, scalars = (
        pl.BlockSpec(memory_space=s) for s in (pltpu.HBM, pltpu.VMEM, pltpu.SMEM))
    ints = vmem(chunks, SEG, kind=jnp.int32)
    dma = pltpu.SemaphoreType.DMA

    def to_half(block, k):
        return lax.ppermute(block, "py", [(i, i ^ k) for i in range(groups)])

    def across(parts):
        return [
            lax.ppermute(parts[k], ("px", "py"), [
                (i * groups + j, (i ^ k) * groups + (j ^ half))
                for i in range(spans) for j in range(groups)])
            for k in range(spans)]

    *w_blocks, slots = call(
        functools.partial(pack_weights_kernel, groups, cap, blk, block_rows),
        (f32(block_rows, SEG),) * half + (jax.ShapeDtypeStruct((chunks, SEG), jnp.int32),),
        [ints, ints, ints, vmem(chunks, SEG), vmem(rows, SEG), vmem(half * block_rows, SEG), ints,
         pltpu.SMEM((chunks, SEG), jnp.int32), dma((5,)), dma((half,)), dma],
        [hbm] * 5,
        (hbm,) * half + (local,),
        limit=PACK_BYTES,
    )(
        obs_owner.reshape(chunks, SEG), cell_key.reshape(chunks, SEG),
        stencil.reshape(chunks, SEG), interp.reshape(chunks, SEG), obs_weight,
    )
    v_blocks = list(call(
        functools.partial(pack_products_kernel, groups, cap),
        (f32(2 * cap, SEG),) * half,
        [vmem(rows, SEG), vmem(rows, SEG), vmem(groups * cap, SEG), dma((2,)), dma((half,))],
        [scalars] + [hbm] * 2,
        (hbm,) * half,
        limit=PACK_BYTES,
    )(slots, obs_weight, innovation))
    w_blocks[1:] = [to_half(w_blocks[k], k) for k in range(1, half)]
    w_blocks[1], *v_blocks[1:] = lax.optimization_barrier((w_blocks[1], *v_blocks[1:]))
    v_blocks[1:] = [to_half(v_blocks[k], k) for k in range(1, half)]

    swap = call(
        pack_swap_kernel,
        f32(spans, LX * ext // SEG + (F + 1) * nx, SEG),
        [vmem(*coef_y.shape[1:]), vmem(F + 1, nx, SEG), vmem(F + 1, nx, SEG), dma((5,))],
        [local] + [hbm] * 3,
        limit=PACK_BYTES,
    )(slots, coef_y[0], c0, cx)
    swap = lax.all_to_all(swap, "px", split_axis=0, concat_axis=0, tiled=True)
    c0_ext, cx_ext, cy_ext, u_ext, token = call(
        start_kernel,
        (f32(F, nx, ext), f32(nx, ext), f32(nx, ext), f32(F, nx, ext), f32(8, SEG)),
    )(c0, cx, swap)

    def sum_weights(side, token, weight):
        return call(
            functools.partial(weights_kernel, half, cap, blk, side),
            (f32(half, meta_rows, SEG),) + (f32(ROWS, SEG),) * 2,
            [vmem(ROWS, 3 * SEG)],
            weight=weight,
        )(*w_blocks, token)

    meta, *side_across = sum_weights(1, w_blocks[0], FIRST)
    side_across = [to_half(values, half) for values in side_across]
    meta, *side = sum_weights(0, token, 1)
    meta, *sums_across = call(
        functools.partial(products_across_kernel, half, cap, blk),
        (f32(half, meta_rows, SEG),) + (f32(F, LX, ext),) * spans,
        [vmem(ROWS, 2 * SEG), vmem(ROWS, SEG)],
    )(meta, *v_blocks)
    far_sums = call(
        functools.partial(join_kernel, spans), f32(F, nx, ext), weight=JOIN,
    )(*across(sums_across))
    parts = call(
        functools.partial(products_kernel, half, cap, blk),
        f32(spans, 3 * F, LX, ext),
        [vmem(ROWS, 2 * SEG), vmem(ROWS, SEG), vmem(2, ROWS, SEG)],
    )(meta, *side, *side_across, *v_blocks)
    parts = lax.all_to_all(parts, "px", split_axis=0, concat_axis=0, tiled=True)

    r, q, h, dots = call(
        solve_kernel,
        (f32(F, nx, width),) * 2 + (f32(F, nx, ext), f32(groups * spans, 1, SEG)),
        [vmem(3, F, nx, ext), vmem(3 * F, nx, ext), vmem(nx, ext)],
    )(c0_ext, cx_ext, cy_ext, u_ext, parts, far_sums)
    dots = lax.all_to_all(dots, ("px", "py"), split_axis=0, concat_axis=0, tiled=True)
    qq = call(last_kernel, f32(F, nx, width), [vmem(nx, ext)] * 2)(h, q, cx_ext, cy_ext)
    control, residual = call(finish_kernel, (f32(F, nx, width),) * 2)(dots, c0, r, q, qq)
    return control[:, None], residual[:, None]


def solution(mesh):
    return jax.shard_map(
        shards,
        mesh=mesh,
        in_specs=(
            P(None, "py", None, "px"),
            P("py", None, "px"),
            P("py", "px", None),
            P(("px", "py"), None),
            P(("px", "py"), None),
            P(("px", "py")),
            P(("px", "py"), None),
            P(("px", "py")),
            P(("px", "py")),
        ),
        out_specs=(P(None, "py", None, "px"), P(None, "py", None, "px")),
        check_vma=False,
    )
```

```python
import functools

import jax
import jax.numpy as jnp
from jax import lax
from jax.experimental import pallas as pl
from jax.experimental.pallas import tpu as pltpu
from jax.sharding import PartitionSpec as P

F = 2
SEG = 128
M = 4
NB = 16
LX = 16
ROWS = F * NB * LX
HALF = SEG // 2
SPLIT = 16
Y_LINES = 16
VMEM_BYTES = 32 * 1024 * 1024
PACK_BYTES = 60 * 1024 * 1024
FIRST = 100_000_000
JOIN = 100_000_000


def iota(shape, axis):
    return lax.broadcasted_iota(jnp.int32, shape, axis)


def flag(condition, kind=jnp.bfloat16):
    return jnp.where(condition, 1.0, 0.0).astype(kind)


def mxu(left, right):
    return jnp.dot(left, right, preferred_element_type=jnp.float32)


def split_parts(values, count):
    parts = []
    for _ in range(count):
        part = values.astype(jnp.bfloat16)
        parts.append(part)
        values = values - part.astype(jnp.float32)
    return parts


def ends_tile(before, after):
    return jnp.where(iota(after.shape, after.ndim - 1) < HALF, after, before)


def start_copies(pairs, sems):
    copies = [pltpu.make_async_copy(*pair, sems.at[i]) for i, pair in enumerate(pairs)]
    for copy in copies:
        copy.start()
    return copies


def pack_weights_kernel(groups, cap, blk, block_rows, own_hbm, key_hbm, sten_hbm, itp_hbm, w_hbm,
                        *rest):
    half = groups // 2
    outs, rest = rest[:half], rest[half:]
    (slot_out, own_ref, key_ref, sten_ref, itp_ref, w_ref, buffer, slot_v, slot_s, sems, out_sems,
     sem) = rest
    loads = start_copies([(own_hbm, own_ref), (key_hbm, key_ref), (sten_hbm, sten_ref),
                          (itp_hbm, itp_ref), (w_hbm, w_ref)], sems)

    def clear(k, carry):
        start = pl.multiple_of(k * block_rows, 8)
        buffer[pl.ds(start, block_rows), :] = jnp.zeros((block_rows, SEG), jnp.float32)
        return carry

    lax.fori_loop(0, half, clear, 0)

    for load in loads[:4]:
        load.wait()
    chunks = own_ref.shape[0]
    nb = cap // blk
    own = own_ref[...]
    high = groups * chunks
    shift = chunks.bit_length() - 1
    masks = [flag(own == o, jnp.float32) for o in range(groups)]
    hits = jnp.concatenate(masks, axis=0).astype(jnp.bfloat16)
    square = (SEG, SEG)
    within = mxu(hits, flag(iota(square, 0) < iota(square, 1)))
    tallies = mxu(hits, jnp.ones(square, jnp.bfloat16)).astype(jnp.bfloat16)
    line, column = iota((high, high), 0), iota((high, high), 1)
    same = (line >> shift) == (column >> shift)
    ranks = within + mxu(flag(same & (column < line)), tallies)
    rank = sum(masks[o] * ranks[o * chunks:(o + 1) * chunks] for o in range(groups))
    rank = rank.astype(jnp.int32)
    relative = own ^ lax.axis_index("py")
    block, across = relative & (half - 1), relative >> (half.bit_length() - 1)
    slot_v[...] = block * block_rows + across * cap + rank
    slot_out[...] = (block * 2 + across) * cap + rank
    copy = pltpu.make_async_copy(slot_v, slot_s, sem)
    copy.start()

    log = blk.bit_length() - 1
    place = relative * nb + (rank >> log)
    lane = rank & (blk - 1)
    key, sten, itp = key_ref[...], sten_ref[...], itp_ref[...]
    tall = groups * nb
    meta = jnp.zeros((5 * tall, SEG), jnp.float32)
    for i in range(chunks):
        chosen = iota((tall, SEG), 0) == place[i:i + 1]
        parts = split_parts(itp[i:i + 1], 3)
        parts += [key[i:i + 1].astype(jnp.bfloat16), (sten[i:i + 1] + 1).astype(jnp.bfloat16)]
        left = [jnp.where(chosen, part.astype(jnp.float32), 0.0) for part in parts]
        right = flag(iota(square, 0) == lane[i:i + 1])
        meta = meta + lax.dot_general(
            jnp.concatenate(left, axis=0).astype(jnp.bfloat16), right,
            (((1,), (1,)), ((), ())), preferred_element_type=jnp.float32)
    shares = meta[:tall] + meta[tall:2 * tall] + meta[2 * tall:3 * tall]
    targets = meta[3 * tall:4 * tall] * LX + meta[4 * tall:]
    for v in range(groups):
        base = (v % half) * block_rows + 2 * cap + (v // half) * 2 * nb
        buffer[base:base + nb, :] = shares[v * nb:(v + 1) * nb]
        buffer[base + nb:base + 2 * nb, :] = targets[v * nb:(v + 1) * nb]

    copy.wait()
    loads[4].wait()

    def place_rows(g, carry):
        weights = w_ref[pl.ds(pl.multiple_of(g * 8, 8), 8), :]
        line, lane = g // 16, (g % 16) * 8
        for i in range(8):
            buffer[pl.ds(slot_s[line, lane + i], 1), :] = weights[i:i + 1]
        return carry

    lax.fori_loop(0, w_ref.shape[0] // 8, place_rows, 0)
    for store in start_copies([(buffer.at[pl.ds(k * block_rows, block_rows)], out)
                               for k, out in enumerate(outs)], out_sems):
        store.wait()


def pack_products_kernel(groups, cap, slot_ref, w_hbm, d_hbm, *rest):
    half = groups // 2
    outs, (w_ref, d_ref, buffer, sems, out_sems) = rest[:half], rest[half:]
    loads = start_copies([(w_hbm, w_ref), (d_hbm, d_ref)], sems)

    def clear(o, carry):
        start = pl.multiple_of(o * cap, 8)
        buffer[pl.ds(start, cap), :] = jnp.zeros((cap, SEG), jnp.float32)
        return carry

    lax.fori_loop(0, groups, clear, 0)

    for load in loads:
        load.wait()

    def place_rows(g, carry):
        start = pl.multiple_of(g * 8, 8)
        products = w_ref[pl.ds(start, 8), :] * d_ref[pl.ds(start, 8), :]
        line, lane = g // 16, (g % 16) * 8
        for i in range(8):
            buffer[pl.ds(slot_ref[line, lane + i], 1), :] = products[i:i + 1]
        return carry

    lax.fori_loop(0, w_ref.shape[0] // 8, place_rows, 0)
    for store in start_copies([(buffer.at[pl.ds(k * 2 * cap, 2 * cap)], out)
                               for k, out in enumerate(outs)], out_sems):
        store.wait()


def pack_swap_kernel(_, cy_hbm, c0_hbm, cx_hbm, swap_out, cy_ref, first, last, sems):
    width = c0_hbm.shape[2]
    for load in start_copies([
        (cy_hbm, cy_ref),
        (c0_hbm.at[:, :, pl.ds(0, SEG)], first.at[pl.ds(0, F)]),
        (cx_hbm.at[:, pl.ds(0, SEG)], first.at[F]),
        (c0_hbm.at[:, :, pl.ds(width - SEG, SEG)], last.at[pl.ds(0, F)]),
        (cx_hbm.at[:, pl.ds(width - SEG, SEG)], last.at[F]),
    ], sems):
        load.wait()
    columns = cy_ref.shape[1]
    cy = cy_ref[...]
    cy = jnp.where(iota(cy.shape, 1) == columns - 1, 0.0, cy)
    empty = jnp.zeros((LX, SEG), jnp.float32)
    me = lax.axis_index("px")
    nx = first.shape[1]
    for q in range(columns // width):
        low, top = q * width, (q + 1) * width
        tiles = [cy[:, t:t + SEG] for t in range(low, top, SEG)]
        before = cy[:, low - SEG:low] if low > 0 else empty
        after = cy[:, top:top + SEG] if top < columns else empty
        tiles.append(ends_tile(before, after))
        for t, tile in enumerate(tiles):
            swap_out[q, t * LX:(t + 1) * LX, :] = tile
        base = len(tiles) * LX
        for i in range(F + 1):
            swap_out[q, base + i * nx:base + (i + 1) * nx, :] = jnp.where(
                q < me, first[i], last[i])


def sum_rows(cap, blk, metas, acc_ref, terms):
    nb = cap // blk
    numbers = 1.0 + iota((ROWS, cap), 0).astype(jnp.float32)
    for source, meta in enumerate(metas):
        upper = jnp.concatenate(
            [jnp.broadcast_to(meta[i:i + 1], (SEG, SEG)).T[:blk] for i in range(nb)], axis=0)
        target = jnp.concatenate([meta[nb + i:nb + i + 1, :blk] for i in range(nb)], axis=1)
        hit = flag(numbers == target)
        values = jnp.concatenate(terms(source, upper), axis=1)
        part = mxu(jnp.concatenate([hit, hit], axis=1),
                   jnp.concatenate(split_parts(values, 2), axis=0))
        if source:
            acc_ref[...] += part
        else:
            acc_ref[...] = part


def cut_part(rows_ref, to, f, q, spans):
    per = to.shape[0] - 1

    def tile(b):
        start = pl.multiple_of((f * NB + b) * LX, LX)
        return rows_ref[pl.ds(start, LX), :]

    for j in range(per):
        to[j] = tile(q * per + j)
    before = tile(jnp.maximum(q * per - 1, 0))
    after = tile(jnp.minimum(q * per + per, NB - 1))
    to[per] = ends_tile(jnp.where(q > 0, before, 0.0), jnp.where(q < spans - 1, after, 0.0))


def weights_kernel(half, cap, blk, across, *rest):
    w_refs, (_, meta_out, diagonal_out, side_out, acc_ref) = rest[:half], rest[half:]
    nb = cap // blk
    for k, w_ref in enumerate(w_refs):
        meta_out[k] = w_ref[2 * cap:, :]
    rows = slice(across * cap, (across + 1) * cap)

    def terms(source, upper):
        lower = 1.0 - upper
        weights = w_refs[source][rows, :]
        lower_w, upper_w = lower * weights, upper * weights
        return [lower * lower_w, upper * lower_w, upper * upper_w]

    low = 2 * cap + across * 2 * nb
    sum_rows(cap, blk, [w_ref[low:low + 2 * nb, :] for w_ref in w_refs], acc_ref, terms)
    diagonal_out[...] = acc_ref[:, :SEG] + pltpu.roll(acc_ref[:, 2 * SEG:], 1, 0)
    side_out[...] = acc_ref[:, SEG:2 * SEG]


def sum_products(half, cap, blk, across, meta_ref, v_refs, acc_ref, sums_ref):
    nb = cap // blk
    rows = slice(across * cap, (across + 1) * cap)

    def terms(source, upper):
        products = v_refs[source][rows, :]
        return [(1.0 - upper) * products, upper * products]

    low = across * 2 * nb
    sum_rows(cap, blk, [meta_ref[k, low:low + 2 * nb, :] for k in range(half)], acc_ref, terms)
    sums_ref[...] = acc_ref[:, :SEG] + pltpu.roll(acc_ref[:, SEG:], 1, 0)


def products_kernel(half, cap, blk, meta_ref, d_ref, e_ref, far_d_ref, far_e_ref, *rest):
    v_refs, (out, *far_outs, acc_ref, sums_ref, far_ref, side) = rest[:half], rest[half:]
    spans = out.shape[0]
    sum_products(half, cap, blk, 1, meta_ref, v_refs, acc_ref, far_ref)
    me = lax.axis_index("px")
    for k, far_out in enumerate(far_outs):
        for f in range(F):
            cut_part(far_ref, far_out.at[f], f, me ^ k, spans)
    sum_products(half, cap, blk, 0, meta_ref, v_refs, acc_ref, sums_ref)
    side[0] = d_ref[...] + far_d_ref[...]
    side[1] = e_ref[...] + far_e_ref[...]
    for q in range(spans):
        for channel, rows_ref in enumerate((side.at[0], side.at[1], sums_ref)):
            for f in range(F):
                cut_part(rows_ref, out.at[q, channel * F + f], f, q, spans)


def x_lines(nx):
    return [pl.ds(i, 8, stride=nx // 8) for i in range(nx // 8)]


def next_line(lines):
    return lines[1:] + [pltpu.roll(lines[0], 7, 0)]


def previous_line(lines):
    return [pltpu.roll(lines[-1], 1, 0)] + lines[:-1]


def sweep_x_into(to_ref, from_ref, cx_ref, plus_ref=None, sign=1.0):
    picks = x_lines(cx_ref.shape[1])
    for t in range(cx_ref.shape[0]):
        values = [from_ref[t, pick, :] for pick in picks]
        coeffs = [cx_ref[t, pick, :] for pick in picks]
        for _ in range(M):
            flux = [c * (b - a) for c, a, b in zip(coeffs, values, next_line(values))]
            values = [a + f - g for a, f, g in zip(values, flux, previous_line(flux))]
        for pick, value in zip(picks, values):
            if plus_ref is not None:
                value = value + sign * plus_ref[t, pick, :]
            to_ref[t, pick, :] = value


def sweep_y_into(to_ref, from_ref, cy_ref):
    tiles, nx, _ = cy_ref.shape
    lane = iota((Y_LINES, SEG), 1)
    for low in range(0, nx, Y_LINES):
        lines = slice(low, low + Y_LINES)
        values = [from_ref[t, lines, :] for t in range(tiles)]
        coeffs = [cy_ref[t, lines, :] for t in range(tiles)]
        for _ in range(M):
            moved = [pltpu.roll(value, SEG - 1, 1) for value in values]
            after = [jnp.where(lane == SEG - 1, b, a) for a, b in zip(moved, moved[1:] + moved[:1])]
            flux = [c * (b - a) for c, a, b in zip(coeffs, values, after)]
            moved = [pltpu.roll(value, 1, 1) for value in flux]
            before = [jnp.where(lane == 0, a, b) for a, b in zip(moved[-1:] + moved[:-1], moved)]
            values = [a + f - g for a, f, g in zip(values, flux, before)]
        for t, value in enumerate(values):
            to_ref[t, lines, :] = value


def normal_into(to_ref, from_ref, diagonal_ref, side_ref, base_ref=None):
    tiles, nx, _ = diagonal_ref.shape
    picks = x_lines(nx)
    for t in range(tiles):
        values = [from_ref[t, pick, :] for pick in picks]
        sides = [side_ref[t, pick, :] for pick in picks]
        low = previous_line([e * a for e, a in zip(sides, values)])
        for i, (pick, after) in enumerate(zip(picks, next_line(values))):
            result = diagonal_ref[t, pick, :] * values[i] + sides[i] * after + low[i]
            if base_ref is not None:
                result = base_ref[t, pick, :] - result
            to_ref[t, pick, :] = result


def start_kernel(c0_ref, cx_ref, swap_ref, c0_out, cx_out, cy_out, u_out, token_out):
    token_out[...] = jnp.zeros_like(token_out)
    nx = cx_ref.shape[0]
    spans, count = swap_ref.shape[0], cy_out.shape[0]
    me = lax.axis_index("px")
    for p in range(spans):
        for t in range(count):
            cy_out[t, p * LX:(p + 1) * LX, :] = swap_ref[p, t * LX:(t + 1) * LX, :]

    def beside(i):
        lines = slice(count * LX + i * nx, count * LX + (i + 1) * nx)
        before = swap_ref[jnp.maximum(me - 1, 0), lines, :]
        after = swap_ref[jnp.minimum(me + 1, spans - 1), lines, :]
        return ends_tile(jnp.where(me > 0, before, 0.0), jnp.where(me < spans - 1, after, 0.0))

    for t in range(count - 1):
        tile = slice(t * SEG, (t + 1) * SEG)
        cx_out[t] = cx_ref[:, tile]
        for f in range(F):
            c0_out[f, t] = c0_ref[f, :, tile]
    cx_out[count - 1] = beside(F)
    cx_out[:, nx - 1:, :] = jnp.zeros((count, 1, SEG), jnp.float32)
    for f in range(F):
        c0_out[f, count - 1] = beside(f)
        sweep_x_into(u_out.at[f], c0_out.at[f], cx_out)
        sweep_y_into(u_out.at[f], u_out.at[f], cy_out)


def join_kernel(spans, *rest):
    parts, out = rest[:spans], rest[spans]
    me = lax.axis_index("px")
    for k, part in enumerate(parts):
        rows = pl.ds(pl.multiple_of((me ^ k) * LX, LX), LX)
        for f in range(F):
            for t in range(out.shape[1]):
                out[f, t, rows, :] = part[f, t]


def solve_kernel(c0_ref, cx_ref, cy_ref, u_ref, obs_ref, far_ref, r_out, q_out, h_out, dots_out,
                 vec, coef, work):
    for p in range(obs_ref.shape[0]):
        rows = slice(p * LX, (p + 1) * LX)
        for channel in range(2 * F):
            coef[channel, :, rows, :] = obs_ref[p, channel]
        for f in range(F):
            coef[2 * F + f, :, rows, :] = obs_ref[p, 2 * F + f] + far_ref[f, :, rows, :]

    def solve_field(f, carry):
        field = (coef.at[f], coef.at[F + f])
        normal_into(work, u_ref.at[f], *field, coef.at[2 * F + f])
        sweep_y_into(work, work, cy_ref)
        sweep_x_into(vec.at[0, f], work, cx_ref, c0_ref.at[f], -1.0)
        sweep_x_into(work, vec.at[0, f], cx_ref)
        sweep_y_into(work, work, cy_ref)
        normal_into(work, work, *field)
        sweep_y_into(work, work, cy_ref)
        sweep_x_into(vec.at[1, f], work, cx_ref, vec.at[0, f])
        sweep_x_into(vec.at[2, f], vec.at[1, f], cx_ref)
        sweep_y_into(vec.at[2, f], vec.at[2, f], cy_ref)
        normal_into(h_out.at[f], vec.at[2, f], *field)
        return carry

    lax.fori_loop(0, F, solve_field, 0)

    tiles, nx = vec.shape[2] - 1, vec.shape[3]
    sums = [jnp.zeros((8, SEG), jnp.float32) for _ in range(4)]
    for f in range(F):
        for t in range(tiles):
            r_out[f, :, t * SEG:(t + 1) * SEG] = vec[0, f, t]
            q_out[f, :, t * SEG:(t + 1) * SEG] = vec[1, f, t]
            for low in range(0, nx, 8):
                lines = slice(low, low + 8)
                r, q, s = (vec[i, f, t, lines, :] for i in range(3))
                for i, product in enumerate((r * r, r * q, q * q, s * h_out[f, t, lines, :])):
                    sums[i] = sums[i] + product
    dots = jnp.zeros((1, SEG), jnp.float32)
    for i, total in enumerate(sums):
        line = jnp.sum(total, axis=0, keepdims=True)
        for distance in (64, 32, 16):
            line = line + pltpu.roll(line, distance, 1)
        dots = jnp.where(iota((1, SEG), 1) // SPLIT == i, line, dots)
    dots_out[...] = jnp.broadcast_to(dots, dots_out.shape)


def last_kernel(h_ref, q_ref, cx_ref, cy_ref, qq_out, work):
    def apply(f, carry):
        sweep_y_into(work, h_ref.at[f], cy_ref)
        sweep_x_into(work, work, cx_ref)
        for t in range(work.shape[0] - 1):
            tile = slice(t * SEG, (t + 1) * SEG)
            qq_out[f, :, tile] = q_ref[f, :, tile] + work[t]
        return carry

    lax.fori_loop(0, F, apply, 0)


def finish_kernel(dots_ref, c0_ref, r_ref, q_ref, qq_ref, control_out, residual_out):
    dots = jnp.sum(dots_ref[...], axis=0)
    lane = iota((1, SEG), 1)
    rr, rq, qq2, energy = (pltpu.roll(dots, (SEG - i * SPLIT) % SEG, 1) for i in range(4))

    def total(line):
        return jnp.sum(jnp.where(lane < SPLIT, line, 0.0), axis=1, keepdims=True)

    rr_sum = total(rr)
    alpha = rr_sum / total(rq)
    new_sum = total(rr - 2.0 * alpha * rq + alpha * alpha * qq2)
    more = 1.0 + new_sum / rr_sum
    curve = total(more * more * rq - 2.0 * more * alpha * qq2 + alpha * alpha * (qq2 + energy))
    second = new_sum / curve
    first_weight = alpha + second * more
    both = alpha * second
    for f in range(F):
        r, q = r_ref[f], q_ref[f]
        control_out[f] = c0_ref[f] + first_weight * r - both * q
        residual_out[f] = r - first_weight * q + both * qq_ref[f]


def call(kernel, out_shape, scratch=(), in_specs=None, out_specs=None, limit=VMEM_BYTES,
         weight=1):
    params = {"in_specs": in_specs, "out_specs": out_specs}
    return pl.pallas_call(
        kernel,
        out_shape=out_shape,
        scratch_shapes=list(scratch),
        compiler_params=pltpu.CompilerParams(vmem_limit_bytes=limit),
        cost_estimate=pl.CostEstimate(flops=weight, bytes_accessed=weight, transcendentals=0),
        **{name: value for name, value in params.items() if value is not None},
    )


def f32(*shape):
    return jax.ShapeDtypeStruct(shape, jnp.float32)


def vmem(*shape, kind=jnp.float32):
    return pltpu.VMEM(shape, kind)


def shards(
    control_start, coef_x, coef_y, innovation, obs_weight, interp, obs_owner, cell_key, stencil
):
    groups, spans = lax.axis_size("py"), lax.axis_size("px")
    half = groups // 2
    rows = innovation.shape[0]
    cap = 3 * rows // groups
    blk = SEG if cap % SEG == 0 else HALF
    meta_rows = -(-4 * (cap // blk) // 8) * 8
    block_rows = 2 * cap + meta_rows
    chunks = rows // SEG
    nx, width = control_start.shape[2], control_start.shape[3]
    tiles = width // SEG + 1
    c0, cx = control_start[:, 0], coef_x[0]
    hbm, local, scalars = (
        pl.BlockSpec(memory_space=s) for s in (pltpu.HBM, pltpu.VMEM, pltpu.SMEM))
    ints = vmem(chunks, SEG, kind=jnp.int32)
    dma = pltpu.SemaphoreType.DMA

    def to_half(block, k):
        return lax.ppermute(block, "py", [(i, i ^ k) for i in range(groups)])

    def across(parts):
        return [
            lax.ppermute(parts[k], ("px", "py"), [
                (i * groups + j, (i ^ k) * groups + (j ^ half))
                for i in range(spans) for j in range(groups)])
            for k in range(spans)]

    *w_blocks, slots = call(
        functools.partial(pack_weights_kernel, groups, cap, blk, block_rows),
        (f32(block_rows, SEG),) * half + (jax.ShapeDtypeStruct((chunks, SEG), jnp.int32),),
        [ints, ints, ints, vmem(chunks, SEG), vmem(rows, SEG), vmem(half * block_rows, SEG), ints,
         pltpu.SMEM((chunks, SEG), jnp.int32), dma((5,)), dma((half,)), dma],
        [hbm] * 5,
        (hbm,) * half + (local,),
        limit=PACK_BYTES,
    )(
        obs_owner.reshape(chunks, SEG), cell_key.reshape(chunks, SEG),
        stencil.reshape(chunks, SEG), interp.reshape(chunks, SEG), obs_weight,
    )
    v_blocks = list(call(
        functools.partial(pack_products_kernel, groups, cap),
        (f32(2 * cap, SEG),) * half,
        [vmem(rows, SEG), vmem(rows, SEG), vmem(groups * cap, SEG), dma((2,)), dma((half,))],
        [scalars] + [hbm] * 2,
        (hbm,) * half,
        limit=PACK_BYTES,
    )(slots, obs_weight, innovation))
    w_blocks[1:] = [to_half(w_blocks[k], k) for k in range(1, half)]
    w_blocks[1], *v_blocks[1:] = lax.optimization_barrier((w_blocks[1], *v_blocks[1:]))
    v_blocks[1:] = [to_half(v_blocks[k], k) for k in range(1, half)]

    swap = call(
        pack_swap_kernel,
        f32(spans, LX * tiles + (F + 1) * nx, SEG),
        [vmem(*coef_y.shape[1:]), vmem(F + 1, nx, SEG), vmem(F + 1, nx, SEG), dma((5,))],
        [local] + [hbm] * 3,
        limit=PACK_BYTES,
    )(slots, coef_y[0], c0, cx)
    swap = lax.all_to_all(swap, "px", split_axis=0, concat_axis=0, tiled=True)
    c0_ext, cx_ext, cy_ext, u_ext, token = call(
        start_kernel,
        (f32(F, tiles, nx, SEG), f32(tiles, nx, SEG), f32(tiles, nx, SEG), f32(F, tiles, nx, SEG),
         f32(8, SEG)),
    )(c0, cx, swap)

    def sum_weights(side, token, weight):
        return call(
            functools.partial(weights_kernel, half, cap, blk, side),
            (f32(half, meta_rows, SEG),) + (f32(ROWS, SEG),) * 2,
            [vmem(ROWS, 3 * SEG)],
            weight=weight,
        )(*w_blocks, token)

    meta, *side_across = sum_weights(1, w_blocks[0], FIRST)
    side_across = [to_half(values, half) for values in side_across]
    meta, *side = sum_weights(0, token, 1)
    parts, *sums_across = call(
        functools.partial(products_kernel, half, cap, blk),
        (f32(spans, 3 * F, tiles, LX, SEG),) + (f32(F, tiles, LX, SEG),) * spans,
        [vmem(ROWS, 2 * SEG), vmem(ROWS, SEG), vmem(ROWS, SEG), vmem(2, ROWS, SEG)],
    )(meta, *side, *side_across, *v_blocks)
    far_sums = call(
        functools.partial(join_kernel, spans), f32(F, tiles, nx, SEG), weight=JOIN,
    )(*across(sums_across))
    parts = lax.all_to_all(parts, "px", split_axis=0, concat_axis=0, tiled=True)

    r, q, h, dots = call(
        solve_kernel,
        (f32(F, nx, width),) * 2 + (f32(F, tiles, nx, SEG), f32(groups * spans, 1, SEG)),
        [vmem(3, F, tiles, nx, SEG), vmem(3 * F, tiles, nx, SEG), vmem(tiles, nx, SEG)],
    )(c0_ext, cx_ext, cy_ext, u_ext, parts, far_sums)
    dots = lax.all_to_all(dots, ("px", "py"), split_axis=0, concat_axis=0, tiled=True)
    qq = call(last_kernel, f32(F, nx, width), [vmem(tiles, nx, SEG)])(h, q, cx_ext, cy_ext)
    control, residual = call(finish_kernel, (f32(F, nx, width),) * 2)(dots, c0, r, q, qq)
    return control[:, None], residual[:, None]


def solution(mesh):
    return jax.shard_map(
        shards,
        mesh=mesh,
        in_specs=(
            P(None, "py", None, "px"),
            P("py", None, "px"),
            P("py", "px", None),
            P(("px", "py"), None),
            P(("px", "py"), None),
            P(("px", "py")),
            P(("px", "py"), None),
            P(("px", "py")),
            P(("px", "py")),
        ),
        out_specs=(P(None, "py", None, "px"), P(None, "py", None, "px")),
        check_vma=False,
    )
```

```python
import functools

import jax
import jax.numpy as jnp
from jax import lax
from jax.experimental import pallas as pl
from jax.experimental.pallas import tpu as pltpu
from jax.sharding import PartitionSpec as P

F = 2
SEG = 128
M = 4
NB = 16
LX = 16
ROWS = F * NB * LX
HALF = SEG // 2
SPLIT = 16
X_TILES = 2
Y_LINES = 16
VMEM_BYTES = 32 * 1024 * 1024
PACK_BYTES = 60 * 1024 * 1024
FIRST = 100_000_000
JOIN = 100_000_000


def iota(shape, axis):
    return lax.broadcasted_iota(jnp.int32, shape, axis)


def flag(condition, kind=jnp.bfloat16):
    return jnp.where(condition, 1.0, 0.0).astype(kind)


def mxu(left, right):
    return jnp.dot(left, right, preferred_element_type=jnp.float32)


def split_parts(values, count):
    parts = []
    for _ in range(count):
        part = values.astype(jnp.bfloat16)
        parts.append(part)
        values = values - part.astype(jnp.float32)
    return parts


def ends_tile(before, after):
    return jnp.where(iota(after.shape, after.ndim - 1) < HALF, after, before)


def start_copies(pairs, sems):
    copies = [pltpu.make_async_copy(*pair, sems.at[i]) for i, pair in enumerate(pairs)]
    for copy in copies:
        copy.start()
    return copies


def pack_weights_kernel(groups, cap, blk, block_rows, own_hbm, key_hbm, sten_hbm, itp_hbm, w_hbm,
                        *rest):
    half = groups // 2
    outs, rest = rest[:half], rest[half:]
    (slot_out, own_ref, key_ref, sten_ref, itp_ref, w_ref, buffer, slot_v, slot_s, sems, out_sems,
     sem) = rest
    loads = start_copies([(own_hbm, own_ref), (key_hbm, key_ref), (sten_hbm, sten_ref),
                          (itp_hbm, itp_ref), (w_hbm, w_ref)], sems)

    def clear(k, carry):
        start = pl.multiple_of(k * block_rows, 8)
        buffer[pl.ds(start, block_rows), :] = jnp.zeros((block_rows, SEG), jnp.float32)
        return carry

    lax.fori_loop(0, half, clear, 0)

    for load in loads[:4]:
        load.wait()
    chunks = own_ref.shape[0]
    nb = cap // blk
    own = own_ref[...]
    high = groups * chunks
    shift = chunks.bit_length() - 1
    masks = [flag(own == o, jnp.float32) for o in range(groups)]
    hits = jnp.concatenate(masks, axis=0).astype(jnp.bfloat16)
    square = (SEG, SEG)
    within = mxu(hits, flag(iota(square, 0) < iota(square, 1)))
    tallies = mxu(hits, jnp.ones(square, jnp.bfloat16)).astype(jnp.bfloat16)
    line, column = iota((high, high), 0), iota((high, high), 1)
    same = (line >> shift) == (column >> shift)
    ranks = within + mxu(flag(same & (column < line)), tallies)
    rank = sum(masks[o] * ranks[o * chunks:(o + 1) * chunks] for o in range(groups))
    rank = rank.astype(jnp.int32)
    relative = own ^ lax.axis_index("py")
    block, across = relative & (half - 1), relative >> (half.bit_length() - 1)
    slot_v[...] = block * block_rows + across * cap + rank
    slot_out[...] = (block * 2 + across) * cap + rank
    copy = pltpu.make_async_copy(slot_v, slot_s, sem)
    copy.start()

    log = blk.bit_length() - 1
    place = relative * nb + (rank >> log)
    lane = rank & (blk - 1)
    key, sten, itp = key_ref[...], sten_ref[...], itp_ref[...]
    tall = groups * nb
    meta = jnp.zeros((5 * tall, SEG), jnp.float32)
    for i in range(chunks):
        chosen = iota((tall, SEG), 0) == place[i:i + 1]
        parts = split_parts(itp[i:i + 1], 3)
        parts += [key[i:i + 1].astype(jnp.bfloat16), (sten[i:i + 1] + 1).astype(jnp.bfloat16)]
        left = [jnp.where(chosen, part.astype(jnp.float32), 0.0) for part in parts]
        right = flag(iota(square, 0) == lane[i:i + 1])
        meta = meta + lax.dot_general(
            jnp.concatenate(left, axis=0).astype(jnp.bfloat16), right,
            (((1,), (1,)), ((), ())), preferred_element_type=jnp.float32)
    shares = meta[:tall] + meta[tall:2 * tall] + meta[2 * tall:3 * tall]
    targets = meta[3 * tall:4 * tall] * LX + meta[4 * tall:]
    for v in range(groups):
        base = (v % half) * block_rows + 2 * cap + (v // half) * 2 * nb
        buffer[base:base + nb, :] = shares[v * nb:(v + 1) * nb]
        buffer[base + nb:base + 2 * nb, :] = targets[v * nb:(v + 1) * nb]

    copy.wait()
    loads[4].wait()

    def place_rows(g, carry):
        weights = w_ref[pl.ds(pl.multiple_of(g * 8, 8), 8), :]
        line, lane = g // 16, (g % 16) * 8
        for i in range(8):
            buffer[pl.ds(slot_s[line, lane + i], 1), :] = weights[i:i + 1]
        return carry

    lax.fori_loop(0, w_ref.shape[0] // 8, place_rows, 0)
    for store in start_copies([(buffer.at[pl.ds(k * block_rows, block_rows)], out)
                               for k, out in enumerate(outs)], out_sems):
        store.wait()


def pack_products_kernel(groups, cap, slot_ref, w_hbm, d_hbm, *rest):
    half = groups // 2
    outs, (w_ref, d_ref, buffer, sems, out_sems) = rest[:half], rest[half:]
    loads = start_copies([(w_hbm, w_ref), (d_hbm, d_ref)], sems)

    def clear(o, carry):
        start = pl.multiple_of(o * cap, 8)
        buffer[pl.ds(start, cap), :] = jnp.zeros((cap, SEG), jnp.float32)
        return carry

    lax.fori_loop(0, groups, clear, 0)

    for load in loads:
        load.wait()

    def place_rows(g, carry):
        start = pl.multiple_of(g * 8, 8)
        products = w_ref[pl.ds(start, 8), :] * d_ref[pl.ds(start, 8), :]
        line, lane = g // 16, (g % 16) * 8
        for i in range(8):
            buffer[pl.ds(slot_ref[line, lane + i], 1), :] = products[i:i + 1]
        return carry

    lax.fori_loop(0, w_ref.shape[0] // 8, place_rows, 0)
    for store in start_copies([(buffer.at[pl.ds(k * 2 * cap, 2 * cap)], out)
                               for k, out in enumerate(outs)], out_sems):
        store.wait()


def pack_swap_kernel(_, cy_hbm, c0_hbm, cx_hbm, swap_out, cy_ref, first, last, sems):
    width = c0_hbm.shape[2]
    for load in start_copies([
        (cy_hbm, cy_ref),
        (c0_hbm.at[:, :, pl.ds(0, SEG)], first.at[pl.ds(0, F)]),
        (cx_hbm.at[:, pl.ds(0, SEG)], first.at[F]),
        (c0_hbm.at[:, :, pl.ds(width - SEG, SEG)], last.at[pl.ds(0, F)]),
        (cx_hbm.at[:, pl.ds(width - SEG, SEG)], last.at[F]),
    ], sems):
        load.wait()
    columns = cy_ref.shape[1]
    cy = cy_ref[...]
    cy = jnp.where(iota(cy.shape, 1) == columns - 1, 0.0, cy)
    empty = jnp.zeros((LX, SEG), jnp.float32)
    me = lax.axis_index("px")
    nx = first.shape[1]
    for q in range(columns // width):
        low, top = q * width, (q + 1) * width
        tiles = [cy[:, t:t + SEG] for t in range(low, top, SEG)]
        before = cy[:, low - SEG:low] if low > 0 else empty
        after = cy[:, top:top + SEG] if top < columns else empty
        tiles.append(ends_tile(before, after))
        for t, tile in enumerate(tiles):
            swap_out[q, t * LX:(t + 1) * LX, :] = tile
        base = len(tiles) * LX
        for i in range(F + 1):
            swap_out[q, base + i * nx:base + (i + 1) * nx, :] = jnp.where(
                q < me, first[i], last[i])


def sum_rows(cap, blk, metas, acc_ref, terms):
    nb = cap // blk
    numbers = 1.0 + iota((ROWS, cap), 0).astype(jnp.float32)
    for source, meta in enumerate(metas):
        upper = jnp.concatenate(
            [jnp.broadcast_to(meta[i:i + 1], (SEG, SEG)).T[:blk] for i in range(nb)], axis=0)
        target = jnp.concatenate([meta[nb + i:nb + i + 1, :blk] for i in range(nb)], axis=1)
        hit = flag(numbers == target)
        values = jnp.concatenate(terms(source, upper), axis=1)
        part = mxu(jnp.concatenate([hit, hit], axis=1),
                   jnp.concatenate(split_parts(values, 2), axis=0))
        if source:
            acc_ref[...] += part
        else:
            acc_ref[...] = part


def cut_part(rows_ref, to, f, q, spans):
    per = to.shape[0] - 1

    def tile(b):
        start = pl.multiple_of((f * NB + b) * LX, LX)
        return rows_ref[pl.ds(start, LX), :]

    for j in range(per):
        to[j] = tile(q * per + j)
    before = tile(jnp.maximum(q * per - 1, 0))
    after = tile(jnp.minimum(q * per + per, NB - 1))
    to[per] = ends_tile(jnp.where(q > 0, before, 0.0), jnp.where(q < spans - 1, after, 0.0))


def weights_kernel(half, cap, blk, across, *rest):
    w_refs, (_, meta_out, diagonal_out, side_out, acc_ref) = rest[:half], rest[half:]
    nb = cap // blk
    for k, w_ref in enumerate(w_refs):
        meta_out[k] = w_ref[2 * cap:, :]
    rows = slice(across * cap, (across + 1) * cap)

    def terms(source, upper):
        lower = 1.0 - upper
        weights = w_refs[source][rows, :]
        lower_w, upper_w = lower * weights, upper * weights
        return [lower * lower_w, upper * lower_w, upper * upper_w]

    low = 2 * cap + across * 2 * nb
    sum_rows(cap, blk, [w_ref[low:low + 2 * nb, :] for w_ref in w_refs], acc_ref, terms)
    diagonal_out[...] = acc_ref[:, :SEG] + pltpu.roll(acc_ref[:, 2 * SEG:], 1, 0)
    side_out[...] = acc_ref[:, SEG:2 * SEG]


def sum_products(half, cap, blk, across, meta_ref, v_refs, acc_ref, sums_ref):
    nb = cap // blk
    rows = slice(across * cap, (across + 1) * cap)

    def terms(source, upper):
        products = v_refs[source][rows, :]
        return [(1.0 - upper) * products, upper * products]

    low = across * 2 * nb
    sum_rows(cap, blk, [meta_ref[k, low:low + 2 * nb, :] for k in range(half)], acc_ref, terms)
    sums_ref[...] = acc_ref[:, :SEG] + pltpu.roll(acc_ref[:, SEG:], 1, 0)


def products_kernel(half, cap, blk, meta_ref, d_ref, e_ref, far_d_ref, far_e_ref, *rest):
    v_refs, (out, *far_outs, acc_ref, sums_ref, far_ref, side) = rest[:half], rest[half:]
    spans = out.shape[0]
    sum_products(half, cap, blk, 1, meta_ref, v_refs, acc_ref, far_ref)
    me = lax.axis_index("px")
    for k, far_out in enumerate(far_outs):
        for f in range(F):
            cut_part(far_ref, far_out.at[f], f, me ^ k, spans)
    sum_products(half, cap, blk, 0, meta_ref, v_refs, acc_ref, sums_ref)
    side[0] = d_ref[...] + far_d_ref[...]
    side[1] = e_ref[...] + far_e_ref[...]
    for q in range(spans):
        for channel, rows_ref in enumerate((side.at[0], side.at[1], sums_ref)):
            for f in range(F):
                cut_part(rows_ref, out.at[q, channel * F + f], f, q, spans)


def x_lines(nx):
    return [pl.ds(i, 8, stride=nx // 8) for i in range(nx // 8)]


def sweep_x_into(to_refs, from_refs, cx_ref, plus_refs=None, sign=1.0):
    tiles, nx, _ = cx_ref.shape
    picks = x_lines(nx)
    for start in range(0, tiles, X_TILES):
        group = range(start, min(start + X_TILES, tiles))
        chains = [(i, t) for t in group for i in range(len(from_refs))]
        coeffs = {t: [cx_ref[t, pick, :] for pick in picks] for t in group}
        wrapped = {t: pltpu.roll(coeffs[t][-1], 1, 0) for t in group}
        fields = {(i, t): [from_refs[i][t, pick, :] for pick in picks] for i, t in chains}
        for _ in range(M):
            for i, t in chains:
                values = fields[i, t]
                after = values[1:] + [pltpu.roll(values[0], 7, 0)]
                low = wrapped[t] * (values[0] - pltpu.roll(values[-1], 1, 0))
                flux = [c * (b - a) for c, a, b in zip(coeffs[t], values, after)]
                fields[i, t] = [a + f - g for a, f, g in zip(values, flux, [low] + flux[:-1])]
        for i, t in chains:
            for pick, value in zip(picks, fields[i, t]):
                if plus_refs is not None:
                    value = value + sign * plus_refs[i][t, pick, :]
                to_refs[i][t, pick, :] = value


def sweep_y_into(to_refs, from_refs, cy_ref):
    tiles, nx, _ = cy_ref.shape
    lane = iota((Y_LINES, SEG), 1)

    def next_cells(values):
        moved = [pltpu.roll(value, SEG - 1, 1) for value in values]
        return [jnp.where(lane == SEG - 1, b, a) for a, b in zip(moved, moved[1:] + moved[:1])]

    def previous_cells(values):
        moved = [pltpu.roll(value, 1, 1) for value in values]
        return [jnp.where(lane == 0, a, b) for a, b in zip(moved[-1:] + moved[:-1], moved)]

    for low in range(0, nx, Y_LINES):
        lines = slice(low, low + Y_LINES)
        coeffs = [cy_ref[t, lines, :] for t in range(tiles)]
        coeffs_low = previous_cells(coeffs)
        fields = [[ref[t, lines, :] for t in range(tiles)] for ref in from_refs]
        for _ in range(M):
            for i, values in enumerate(fields):
                after, before = next_cells(values), previous_cells(values)
                fields[i] = [
                    a + c * (b - a) - d * (a - e)
                    for a, b, c, d, e in zip(values, after, coeffs, coeffs_low, before)]
        for to_ref, values in zip(to_refs, fields):
            for t, value in enumerate(values):
                to_ref[t, lines, :] = value


def normal_into(to_refs, from_refs, diagonal_refs, side_refs, base_refs=None):
    tiles, nx, _ = from_refs[0].shape
    picks = x_lines(nx)
    for t in range(tiles):
        for i, from_ref in enumerate(from_refs):
            values = [from_ref[t, pick, :] for pick in picks]
            sides = [side_refs[i][t, pick, :] for pick in picks]
            low = [e * a for e, a in zip(sides, values)]
            low = [pltpu.roll(low[-1], 1, 0)] + low[:-1]
            after = values[1:] + [pltpu.roll(values[0], 7, 0)]
            for line, pick in enumerate(picks):
                result = (diagonal_refs[i][t, pick, :] * values[line] + sides[line] * after[line]
                          + low[line])
                if base_refs is not None:
                    result = base_refs[i][t, pick, :] - result
                to_refs[i][t, pick, :] = result


def of_fields(ref, start=0):
    return [ref.at[start + f] for f in range(F)]


def start_kernel(c0_ref, cx_ref, swap_ref, c0_out, cx_out, cy_out, u_out, token_out, work):
    token_out[...] = jnp.zeros_like(token_out)
    nx = cx_ref.shape[0]
    spans, count = swap_ref.shape[0], cy_out.shape[0]
    me = lax.axis_index("px")
    for p in range(spans):
        for t in range(count):
            cy_out[t, p * LX:(p + 1) * LX, :] = swap_ref[p, t * LX:(t + 1) * LX, :]

    def beside(i):
        lines = slice(count * LX + i * nx, count * LX + (i + 1) * nx)
        before = swap_ref[jnp.maximum(me - 1, 0), lines, :]
        after = swap_ref[jnp.minimum(me + 1, spans - 1), lines, :]
        return ends_tile(jnp.where(me > 0, before, 0.0), jnp.where(me < spans - 1, after, 0.0))

    for t in range(count - 1):
        tile = slice(t * SEG, (t + 1) * SEG)
        cx_out[t] = cx_ref[:, tile]
        for f in range(F):
            c0_out[f, t] = c0_ref[f, :, tile]
    cx_out[count - 1] = beside(F)
    cx_out[:, nx - 1:, :] = jnp.zeros((count, 1, SEG), jnp.float32)
    for f in range(F):
        c0_out[f, count - 1] = beside(f)
    sweep_x_into(of_fields(work), of_fields(c0_out), cx_out)
    sweep_y_into(of_fields(u_out), of_fields(work), cy_out)


def join_kernel(spans, *rest):
    parts, out = rest[:spans], rest[spans]
    me = lax.axis_index("px")
    for k, part in enumerate(parts):
        rows = pl.ds(pl.multiple_of((me ^ k) * LX, LX), LX)
        for f in range(F):
            for t in range(out.shape[1]):
                out[f, t, rows, :] = part[f, t]


def solve_kernel(c0_ref, cx_ref, cy_ref, u_ref, obs_ref, far_ref, r_out, q_out, h_out, dots_out,
                 vec, coef, work):
    for p in range(obs_ref.shape[0]):
        rows = slice(p * LX, (p + 1) * LX)
        for channel in range(2 * F):
            coef[channel, :, rows, :] = obs_ref[p, channel]
        for f in range(F):
            coef[2 * F + f, :, rows, :] = obs_ref[p, 2 * F + f] + far_ref[f, :, rows, :]

    sides = (of_fields(coef), of_fields(coef, F))
    one, two, r, q, s, h = (of_fields(ref) for ref in (
        work.at[0], work.at[1], vec.at[0], vec.at[1], vec.at[2], h_out))
    normal_into(one, of_fields(u_ref), *sides, of_fields(coef, 2 * F))
    sweep_y_into(two, one, cy_ref)
    sweep_x_into(r, two, cx_ref, of_fields(c0_ref), -1.0)
    sweep_x_into(one, r, cx_ref)
    sweep_y_into(two, one, cy_ref)
    normal_into(one, two, *sides)
    sweep_y_into(two, one, cy_ref)
    sweep_x_into(q, two, cx_ref, r)
    sweep_x_into(one, q, cx_ref)
    sweep_y_into(s, one, cy_ref)
    normal_into(h, s, *sides)

    tiles, nx = vec.shape[2] - 1, vec.shape[3]
    sums = [jnp.zeros((8, SEG), jnp.float32) for _ in range(4)]
    for f in range(F):
        for t in range(tiles):
            r_out[f, :, t * SEG:(t + 1) * SEG] = vec[0, f, t]
            q_out[f, :, t * SEG:(t + 1) * SEG] = vec[1, f, t]
            for low in range(0, nx, 8):
                lines = slice(low, low + 8)
                r, q, s = (vec[i, f, t, lines, :] for i in range(3))
                for i, product in enumerate((r * r, r * q, q * q, s * h_out[f, t, lines, :])):
                    sums[i] = sums[i] + product
    dots = jnp.zeros((1, SEG), jnp.float32)
    for i, total in enumerate(sums):
        line = jnp.sum(total, axis=0, keepdims=True)
        for distance in (64, 32, 16):
            line = line + pltpu.roll(line, distance, 1)
        dots = jnp.where(iota((1, SEG), 1) // SPLIT == i, line, dots)
    dots_out[...] = jnp.broadcast_to(dots, dots_out.shape)


def last_kernel(h_ref, q_ref, cx_ref, cy_ref, qq_out, work):
    sweep_y_into(of_fields(work.at[0]), of_fields(h_ref), cy_ref)
    sweep_x_into(of_fields(work.at[1]), of_fields(work.at[0]), cx_ref)
    for f in range(F):
        for t in range(work.shape[2] - 1):
            tile = slice(t * SEG, (t + 1) * SEG)
            qq_out[f, :, tile] = q_ref[f, :, tile] + work[1, f, t]


def finish_kernel(dots_ref, c0_ref, r_ref, q_ref, qq_ref, control_out, residual_out):
    dots = jnp.sum(dots_ref[...], axis=0)
    lane = iota((1, SEG), 1)
    rr, rq, qq2, energy = (pltpu.roll(dots, (SEG - i * SPLIT) % SEG, 1) for i in range(4))

    def total(line):
        return jnp.sum(jnp.where(lane < SPLIT, line, 0.0), axis=1, keepdims=True)

    rr_sum = total(rr)
    alpha = rr_sum / total(rq)
    new_sum = total(rr - 2.0 * alpha * rq + alpha * alpha * qq2)
    more = 1.0 + new_sum / rr_sum
    curve = total(more * more * rq - 2.0 * more * alpha * qq2 + alpha * alpha * (qq2 + energy))
    second = new_sum / curve
    first_weight = alpha + second * more
    both = alpha * second
    for f in range(F):
        r, q = r_ref[f], q_ref[f]
        control_out[f] = c0_ref[f] + first_weight * r - both * q
        residual_out[f] = r - first_weight * q + both * qq_ref[f]


def call(kernel, out_shape, scratch=(), in_specs=None, out_specs=None, limit=VMEM_BYTES,
         weight=1):
    params = {"in_specs": in_specs, "out_specs": out_specs}
    return pl.pallas_call(
        kernel,
        out_shape=out_shape,
        scratch_shapes=list(scratch),
        compiler_params=pltpu.CompilerParams(vmem_limit_bytes=limit),
        cost_estimate=pl.CostEstimate(flops=weight, bytes_accessed=weight, transcendentals=0),
        **{name: value for name, value in params.items() if value is not None},
    )


def f32(*shape):
    return jax.ShapeDtypeStruct(shape, jnp.float32)


def vmem(*shape, kind=jnp.float32):
    return pltpu.VMEM(shape, kind)


def shards(
    control_start, coef_x, coef_y, innovation, obs_weight, interp, obs_owner, cell_key, stencil
):
    groups, spans = lax.axis_size("py"), lax.axis_size("px")
    half = groups // 2
    rows = innovation.shape[0]
    cap = 3 * rows // groups
    blk = SEG if cap % SEG == 0 else HALF
    meta_rows = -(-4 * (cap // blk) // 8) * 8
    block_rows = 2 * cap + meta_rows
    chunks = rows // SEG
    nx, width = control_start.shape[2], control_start.shape[3]
    tiles = width // SEG + 1
    c0, cx = control_start[:, 0], coef_x[0]
    hbm, local, scalars = (
        pl.BlockSpec(memory_space=s) for s in (pltpu.HBM, pltpu.VMEM, pltpu.SMEM))
    ints = vmem(chunks, SEG, kind=jnp.int32)
    dma = pltpu.SemaphoreType.DMA

    def to_half(block, k):
        return lax.ppermute(block, "py", [(i, i ^ k) for i in range(groups)])

    def across(parts):
        return [
            lax.ppermute(parts[k], ("px", "py"), [
                (i * groups + j, (i ^ k) * groups + (j ^ half))
                for i in range(spans) for j in range(groups)])
            for k in range(spans)]

    *w_blocks, slots = call(
        functools.partial(pack_weights_kernel, groups, cap, blk, block_rows),
        (f32(block_rows, SEG),) * half + (jax.ShapeDtypeStruct((chunks, SEG), jnp.int32),),
        [ints, ints, ints, vmem(chunks, SEG), vmem(rows, SEG), vmem(half * block_rows, SEG), ints,
         pltpu.SMEM((chunks, SEG), jnp.int32), dma((5,)), dma((half,)), dma],
        [hbm] * 5,
        (hbm,) * half + (local,),
        limit=PACK_BYTES,
    )(
        obs_owner.reshape(chunks, SEG), cell_key.reshape(chunks, SEG),
        stencil.reshape(chunks, SEG), interp.reshape(chunks, SEG), obs_weight,
    )
    v_blocks = list(call(
        functools.partial(pack_products_kernel, groups, cap),
        (f32(2 * cap, SEG),) * half,
        [vmem(rows, SEG), vmem(rows, SEG), vmem(groups * cap, SEG), dma((2,)), dma((half,))],
        [scalars] + [hbm] * 2,
        (hbm,) * half,
        limit=PACK_BYTES,
    )(slots, obs_weight, innovation))
    w_blocks[1:] = [to_half(w_blocks[k], k) for k in range(1, half)]
    w_blocks[1], *v_blocks[1:] = lax.optimization_barrier((w_blocks[1], *v_blocks[1:]))
    v_blocks[1:] = [to_half(v_blocks[k], k) for k in range(1, half)]

    swap = call(
        pack_swap_kernel,
        f32(spans, LX * tiles + (F + 1) * nx, SEG),
        [vmem(*coef_y.shape[1:]), vmem(F + 1, nx, SEG), vmem(F + 1, nx, SEG), dma((5,))],
        [local] + [hbm] * 3,
        limit=PACK_BYTES,
    )(slots, coef_y[0], c0, cx)
    swap = lax.all_to_all(swap, "px", split_axis=0, concat_axis=0, tiled=True)
    c0_ext, cx_ext, cy_ext, u_ext, token = call(
        start_kernel,
        (f32(F, tiles, nx, SEG), f32(tiles, nx, SEG), f32(tiles, nx, SEG), f32(F, tiles, nx, SEG),
         f32(8, SEG)),
        [vmem(F, tiles, nx, SEG)],
    )(c0, cx, swap)

    def sum_weights(side, token, weight):
        return call(
            functools.partial(weights_kernel, half, cap, blk, side),
            (f32(half, meta_rows, SEG),) + (f32(ROWS, SEG),) * 2,
            [vmem(ROWS, 3 * SEG)],
            weight=weight,
        )(*w_blocks, token)

    meta, *side_across = sum_weights(1, w_blocks[0], FIRST)
    side_across = [to_half(values, half) for values in side_across]
    meta, *side = sum_weights(0, token, 1)
    parts, *sums_across = call(
        functools.partial(products_kernel, half, cap, blk),
        (f32(spans, 3 * F, tiles, LX, SEG),) + (f32(F, tiles, LX, SEG),) * spans,
        [vmem(ROWS, 2 * SEG), vmem(ROWS, SEG), vmem(ROWS, SEG), vmem(2, ROWS, SEG)],
    )(meta, *side, *side_across, *v_blocks)
    far_sums = call(
        functools.partial(join_kernel, spans), f32(F, tiles, nx, SEG), weight=JOIN,
    )(*across(sums_across))
    parts = lax.all_to_all(parts, "px", split_axis=0, concat_axis=0, tiled=True)

    r, q, h, dots = call(
        solve_kernel,
        (f32(F, nx, width),) * 2 + (f32(F, tiles, nx, SEG), f32(groups * spans, 1, SEG)),
        [vmem(3, F, tiles, nx, SEG), vmem(3 * F, tiles, nx, SEG), vmem(2, F, tiles, nx, SEG)],
    )(c0_ext, cx_ext, cy_ext, u_ext, parts, far_sums)
    dots = lax.all_to_all(dots, ("px", "py"), split_axis=0, concat_axis=0, tiled=True)
    qq = call(last_kernel, f32(F, nx, width), [vmem(2, F, tiles, nx, SEG)])(
        h, q, cx_ext, cy_ext)
    control, residual = call(finish_kernel, (f32(F, nx, width),) * 2)(dots, c0, r, q, qq)
    return control[:, None], residual[:, None]


def solution(mesh):
    return jax.shard_map(
        shards,
        mesh=mesh,
        in_specs=(
            P(None, "py", None, "px"),
            P("py", None, "px"),
            P("py", "px", None),
            P(("px", "py"), None),
            P(("px", "py"), None),
            P(("px", "py")),
            P(("px", "py"), None),
            P(("px", "py")),
            P(("px", "py")),
        ),
        out_specs=(P(None, "py", None, "px"), P(None, "py", None, "px")),
        check_vma=False,
    )
```

```python
import functools

import jax
import jax.numpy as jnp
from jax import lax
from jax.experimental import pallas as pl
from jax.experimental.pallas import tpu as pltpu
from jax.sharding import PartitionSpec as P

F = 2
SEG = 128
M = 4
NB = 16
LX = 16
ROWS = F * NB * LX
HALF = SEG // 2
SPLIT = 16
Y_LINES = 16
VMEM_BYTES = 32 * 1024 * 1024
PACK_BYTES = 60 * 1024 * 1024
FIRST = 100_000_000
JOIN = 100_000_000


def iota(shape, axis):
    return lax.broadcasted_iota(jnp.int32, shape, axis)


def flag(condition, kind=jnp.bfloat16):
    return jnp.where(condition, 1.0, 0.0).astype(kind)


def mxu(left, right):
    return jnp.dot(left, right, preferred_element_type=jnp.float32)


def split_parts(values, count):
    parts = []
    for _ in range(count):
        part = values.astype(jnp.bfloat16)
        parts.append(part)
        values = values - part.astype(jnp.float32)
    return parts


def ends_tile(before, after):
    return jnp.where(iota(after.shape, after.ndim - 1) < HALF, after, before)


def start_copies(pairs, sems):
    copies = [pltpu.make_async_copy(*pair, sems.at[i]) for i, pair in enumerate(pairs)]
    for copy in copies:
        copy.start()
    return copies


def pack_weights_kernel(groups, cap, blk, block_rows, own_hbm, key_hbm, sten_hbm, itp_hbm, w_hbm,
                        *rest):
    half = groups // 2
    outs, rest = rest[:half], rest[half:]
    (slot_out, own_ref, key_ref, sten_ref, itp_ref, w_ref, buffer, slot_v, slot_s, sems, out_sems,
     sem) = rest
    loads = start_copies([(own_hbm, own_ref), (key_hbm, key_ref), (sten_hbm, sten_ref),
                          (itp_hbm, itp_ref), (w_hbm, w_ref)], sems)

    def clear(k, carry):
        start = pl.multiple_of(k * block_rows, 8)
        buffer[pl.ds(start, block_rows), :] = jnp.zeros((block_rows, SEG), jnp.float32)
        return carry

    lax.fori_loop(0, half, clear, 0)

    for load in loads[:4]:
        load.wait()
    chunks = own_ref.shape[0]
    nb = cap // blk
    own = own_ref[...]
    high = groups * chunks
    shift = chunks.bit_length() - 1
    masks = [flag(own == o, jnp.float32) for o in range(groups)]
    hits = jnp.concatenate(masks, axis=0).astype(jnp.bfloat16)
    square = (SEG, SEG)
    within = mxu(hits, flag(iota(square, 0) < iota(square, 1)))
    tallies = mxu(hits, jnp.ones(square, jnp.bfloat16)).astype(jnp.bfloat16)
    line, column = iota((high, high), 0), iota((high, high), 1)
    same = (line >> shift) == (column >> shift)
    ranks = within + mxu(flag(same & (column < line)), tallies)
    rank = sum(masks[o] * ranks[o * chunks:(o + 1) * chunks] for o in range(groups))
    rank = rank.astype(jnp.int32)
    relative = own ^ lax.axis_index("py")
    block, across = relative & (half - 1), relative >> (half.bit_length() - 1)
    slot_v[...] = block * block_rows + across * cap + rank
    slot_out[...] = (block * 2 + across) * cap + rank
    copy = pltpu.make_async_copy(slot_v, slot_s, sem)
    copy.start()

    log = blk.bit_length() - 1
    place = relative * nb + (rank >> log)
    lane = rank & (blk - 1)
    key, sten, itp = key_ref[...], sten_ref[...], itp_ref[...]
    tall = groups * nb
    meta = jnp.zeros((5 * tall, SEG), jnp.float32)
    for i in range(chunks):
        chosen = iota((tall, SEG), 0) == place[i:i + 1]
        parts = split_parts(itp[i:i + 1], 3)
        parts += [key[i:i + 1].astype(jnp.bfloat16), (sten[i:i + 1] + 1).astype(jnp.bfloat16)]
        left = [jnp.where(chosen, part.astype(jnp.float32), 0.0) for part in parts]
        right = flag(iota(square, 0) == lane[i:i + 1])
        meta = meta + lax.dot_general(
            jnp.concatenate(left, axis=0).astype(jnp.bfloat16), right,
            (((1,), (1,)), ((), ())), preferred_element_type=jnp.float32)
    shares = meta[:tall] + meta[tall:2 * tall] + meta[2 * tall:3 * tall]
    targets = meta[3 * tall:4 * tall] * LX + meta[4 * tall:]
    for v in range(groups):
        base = (v % half) * block_rows + 2 * cap + (v // half) * 2 * nb
        buffer[base:base + nb, :] = shares[v * nb:(v + 1) * nb]
        buffer[base + nb:base + 2 * nb, :] = targets[v * nb:(v + 1) * nb]

    copy.wait()
    loads[4].wait()

    def place_rows(g, carry):
        weights = w_ref[pl.ds(pl.multiple_of(g * 8, 8), 8), :]
        line, lane = g // 16, (g % 16) * 8
        for i in range(8):
            buffer[pl.ds(slot_s[line, lane + i], 1), :] = weights[i:i + 1]
        return carry

    lax.fori_loop(0, w_ref.shape[0] // 8, place_rows, 0)
    for store in start_copies([(buffer.at[pl.ds(k * block_rows, block_rows)], out)
                               for k, out in enumerate(outs)], out_sems):
        store.wait()


def pack_products_kernel(groups, cap, slot_ref, w_hbm, d_hbm, *rest):
    half = groups // 2
    outs, (w_ref, d_ref, buffer, sems, out_sems) = rest[:half], rest[half:]
    loads = start_copies([(w_hbm, w_ref), (d_hbm, d_ref)], sems)

    def clear(o, carry):
        start = pl.multiple_of(o * cap, 8)
        buffer[pl.ds(start, cap), :] = jnp.zeros((cap, SEG), jnp.float32)
        return carry

    lax.fori_loop(0, groups, clear, 0)

    for load in loads:
        load.wait()

    def place_rows(g, carry):
        start = pl.multiple_of(g * 8, 8)
        products = w_ref[pl.ds(start, 8), :] * d_ref[pl.ds(start, 8), :]
        line, lane = g // 16, (g % 16) * 8
        for i in range(8):
            buffer[pl.ds(slot_ref[line, lane + i], 1), :] = products[i:i + 1]
        return carry

    lax.fori_loop(0, w_ref.shape[0] // 8, place_rows, 0)
    for store in start_copies([(buffer.at[pl.ds(k * 2 * cap, 2 * cap)], out)
                               for k, out in enumerate(outs)], out_sems):
        store.wait()


def pack_swap_kernel(_, cy_hbm, c0_hbm, cx_hbm, swap_out, cy_ref, first, last, sems):
    width = c0_hbm.shape[2]
    for load in start_copies([
        (cy_hbm, cy_ref),
        (c0_hbm.at[:, :, pl.ds(0, SEG)], first.at[pl.ds(0, F)]),
        (cx_hbm.at[:, pl.ds(0, SEG)], first.at[F]),
        (c0_hbm.at[:, :, pl.ds(width - SEG, SEG)], last.at[pl.ds(0, F)]),
        (cx_hbm.at[:, pl.ds(width - SEG, SEG)], last.at[F]),
    ], sems):
        load.wait()
    columns = cy_ref.shape[1]
    cy = cy_ref[...]
    cy = jnp.where(iota(cy.shape, 1) == columns - 1, 0.0, cy)
    empty = jnp.zeros((LX, SEG), jnp.float32)
    me = lax.axis_index("px")
    nx = first.shape[1]
    for q in range(columns // width):
        low, top = q * width, (q + 1) * width
        tiles = [cy[:, t:t + SEG] for t in range(low, top, SEG)]
        before = cy[:, low - SEG:low] if low > 0 else empty
        after = cy[:, top:top + SEG] if top < columns else empty
        tiles.append(ends_tile(before, after))
        for t, tile in enumerate(tiles):
            swap_out[q, t * LX:(t + 1) * LX, :] = tile
        base = len(tiles) * LX
        for i in range(F + 1):
            swap_out[q, base + i * nx:base + (i + 1) * nx, :] = jnp.where(
                q < me, first[i], last[i])


def sum_rows(cap, blk, metas, acc_ref, terms):
    nb = cap // blk
    numbers = 1.0 + iota((ROWS, cap), 0).astype(jnp.float32)
    for source, meta in enumerate(metas):
        upper = jnp.concatenate(
            [jnp.broadcast_to(meta[i:i + 1], (SEG, SEG)).T[:blk] for i in range(nb)], axis=0)
        target = jnp.concatenate([meta[nb + i:nb + i + 1, :blk] for i in range(nb)], axis=1)
        hit = flag(numbers == target)
        values = jnp.concatenate(terms(source, upper), axis=1)
        part = mxu(jnp.concatenate([hit, hit], axis=1),
                   jnp.concatenate(split_parts(values, 2), axis=0))
        if source:
            acc_ref[...] += part
        else:
            acc_ref[...] = part


def cut_part(rows_ref, to, f, q, spans):
    per = to.shape[0] - 1

    def tile(b):
        start = pl.multiple_of((f * NB + b) * LX, LX)
        return rows_ref[pl.ds(start, LX), :]

    for j in range(per):
        to[j] = tile(q * per + j)
    before = tile(jnp.maximum(q * per - 1, 0))
    after = tile(jnp.minimum(q * per + per, NB - 1))
    to[per] = ends_tile(jnp.where(q > 0, before, 0.0), jnp.where(q < spans - 1, after, 0.0))


def weights_kernel(half, cap, blk, across, *rest):
    w_refs, (_, meta_out, diagonal_out, side_out, acc_ref) = rest[:half], rest[half:]
    nb = cap // blk
    for k, w_ref in enumerate(w_refs):
        meta_out[k] = w_ref[2 * cap:, :]
    rows = slice(across * cap, (across + 1) * cap)

    def terms(source, upper):
        lower = 1.0 - upper
        weights = w_refs[source][rows, :]
        lower_w, upper_w = lower * weights, upper * weights
        return [lower * lower_w, upper * lower_w, upper * upper_w]

    low = 2 * cap + across * 2 * nb
    sum_rows(cap, blk, [w_ref[low:low + 2 * nb, :] for w_ref in w_refs], acc_ref, terms)
    diagonal_out[...] = acc_ref[:, :SEG] + pltpu.roll(acc_ref[:, 2 * SEG:], 1, 0)
    side_out[...] = acc_ref[:, SEG:2 * SEG]


def sum_products(half, cap, blk, across, meta_ref, v_refs, acc_ref, sums_ref):
    nb = cap // blk
    rows = slice(across * cap, (across + 1) * cap)

    def terms(source, upper):
        products = v_refs[source][rows, :]
        return [(1.0 - upper) * products, upper * products]

    low = across * 2 * nb
    sum_rows(cap, blk, [meta_ref[k, low:low + 2 * nb, :] for k in range(half)], acc_ref, terms)
    sums_ref[...] = acc_ref[:, :SEG] + pltpu.roll(acc_ref[:, SEG:], 1, 0)


def products_kernel(half, cap, blk, meta_ref, d_ref, e_ref, far_d_ref, far_e_ref, *rest):
    v_refs, (out, *far_outs, acc_ref, sums_ref, far_ref, side) = rest[:half], rest[half:]
    spans = out.shape[0]
    sum_products(half, cap, blk, 1, meta_ref, v_refs, acc_ref, far_ref)
    me = lax.axis_index("px")
    for k, far_out in enumerate(far_outs):
        for f in range(F):
            cut_part(far_ref, far_out.at[f], f, me ^ k, spans)
    sum_products(half, cap, blk, 0, meta_ref, v_refs, acc_ref, sums_ref)
    side[0] = d_ref[...] + far_d_ref[...]
    side[1] = e_ref[...] + far_e_ref[...]
    for q in range(spans):
        for channel, rows_ref in enumerate((side.at[0], side.at[1], sums_ref)):
            for f in range(F):
                cut_part(rows_ref, out.at[q, channel * F + f], f, q, spans)


def x_lines(nx):
    return [pl.ds(i, 8, stride=nx // 8) for i in range(nx // 8)]


def sweep_x_into(to_refs, from_refs, cx_ref, plus_refs=None, sign=1.0):
    tiles, nx, _ = cx_ref.shape
    picks = x_lines(nx)

    def sweep_tile(t, carry):
        coeffs = [cx_ref[t, pick, :] for pick in picks]
        wrapped = pltpu.roll(coeffs[-1], 1, 0)
        fields = [[ref[t, pick, :] for pick in picks] for ref in from_refs]
        for _ in range(M):
            for i, values in enumerate(fields):
                after = values[1:] + [pltpu.roll(values[0], 7, 0)]
                low = wrapped * (values[0] - pltpu.roll(values[-1], 1, 0))
                flux = [c * (b - a) for c, a, b in zip(coeffs, values, after)]
                fields[i] = [a + f - g for a, f, g in zip(values, flux, [low] + flux[:-1])]
        for i, values in enumerate(fields):
            for pick, value in zip(picks, values):
                if plus_refs is not None:
                    value = value + sign * plus_refs[i][t, pick, :]
                to_refs[i][t, pick, :] = value
        return carry

    lax.fori_loop(0, tiles, sweep_tile, 0)


def sweep_y_into(to_refs, from_refs, cy_ref):
    tiles, nx, _ = cy_ref.shape
    lane = iota((Y_LINES, SEG), 1)

    def next_cells(values):
        moved = [pltpu.roll(value, SEG - 1, 1) for value in values]
        return [jnp.where(lane == SEG - 1, b, a) for a, b in zip(moved, moved[1:] + moved[:1])]

    def previous_cells(values):
        moved = [pltpu.roll(value, 1, 1) for value in values]
        return [jnp.where(lane == 0, a, b) for a, b in zip(moved[-1:] + moved[:-1], moved)]

    def sweep_lines(group, carry):
        lines = pl.ds(pl.multiple_of(group * Y_LINES, Y_LINES), Y_LINES)
        coeffs = [cy_ref[t, lines, :] for t in range(tiles)]
        fields = [[ref[t, lines, :] for t in range(tiles)] for ref in from_refs]
        for _ in range(M):
            for i, values in enumerate(fields):
                flux = [c * (b - a) for c, a, b in zip(coeffs, values, next_cells(values))]
                fields[i] = [
                    a + f - g for a, f, g in zip(values, flux, previous_cells(flux))]
        for to_ref, values in zip(to_refs, fields):
            for t, value in enumerate(values):
                to_ref[t, lines, :] = value
        return carry

    lax.fori_loop(0, nx // Y_LINES, sweep_lines, 0)


def normal_into(to_refs, from_refs, diagonal_refs, side_refs, base_refs=None):
    tiles, nx, _ = from_refs[0].shape
    picks = x_lines(nx)

    def tile(t, carry):
        for i, from_ref in enumerate(from_refs):
            values = [from_ref[t, pick, :] for pick in picks]
            sides = [side_refs[i][t, pick, :] for pick in picks]
            low = [e * a for e, a in zip(sides, values)]
            low = [pltpu.roll(low[-1], 1, 0)] + low[:-1]
            after = values[1:] + [pltpu.roll(values[0], 7, 0)]
            for line, pick in enumerate(picks):
                result = (diagonal_refs[i][t, pick, :] * values[line] + sides[line] * after[line]
                          + low[line])
                if base_refs is not None:
                    result = base_refs[i][t, pick, :] - result
                to_refs[i][t, pick, :] = result
        return carry

    lax.fori_loop(0, tiles, tile, 0)


def of_fields(ref, start=0):
    return [ref.at[start + f] for f in range(F)]


def start_kernel(c0_ref, cx_ref, swap_ref, c0_out, cx_out, cy_out, u_out, token_out, work):
    token_out[...] = jnp.zeros_like(token_out)
    nx = cx_ref.shape[0]
    spans, count = swap_ref.shape[0], cy_out.shape[0]
    me = lax.axis_index("px")
    for p in range(spans):
        for t in range(count):
            cy_out[t, p * LX:(p + 1) * LX, :] = swap_ref[p, t * LX:(t + 1) * LX, :]

    def beside(i):
        lines = slice(count * LX + i * nx, count * LX + (i + 1) * nx)
        before = swap_ref[jnp.maximum(me - 1, 0), lines, :]
        after = swap_ref[jnp.minimum(me + 1, spans - 1), lines, :]
        return ends_tile(jnp.where(me > 0, before, 0.0), jnp.where(me < spans - 1, after, 0.0))

    for t in range(count - 1):
        tile = slice(t * SEG, (t + 1) * SEG)
        cx_out[t] = cx_ref[:, tile]
        for f in range(F):
            c0_out[f, t] = c0_ref[f, :, tile]
    cx_out[count - 1] = beside(F)
    cx_out[:, nx - 1:, :] = jnp.zeros((count, 1, SEG), jnp.float32)
    for f in range(F):
        c0_out[f, count - 1] = beside(f)
    sweep_x_into(of_fields(work), of_fields(c0_out), cx_out)
    sweep_y_into(of_fields(u_out), of_fields(work), cy_out)


def join_kernel(spans, *rest):
    parts, out = rest[:spans], rest[spans]
    me = lax.axis_index("px")
    for k, part in enumerate(parts):
        rows = pl.ds(pl.multiple_of((me ^ k) * LX, LX), LX)
        for f in range(F):
            for t in range(out.shape[1]):
                out[f, t, rows, :] = part[f, t]


def solve_kernel(c0_ref, cx_ref, cy_ref, u_ref, obs_ref, far_ref, r_out, q_out, h_out, dots_out,
                 vec, coef, work):
    for p in range(obs_ref.shape[0]):
        rows = slice(p * LX, (p + 1) * LX)
        for channel in range(2 * F):
            coef[channel, :, rows, :] = obs_ref[p, channel]
        for f in range(F):
            coef[2 * F + f, :, rows, :] = obs_ref[p, 2 * F + f] + far_ref[f, :, rows, :]

    sides = (of_fields(coef), of_fields(coef, F))
    one, two, r, q, s, h = (of_fields(ref) for ref in (
        work.at[0], work.at[1], vec.at[0], vec.at[1], vec.at[2], h_out))
    normal_into(one, of_fields(u_ref), *sides, of_fields(coef, 2 * F))
    sweep_y_into(two, one, cy_ref)
    sweep_x_into(r, two, cx_ref, of_fields(c0_ref), -1.0)
    sweep_x_into(one, r, cx_ref)
    sweep_y_into(two, one, cy_ref)
    normal_into(one, two, *sides)
    sweep_y_into(two, one, cy_ref)
    sweep_x_into(q, two, cx_ref, r)
    sweep_x_into(one, q, cx_ref)
    sweep_y_into(s, one, cy_ref)
    normal_into(h, s, *sides)

    tiles, nx = vec.shape[2] - 1, vec.shape[3]
    for f in range(F):
        for t in range(tiles):
            r_out[f, :, t * SEG:(t + 1) * SEG] = vec[0, f, t]
            q_out[f, :, t * SEG:(t + 1) * SEG] = vec[1, f, t]

    def products(index, sums):
        f, t = index // tiles, index % tiles
        for low in range(0, nx, 8):
            lines = slice(low, low + 8)
            r, q, s = (vec[i, f, t, lines, :] for i in range(3))
            terms = (r * r, r * q, q * q, s * h_out[f, t, lines, :])
            sums = tuple(a + b for a, b in zip(sums, terms))
        return sums

    sums = lax.fori_loop(0, F * tiles, products, (jnp.zeros((8, SEG), jnp.float32),) * 4)
    dots = jnp.zeros((1, SEG), jnp.float32)
    for i, total in enumerate(sums):
        line = jnp.sum(total, axis=0, keepdims=True)
        for distance in (64, 32, 16):
            line = line + pltpu.roll(line, distance, 1)
        dots = jnp.where(iota((1, SEG), 1) // SPLIT == i, line, dots)
    dots_out[...] = jnp.broadcast_to(dots, dots_out.shape)


def last_kernel(h_ref, q_ref, cx_ref, cy_ref, qq_out, work):
    sweep_y_into(of_fields(work.at[0]), of_fields(h_ref), cy_ref)
    sweep_x_into(of_fields(work.at[1]), of_fields(work.at[0]), cx_ref)
    for f in range(F):
        for t in range(work.shape[2] - 1):
            tile = slice(t * SEG, (t + 1) * SEG)
            qq_out[f, :, tile] = q_ref[f, :, tile] + work[1, f, t]


def finish_kernel(dots_ref, c0_ref, r_ref, q_ref, qq_ref, control_out, residual_out):
    dots = jnp.sum(dots_ref[...], axis=0)
    lane = iota((1, SEG), 1)
    rr, rq, qq2, energy = (pltpu.roll(dots, (SEG - i * SPLIT) % SEG, 1) for i in range(4))

    def total(line):
        return jnp.sum(jnp.where(lane < SPLIT, line, 0.0), axis=1, keepdims=True)

    rr_sum = total(rr)
    alpha = rr_sum / total(rq)
    new_sum = total(rr - 2.0 * alpha * rq + alpha * alpha * qq2)
    more = 1.0 + new_sum / rr_sum
    curve = total(more * more * rq - 2.0 * more * alpha * qq2 + alpha * alpha * (qq2 + energy))
    second = new_sum / curve
    first_weight = alpha + second * more
    both = alpha * second
    for f in range(F):
        r, q = r_ref[f], q_ref[f]
        control_out[f] = c0_ref[f] + first_weight * r - both * q
        residual_out[f] = r - first_weight * q + both * qq_ref[f]


def call(kernel, out_shape, scratch=(), in_specs=None, out_specs=None, limit=VMEM_BYTES,
         weight=1):
    params = {"in_specs": in_specs, "out_specs": out_specs}
    return pl.pallas_call(
        kernel,
        out_shape=out_shape,
        scratch_shapes=list(scratch),
        compiler_params=pltpu.CompilerParams(vmem_limit_bytes=limit),
        cost_estimate=pl.CostEstimate(flops=weight, bytes_accessed=weight, transcendentals=0),
        **{name: value for name, value in params.items() if value is not None},
    )


def f32(*shape):
    return jax.ShapeDtypeStruct(shape, jnp.float32)


def vmem(*shape, kind=jnp.float32):
    return pltpu.VMEM(shape, kind)


def shards(
    control_start, coef_x, coef_y, innovation, obs_weight, interp, obs_owner, cell_key, stencil
):
    groups, spans = lax.axis_size("py"), lax.axis_size("px")
    half = groups // 2
    rows = innovation.shape[0]
    cap = 3 * rows // groups
    blk = SEG if cap % SEG == 0 else HALF
    meta_rows = -(-4 * (cap // blk) // 8) * 8
    block_rows = 2 * cap + meta_rows
    chunks = rows // SEG
    nx, width = control_start.shape[2], control_start.shape[3]
    tiles = width // SEG + 1
    c0, cx = control_start[:, 0], coef_x[0]
    hbm, local, scalars = (
        pl.BlockSpec(memory_space=s) for s in (pltpu.HBM, pltpu.VMEM, pltpu.SMEM))
    ints = vmem(chunks, SEG, kind=jnp.int32)
    dma = pltpu.SemaphoreType.DMA

    def to_half(block, k):
        return lax.ppermute(block, "py", [(i, i ^ k) for i in range(groups)])

    def across(parts):
        return [
            lax.ppermute(parts[k], ("px", "py"), [
                (i * groups + j, (i ^ k) * groups + (j ^ half))
                for i in range(spans) for j in range(groups)])
            for k in range(spans)]

    *w_blocks, slots = call(
        functools.partial(pack_weights_kernel, groups, cap, blk, block_rows),
        (f32(block_rows, SEG),) * half + (jax.ShapeDtypeStruct((chunks, SEG), jnp.int32),),
        [ints, ints, ints, vmem(chunks, SEG), vmem(rows, SEG), vmem(half * block_rows, SEG), ints,
         pltpu.SMEM((chunks, SEG), jnp.int32), dma((5,)), dma((half,)), dma],
        [hbm] * 5,
        (hbm,) * half + (local,),
        limit=PACK_BYTES,
    )(
        obs_owner.reshape(chunks, SEG), cell_key.reshape(chunks, SEG),
        stencil.reshape(chunks, SEG), interp.reshape(chunks, SEG), obs_weight,
    )
    v_blocks = list(call(
        functools.partial(pack_products_kernel, groups, cap),
        (f32(2 * cap, SEG),) * half,
        [vmem(rows, SEG), vmem(rows, SEG), vmem(groups * cap, SEG), dma((2,)), dma((half,))],
        [scalars] + [hbm] * 2,
        (hbm,) * half,
        limit=PACK_BYTES,
    )(slots, obs_weight, innovation))
    w_blocks[1:] = [to_half(w_blocks[k], k) for k in range(1, half)]
    w_blocks[1], *v_blocks[1:] = lax.optimization_barrier((w_blocks[1], *v_blocks[1:]))
    v_blocks[1:] = [to_half(v_blocks[k], k) for k in range(1, half)]

    swap = call(
        pack_swap_kernel,
        f32(spans, LX * tiles + (F + 1) * nx, SEG),
        [vmem(*coef_y.shape[1:]), vmem(F + 1, nx, SEG), vmem(F + 1, nx, SEG), dma((5,))],
        [local] + [hbm] * 3,
        limit=PACK_BYTES,
    )(slots, coef_y[0], c0, cx)
    swap = lax.all_to_all(swap, "px", split_axis=0, concat_axis=0, tiled=True)
    c0_ext, cx_ext, cy_ext, u_ext, token = call(
        start_kernel,
        (f32(F, tiles, nx, SEG), f32(tiles, nx, SEG), f32(tiles, nx, SEG), f32(F, tiles, nx, SEG),
         f32(8, SEG)),
        [vmem(F, tiles, nx, SEG)],
    )(c0, cx, swap)

    def sum_weights(side, token, weight):
        return call(
            functools.partial(weights_kernel, half, cap, blk, side),
            (f32(half, meta_rows, SEG),) + (f32(ROWS, SEG),) * 2,
            [vmem(ROWS, 3 * SEG)],
            weight=weight,
        )(*w_blocks, token)

    meta, *side_across = sum_weights(1, w_blocks[0], FIRST)
    side_across = [to_half(values, half) for values in side_across]
    meta, *side = sum_weights(0, token, 1)
    parts, *sums_across = call(
        functools.partial(products_kernel, half, cap, blk),
        (f32(spans, 3 * F, tiles, LX, SEG),) + (f32(F, tiles, LX, SEG),) * spans,
        [vmem(ROWS, 2 * SEG), vmem(ROWS, SEG), vmem(ROWS, SEG), vmem(2, ROWS, SEG)],
    )(meta, *side, *side_across, *v_blocks)
    far_sums = call(
        functools.partial(join_kernel, spans), f32(F, tiles, nx, SEG), weight=JOIN,
    )(*across(sums_across))
    parts = lax.all_to_all(parts, "px", split_axis=0, concat_axis=0, tiled=True)

    r, q, h, dots = call(
        solve_kernel,
        (f32(F, nx, width),) * 2 + (f32(F, tiles, nx, SEG), f32(groups * spans, 1, SEG)),
        [vmem(3, F, tiles, nx, SEG), vmem(3 * F, tiles, nx, SEG), vmem(2, F, tiles, nx, SEG)],
    )(c0_ext, cx_ext, cy_ext, u_ext, parts, far_sums)
    dots = lax.all_to_all(dots, ("px", "py"), split_axis=0, concat_axis=0, tiled=True)
    qq = call(last_kernel, f32(F, nx, width), [vmem(2, F, tiles, nx, SEG)])(
        h, q, cx_ext, cy_ext)
    control, residual = call(finish_kernel, (f32(F, nx, width),) * 2)(dots, c0, r, q, qq)
    return control[:, None], residual[:, None]


def solution(mesh):
    return jax.shard_map(
        shards,
        mesh=mesh,
        in_specs=(
            P(None, "py", None, "px"),
            P("py", None, "px"),
            P("py", "px", None),
            P(("px", "py"), None),
            P(("px", "py"), None),
            P(("px", "py")),
            P(("px", "py"), None),
            P(("px", "py")),
            P(("px", "py")),
        ),
        out_specs=(P(None, "py", None, "px"), P(None, "py", None, "px")),
        check_vma=False,
    )
```

```python
import functools

import jax
import jax.numpy as jnp
from jax import lax
from jax.experimental import pallas as pl
from jax.experimental.pallas import tpu as pltpu
from jax.sharding import PartitionSpec as P

F = 2
SEG = 128
M = 4
NB = 16
LX = 16
ROWS = F * NB * LX
HALF = SEG // 2
SPLIT = 16
REACH = M
VMEM_BYTES = 32 * 1024 * 1024
PACK_BYTES = 60 * 1024 * 1024
FIRST = 100_000_000
JOIN = 100_000_000


def iota(shape, axis):
    return lax.broadcasted_iota(jnp.int32, shape, axis)


def flag(condition, kind=jnp.bfloat16):
    return jnp.where(condition, 1.0, 0.0).astype(kind)


def mxu(left, right):
    return jnp.dot(left, right, preferred_element_type=jnp.float32)


def split_parts(values, count):
    parts = []
    for _ in range(count):
        part = values.astype(jnp.bfloat16)
        parts.append(part)
        values = values - part.astype(jnp.float32)
    return parts


def ends_tile(before, after):
    return jnp.where(iota(after.shape, after.ndim - 1) < HALF, after, before)


def start_copies(pairs, sems):
    copies = [pltpu.make_async_copy(*pair, sems.at[i]) for i, pair in enumerate(pairs)]
    for copy in copies:
        copy.start()
    return copies


def pack_weights_kernel(groups, cap, blk, block_rows, own_hbm, key_hbm, sten_hbm, itp_hbm, w_hbm,
                        *rest):
    half = groups // 2
    outs, rest = rest[:half], rest[half:]
    (slot_out, own_ref, key_ref, sten_ref, itp_ref, w_ref, buffer, slot_v, slot_s, sems, out_sems,
     sem) = rest
    loads = start_copies([(own_hbm, own_ref), (key_hbm, key_ref), (sten_hbm, sten_ref),
                          (itp_hbm, itp_ref), (w_hbm, w_ref)], sems)

    def clear(k, carry):
        start = pl.multiple_of(k * block_rows, 8)
        buffer[pl.ds(start, block_rows), :] = jnp.zeros((block_rows, SEG), jnp.float32)
        return carry

    lax.fori_loop(0, half, clear, 0)

    for load in loads[:4]:
        load.wait()
    chunks = own_ref.shape[0]
    nb = cap // blk
    own = own_ref[...]
    high = groups * chunks
    shift = chunks.bit_length() - 1
    masks = [flag(own == o, jnp.float32) for o in range(groups)]
    hits = jnp.concatenate(masks, axis=0).astype(jnp.bfloat16)
    square = (SEG, SEG)
    within = mxu(hits, flag(iota(square, 0) < iota(square, 1)))
    tallies = mxu(hits, jnp.ones(square, jnp.bfloat16)).astype(jnp.bfloat16)
    line, column = iota((high, high), 0), iota((high, high), 1)
    same = (line >> shift) == (column >> shift)
    ranks = within + mxu(flag(same & (column < line)), tallies)
    rank = sum(masks[o] * ranks[o * chunks:(o + 1) * chunks] for o in range(groups))
    rank = rank.astype(jnp.int32)
    relative = own ^ lax.axis_index("py")
    block, across = relative & (half - 1), relative >> (half.bit_length() - 1)
    slot_v[...] = block * block_rows + across * cap + rank
    slot_out[...] = (block * 2 + across) * cap + rank
    copy = pltpu.make_async_copy(slot_v, slot_s, sem)
    copy.start()

    log = blk.bit_length() - 1
    place = relative * nb + (rank >> log)
    lane = rank & (blk - 1)
    key, sten, itp = key_ref[...], sten_ref[...], itp_ref[...]
    tall = groups * nb
    meta = jnp.zeros((5 * tall, SEG), jnp.float32)
    for i in range(chunks):
        chosen = iota((tall, SEG), 0) == place[i:i + 1]
        parts = split_parts(itp[i:i + 1], 3)
        parts += [key[i:i + 1].astype(jnp.bfloat16), (sten[i:i + 1] + 1).astype(jnp.bfloat16)]
        left = [jnp.where(chosen, part.astype(jnp.float32), 0.0) for part in parts]
        right = flag(iota(square, 0) == lane[i:i + 1])
        meta = meta + lax.dot_general(
            jnp.concatenate(left, axis=0).astype(jnp.bfloat16), right,
            (((1,), (1,)), ((), ())), preferred_element_type=jnp.float32)
    shares = meta[:tall] + meta[tall:2 * tall] + meta[2 * tall:3 * tall]
    targets = meta[3 * tall:4 * tall] * LX + meta[4 * tall:]
    for v in range(groups):
        base = (v % half) * block_rows + 2 * cap + (v // half) * 2 * nb
        buffer[base:base + nb, :] = shares[v * nb:(v + 1) * nb]
        buffer[base + nb:base + 2 * nb, :] = targets[v * nb:(v + 1) * nb]

    copy.wait()
    loads[4].wait()

    def place_rows(g, carry):
        weights = w_ref[pl.ds(pl.multiple_of(g * 8, 8), 8), :]
        line, lane = g // 16, (g % 16) * 8
        for i in range(8):
            buffer[pl.ds(slot_s[line, lane + i], 1), :] = weights[i:i + 1]
        return carry

    lax.fori_loop(0, w_ref.shape[0] // 8, place_rows, 0)
    for store in start_copies([(buffer.at[pl.ds(k * block_rows, block_rows)], out)
                               for k, out in enumerate(outs)], out_sems):
        store.wait()


def pack_products_kernel(groups, cap, slot_ref, w_hbm, d_hbm, *rest):
    half = groups // 2
    outs, (w_ref, d_ref, buffer, sems, out_sems) = rest[:half], rest[half:]
    loads = start_copies([(w_hbm, w_ref), (d_hbm, d_ref)], sems)

    def clear(o, carry):
        start = pl.multiple_of(o * cap, 8)
        buffer[pl.ds(start, cap), :] = jnp.zeros((cap, SEG), jnp.float32)
        return carry

    lax.fori_loop(0, groups, clear, 0)

    for load in loads:
        load.wait()

    def place_rows(g, carry):
        start = pl.multiple_of(g * 8, 8)
        products = w_ref[pl.ds(start, 8), :] * d_ref[pl.ds(start, 8), :]
        line, lane = g // 16, (g % 16) * 8
        for i in range(8):
            buffer[pl.ds(slot_ref[line, lane + i], 1), :] = products[i:i + 1]
        return carry

    lax.fori_loop(0, w_ref.shape[0] // 8, place_rows, 0)
    for store in start_copies([(buffer.at[pl.ds(k * 2 * cap, 2 * cap)], out)
                               for k, out in enumerate(outs)], out_sems):
        store.wait()


def pack_swap_kernel(_, cy_hbm, c0_hbm, cx_hbm, swap_out, cy_ref, first, last, sems):
    width = c0_hbm.shape[2]
    for load in start_copies([
        (cy_hbm, cy_ref),
        (c0_hbm.at[:, :, pl.ds(0, SEG)], first.at[pl.ds(0, F)]),
        (cx_hbm.at[:, pl.ds(0, SEG)], first.at[F]),
        (c0_hbm.at[:, :, pl.ds(width - SEG, SEG)], last.at[pl.ds(0, F)]),
        (cx_hbm.at[:, pl.ds(width - SEG, SEG)], last.at[F]),
    ], sems):
        load.wait()
    columns = cy_ref.shape[1]
    cy = cy_ref[...]
    cy = jnp.where(iota(cy.shape, 1) == columns - 1, 0.0, cy)
    empty = jnp.zeros((LX, SEG), jnp.float32)
    me = lax.axis_index("px")
    nx = first.shape[1]
    for q in range(columns // width):
        low, top = q * width, (q + 1) * width
        tiles = [cy[:, t:t + SEG] for t in range(low, top, SEG)]
        before = cy[:, low - SEG:low] if low > 0 else empty
        after = cy[:, top:top + SEG] if top < columns else empty
        tiles.append(ends_tile(before, after))
        for t, tile in enumerate(tiles):
            swap_out[q, t * LX:(t + 1) * LX, :] = tile
        base = len(tiles) * LX
        for i in range(F + 1):
            swap_out[q, base + i * nx:base + (i + 1) * nx, :] = jnp.where(
                q < me, first[i], last[i])


def sum_rows(cap, blk, metas, acc_ref, terms):
    nb = cap // blk
    numbers = 1.0 + iota((ROWS, cap), 0).astype(jnp.float32)
    for source, meta in enumerate(metas):
        upper = jnp.concatenate(
            [jnp.broadcast_to(meta[i:i + 1], (SEG, SEG)).T[:blk] for i in range(nb)], axis=0)
        target = jnp.concatenate([meta[nb + i:nb + i + 1, :blk] for i in range(nb)], axis=1)
        hit = flag(numbers == target)
        values = jnp.concatenate(terms(source, upper), axis=1)
        part = mxu(jnp.concatenate([hit, hit], axis=1),
                   jnp.concatenate(split_parts(values, 2), axis=0))
        if source:
            acc_ref[...] += part
        else:
            acc_ref[...] = part


def cut_part(rows_ref, to, f, q, spans):
    per = to.shape[0] - 1

    def tile(b):
        start = pl.multiple_of((f * NB + b) * LX, LX)
        return rows_ref[pl.ds(start, LX), :]

    for j in range(per):
        to[j] = tile(q * per + j)
    before = tile(jnp.maximum(q * per - 1, 0))
    after = tile(jnp.minimum(q * per + per, NB - 1))
    to[per] = ends_tile(jnp.where(q > 0, before, 0.0), jnp.where(q < spans - 1, after, 0.0))


def weights_kernel(half, cap, blk, across, *rest):
    w_refs, (_, meta_out, diagonal_out, side_out, acc_ref) = rest[:half], rest[half:]
    nb = cap // blk
    for k, w_ref in enumerate(w_refs):
        meta_out[k] = w_ref[2 * cap:, :]
    rows = slice(across * cap, (across + 1) * cap)

    def terms(source, upper):
        lower = 1.0 - upper
        weights = w_refs[source][rows, :]
        lower_w, upper_w = lower * weights, upper * weights
        return [lower * lower_w, upper * lower_w, upper * upper_w]

    low = 2 * cap + across * 2 * nb
    sum_rows(cap, blk, [w_ref[low:low + 2 * nb, :] for w_ref in w_refs], acc_ref, terms)
    diagonal_out[...] = acc_ref[:, :SEG] + pltpu.roll(acc_ref[:, 2 * SEG:], 1, 0)
    side_out[...] = acc_ref[:, SEG:2 * SEG]


def sum_products(half, cap, blk, across, meta_ref, v_refs, acc_ref, sums_ref):
    nb = cap // blk
    rows = slice(across * cap, (across + 1) * cap)

    def terms(source, upper):
        products = v_refs[source][rows, :]
        return [(1.0 - upper) * products, upper * products]

    low = across * 2 * nb
    sum_rows(cap, blk, [meta_ref[k, low:low + 2 * nb, :] for k in range(half)], acc_ref, terms)
    sums_ref[...] = acc_ref[:, :SEG] + pltpu.roll(acc_ref[:, SEG:], 1, 0)


def products_kernel(half, cap, blk, meta_ref, d_ref, e_ref, far_d_ref, far_e_ref, *rest):
    v_refs, (out, *far_outs, acc_ref, sums_ref, far_ref, side) = rest[:half], rest[half:]
    spans = out.shape[0]
    sum_products(half, cap, blk, 1, meta_ref, v_refs, acc_ref, far_ref)
    me = lax.axis_index("px")
    for k, far_out in enumerate(far_outs):
        for f in range(F):
            cut_part(far_ref, far_out.at[f], f, me ^ k, spans)
    sum_products(half, cap, blk, 0, meta_ref, v_refs, acc_ref, sums_ref)
    side[0] = d_ref[...] + far_d_ref[...]
    side[1] = e_ref[...] + far_e_ref[...]
    for q in range(spans):
        for channel, rows_ref in enumerate((side.at[0], side.at[1], sums_ref)):
            for f in range(F):
                cut_part(rows_ref, out.at[q, channel * F + f], f, q, spans)


def x_lines(nx):
    return [pl.ds(i, 8, stride=nx // 8) for i in range(nx // 8)]


def shift_x(lines, distance):
    size = len(lines)
    moved = []
    for i in range(size):
        j = i + distance
        line = lines[j % size]
        moved.append(line if 0 <= j < size else pltpu.roll(line, 7 if j >= size else 1, 0))
    return moved


def shift_y(tiles, distance):
    if distance == 0:
        return tiles
    lane = iota(tiles[0].shape, 1)
    moved = [pltpu.roll(tile, -distance % SEG, 1) for tile in tiles]
    if distance > 0:
        return [jnp.where(lane >= SEG - distance, b, a) for a, b in zip(moved, moved[1:] + moved[:1])]
    return [jnp.where(lane < -distance, a, b) for a, b in zip(moved[-1:] + moved[:-1], moved)]


def sweep_diagonals(coeffs, shift):
    def each(function, *lists):
        return [function(*items) for items in zip(*lists)]

    back = functools.partial(shift, coeffs)
    main = each(lambda c, d: 1.0 - c - d, coeffs, back(-1))
    q0 = each(lambda a, c, d: a * a + c * c + d * d, main, coeffs, back(-1))
    q1 = each(lambda a, b, c: c * (a + b), main, shift(main, 1), coeffs)
    q2 = each(lambda c, d: c * d, coeffs, back(1))
    up0, up1, up2 = shift(q0, 1), shift(q1, 1), shift(q2, 1)
    low1, low2 = shift(q1, -1), shift(q2, -1)
    r0 = each(lambda a, b, c, d, e: a * a + b * b + c * c + d * d + e * e,
              q0, q1, low1, q2, shift(q2, -2))
    r1 = each(lambda a, b, c, d, e, f, g: a * b + c * (d + e) + f * g,
              low1, low2, q1, q0, up0, q2, up1)
    r2 = each(lambda a, b, c, d, e: a * (b + c) + d * e, q2, q0, shift(q0, 2), q1, up1)
    r3 = each(lambda a, b, c, d: a * b + c * d, q1, up2, q2, shift(q1, 2))
    r4 = each(lambda a, b: a * b, q2, shift(q2, 2))
    upper = [r0, r1, r2, r3, r4]
    return [shift(upper[d], -d) for d in range(REACH, 0, -1)] + upper


def make_x_diagonals(out, cx_ref):
    tiles, nx, _ = cx_ref.shape
    picks = x_lines(nx)
    for t in range(tiles):
        coeffs = [cx_ref[t, pick, :] for pick in picks]
        for d, lines in enumerate(sweep_diagonals(coeffs, shift_x)):
            for pick, line in zip(picks, lines):
                out[d, t, pick, :] = line


def make_y_diagonals(out, cy_ref):
    tiles, nx, _ = cy_ref.shape
    for low in range(0, nx, 8):
        rows = slice(low, low + 8)
        coeffs = [cy_ref[t, rows, :] for t in range(tiles)]
        for d, parts in enumerate(sweep_diagonals(coeffs, shift_y)):
            for t, part in enumerate(parts):
                out[d, t, rows, :] = part


def banded(diagonals, values, shift):
    total = None
    for d, diagonal in enumerate(diagonals):
        terms = [c * v for c, v in zip(diagonal, shift(values, d - REACH))]
        total = terms if total is None else [a + b for a, b in zip(total, terms)]
    return total


def sweep_x_into(to_refs, from_refs, x_ref, plus_refs=None, sign=1.0):
    count, tiles, nx, _ = x_ref.shape
    picks = x_lines(nx)
    for t in range(tiles):
        diagonals = [[x_ref[d, t, pick, :] for pick in picks] for d in range(count)]
        for i, from_ref in enumerate(from_refs):
            values = [from_ref[t, pick, :] for pick in picks]
            for pick, value in zip(picks, banded(diagonals, values, shift_x)):
                if plus_refs is not None:
                    value = value + sign * plus_refs[i][t, pick, :]
                to_refs[i][t, pick, :] = value


def sweep_y_into(to_refs, from_refs, y_ref):
    count, tiles, nx, _ = y_ref.shape
    for low in range(0, nx, 8):
        rows = slice(low, low + 8)
        diagonals = [[y_ref[d, t, rows, :] for t in range(tiles)] for d in range(count)]
        for to_ref, from_ref in zip(to_refs, from_refs):
            values = [from_ref[t, rows, :] for t in range(tiles)]
            for t, value in enumerate(banded(diagonals, values, shift_y)):
                to_ref[t, rows, :] = value


def normal_into(to_refs, from_refs, diagonal_refs, side_refs, base_refs=None):
    tiles, nx, _ = from_refs[0].shape
    picks = x_lines(nx)
    for t in range(tiles):
        for i, from_ref in enumerate(from_refs):
            values = [from_ref[t, pick, :] for pick in picks]
            sides = [side_refs[i][t, pick, :] for pick in picks]
            low = [e * a for e, a in zip(sides, values)]
            low = [pltpu.roll(low[-1], 1, 0)] + low[:-1]
            after = values[1:] + [pltpu.roll(values[0], 7, 0)]
            for line, pick in enumerate(picks):
                result = (diagonal_refs[i][t, pick, :] * values[line] + sides[line] * after[line]
                          + low[line])
                if base_refs is not None:
                    result = base_refs[i][t, pick, :] - result
                to_refs[i][t, pick, :] = result


def of_fields(ref, start=0):
    return [ref.at[start + f] for f in range(F)]


def start_kernel(c0_ref, cx_ref, swap_ref, c0_out, x_out, y_out, u_out, token_out, cx_out, cy_out,
                 work):
    token_out[...] = jnp.zeros_like(token_out)
    nx = cx_ref.shape[0]
    spans, count = swap_ref.shape[0], cy_out.shape[0]
    me = lax.axis_index("px")
    for p in range(spans):
        for t in range(count):
            cy_out[t, p * LX:(p + 1) * LX, :] = swap_ref[p, t * LX:(t + 1) * LX, :]

    def beside(i):
        lines = slice(count * LX + i * nx, count * LX + (i + 1) * nx)
        before = swap_ref[jnp.maximum(me - 1, 0), lines, :]
        after = swap_ref[jnp.minimum(me + 1, spans - 1), lines, :]
        return ends_tile(jnp.where(me > 0, before, 0.0), jnp.where(me < spans - 1, after, 0.0))

    for t in range(count - 1):
        tile = slice(t * SEG, (t + 1) * SEG)
        cx_out[t] = cx_ref[:, tile]
        for f in range(F):
            c0_out[f, t] = c0_ref[f, :, tile]
    cx_out[count - 1] = beside(F)
    cx_out[:, nx - 1:, :] = jnp.zeros((count, 1, SEG), jnp.float32)
    for f in range(F):
        c0_out[f, count - 1] = beside(f)
    make_x_diagonals(x_out, cx_out)
    make_y_diagonals(y_out, cy_out)
    sweep_x_into(of_fields(work), of_fields(c0_out), x_out)
    sweep_y_into(of_fields(u_out), of_fields(work), y_out)


def join_kernel(spans, *rest):
    parts, out = rest[:spans], rest[spans]
    me = lax.axis_index("px")
    for k, part in enumerate(parts):
        rows = pl.ds(pl.multiple_of((me ^ k) * LX, LX), LX)
        for f in range(F):
            for t in range(out.shape[1]):
                out[f, t, rows, :] = part[f, t]


def solve_kernel(c0_ref, x_ref, y_ref, u_ref, obs_ref, far_ref, r_out, q_out, h_out, dots_out,
                 vec, coef, work):
    for p in range(obs_ref.shape[0]):
        rows = slice(p * LX, (p + 1) * LX)
        for channel in range(2 * F):
            coef[channel, :, rows, :] = obs_ref[p, channel]
        for f in range(F):
            coef[2 * F + f, :, rows, :] = obs_ref[p, 2 * F + f] + far_ref[f, :, rows, :]

    sides = (of_fields(coef), of_fields(coef, F))
    one, two, r, q, s, h = (of_fields(ref) for ref in (
        work.at[0], work.at[1], vec.at[0], vec.at[1], vec.at[2], h_out))
    normal_into(one, of_fields(u_ref), *sides, of_fields(coef, 2 * F))
    sweep_y_into(two, one, y_ref)
    sweep_x_into(r, two, x_ref, of_fields(c0_ref), -1.0)
    sweep_x_into(one, r, x_ref)
    sweep_y_into(two, one, y_ref)
    normal_into(one, two, *sides)
    sweep_y_into(two, one, y_ref)
    sweep_x_into(q, two, x_ref, r)
    sweep_x_into(one, q, x_ref)
    sweep_y_into(s, one, y_ref)
    normal_into(h, s, *sides)

    tiles, nx = vec.shape[2] - 1, vec.shape[3]
    sums = [jnp.zeros((8, SEG), jnp.float32) for _ in range(4)]
    for f in range(F):
        for t in range(tiles):
            r_out[f, :, t * SEG:(t + 1) * SEG] = vec[0, f, t]
            q_out[f, :, t * SEG:(t + 1) * SEG] = vec[1, f, t]
            for low in range(0, nx, 8):
                lines = slice(low, low + 8)
                r, q, s = (vec[i, f, t, lines, :] for i in range(3))
                for i, product in enumerate((r * r, r * q, q * q, s * h_out[f, t, lines, :])):
                    sums[i] = sums[i] + product
    dots = jnp.zeros((1, SEG), jnp.float32)
    for i, total in enumerate(sums):
        line = jnp.sum(total, axis=0, keepdims=True)
        for distance in (64, 32, 16):
            line = line + pltpu.roll(line, distance, 1)
        dots = jnp.where(iota((1, SEG), 1) // SPLIT == i, line, dots)
    dots_out[...] = jnp.broadcast_to(dots, dots_out.shape)


def last_kernel(h_ref, q_ref, x_ref, y_ref, qq_out, work):
    sweep_y_into(of_fields(work.at[0]), of_fields(h_ref), y_ref)
    sweep_x_into(of_fields(work.at[1]), of_fields(work.at[0]), x_ref)
    for f in range(F):
        for t in range(work.shape[2] - 1):
            tile = slice(t * SEG, (t + 1) * SEG)
            qq_out[f, :, tile] = q_ref[f, :, tile] + work[1, f, t]


def finish_kernel(dots_ref, c0_ref, r_ref, q_ref, qq_ref, control_out, residual_out):
    dots = jnp.sum(dots_ref[...], axis=0)
    lane = iota((1, SEG), 1)
    rr, rq, qq2, energy = (pltpu.roll(dots, (SEG - i * SPLIT) % SEG, 1) for i in range(4))

    def total(line):
        return jnp.sum(jnp.where(lane < SPLIT, line, 0.0), axis=1, keepdims=True)

    rr_sum = total(rr)
    alpha = rr_sum / total(rq)
    new_sum = total(rr - 2.0 * alpha * rq + alpha * alpha * qq2)
    more = 1.0 + new_sum / rr_sum
    curve = total(more * more * rq - 2.0 * more * alpha * qq2 + alpha * alpha * (qq2 + energy))
    second = new_sum / curve
    first_weight = alpha + second * more
    both = alpha * second
    for f in range(F):
        r, q = r_ref[f], q_ref[f]
        control_out[f] = c0_ref[f] + first_weight * r - both * q
        residual_out[f] = r - first_weight * q + both * qq_ref[f]


def call(kernel, out_shape, scratch=(), in_specs=None, out_specs=None, limit=VMEM_BYTES,
         weight=1):
    params = {"in_specs": in_specs, "out_specs": out_specs}
    return pl.pallas_call(
        kernel,
        out_shape=out_shape,
        scratch_shapes=list(scratch),
        compiler_params=pltpu.CompilerParams(vmem_limit_bytes=limit),
        cost_estimate=pl.CostEstimate(flops=weight, bytes_accessed=weight, transcendentals=0),
        **{name: value for name, value in params.items() if value is not None},
    )


def f32(*shape):
    return jax.ShapeDtypeStruct(shape, jnp.float32)


def vmem(*shape, kind=jnp.float32):
    return pltpu.VMEM(shape, kind)


def shards(
    control_start, coef_x, coef_y, innovation, obs_weight, interp, obs_owner, cell_key, stencil
):
    groups, spans = lax.axis_size("py"), lax.axis_size("px")
    half = groups // 2
    rows = innovation.shape[0]
    cap = 3 * rows // groups
    blk = SEG if cap % SEG == 0 else HALF
    meta_rows = -(-4 * (cap // blk) // 8) * 8
    block_rows = 2 * cap + meta_rows
    chunks = rows // SEG
    nx, width = control_start.shape[2], control_start.shape[3]
    tiles = width // SEG + 1
    c0, cx = control_start[:, 0], coef_x[0]
    hbm, local, scalars = (
        pl.BlockSpec(memory_space=s) for s in (pltpu.HBM, pltpu.VMEM, pltpu.SMEM))
    ints = vmem(chunks, SEG, kind=jnp.int32)
    dma = pltpu.SemaphoreType.DMA

    def to_half(block, k):
        return lax.ppermute(block, "py", [(i, i ^ k) for i in range(groups)])

    def across(parts):
        return [
            lax.ppermute(parts[k], ("px", "py"), [
                (i * groups + j, (i ^ k) * groups + (j ^ half))
                for i in range(spans) for j in range(groups)])
            for k in range(spans)]

    *w_blocks, slots = call(
        functools.partial(pack_weights_kernel, groups, cap, blk, block_rows),
        (f32(block_rows, SEG),) * half + (jax.ShapeDtypeStruct((chunks, SEG), jnp.int32),),
        [ints, ints, ints, vmem(chunks, SEG), vmem(rows, SEG), vmem(half * block_rows, SEG), ints,
         pltpu.SMEM((chunks, SEG), jnp.int32), dma((5,)), dma((half,)), dma],
        [hbm] * 5,
        (hbm,) * half + (local,),
        limit=PACK_BYTES,
    )(
        obs_owner.reshape(chunks, SEG), cell_key.reshape(chunks, SEG),
        stencil.reshape(chunks, SEG), interp.reshape(chunks, SEG), obs_weight,
    )
    v_blocks = list(call(
        functools.partial(pack_products_kernel, groups, cap),
        (f32(2 * cap, SEG),) * half,
        [vmem(rows, SEG), vmem(rows, SEG), vmem(groups * cap, SEG), dma((2,)), dma((half,))],
        [scalars] + [hbm] * 2,
        (hbm,) * half,
        limit=PACK_BYTES,
    )(slots, obs_weight, innovation))
    w_blocks[1:] = [to_half(w_blocks[k], k) for k in range(1, half)]
    w_blocks[1], *v_blocks[1:] = lax.optimization_barrier((w_blocks[1], *v_blocks[1:]))
    v_blocks[1:] = [to_half(v_blocks[k], k) for k in range(1, half)]

    swap = call(
        pack_swap_kernel,
        f32(spans, LX * tiles + (F + 1) * nx, SEG),
        [vmem(*coef_y.shape[1:]), vmem(F + 1, nx, SEG), vmem(F + 1, nx, SEG), dma((5,))],
        [local] + [hbm] * 3,
        limit=PACK_BYTES,
    )(slots, coef_y[0], c0, cx)
    swap = lax.all_to_all(swap, "px", split_axis=0, concat_axis=0, tiled=True)
    c0_ext, x_sweep, y_sweep, u_ext, token = call(
        start_kernel,
        (f32(F, tiles, nx, SEG), f32(2 * REACH + 1, tiles, nx, SEG),
         f32(2 * REACH + 1, tiles, nx, SEG), f32(F, tiles, nx, SEG), f32(8, SEG)),
        [vmem(tiles, nx, SEG), vmem(tiles, nx, SEG), vmem(F, tiles, nx, SEG)],
    )(c0, cx, swap)

    def sum_weights(side, token, weight):
        return call(
            functools.partial(weights_kernel, half, cap, blk, side),
            (f32(half, meta_rows, SEG),) + (f32(ROWS, SEG),) * 2,
            [vmem(ROWS, 3 * SEG)],
            weight=weight,
        )(*w_blocks, token)

    meta, *side_across = sum_weights(1, w_blocks[0], FIRST)
    side_across = [to_half(values, half) for values in side_across]
    meta, *side = sum_weights(0, token, 1)
    parts, *sums_across = call(
        functools.partial(products_kernel, half, cap, blk),
        (f32(spans, 3 * F, tiles, LX, SEG),) + (f32(F, tiles, LX, SEG),) * spans,
        [vmem(ROWS, 2 * SEG), vmem(ROWS, SEG), vmem(ROWS, SEG), vmem(2, ROWS, SEG)],
    )(meta, *side, *side_across, *v_blocks)
    far_sums = call(
        functools.partial(join_kernel, spans), f32(F, tiles, nx, SEG), weight=JOIN,
    )(*across(sums_across))
    parts = lax.all_to_all(parts, "px", split_axis=0, concat_axis=0, tiled=True)

    r, q, h, dots = call(
        solve_kernel,
        (f32(F, nx, width),) * 2 + (f32(F, tiles, nx, SEG), f32(groups * spans, 1, SEG)),
        [vmem(3, F, tiles, nx, SEG), vmem(3 * F, tiles, nx, SEG), vmem(2, F, tiles, nx, SEG)],
    )(c0_ext, x_sweep, y_sweep, u_ext, parts, far_sums)
    dots = lax.all_to_all(dots, ("px", "py"), split_axis=0, concat_axis=0, tiled=True)
    qq = call(last_kernel, f32(F, nx, width), [vmem(2, F, tiles, nx, SEG)])(
        h, q, x_sweep, y_sweep)
    control, residual = call(finish_kernel, (f32(F, nx, width),) * 2)(dots, c0, r, q, qq)
    return control[:, None], residual[:, None]


def solution(mesh):
    return jax.shard_map(
        shards,
        mesh=mesh,
        in_specs=(
            P(None, "py", None, "px"),
            P("py", None, "px"),
            P("py", "px", None),
            P(("px", "py"), None),
            P(("px", "py"), None),
            P(("px", "py")),
            P(("px", "py"), None),
            P(("px", "py")),
            P(("px", "py")),
        ),
        out_specs=(P(None, "py", None, "px"), P(None, "py", None, "px")),
        check_vma=False,
    )
```

```python
import functools

import jax
import jax.numpy as jnp
from jax import lax
from jax.experimental import pallas as pl
from jax.experimental.pallas import tpu as pltpu
from jax.sharding import PartitionSpec as P

F = 2
SEG = 128
M = 4
NB = 16
LX = 16
ROWS = F * NB * LX
HALF = SEG // 2
SPLIT = 16
REACH = M
VMEM_BYTES = 16 * 1024 * 1024
PACK_BYTES = 60 * 1024 * 1024
FIRST = 100_000_000
JOIN = 100_000_000


def iota(shape, axis):
    return lax.broadcasted_iota(jnp.int32, shape, axis)


def flag(condition, kind=jnp.bfloat16):
    return jnp.where(condition, 1.0, 0.0).astype(kind)


def mxu(left, right):
    return jnp.dot(left, right, preferred_element_type=jnp.float32)


def split_parts(values, count):
    parts = []
    for _ in range(count):
        part = values.astype(jnp.bfloat16)
        parts.append(part)
        values = values - part.astype(jnp.float32)
    return parts


def ends_tile(before, after):
    return jnp.where(iota(after.shape, after.ndim - 1) < HALF, after, before)


def start_copies(pairs, sems):
    copies = [pltpu.make_async_copy(*pair, sems.at[i]) for i, pair in enumerate(pairs)]
    for copy in copies:
        copy.start()
    return copies


def pack_weights_kernel(groups, cap, blk, block_rows, own_hbm, key_hbm, sten_hbm, itp_hbm, w_hbm,
                        *rest):
    half = groups // 2
    outs, rest = rest[:half], rest[half:]
    (slot_out, own_ref, key_ref, sten_ref, itp_ref, w_ref, buffer, slot_v, slot_s, sems, out_sems,
     sem) = rest
    loads = start_copies([(own_hbm, own_ref), (key_hbm, key_ref), (sten_hbm, sten_ref),
                          (itp_hbm, itp_ref), (w_hbm, w_ref)], sems)

    def clear(k, carry):
        start = pl.multiple_of(k * block_rows, 8)
        buffer[pl.ds(start, block_rows), :] = jnp.zeros((block_rows, SEG), jnp.float32)
        return carry

    lax.fori_loop(0, half, clear, 0)

    for load in loads[:4]:
        load.wait()
    chunks = own_ref.shape[0]
    nb = cap // blk
    own = own_ref[...]
    high = groups * chunks
    shift = chunks.bit_length() - 1
    masks = [flag(own == o, jnp.float32) for o in range(groups)]
    hits = jnp.concatenate(masks, axis=0).astype(jnp.bfloat16)
    square = (SEG, SEG)
    within = mxu(hits, flag(iota(square, 0) < iota(square, 1)))
    tallies = mxu(hits, jnp.ones(square, jnp.bfloat16)).astype(jnp.bfloat16)
    line, column = iota((high, high), 0), iota((high, high), 1)
    same = (line >> shift) == (column >> shift)
    ranks = within + mxu(flag(same & (column < line)), tallies)
    rank = sum(masks[o] * ranks[o * chunks:(o + 1) * chunks] for o in range(groups))
    rank = rank.astype(jnp.int32)
    relative = own ^ lax.axis_index("py")
    block, across = relative & (half - 1), relative >> (half.bit_length() - 1)
    slot_v[...] = block * block_rows + across * cap + rank
    slot_out[...] = (block * 2 + across) * cap + rank
    copy = pltpu.make_async_copy(slot_v, slot_s, sem)
    copy.start()

    log = blk.bit_length() - 1
    place = relative * nb + (rank >> log)
    lane = rank & (blk - 1)
    key, sten, itp = key_ref[...], sten_ref[...], itp_ref[...]
    tall = groups * nb
    meta = jnp.zeros((5 * tall, SEG), jnp.float32)
    for i in range(chunks):
        chosen = iota((tall, SEG), 0) == place[i:i + 1]
        parts = split_parts(itp[i:i + 1], 3)
        parts += [key[i:i + 1].astype(jnp.bfloat16), (sten[i:i + 1] + 1).astype(jnp.bfloat16)]
        left = [jnp.where(chosen, part.astype(jnp.float32), 0.0) for part in parts]
        right = flag(iota(square, 0) == lane[i:i + 1])
        meta = meta + lax.dot_general(
            jnp.concatenate(left, axis=0).astype(jnp.bfloat16), right,
            (((1,), (1,)), ((), ())), preferred_element_type=jnp.float32)
    shares = meta[:tall] + meta[tall:2 * tall] + meta[2 * tall:3 * tall]
    targets = meta[3 * tall:4 * tall] * LX + meta[4 * tall:]
    for v in range(groups):
        base = (v % half) * block_rows + 2 * cap + (v // half) * 2 * nb
        buffer[base:base + nb, :] = shares[v * nb:(v + 1) * nb]
        buffer[base + nb:base + 2 * nb, :] = targets[v * nb:(v + 1) * nb]

    copy.wait()
    loads[4].wait()

    def place_rows(g, carry):
        weights = w_ref[pl.ds(pl.multiple_of(g * 8, 8), 8), :]
        line, lane = g // 16, (g % 16) * 8
        for i in range(8):
            buffer[pl.ds(slot_s[line, lane + i], 1), :] = weights[i:i + 1]
        return carry

    lax.fori_loop(0, w_ref.shape[0] // 8, place_rows, 0)
    for store in start_copies([(buffer.at[pl.ds(k * block_rows, block_rows)], out)
                               for k, out in enumerate(outs)], out_sems):
        store.wait()


def pack_products_kernel(groups, cap, slot_ref, w_hbm, d_hbm, *rest):
    half = groups // 2
    outs, (w_ref, d_ref, buffer, sems, out_sems) = rest[:half], rest[half:]
    loads = start_copies([(w_hbm, w_ref), (d_hbm, d_ref)], sems)

    def clear(o, carry):
        start = pl.multiple_of(o * cap, 8)
        buffer[pl.ds(start, cap), :] = jnp.zeros((cap, SEG), jnp.float32)
        return carry

    lax.fori_loop(0, groups, clear, 0)

    for load in loads:
        load.wait()

    def place_rows(g, carry):
        start = pl.multiple_of(g * 8, 8)
        products = w_ref[pl.ds(start, 8), :] * d_ref[pl.ds(start, 8), :]
        line, lane = g // 16, (g % 16) * 8
        for i in range(8):
            buffer[pl.ds(slot_ref[line, lane + i], 1), :] = products[i:i + 1]
        return carry

    lax.fori_loop(0, w_ref.shape[0] // 8, place_rows, 0)
    for store in start_copies([(buffer.at[pl.ds(k * 2 * cap, 2 * cap)], out)
                               for k, out in enumerate(outs)], out_sems):
        store.wait()


def pack_swap_kernel(_, cy_hbm, c0_hbm, cx_hbm, swap_out, cy_ref, first, last, sems):
    width = c0_hbm.shape[2]
    for load in start_copies([
        (cy_hbm, cy_ref),
        (c0_hbm.at[:, :, pl.ds(0, SEG)], first.at[pl.ds(0, F)]),
        (cx_hbm.at[:, pl.ds(0, SEG)], first.at[F]),
        (c0_hbm.at[:, :, pl.ds(width - SEG, SEG)], last.at[pl.ds(0, F)]),
        (cx_hbm.at[:, pl.ds(width - SEG, SEG)], last.at[F]),
    ], sems):
        load.wait()
    columns = cy_ref.shape[1]
    cy = cy_ref[...]
    cy = jnp.where(iota(cy.shape, 1) == columns - 1, 0.0, cy)
    empty = jnp.zeros((LX, SEG), jnp.float32)
    me = lax.axis_index("px")
    nx = first.shape[1]
    for q in range(columns // width):
        low, top = q * width, (q + 1) * width
        tiles = [cy[:, t:t + SEG] for t in range(low, top, SEG)]
        before = cy[:, low - SEG:low] if low > 0 else empty
        after = cy[:, top:top + SEG] if top < columns else empty
        tiles.append(ends_tile(before, after))
        for t, tile in enumerate(tiles):
            swap_out[q, t * LX:(t + 1) * LX, :] = tile
        base = len(tiles) * LX
        for i in range(F + 1):
            swap_out[q, base + i * nx:base + (i + 1) * nx, :] = jnp.where(
                q < me, first[i], last[i])


def sum_rows(cap, blk, metas, acc_ref, terms):
    nb = cap // blk
    numbers = 1.0 + iota((ROWS, cap), 0).astype(jnp.float32)
    for source, meta in enumerate(metas):
        upper = jnp.concatenate(
            [jnp.broadcast_to(meta[i:i + 1], (SEG, SEG)).T[:blk] for i in range(nb)], axis=0)
        target = jnp.concatenate([meta[nb + i:nb + i + 1, :blk] for i in range(nb)], axis=1)
        hit = flag(numbers == target)
        values = jnp.concatenate(terms(source, upper), axis=1)
        part = mxu(jnp.concatenate([hit, hit], axis=1),
                   jnp.concatenate(split_parts(values, 2), axis=0))
        if source:
            acc_ref[...] += part
        else:
            acc_ref[...] = part


def cut_part(rows_ref, to, f, q, spans):
    per = to.shape[0] - 1

    def tile(b):
        start = pl.multiple_of((f * NB + b) * LX, LX)
        return rows_ref[pl.ds(start, LX), :]

    for j in range(per):
        to[j] = tile(q * per + j)
    before = tile(jnp.maximum(q * per - 1, 0))
    after = tile(jnp.minimum(q * per + per, NB - 1))
    to[per] = ends_tile(jnp.where(q > 0, before, 0.0), jnp.where(q < spans - 1, after, 0.0))


def weights_kernel(half, cap, blk, across, *rest):
    w_refs, (_, meta_out, diagonal_out, side_out, acc_ref) = rest[:half], rest[half:]
    nb = cap // blk
    for k, w_ref in enumerate(w_refs):
        meta_out[k] = w_ref[2 * cap:, :]
    rows = slice(across * cap, (across + 1) * cap)

    def terms(source, upper):
        lower = 1.0 - upper
        weights = w_refs[source][rows, :]
        lower_w, upper_w = lower * weights, upper * weights
        return [lower * lower_w, upper * lower_w, upper * upper_w]

    low = 2 * cap + across * 2 * nb
    sum_rows(cap, blk, [w_ref[low:low + 2 * nb, :] for w_ref in w_refs], acc_ref, terms)
    diagonal_out[...] = acc_ref[:, :SEG] + pltpu.roll(acc_ref[:, 2 * SEG:], 1, 0)
    side_out[...] = acc_ref[:, SEG:2 * SEG]


def sum_products(half, cap, blk, across, meta_ref, v_refs, acc_ref, sums_ref):
    nb = cap // blk
    rows = slice(across * cap, (across + 1) * cap)

    def terms(source, upper):
        products = v_refs[source][rows, :]
        return [(1.0 - upper) * products, upper * products]

    low = across * 2 * nb
    sum_rows(cap, blk, [meta_ref[k, low:low + 2 * nb, :] for k in range(half)], acc_ref, terms)
    sums_ref[...] = acc_ref[:, :SEG] + pltpu.roll(acc_ref[:, SEG:], 1, 0)


def products_kernel(half, cap, blk, meta_ref, d_ref, e_ref, far_d_ref, far_e_ref, *rest):
    v_refs, (out, *far_outs, acc_ref, sums_ref, far_ref, side) = rest[:half], rest[half:]
    spans = out.shape[0]
    sum_products(half, cap, blk, 1, meta_ref, v_refs, acc_ref, far_ref)
    me = lax.axis_index("px")
    for k, far_out in enumerate(far_outs):
        for f in range(F):
            cut_part(far_ref, far_out.at[f], f, me ^ k, spans)
    sum_products(half, cap, blk, 0, meta_ref, v_refs, acc_ref, sums_ref)
    side[0] = d_ref[...] + far_d_ref[...]
    side[1] = e_ref[...] + far_e_ref[...]
    for q in range(spans):
        for channel, rows_ref in enumerate((side.at[0], side.at[1], sums_ref)):
            for f in range(F):
                cut_part(rows_ref, out.at[q, channel * F + f], f, q, spans)


def x_lines(nx):
    return [pl.ds(i, 8, stride=nx // 8) for i in range(nx // 8)]


def shift_x(lines, distance):
    size = len(lines)
    moved = []
    for i in range(size):
        j = i + distance
        line = lines[j % size]
        moved.append(line if 0 <= j < size else pltpu.roll(line, 7 if j >= size else 1, 0))
    return moved


def shift_y(tiles, distance):
    if distance == 0:
        return tiles
    lane = iota(tiles[0].shape, 1)
    moved = [pltpu.roll(tile, -distance % SEG, 1) for tile in tiles]
    if distance > 0:
        return [jnp.where(lane >= SEG - distance, b, a) for a, b in zip(moved, moved[1:] + moved[:1])]
    return [jnp.where(lane < -distance, a, b) for a, b in zip(moved[-1:] + moved[:-1], moved)]


def sweep_diagonals(coeffs, shift):
    def each(function, *lists):
        return [function(*items) for items in zip(*lists)]

    back = functools.partial(shift, coeffs)
    main = each(lambda c, d: 1.0 - c - d, coeffs, back(-1))
    q0 = each(lambda a, c, d: a * a + c * c + d * d, main, coeffs, back(-1))
    q1 = each(lambda a, b, c: c * (a + b), main, shift(main, 1), coeffs)
    q2 = each(lambda c, d: c * d, coeffs, back(1))
    up0, up1, up2 = shift(q0, 1), shift(q1, 1), shift(q2, 1)
    low1, low2 = shift(q1, -1), shift(q2, -1)
    r0 = each(lambda a, b, c, d, e: a * a + b * b + c * c + d * d + e * e,
              q0, q1, low1, q2, shift(q2, -2))
    r1 = each(lambda a, b, c, d, e, f, g: a * b + c * (d + e) + f * g,
              low1, low2, q1, q0, up0, q2, up1)
    r2 = each(lambda a, b, c, d, e: a * (b + c) + d * e, q2, q0, shift(q0, 2), q1, up1)
    r3 = each(lambda a, b, c, d: a * b + c * d, q1, up2, q2, shift(q1, 2))
    r4 = each(lambda a, b: a * b, q2, shift(q2, 2))
    return [r0, r1, r2, r3, r4]


def make_x_diagonals(out, cx_ref):
    tiles, nx, _ = cx_ref.shape
    picks = x_lines(nx)
    for t in range(tiles):
        coeffs = [cx_ref[t, pick, :] for pick in picks]
        for d, lines in enumerate(sweep_diagonals(coeffs, shift_x)):
            for pick, line in zip(picks, lines):
                out[d, t, pick, :] = line


def make_y_diagonals(out, cy_ref):
    tiles, nx, _ = cy_ref.shape
    for low in range(0, nx, 8):
        rows = slice(low, low + 8)
        coeffs = [cy_ref[t, rows, :] for t in range(tiles)]
        for d, parts in enumerate(sweep_diagonals(coeffs, shift_y)):
            for t, part in enumerate(parts):
                out[d, t, rows, :] = part


def banded(diagonals, values, shift):
    total = [c * v for c, v in zip(diagonals[0], values)]
    for d in range(1, REACH + 1):
        above = [c * v for c, v in zip(diagonals[d], shift(values, d))]
        below = shift([c * v for c, v in zip(diagonals[d], values)], -d)
        total = [a + (b + c) for a, b, c in zip(total, above, below)]
    return total


def sweep_x_into(to_refs, from_refs, x_ref, plus_refs=None, sign=1.0):
    count, tiles, nx, _ = x_ref.shape
    picks = x_lines(nx)
    for t in range(tiles):
        diagonals = [[x_ref[d, t, pick, :] for pick in picks] for d in range(count)]
        for i, from_ref in enumerate(from_refs):
            values = [from_ref[t, pick, :] for pick in picks]
            for pick, value in zip(picks, banded(diagonals, values, shift_x)):
                if plus_refs is not None:
                    value = value + sign * plus_refs[i][t, pick, :]
                to_refs[i][t, pick, :] = value


def sweep_y_into(to_refs, from_refs, y_ref):
    count, tiles, nx, _ = y_ref.shape
    for low in range(0, nx, 8):
        rows = slice(low, low + 8)
        diagonals = [[y_ref[d, t, rows, :] for t in range(tiles)] for d in range(count)]
        for to_ref, from_ref in zip(to_refs, from_refs):
            values = [from_ref[t, rows, :] for t in range(tiles)]
            for t, value in enumerate(banded(diagonals, values, shift_y)):
                to_ref[t, rows, :] = value


def normal_into(to_refs, from_refs, diagonal_refs, side_refs, base_refs=None):
    tiles, nx, _ = from_refs[0].shape
    picks = x_lines(nx)
    for t in range(tiles):
        for i, from_ref in enumerate(from_refs):
            values = [from_ref[t, pick, :] for pick in picks]
            sides = [side_refs[i][t, pick, :] for pick in picks]
            low = [e * a for e, a in zip(sides, values)]
            low = [pltpu.roll(low[-1], 1, 0)] + low[:-1]
            after = values[1:] + [pltpu.roll(values[0], 7, 0)]
            for line, pick in enumerate(picks):
                result = (diagonal_refs[i][t, pick, :] * values[line] + sides[line] * after[line]
                          + low[line])
                if base_refs is not None:
                    result = base_refs[i][t, pick, :] - result
                to_refs[i][t, pick, :] = result


def of_fields(ref, start=0):
    return [ref.at[start + f] for f in range(F)]


def start_kernel(c0_ref, cx_ref, swap_ref, c0_out, x_out, y_out, u_out, token_out, cx_out, cy_out,
                 work):
    token_out[...] = jnp.zeros_like(token_out)
    nx = cx_ref.shape[0]
    spans, count = swap_ref.shape[0], cy_out.shape[0]
    me = lax.axis_index("px")
    for p in range(spans):
        for t in range(count):
            cy_out[t, p * LX:(p + 1) * LX, :] = swap_ref[p, t * LX:(t + 1) * LX, :]

    def beside(i):
        lines = slice(count * LX + i * nx, count * LX + (i + 1) * nx)
        before = swap_ref[jnp.maximum(me - 1, 0), lines, :]
        after = swap_ref[jnp.minimum(me + 1, spans - 1), lines, :]
        return ends_tile(jnp.where(me > 0, before, 0.0), jnp.where(me < spans - 1, after, 0.0))

    for t in range(count - 1):
        tile = slice(t * SEG, (t + 1) * SEG)
        cx_out[t] = cx_ref[:, tile]
        for f in range(F):
            c0_out[f, t] = c0_ref[f, :, tile]
    cx_out[count - 1] = beside(F)
    cx_out[:, nx - 1:, :] = jnp.zeros((count, 1, SEG), jnp.float32)
    for f in range(F):
        c0_out[f, count - 1] = beside(f)
    make_x_diagonals(x_out, cx_out)
    make_y_diagonals(y_out, cy_out)
    sweep_x_into(of_fields(work), of_fields(c0_out), x_out)
    sweep_y_into(of_fields(u_out), of_fields(work), y_out)


def join_kernel(spans, *rest):
    parts, out = rest[:spans], rest[spans]
    me = lax.axis_index("px")
    for k, part in enumerate(parts):
        rows = pl.ds(pl.multiple_of((me ^ k) * LX, LX), LX)
        for f in range(F):
            for t in range(out.shape[1]):
                out[f, t, rows, :] = part[f, t]


def solve_kernel(c0_ref, x_ref, y_ref, u_ref, obs_ref, far_ref, r_out, q_out, h_out, dots_out,
                 vec, coef, work):
    for p in range(obs_ref.shape[0]):
        rows = slice(p * LX, (p + 1) * LX)
        for channel in range(2 * F):
            coef[channel, :, rows, :] = obs_ref[p, channel]
        for f in range(F):
            coef[2 * F + f, :, rows, :] = obs_ref[p, 2 * F + f] + far_ref[f, :, rows, :]

    sides = (of_fields(coef), of_fields(coef, F))
    one, two, r, q, s, h = (of_fields(ref) for ref in (
        work.at[0], work.at[1], vec.at[0], vec.at[1], vec.at[2], h_out))
    normal_into(one, of_fields(u_ref), *sides, of_fields(coef, 2 * F))
    sweep_y_into(two, one, y_ref)
    sweep_x_into(r, two, x_ref, of_fields(c0_ref), -1.0)
    sweep_x_into(one, r, x_ref)
    sweep_y_into(two, one, y_ref)
    normal_into(one, two, *sides)
    sweep_y_into(two, one, y_ref)
    sweep_x_into(q, two, x_ref, r)
    sweep_x_into(one, q, x_ref)
    sweep_y_into(s, one, y_ref)
    normal_into(h, s, *sides)

    tiles, nx = vec.shape[2] - 1, vec.shape[3]
    sums = [jnp.zeros((8, SEG), jnp.float32) for _ in range(4)]
    for f in range(F):
        for t in range(tiles):
            r_out[f, :, t * SEG:(t + 1) * SEG] = vec[0, f, t]
            q_out[f, :, t * SEG:(t + 1) * SEG] = vec[1, f, t]
            for low in range(0, nx, 8):
                lines = slice(low, low + 8)
                r, q, s = (vec[i, f, t, lines, :] for i in range(3))
                for i, product in enumerate((r * r, r * q, q * q, s * h_out[f, t, lines, :])):
                    sums[i] = sums[i] + product
    dots = jnp.zeros((1, SEG), jnp.float32)
    for i, total in enumerate(sums):
        line = jnp.sum(total, axis=0, keepdims=True)
        for distance in (64, 32, 16):
            line = line + pltpu.roll(line, distance, 1)
        dots = jnp.where(iota((1, SEG), 1) // SPLIT == i, line, dots)
    dots_out[...] = jnp.broadcast_to(dots, dots_out.shape)


def last_kernel(h_ref, q_ref, x_ref, y_ref, qq_out, work):
    sweep_y_into(of_fields(work.at[0]), of_fields(h_ref), y_ref)
    sweep_x_into(of_fields(work.at[1]), of_fields(work.at[0]), x_ref)
    for f in range(F):
        for t in range(work.shape[2] - 1):
            tile = slice(t * SEG, (t + 1) * SEG)
            qq_out[f, :, tile] = q_ref[f, :, tile] + work[1, f, t]


def finish_kernel(dots_ref, c0_ref, r_ref, q_ref, qq_ref, control_out, residual_out):
    dots = jnp.sum(dots_ref[...], axis=0)
    lane = iota((1, SEG), 1)
    rr, rq, qq2, energy = (pltpu.roll(dots, (SEG - i * SPLIT) % SEG, 1) for i in range(4))

    def total(line):
        return jnp.sum(jnp.where(lane < SPLIT, line, 0.0), axis=1, keepdims=True)

    rr_sum = total(rr)
    alpha = rr_sum / total(rq)
    new_sum = total(rr - 2.0 * alpha * rq + alpha * alpha * qq2)
    more = 1.0 + new_sum / rr_sum
    curve = total(more * more * rq - 2.0 * more * alpha * qq2 + alpha * alpha * (qq2 + energy))
    second = new_sum / curve
    first_weight = alpha + second * more
    both = alpha * second
    for f in range(F):
        r, q = r_ref[f], q_ref[f]
        control_out[f] = c0_ref[f] + first_weight * r - both * q
        residual_out[f] = r - first_weight * q + both * qq_ref[f]


def call(kernel, out_shape, scratch=(), in_specs=None, out_specs=None, limit=VMEM_BYTES,
         weight=1):
    params = {"in_specs": in_specs, "out_specs": out_specs}
    return pl.pallas_call(
        kernel,
        out_shape=out_shape,
        scratch_shapes=list(scratch),
        compiler_params=pltpu.CompilerParams(vmem_limit_bytes=limit),
        cost_estimate=pl.CostEstimate(flops=weight, bytes_accessed=weight, transcendentals=0),
        **{name: value for name, value in params.items() if value is not None},
    )


def f32(*shape):
    return jax.ShapeDtypeStruct(shape, jnp.float32)


def vmem(*shape, kind=jnp.float32):
    return pltpu.VMEM(shape, kind)


def shards(
    control_start, coef_x, coef_y, innovation, obs_weight, interp, obs_owner, cell_key, stencil
):
    groups, spans = lax.axis_size("py"), lax.axis_size("px")
    half = groups // 2
    rows = innovation.shape[0]
    cap = 3 * rows // groups
    blk = SEG if cap % SEG == 0 else HALF
    meta_rows = -(-4 * (cap // blk) // 8) * 8
    block_rows = 2 * cap + meta_rows
    chunks = rows // SEG
    nx, width = control_start.shape[2], control_start.shape[3]
    tiles = width // SEG + 1
    c0, cx = control_start[:, 0], coef_x[0]
    hbm, local, scalars = (
        pl.BlockSpec(memory_space=s) for s in (pltpu.HBM, pltpu.VMEM, pltpu.SMEM))
    ints = vmem(chunks, SEG, kind=jnp.int32)
    dma = pltpu.SemaphoreType.DMA

    def to_half(block, k):
        return lax.ppermute(block, "py", [(i, i ^ k) for i in range(groups)])

    def across(parts):
        return [
            lax.ppermute(parts[k], ("px", "py"), [
                (i * groups + j, (i ^ k) * groups + (j ^ half))
                for i in range(spans) for j in range(groups)])
            for k in range(spans)]

    *w_blocks, slots = call(
        functools.partial(pack_weights_kernel, groups, cap, blk, block_rows),
        (f32(block_rows, SEG),) * half + (jax.ShapeDtypeStruct((chunks, SEG), jnp.int32),),
        [ints, ints, ints, vmem(chunks, SEG), vmem(rows, SEG), vmem(half * block_rows, SEG), ints,
         pltpu.SMEM((chunks, SEG), jnp.int32), dma((5,)), dma((half,)), dma],
        [hbm] * 5,
        (hbm,) * half + (local,),
        limit=PACK_BYTES,
    )(
        obs_owner.reshape(chunks, SEG), cell_key.reshape(chunks, SEG),
        stencil.reshape(chunks, SEG), interp.reshape(chunks, SEG), obs_weight,
    )
    v_blocks = list(call(
        functools.partial(pack_products_kernel, groups, cap),
        (f32(2 * cap, SEG),) * half,
        [vmem(rows, SEG), vmem(rows, SEG), vmem(groups * cap, SEG), dma((2,)), dma((half,))],
        [scalars] + [hbm] * 2,
        (hbm,) * half,
        limit=PACK_BYTES,
    )(slots, obs_weight, innovation))
    w_blocks[1:] = [to_half(w_blocks[k], k) for k in range(1, half)]
    w_blocks[1], *v_blocks[1:] = lax.optimization_barrier((w_blocks[1], *v_blocks[1:]))
    v_blocks[1:] = [to_half(v_blocks[k], k) for k in range(1, half)]

    swap = call(
        pack_swap_kernel,
        f32(spans, LX * tiles + (F + 1) * nx, SEG),
        [vmem(*coef_y.shape[1:]), vmem(F + 1, nx, SEG), vmem(F + 1, nx, SEG), dma((5,))],
        [local] + [hbm] * 3,
        limit=PACK_BYTES,
    )(slots, coef_y[0], c0, cx)
    swap = lax.all_to_all(swap, "px", split_axis=0, concat_axis=0, tiled=True)
    c0_ext, x_sweep, y_sweep, u_ext, token = call(
        start_kernel,
        (f32(F, tiles, nx, SEG), f32(REACH + 1, tiles, nx, SEG),
         f32(REACH + 1, tiles, nx, SEG), f32(F, tiles, nx, SEG), f32(8, SEG)),
        [vmem(tiles, nx, SEG), vmem(tiles, nx, SEG), vmem(F, tiles, nx, SEG)],
    )(c0, cx, swap)

    def sum_weights(side, token, weight):
        return call(
            functools.partial(weights_kernel, half, cap, blk, side),
            (f32(half, meta_rows, SEG),) + (f32(ROWS, SEG),) * 2,
            [vmem(ROWS, 3 * SEG)],
            weight=weight,
        )(*w_blocks, token)

    meta, *side_across = sum_weights(1, w_blocks[0], FIRST)
    side_across = [to_half(values, half) for values in side_across]
    meta, *side = sum_weights(0, token, 1)
    parts, *sums_across = call(
        functools.partial(products_kernel, half, cap, blk),
        (f32(spans, 3 * F, tiles, LX, SEG),) + (f32(F, tiles, LX, SEG),) * spans,
        [vmem(ROWS, 2 * SEG), vmem(ROWS, SEG), vmem(ROWS, SEG), vmem(2, ROWS, SEG)],
    )(meta, *side, *side_across, *v_blocks)
    far_sums = call(
        functools.partial(join_kernel, spans), f32(F, tiles, nx, SEG), weight=JOIN,
    )(*across(sums_across))
    parts = lax.all_to_all(parts, "px", split_axis=0, concat_axis=0, tiled=True)

    r, q, h, dots = call(
        solve_kernel,
        (f32(F, nx, width),) * 2 + (f32(F, tiles, nx, SEG), f32(groups * spans, 1, SEG)),
        [vmem(3, F, tiles, nx, SEG), vmem(3 * F, tiles, nx, SEG), vmem(2, F, tiles, nx, SEG)],
    )(c0_ext, x_sweep, y_sweep, u_ext, parts, far_sums)
    dots = lax.all_to_all(dots, ("px", "py"), split_axis=0, concat_axis=0, tiled=True)
    qq = call(last_kernel, f32(F, nx, width), [vmem(2, F, tiles, nx, SEG)])(
        h, q, x_sweep, y_sweep)
    control, residual = call(finish_kernel, (f32(F, nx, width),) * 2)(dots, c0, r, q, qq)
    return control[:, None], residual[:, None]


def solution(mesh):
    return jax.shard_map(
        shards,
        mesh=mesh,
        in_specs=(
            P(None, "py", None, "px"),
            P("py", None, "px"),
            P("py", "px", None),
            P(("px", "py"), None),
            P(("px", "py"), None),
            P(("px", "py")),
            P(("px", "py"), None),
            P(("px", "py")),
            P(("px", "py")),
        ),
        out_specs=(P(None, "py", None, "px"), P(None, "py", None, "px")),
        check_vma=False,
    )
```

```python
import functools

import jax
import jax.numpy as jnp
from jax import lax
from jax.experimental import pallas as pl
from jax.experimental.pallas import tpu as pltpu
from jax.sharding import PartitionSpec as P

F = 2
SEG = 128
M = 4
NB = 16
LX = 16
ROWS = F * NB * LX
HALF = SEG // 2
SPLIT = 16
REACH = M
VMEM_BYTES = 16 * 1024 * 1024
PACK_BYTES = 60 * 1024 * 1024
FIRST = 100_000_000
JOIN = 100_000_000


def iota(shape, axis):
    return lax.broadcasted_iota(jnp.int32, shape, axis)


def flag(condition, kind=jnp.bfloat16):
    return jnp.where(condition, 1.0, 0.0).astype(kind)


def mxu(left, right):
    return jnp.dot(left, right, preferred_element_type=jnp.float32)


def split_parts(values, count):
    parts = []
    for _ in range(count):
        part = values.astype(jnp.bfloat16)
        parts.append(part)
        values = values - part.astype(jnp.float32)
    return parts


def ends_tile(before, after):
    return jnp.where(iota(after.shape, after.ndim - 1) < HALF, after, before)


def start_copies(pairs, sems):
    copies = [pltpu.make_async_copy(*pair, sems.at[i]) for i, pair in enumerate(pairs)]
    for copy in copies:
        copy.start()
    return copies


def pack_weights_kernel(groups, cap, blk, block_rows, own_hbm, key_hbm, sten_hbm, itp_hbm, w_hbm,
                        *rest):
    half = groups // 2
    outs, rest = rest[:half], rest[half:]
    (slot_out, own_ref, key_ref, sten_ref, itp_ref, w_ref, buffer, slot_v, slot_s, sems, out_sems,
     sem) = rest
    loads = start_copies([(own_hbm, own_ref), (key_hbm, key_ref), (sten_hbm, sten_ref),
                          (itp_hbm, itp_ref), (w_hbm, w_ref)], sems)

    def clear(k, carry):
        start = pl.multiple_of(k * block_rows, 8)
        buffer[pl.ds(start, block_rows), :] = jnp.zeros((block_rows, SEG), jnp.float32)
        return carry

    lax.fori_loop(0, half, clear, 0)

    for load in loads[:4]:
        load.wait()
    chunks = own_ref.shape[0]
    nb = cap // blk
    own = own_ref[...]
    high = groups * chunks
    shift = chunks.bit_length() - 1
    masks = [flag(own == o, jnp.float32) for o in range(groups)]
    hits = jnp.concatenate(masks, axis=0).astype(jnp.bfloat16)
    square = (SEG, SEG)
    within = mxu(hits, flag(iota(square, 0) < iota(square, 1)))
    tallies = mxu(hits, jnp.ones(square, jnp.bfloat16)).astype(jnp.bfloat16)
    line, column = iota((high, high), 0), iota((high, high), 1)
    same = (line >> shift) == (column >> shift)
    ranks = within + mxu(flag(same & (column < line)), tallies)
    rank = sum(masks[o] * ranks[o * chunks:(o + 1) * chunks] for o in range(groups))
    rank = rank.astype(jnp.int32)
    relative = own ^ lax.axis_index("py")
    block, across = relative & (half - 1), relative >> (half.bit_length() - 1)
    slot_v[...] = block * block_rows + across * cap + rank
    slot_out[...] = (block * 2 + across) * cap + rank
    copy = pltpu.make_async_copy(slot_v, slot_s, sem)
    copy.start()

    log = blk.bit_length() - 1
    place = relative * nb + (rank >> log)
    lane = rank & (blk - 1)
    key, sten, itp = key_ref[...], sten_ref[...], itp_ref[...]
    tall = groups * nb
    meta = jnp.zeros((5 * tall, SEG), jnp.float32)
    for i in range(chunks):
        chosen = iota((tall, SEG), 0) == place[i:i + 1]
        parts = split_parts(itp[i:i + 1], 3)
        parts += [key[i:i + 1].astype(jnp.bfloat16), (sten[i:i + 1] + 1).astype(jnp.bfloat16)]
        left = [jnp.where(chosen, part.astype(jnp.float32), 0.0) for part in parts]
        right = flag(iota(square, 0) == lane[i:i + 1])
        meta = meta + lax.dot_general(
            jnp.concatenate(left, axis=0).astype(jnp.bfloat16), right,
            (((1,), (1,)), ((), ())), preferred_element_type=jnp.float32)
    shares = meta[:tall] + meta[tall:2 * tall] + meta[2 * tall:3 * tall]
    targets = meta[3 * tall:4 * tall] * LX + meta[4 * tall:]
    for v in range(groups):
        base = (v % half) * block_rows + 2 * cap + (v // half) * 2 * nb
        buffer[base:base + nb, :] = shares[v * nb:(v + 1) * nb]
        buffer[base + nb:base + 2 * nb, :] = targets[v * nb:(v + 1) * nb]

    copy.wait()
    loads[4].wait()

    def place_rows(g, carry):
        weights = w_ref[pl.ds(pl.multiple_of(g * 8, 8), 8), :]
        line, lane = g // 16, (g % 16) * 8
        for i in range(8):
            buffer[pl.ds(slot_s[line, lane + i], 1), :] = weights[i:i + 1]
        return carry

    lax.fori_loop(0, w_ref.shape[0] // 8, place_rows, 0)
    for store in start_copies([(buffer.at[pl.ds(k * block_rows, block_rows)], out)
                               for k, out in enumerate(outs)], out_sems):
        store.wait()


def pack_products_kernel(groups, cap, slot_ref, w_hbm, d_hbm, *rest):
    half = groups // 2
    outs, (w_ref, d_ref, buffer, sems, out_sems) = rest[:half], rest[half:]
    loads = start_copies([(w_hbm, w_ref), (d_hbm, d_ref)], sems)

    def clear(o, carry):
        start = pl.multiple_of(o * cap, 8)
        buffer[pl.ds(start, cap), :] = jnp.zeros((cap, SEG), jnp.float32)
        return carry

    lax.fori_loop(0, groups, clear, 0)

    for load in loads:
        load.wait()

    def place_rows(g, carry):
        start = pl.multiple_of(g * 8, 8)
        products = w_ref[pl.ds(start, 8), :] * d_ref[pl.ds(start, 8), :]
        line, lane = g // 16, (g % 16) * 8
        for i in range(8):
            buffer[pl.ds(slot_ref[line, lane + i], 1), :] = products[i:i + 1]
        return carry

    lax.fori_loop(0, w_ref.shape[0] // 8, place_rows, 0)
    for store in start_copies([(buffer.at[pl.ds(k * 2 * cap, 2 * cap)], out)
                               for k, out in enumerate(outs)], out_sems):
        store.wait()


def pack_swap_kernel(_, cy_hbm, c0_hbm, cx_hbm, swap_out, cy_ref, first, last, sems):
    width = c0_hbm.shape[2]
    for load in start_copies([
        (cy_hbm, cy_ref),
        (c0_hbm.at[:, :, pl.ds(0, SEG)], first.at[pl.ds(0, F)]),
        (cx_hbm.at[:, pl.ds(0, SEG)], first.at[F]),
        (c0_hbm.at[:, :, pl.ds(width - SEG, SEG)], last.at[pl.ds(0, F)]),
        (cx_hbm.at[:, pl.ds(width - SEG, SEG)], last.at[F]),
    ], sems):
        load.wait()
    columns = cy_ref.shape[1]
    cy = cy_ref[...]
    cy = jnp.where(iota(cy.shape, 1) == columns - 1, 0.0, cy)
    empty = jnp.zeros((LX, SEG), jnp.float32)
    me = lax.axis_index("px")
    nx = first.shape[1]
    for q in range(columns // width):
        low, top = q * width, (q + 1) * width
        tiles = [cy[:, t:t + SEG] for t in range(low, top, SEG)]
        before = cy[:, low - SEG:low] if low > 0 else empty
        after = cy[:, top:top + SEG] if top < columns else empty
        tiles.append(ends_tile(before, after))
        for t, tile in enumerate(tiles):
            swap_out[q, t * LX:(t + 1) * LX, :] = tile
        base = len(tiles) * LX
        for i in range(F + 1):
            swap_out[q, base + i * nx:base + (i + 1) * nx, :] = jnp.where(
                q < me, first[i], last[i])


def sum_rows(cap, blk, metas, acc_ref, terms):
    nb = cap // blk
    numbers = 1.0 + iota((ROWS, cap), 0).astype(jnp.float32)
    for source, meta in enumerate(metas):
        upper = jnp.concatenate(
            [jnp.broadcast_to(meta[i:i + 1], (SEG, SEG)).T[:blk] for i in range(nb)], axis=0)
        target = jnp.concatenate([meta[nb + i:nb + i + 1, :blk] for i in range(nb)], axis=1)
        hit = flag(numbers == target)
        values = jnp.concatenate(terms(source, upper), axis=1)
        part = mxu(jnp.concatenate([hit, hit], axis=1),
                   jnp.concatenate(split_parts(values, 2), axis=0))
        if source:
            acc_ref[...] += part
        else:
            acc_ref[...] = part


def cut_part(rows_ref, to, f, q, spans):
    per = to.shape[0] - 1

    def tile(b):
        start = pl.multiple_of((f * NB + b) * LX, LX)
        return rows_ref[pl.ds(start, LX), :]

    for j in range(per):
        to[j] = tile(q * per + j)
    before = tile(jnp.maximum(q * per - 1, 0))
    after = tile(jnp.minimum(q * per + per, NB - 1))
    to[per] = ends_tile(jnp.where(q > 0, before, 0.0), jnp.where(q < spans - 1, after, 0.0))


def weights_kernel(half, cap, blk, across, *rest):
    w_refs, (_, meta_out, diagonal_out, side_out, acc_ref) = rest[:half], rest[half:]
    nb = cap // blk
    for k, w_ref in enumerate(w_refs):
        meta_out[k] = w_ref[2 * cap:, :]
    rows = slice(across * cap, (across + 1) * cap)

    def terms(source, upper):
        lower = 1.0 - upper
        weights = w_refs[source][rows, :]
        lower_w, upper_w = lower * weights, upper * weights
        return [lower * lower_w, upper * lower_w, upper * upper_w]

    low = 2 * cap + across * 2 * nb
    sum_rows(cap, blk, [w_ref[low:low + 2 * nb, :] for w_ref in w_refs], acc_ref, terms)
    diagonal_out[...] = acc_ref[:, :SEG] + pltpu.roll(acc_ref[:, 2 * SEG:], 1, 0)
    side_out[...] = acc_ref[:, SEG:2 * SEG]


def sum_products(half, cap, blk, across, meta_ref, v_refs, acc_ref, sums_ref):
    nb = cap // blk
    rows = slice(across * cap, (across + 1) * cap)

    def terms(source, upper):
        products = v_refs[source][rows, :]
        return [(1.0 - upper) * products, upper * products]

    low = across * 2 * nb
    sum_rows(cap, blk, [meta_ref[k, low:low + 2 * nb, :] for k in range(half)], acc_ref, terms)
    sums_ref[...] = acc_ref[:, :SEG] + pltpu.roll(acc_ref[:, SEG:], 1, 0)


def products_kernel(half, cap, blk, meta_ref, d_ref, e_ref, far_d_ref, far_e_ref, *rest):
    v_refs, (out, token_out, *far_outs, acc_ref, sums_ref, far_ref, side) = (
        rest[:half], rest[half:])
    token_out[...] = jnp.zeros_like(token_out)
    spans = out.shape[0]
    sum_products(half, cap, blk, 1, meta_ref, v_refs, acc_ref, far_ref)
    me = lax.axis_index("px")
    for k, far_out in enumerate(far_outs):
        for f in range(F):
            cut_part(far_ref, far_out.at[f], f, me ^ k, spans)
    sum_products(half, cap, blk, 0, meta_ref, v_refs, acc_ref, sums_ref)
    side[0] = d_ref[...] + far_d_ref[...]
    side[1] = e_ref[...] + far_e_ref[...]
    for q in range(spans):
        for channel, rows_ref in enumerate((side.at[0], side.at[1], sums_ref)):
            for f in range(F):
                cut_part(rows_ref, out.at[q, channel * F + f], f, q, spans)


def x_lines(nx):
    return [pl.ds(i, 8, stride=nx // 8) for i in range(nx // 8)]


def shift_x(lines, distance):
    size = len(lines)
    moved = []
    for i in range(size):
        j = i + distance
        line = lines[j % size]
        moved.append(line if 0 <= j < size else pltpu.roll(line, 7 if j >= size else 1, 0))
    return moved


def shift_y(tiles, distance):
    if distance == 0:
        return tiles
    lane = iota(tiles[0].shape, 1)
    moved = [pltpu.roll(tile, -distance % SEG, 1) for tile in tiles]
    if distance > 0:
        return [jnp.where(lane >= SEG - distance, b, a) for a, b in zip(moved, moved[1:] + moved[:1])]
    return [jnp.where(lane < -distance, a, b) for a, b in zip(moved[-1:] + moved[:-1], moved)]


def sweep_diagonals(coeffs, shift):
    def each(function, *lists):
        return [function(*items) for items in zip(*lists)]

    back = functools.partial(shift, coeffs)
    main = each(lambda c, d: 1.0 - c - d, coeffs, back(-1))
    q0 = each(lambda a, c, d: a * a + c * c + d * d, main, coeffs, back(-1))
    q1 = each(lambda a, b, c: c * (a + b), main, shift(main, 1), coeffs)
    q2 = each(lambda c, d: c * d, coeffs, back(1))
    up0, up1, up2 = shift(q0, 1), shift(q1, 1), shift(q2, 1)
    low1, low2 = shift(q1, -1), shift(q2, -1)
    r0 = each(lambda a, b, c, d, e: a * a + b * b + c * c + d * d + e * e,
              q0, q1, low1, q2, shift(q2, -2))
    r1 = each(lambda a, b, c, d, e, f, g: a * b + c * (d + e) + f * g,
              low1, low2, q1, q0, up0, q2, up1)
    r2 = each(lambda a, b, c, d, e: a * (b + c) + d * e, q2, q0, shift(q0, 2), q1, up1)
    r3 = each(lambda a, b, c, d: a * b + c * d, q1, up2, q2, shift(q1, 2))
    r4 = each(lambda a, b: a * b, q2, shift(q2, 2))
    return [r0, r1, r2, r3, r4]


def make_x_diagonals(out, cx_ref):
    tiles, nx, _ = cx_ref.shape
    picks = x_lines(nx)
    for t in range(tiles):
        coeffs = [cx_ref[t, pick, :] for pick in picks]
        for d, lines in enumerate(sweep_diagonals(coeffs, shift_x)):
            for pick, line in zip(picks, lines):
                out[d, t, pick, :] = line


def make_y_diagonals(out, cy_ref):
    tiles, nx, _ = cy_ref.shape
    for low in range(0, nx, 8):
        rows = slice(low, low + 8)
        coeffs = [cy_ref[t, rows, :] for t in range(tiles)]
        for d, parts in enumerate(sweep_diagonals(coeffs, shift_y)):
            for t, part in enumerate(parts):
                out[d, t, rows, :] = part


def banded(diagonals, values, shift):
    total = [c * v for c, v in zip(diagonals[0], values)]
    for d in range(1, REACH + 1):
        above = [c * v for c, v in zip(diagonals[d], shift(values, d))]
        below = shift([c * v for c, v in zip(diagonals[d], values)], -d)
        total = [a + (b + c) for a, b, c in zip(total, above, below)]
    return total


def sweep_x_into(to_refs, from_refs, x_ref, plus_refs=None, sign=1.0):
    count, tiles, nx, _ = x_ref.shape
    picks = x_lines(nx)
    for t in range(tiles):
        diagonals = [[x_ref[d, t, pick, :] for pick in picks] for d in range(count)]
        for i, from_ref in enumerate(from_refs):
            values = [from_ref[t, pick, :] for pick in picks]
            for pick, value in zip(picks, banded(diagonals, values, shift_x)):
                if plus_refs is not None:
                    value = value + sign * plus_refs[i][t, pick, :]
                to_refs[i][t, pick, :] = value


def sweep_y_into(to_refs, from_refs, y_ref):
    count, tiles, nx, _ = y_ref.shape
    for low in range(0, nx, 8):
        rows = slice(low, low + 8)
        diagonals = [[y_ref[d, t, rows, :] for t in range(tiles)] for d in range(count)]
        for to_ref, from_ref in zip(to_refs, from_refs):
            values = [from_ref[t, rows, :] for t in range(tiles)]
            for t, value in enumerate(banded(diagonals, values, shift_y)):
                to_ref[t, rows, :] = value


def normal_into(to_refs, from_refs, diagonal_refs, side_refs, base_refs=None):
    tiles, nx, _ = from_refs[0].shape
    picks = x_lines(nx)
    for t in range(tiles):
        for i, from_ref in enumerate(from_refs):
            values = [from_ref[t, pick, :] for pick in picks]
            sides = [side_refs[i][t, pick, :] for pick in picks]
            low = [e * a for e, a in zip(sides, values)]
            low = [pltpu.roll(low[-1], 1, 0)] + low[:-1]
            after = values[1:] + [pltpu.roll(values[0], 7, 0)]
            for line, pick in enumerate(picks):
                result = (diagonal_refs[i][t, pick, :] * values[line] + sides[line] * after[line]
                          + low[line])
                if base_refs is not None:
                    result = base_refs[i][t, pick, :] - result
                to_refs[i][t, pick, :] = result


def of_fields(ref, start=0):
    return [ref.at[start + f] for f in range(F)]


def start_kernel(c0_ref, cx_ref, swap_ref, c0_out, cx_out, cy_out, u_out, token_out, x_ref, y_ref,
                 work):
    token_out[...] = jnp.zeros_like(token_out)
    nx = cx_ref.shape[0]
    spans, count = swap_ref.shape[0], cy_out.shape[0]
    me = lax.axis_index("px")
    for p in range(spans):
        for t in range(count):
            cy_out[t, p * LX:(p + 1) * LX, :] = swap_ref[p, t * LX:(t + 1) * LX, :]

    def beside(i):
        lines = slice(count * LX + i * nx, count * LX + (i + 1) * nx)
        before = swap_ref[jnp.maximum(me - 1, 0), lines, :]
        after = swap_ref[jnp.minimum(me + 1, spans - 1), lines, :]
        return ends_tile(jnp.where(me > 0, before, 0.0), jnp.where(me < spans - 1, after, 0.0))

    for t in range(count - 1):
        tile = slice(t * SEG, (t + 1) * SEG)
        cx_out[t] = cx_ref[:, tile]
        for f in range(F):
            c0_out[f, t] = c0_ref[f, :, tile]
    cx_out[count - 1] = beside(F)
    cx_out[:, nx - 1:, :] = jnp.zeros((count, 1, SEG), jnp.float32)
    for f in range(F):
        c0_out[f, count - 1] = beside(f)
    make_x_diagonals(x_ref, cx_out)
    make_y_diagonals(y_ref, cy_out)
    sweep_x_into(of_fields(work), of_fields(c0_out), x_ref)
    sweep_y_into(of_fields(u_out), of_fields(work), y_ref)


def diagonals_kernel(_, cx_ref, cy_ref, x_out, y_out):
    make_x_diagonals(x_out, cx_ref)
    make_y_diagonals(y_out, cy_ref)


def join_kernel(spans, *rest):
    parts, out = rest[:spans], rest[spans]
    me = lax.axis_index("px")
    for k, part in enumerate(parts):
        rows = pl.ds(pl.multiple_of((me ^ k) * LX, LX), LX)
        for f in range(F):
            for t in range(out.shape[1]):
                out[f, t, rows, :] = part[f, t]


def solve_kernel(c0_ref, x_ref, y_ref, u_ref, obs_ref, far_ref, r_out, q_out, h_out, dots_out,
                 vec, coef, work):
    for p in range(obs_ref.shape[0]):
        rows = slice(p * LX, (p + 1) * LX)
        for channel in range(2 * F):
            coef[channel, :, rows, :] = obs_ref[p, channel]
        for f in range(F):
            coef[2 * F + f, :, rows, :] = obs_ref[p, 2 * F + f] + far_ref[f, :, rows, :]

    sides = (of_fields(coef), of_fields(coef, F))
    one, two, r, q, s, h = (of_fields(ref) for ref in (
        work.at[0], work.at[1], vec.at[0], vec.at[1], vec.at[2], h_out))
    normal_into(one, of_fields(u_ref), *sides, of_fields(coef, 2 * F))
    sweep_y_into(two, one, y_ref)
    sweep_x_into(r, two, x_ref, of_fields(c0_ref), -1.0)
    sweep_x_into(one, r, x_ref)
    sweep_y_into(two, one, y_ref)
    normal_into(one, two, *sides)
    sweep_y_into(two, one, y_ref)
    sweep_x_into(q, two, x_ref, r)
    sweep_x_into(one, q, x_ref)
    sweep_y_into(s, one, y_ref)
    normal_into(h, s, *sides)

    tiles, nx = vec.shape[2] - 1, vec.shape[3]
    sums = [jnp.zeros((8, SEG), jnp.float32) for _ in range(4)]
    for f in range(F):
        for t in range(tiles):
            r_out[f, :, t * SEG:(t + 1) * SEG] = vec[0, f, t]
            q_out[f, :, t * SEG:(t + 1) * SEG] = vec[1, f, t]
            for low in range(0, nx, 8):
                lines = slice(low, low + 8)
                r, q, s = (vec[i, f, t, lines, :] for i in range(3))
                for i, product in enumerate((r * r, r * q, q * q, s * h_out[f, t, lines, :])):
                    sums[i] = sums[i] + product
    dots = jnp.zeros((1, SEG), jnp.float32)
    for i, total in enumerate(sums):
        line = jnp.sum(total, axis=0, keepdims=True)
        for distance in (64, 32, 16):
            line = line + pltpu.roll(line, distance, 1)
        dots = jnp.where(iota((1, SEG), 1) // SPLIT == i, line, dots)
    dots_out[...] = jnp.broadcast_to(dots, dots_out.shape)


def last_kernel(h_ref, q_ref, x_ref, y_ref, qq_out, work):
    sweep_y_into(of_fields(work.at[0]), of_fields(h_ref), y_ref)
    sweep_x_into(of_fields(work.at[1]), of_fields(work.at[0]), x_ref)
    for f in range(F):
        for t in range(work.shape[2] - 1):
            tile = slice(t * SEG, (t + 1) * SEG)
            qq_out[f, :, tile] = q_ref[f, :, tile] + work[1, f, t]


def finish_kernel(dots_ref, c0_ref, r_ref, q_ref, qq_ref, control_out, residual_out):
    dots = jnp.sum(dots_ref[...], axis=0)
    lane = iota((1, SEG), 1)
    rr, rq, qq2, energy = (pltpu.roll(dots, (SEG - i * SPLIT) % SEG, 1) for i in range(4))

    def total(line):
        return jnp.sum(jnp.where(lane < SPLIT, line, 0.0), axis=1, keepdims=True)

    rr_sum = total(rr)
    alpha = rr_sum / total(rq)
    new_sum = total(rr - 2.0 * alpha * rq + alpha * alpha * qq2)
    more = 1.0 + new_sum / rr_sum
    curve = total(more * more * rq - 2.0 * more * alpha * qq2 + alpha * alpha * (qq2 + energy))
    second = new_sum / curve
    first_weight = alpha + second * more
    both = alpha * second
    for f in range(F):
        r, q = r_ref[f], q_ref[f]
        control_out[f] = c0_ref[f] + first_weight * r - both * q
        residual_out[f] = r - first_weight * q + both * qq_ref[f]


def call(kernel, out_shape, scratch=(), in_specs=None, out_specs=None, limit=VMEM_BYTES,
         weight=1):
    params = {"in_specs": in_specs, "out_specs": out_specs}
    return pl.pallas_call(
        kernel,
        out_shape=out_shape,
        scratch_shapes=list(scratch),
        compiler_params=pltpu.CompilerParams(vmem_limit_bytes=limit),
        cost_estimate=pl.CostEstimate(flops=weight, bytes_accessed=weight, transcendentals=0),
        **{name: value for name, value in params.items() if value is not None},
    )


def f32(*shape):
    return jax.ShapeDtypeStruct(shape, jnp.float32)


def vmem(*shape, kind=jnp.float32):
    return pltpu.VMEM(shape, kind)


def shards(
    control_start, coef_x, coef_y, innovation, obs_weight, interp, obs_owner, cell_key, stencil
):
    groups, spans = lax.axis_size("py"), lax.axis_size("px")
    half = groups // 2
    rows = innovation.shape[0]
    cap = 3 * rows // groups
    blk = SEG if cap % SEG == 0 else HALF
    meta_rows = -(-4 * (cap // blk) // 8) * 8
    block_rows = 2 * cap + meta_rows
    chunks = rows // SEG
    nx, width = control_start.shape[2], control_start.shape[3]
    tiles = width // SEG + 1
    c0, cx = control_start[:, 0], coef_x[0]
    hbm, local, scalars = (
        pl.BlockSpec(memory_space=s) for s in (pltpu.HBM, pltpu.VMEM, pltpu.SMEM))
    ints = vmem(chunks, SEG, kind=jnp.int32)
    dma = pltpu.SemaphoreType.DMA

    def to_half(block, k):
        return lax.ppermute(block, "py", [(i, i ^ k) for i in range(groups)])

    def across(parts):
        return [
            lax.ppermute(parts[k], ("px", "py"), [
                (i * groups + j, (i ^ k) * groups + (j ^ half))
                for i in range(spans) for j in range(groups)])
            for k in range(spans)]

    *w_blocks, slots = call(
        functools.partial(pack_weights_kernel, groups, cap, blk, block_rows),
        (f32(block_rows, SEG),) * half + (jax.ShapeDtypeStruct((chunks, SEG), jnp.int32),),
        [ints, ints, ints, vmem(chunks, SEG), vmem(rows, SEG), vmem(half * block_rows, SEG), ints,
         pltpu.SMEM((chunks, SEG), jnp.int32), dma((5,)), dma((half,)), dma],
        [hbm] * 5,
        (hbm,) * half + (local,),
        limit=PACK_BYTES,
    )(
        obs_owner.reshape(chunks, SEG), cell_key.reshape(chunks, SEG),
        stencil.reshape(chunks, SEG), interp.reshape(chunks, SEG), obs_weight,
    )
    v_blocks = list(call(
        functools.partial(pack_products_kernel, groups, cap),
        (f32(2 * cap, SEG),) * half,
        [vmem(rows, SEG), vmem(rows, SEG), vmem(groups * cap, SEG), dma((2,)), dma((half,))],
        [scalars] + [hbm] * 2,
        (hbm,) * half,
        limit=PACK_BYTES,
    )(slots, obs_weight, innovation))
    w_blocks[1:] = [to_half(w_blocks[k], k) for k in range(1, half)]
    w_blocks[1], *v_blocks[1:] = lax.optimization_barrier((w_blocks[1], *v_blocks[1:]))
    v_blocks[1:] = [to_half(v_blocks[k], k) for k in range(1, half)]

    swap = call(
        pack_swap_kernel,
        f32(spans, LX * tiles + (F + 1) * nx, SEG),
        [vmem(*coef_y.shape[1:]), vmem(F + 1, nx, SEG), vmem(F + 1, nx, SEG), dma((5,))],
        [local] + [hbm] * 3,
        limit=PACK_BYTES,
    )(slots, coef_y[0], c0, cx)
    swap = lax.all_to_all(swap, "px", split_axis=0, concat_axis=0, tiled=True)
    c0_ext, cx_ext, cy_ext, u_ext, token = call(
        start_kernel,
        (f32(F, tiles, nx, SEG), f32(tiles, nx, SEG), f32(tiles, nx, SEG), f32(F, tiles, nx, SEG),
         f32(8, SEG)),
        [vmem(REACH + 1, tiles, nx, SEG), vmem(REACH + 1, tiles, nx, SEG),
         vmem(F, tiles, nx, SEG)],
    )(c0, cx, swap)

    def sum_weights(side, token, weight):
        return call(
            functools.partial(weights_kernel, half, cap, blk, side),
            (f32(half, meta_rows, SEG),) + (f32(ROWS, SEG),) * 2,
            [vmem(ROWS, 3 * SEG)],
            weight=weight,
        )(*w_blocks, token)

    meta, *side_across = sum_weights(1, w_blocks[0], FIRST)
    side_across = [to_half(values, half) for values in side_across]
    meta, *side = sum_weights(0, token, 1)
    parts, token, *sums_across = call(
        functools.partial(products_kernel, half, cap, blk),
        (f32(spans, 3 * F, tiles, LX, SEG), f32(8, SEG)) + (f32(F, tiles, LX, SEG),) * spans,
        [vmem(ROWS, 2 * SEG), vmem(ROWS, SEG), vmem(ROWS, SEG), vmem(2, ROWS, SEG)],
    )(meta, *side, *side_across, *v_blocks)
    far_sums = call(
        functools.partial(join_kernel, spans), f32(F, tiles, nx, SEG), weight=JOIN,
    )(*across(sums_across))
    x_sweep, y_sweep = call(
        diagonals_kernel, (f32(REACH + 1, tiles, nx, SEG),) * 2)(token, cx_ext, cy_ext)
    parts = lax.all_to_all(parts, "px", split_axis=0, concat_axis=0, tiled=True)

    r, q, h, dots = call(
        solve_kernel,
        (f32(F, nx, width),) * 2 + (f32(F, tiles, nx, SEG), f32(groups * spans, 1, SEG)),
        [vmem(3, F, tiles, nx, SEG), vmem(3 * F, tiles, nx, SEG), vmem(2, F, tiles, nx, SEG)],
    )(c0_ext, x_sweep, y_sweep, u_ext, parts, far_sums)
    dots = lax.all_to_all(dots, ("px", "py"), split_axis=0, concat_axis=0, tiled=True)
    qq = call(last_kernel, f32(F, nx, width), [vmem(2, F, tiles, nx, SEG)])(
        h, q, x_sweep, y_sweep)
    control, residual = call(finish_kernel, (f32(F, nx, width),) * 2)(dots, c0, r, q, qq)
    return control[:, None], residual[:, None]


def solution(mesh):
    return jax.shard_map(
        shards,
        mesh=mesh,
        in_specs=(
            P(None, "py", None, "px"),
            P("py", None, "px"),
            P("py", "px", None),
            P(("px", "py"), None),
            P(("px", "py"), None),
            P(("px", "py")),
            P(("px", "py"), None),
            P(("px", "py")),
            P(("px", "py")),
        ),
        out_specs=(P(None, "py", None, "px"), P(None, "py", None, "px")),
        check_vma=False,
    )
```

```python
import functools

import jax
import jax.numpy as jnp
from jax import lax
from jax.experimental import pallas as pl
from jax.experimental.pallas import tpu as pltpu
from jax.sharding import PartitionSpec as P

F = 2
SEG = 128
M = 4
NB = 16
LX = 16
ROWS = F * NB * LX
HALF = SEG // 2
SPLIT = 16
REACH = M
VMEM_BYTES = 16 * 1024 * 1024
PACK_BYTES = 57 * 1024 * 1024
FIRST = 100_000_000
JOIN = 100_000_000


def iota(shape, axis):
    return lax.broadcasted_iota(jnp.int32, shape, axis)


def flag(condition, kind=jnp.bfloat16):
    return jnp.where(condition, 1.0, 0.0).astype(kind)


def mxu(left, right):
    return jnp.dot(left, right, preferred_element_type=jnp.float32)


def split_parts(values, count):
    parts = []
    for _ in range(count):
        part = values.astype(jnp.bfloat16)
        parts.append(part)
        values = values - part.astype(jnp.float32)
    return parts


def ends_tile(before, after):
    return jnp.where(iota(after.shape, after.ndim - 1) < HALF, after, before)


def start_copies(pairs, sems):
    copies = [pltpu.make_async_copy(*pair, sems.at[i]) for i, pair in enumerate(pairs)]
    for copy in copies:
        copy.start()
    return copies


def pack_weights_kernel(groups, cap, blk, block_rows, own_hbm, key_hbm, sten_hbm, itp_hbm, w_hbm,
                        *rest):
    half = groups // 2
    outs, rest = rest[:half], rest[half:]
    (slot_out, own_ref, key_ref, sten_ref, itp_ref, w_ref, buffer, slot_v, slot_s, sems, out_sems,
     sem) = rest
    loads = start_copies([(own_hbm, own_ref), (key_hbm, key_ref), (sten_hbm, sten_ref),
                          (itp_hbm, itp_ref), (w_hbm, w_ref)], sems)

    def clear(k, carry):
        start = pl.multiple_of(k * block_rows, 8)
        buffer[pl.ds(start, block_rows), :] = jnp.zeros((block_rows, SEG), jnp.float32)
        return carry

    lax.fori_loop(0, half, clear, 0)

    for load in loads[:4]:
        load.wait()
    chunks = own_ref.shape[0]
    nb = cap // blk
    own = own_ref[...]
    high = groups * chunks
    shift = chunks.bit_length() - 1
    masks = [flag(own == o, jnp.float32) for o in range(groups)]
    hits = jnp.concatenate(masks, axis=0).astype(jnp.bfloat16)
    square = (SEG, SEG)
    within = mxu(hits, flag(iota(square, 0) < iota(square, 1)))
    tallies = mxu(hits, jnp.ones(square, jnp.bfloat16)).astype(jnp.bfloat16)
    line, column = iota((high, high), 0), iota((high, high), 1)
    same = (line >> shift) == (column >> shift)
    ranks = within + mxu(flag(same & (column < line)), tallies)
    rank = sum(masks[o] * ranks[o * chunks:(o + 1) * chunks] for o in range(groups))
    rank = rank.astype(jnp.int32)
    relative = own ^ lax.axis_index("py")
    block, across = relative & (half - 1), relative >> (half.bit_length() - 1)
    slot_v[...] = block * block_rows + across * cap + rank
    slot_out[...] = (block * 2 + across) * cap + rank
    copy = pltpu.make_async_copy(slot_v, slot_s, sem)
    copy.start()

    log = blk.bit_length() - 1
    place = relative * nb + (rank >> log)
    lane = rank & (blk - 1)
    key, sten, itp = key_ref[...], sten_ref[...], itp_ref[...]
    tall = groups * nb
    meta = jnp.zeros((5 * tall, SEG), jnp.float32)
    for i in range(chunks):
        chosen = iota((tall, SEG), 0) == place[i:i + 1]
        parts = split_parts(itp[i:i + 1], 3)
        parts += [key[i:i + 1].astype(jnp.bfloat16), (sten[i:i + 1] + 1).astype(jnp.bfloat16)]
        left = [jnp.where(chosen, part.astype(jnp.float32), 0.0) for part in parts]
        right = flag(iota(square, 0) == lane[i:i + 1])
        meta = meta + lax.dot_general(
            jnp.concatenate(left, axis=0).astype(jnp.bfloat16), right,
            (((1,), (1,)), ((), ())), preferred_element_type=jnp.float32)
    shares = meta[:tall] + meta[tall:2 * tall] + meta[2 * tall:3 * tall]
    targets = meta[3 * tall:4 * tall] * LX + meta[4 * tall:]
    for v in range(groups):
        base = (v % half) * block_rows + 2 * cap + (v // half) * 2 * nb
        buffer[base:base + nb, :] = shares[v * nb:(v + 1) * nb]
        buffer[base + nb:base + 2 * nb, :] = targets[v * nb:(v + 1) * nb]

    copy.wait()
    loads[4].wait()

    def place_rows(g, carry):
        weights = w_ref[pl.ds(pl.multiple_of(g * 8, 8), 8), :]
        line, lane = g // 16, (g % 16) * 8
        for i in range(8):
            buffer[pl.ds(slot_s[line, lane + i], 1), :] = weights[i:i + 1]
        return carry

    lax.fori_loop(0, w_ref.shape[0] // 8, place_rows, 0)
    for store in start_copies([(buffer.at[pl.ds(k * block_rows, block_rows)], out)
                               for k, out in enumerate(outs)], out_sems):
        store.wait()


def pack_products_kernel(groups, cap, slot_ref, w_hbm, d_hbm, *rest):
    half = groups // 2
    outs, (w_ref, d_ref, buffer, sems, out_sems) = rest[:half], rest[half:]
    loads = start_copies([(w_hbm, w_ref), (d_hbm, d_ref)], sems)

    def clear(o, carry):
        start = pl.multiple_of(o * cap, 8)
        buffer[pl.ds(start, cap), :] = jnp.zeros((cap, SEG), jnp.float32)
        return carry

    lax.fori_loop(0, groups, clear, 0)

    for load in loads:
        load.wait()

    def place_rows(g, carry):
        start = pl.multiple_of(g * 8, 8)
        products = w_ref[pl.ds(start, 8), :] * d_ref[pl.ds(start, 8), :]
        line, lane = g // 16, (g % 16) * 8
        for i in range(8):
            buffer[pl.ds(slot_ref[line, lane + i], 1), :] = products[i:i + 1]
        return carry

    lax.fori_loop(0, w_ref.shape[0] // 8, place_rows, 0)
    for store in start_copies([(buffer.at[pl.ds(k * 2 * cap, 2 * cap)], out)
                               for k, out in enumerate(outs)], out_sems):
        store.wait()


def pack_swap_kernel(_, cy_hbm, c0_hbm, cx_hbm, swap_out, cy_ref, first, last, sems):
    width = c0_hbm.shape[2]
    for load in start_copies([
        (cy_hbm, cy_ref),
        (c0_hbm.at[:, :, pl.ds(0, SEG)], first.at[pl.ds(0, F)]),
        (cx_hbm.at[:, pl.ds(0, SEG)], first.at[F]),
        (c0_hbm.at[:, :, pl.ds(width - SEG, SEG)], last.at[pl.ds(0, F)]),
        (cx_hbm.at[:, pl.ds(width - SEG, SEG)], last.at[F]),
    ], sems):
        load.wait()
    columns = cy_ref.shape[1]
    cy = cy_ref[...]
    cy = jnp.where(iota(cy.shape, 1) == columns - 1, 0.0, cy)
    empty = jnp.zeros((LX, SEG), jnp.float32)
    me = lax.axis_index("px")
    nx = first.shape[1]
    for q in range(columns // width):
        low, top = q * width, (q + 1) * width
        tiles = [cy[:, t:t + SEG] for t in range(low, top, SEG)]
        before = cy[:, low - SEG:low] if low > 0 else empty
        after = cy[:, top:top + SEG] if top < columns else empty
        tiles.append(ends_tile(before, after))
        for t, tile in enumerate(tiles):
            swap_out[q, t * LX:(t + 1) * LX, :] = tile
        base = len(tiles) * LX
        for i in range(F + 1):
            swap_out[q, base + i * nx:base + (i + 1) * nx, :] = jnp.where(
                q < me, first[i], last[i])


def sum_rows(cap, blk, metas, acc_ref, terms):
    nb = cap // blk
    numbers = 1.0 + iota((ROWS, cap), 0).astype(jnp.float32)
    for source, meta in enumerate(metas):
        upper = jnp.concatenate(
            [jnp.broadcast_to(meta[i:i + 1], (SEG, SEG)).T[:blk] for i in range(nb)], axis=0)
        target = jnp.concatenate([meta[nb + i:nb + i + 1, :blk] for i in range(nb)], axis=1)
        hit = flag(numbers == target)
        values = jnp.concatenate(terms(source, upper), axis=1)
        part = mxu(jnp.concatenate([hit, hit], axis=1),
                   jnp.concatenate(split_parts(values, 2), axis=0))
        if source:
            acc_ref[...] += part
        else:
            acc_ref[...] = part


def cut_part(rows_ref, to, f, q, spans):
    per = to.shape[0] - 1

    def tile(b):
        start = pl.multiple_of((f * NB + b) * LX, LX)
        return rows_ref[pl.ds(start, LX), :]

    for j in range(per):
        to[j] = tile(q * per + j)
    before = tile(jnp.maximum(q * per - 1, 0))
    after = tile(jnp.minimum(q * per + per, NB - 1))
    to[per] = ends_tile(jnp.where(q > 0, before, 0.0), jnp.where(q < spans - 1, after, 0.0))


def weights_kernel(half, cap, blk, across, *rest):
    w_refs, (_, meta_out, diagonal_out, side_out, acc_ref) = rest[:half], rest[half:]
    nb = cap // blk
    for k, w_ref in enumerate(w_refs):
        meta_out[k] = w_ref[2 * cap:, :]
    rows = slice(across * cap, (across + 1) * cap)

    def terms(source, upper):
        lower = 1.0 - upper
        weights = w_refs[source][rows, :]
        lower_w, upper_w = lower * weights, upper * weights
        return [lower * lower_w, upper * lower_w, upper * upper_w]

    low = 2 * cap + across * 2 * nb
    sum_rows(cap, blk, [w_ref[low:low + 2 * nb, :] for w_ref in w_refs], acc_ref, terms)
    diagonal_out[...] = acc_ref[:, :SEG] + pltpu.roll(acc_ref[:, 2 * SEG:], 1, 0)
    side_out[...] = acc_ref[:, SEG:2 * SEG]


def sum_products(half, cap, blk, across, meta_ref, v_refs, acc_ref, sums_ref):
    nb = cap // blk
    rows = slice(across * cap, (across + 1) * cap)

    def terms(source, upper):
        products = v_refs[source][rows, :]
        return [(1.0 - upper) * products, upper * products]

    low = across * 2 * nb
    sum_rows(cap, blk, [meta_ref[k, low:low + 2 * nb, :] for k in range(half)], acc_ref, terms)
    sums_ref[...] = acc_ref[:, :SEG] + pltpu.roll(acc_ref[:, SEG:], 1, 0)


def products_kernel(half, cap, blk, meta_ref, d_ref, e_ref, far_d_ref, far_e_ref, *rest):
    v_refs, (out, token_out, *far_outs, acc_ref, sums_ref, far_ref, side) = (
        rest[:half], rest[half:])
    token_out[...] = jnp.zeros_like(token_out)
    spans = out.shape[0]
    sum_products(half, cap, blk, 1, meta_ref, v_refs, acc_ref, far_ref)
    me = lax.axis_index("px")
    for k, far_out in enumerate(far_outs):
        for f in range(F):
            cut_part(far_ref, far_out.at[f], f, me ^ k, spans)
    sum_products(half, cap, blk, 0, meta_ref, v_refs, acc_ref, sums_ref)
    side[0] = d_ref[...] + far_d_ref[...]
    side[1] = e_ref[...] + far_e_ref[...]
    for q in range(spans):
        for channel, rows_ref in enumerate((side.at[0], side.at[1], sums_ref)):
            for f in range(F):
                cut_part(rows_ref, out.at[q, channel * F + f], f, q, spans)


def x_lines(nx):
    return [pl.ds(i, 8, stride=nx // 8) for i in range(nx // 8)]


def shift_x(lines, distance):
    size = len(lines)
    moved = []
    for i in range(size):
        j = i + distance
        line = lines[j % size]
        moved.append(line if 0 <= j < size else pltpu.roll(line, 7 if j >= size else 1, 0))
    return moved


def shift_y(tiles, distance):
    if distance == 0:
        return tiles
    lane = iota(tiles[0].shape, 1)
    moved = [pltpu.roll(tile, -distance % SEG, 1) for tile in tiles]
    if distance > 0:
        return [jnp.where(lane >= SEG - distance, b, a) for a, b in zip(moved, moved[1:] + moved[:1])]
    return [jnp.where(lane < -distance, a, b) for a, b in zip(moved[-1:] + moved[:-1], moved)]


def sweep_diagonals(coeffs, shift):
    def each(function, *lists):
        return [function(*items) for items in zip(*lists)]

    back = functools.partial(shift, coeffs)
    main = each(lambda c, d: 1.0 - c - d, coeffs, back(-1))
    q0 = each(lambda a, c, d: a * a + c * c + d * d, main, coeffs, back(-1))
    q1 = each(lambda a, b, c: c * (a + b), main, shift(main, 1), coeffs)
    q2 = each(lambda c, d: c * d, coeffs, back(1))
    up0, up1, up2 = shift(q0, 1), shift(q1, 1), shift(q2, 1)
    low1, low2 = shift(q1, -1), shift(q2, -1)
    r0 = each(lambda a, b, c, d, e: a * a + b * b + c * c + d * d + e * e,
              q0, q1, low1, q2, shift(q2, -2))
    r1 = each(lambda a, b, c, d, e, f, g: a * b + c * (d + e) + f * g,
              low1, low2, q1, q0, up0, q2, up1)
    r2 = each(lambda a, b, c, d, e: a * (b + c) + d * e, q2, q0, shift(q0, 2), q1, up1)
    r3 = each(lambda a, b, c, d: a * b + c * d, q1, up2, q2, shift(q1, 2))
    r4 = each(lambda a, b: a * b, q2, shift(q2, 2))
    return [r0, r1, r2, r3, r4]


def make_x_diagonals(out, cx_ref):
    tiles, nx, _ = cx_ref.shape
    picks = x_lines(nx)
    for t in range(tiles):
        coeffs = [cx_ref[t, pick, :] for pick in picks]
        for d, lines in enumerate(sweep_diagonals(coeffs, shift_x)):
            for pick, line in zip(picks, lines):
                out[d, t, pick, :] = line


def make_y_diagonals(out, cy_ref):
    tiles, nx, _ = cy_ref.shape
    for low in range(0, nx, 8):
        rows = slice(low, low + 8)
        coeffs = [cy_ref[t, rows, :] for t in range(tiles)]
        for d, parts in enumerate(sweep_diagonals(coeffs, shift_y)):
            for t, part in enumerate(parts):
                out[d, t, rows, :] = part


def banded(diagonals, values, shift):
    total = [c * v for c, v in zip(diagonals[0], values)]
    for d in range(1, REACH + 1):
        above = [c * v for c, v in zip(diagonals[d], shift(values, d))]
        below = shift([c * v for c, v in zip(diagonals[d], values)], -d)
        total = [a + (b + c) for a, b, c in zip(total, above, below)]
    return total


def sweep_x_into(to_refs, from_refs, x_ref, plus_refs=None, sign=1.0):
    count, tiles, nx, _ = x_ref.shape
    picks = x_lines(nx)
    for t in range(tiles):
        diagonals = [[x_ref[d, t, pick, :] for pick in picks] for d in range(count)]
        for i, from_ref in enumerate(from_refs):
            values = [from_ref[t, pick, :] for pick in picks]
            for pick, value in zip(picks, banded(diagonals, values, shift_x)):
                if plus_refs is not None:
                    value = value + sign * plus_refs[i][t, pick, :]
                to_refs[i][t, pick, :] = value


def sweep_y_into(to_refs, from_refs, y_ref):
    count, tiles, nx, _ = y_ref.shape
    for low in range(0, nx, 8):
        rows = slice(low, low + 8)
        diagonals = [[y_ref[d, t, rows, :] for t in range(tiles)] for d in range(count)]
        for to_ref, from_ref in zip(to_refs, from_refs):
            values = [from_ref[t, rows, :] for t in range(tiles)]
            for t, value in enumerate(banded(diagonals, values, shift_y)):
                to_ref[t, rows, :] = value


def normal_into(to_refs, from_refs, diagonal_refs, side_refs, base_refs=None):
    tiles, nx, _ = from_refs[0].shape
    picks = x_lines(nx)
    for t in range(tiles):
        for i, from_ref in enumerate(from_refs):
            values = [from_ref[t, pick, :] for pick in picks]
            sides = [side_refs[i][t, pick, :] for pick in picks]
            low = [e * a for e, a in zip(sides, values)]
            low = [pltpu.roll(low[-1], 1, 0)] + low[:-1]
            after = values[1:] + [pltpu.roll(values[0], 7, 0)]
            for line, pick in enumerate(picks):
                result = (diagonal_refs[i][t, pick, :] * values[line] + sides[line] * after[line]
                          + low[line])
                if base_refs is not None:
                    result = base_refs[i][t, pick, :] - result
                to_refs[i][t, pick, :] = result


def of_fields(ref, start=0):
    return [ref.at[start + f] for f in range(F)]


def start_kernel(c0_ref, cx_ref, swap_ref, c0_out, cx_out, cy_out, u_out, token_out, x_ref, y_ref,
                 work):
    token_out[...] = jnp.zeros_like(token_out)
    nx = cx_ref.shape[0]
    spans, count = swap_ref.shape[0], cy_out.shape[0]
    me = lax.axis_index("px")
    for p in range(spans):
        for t in range(count):
            cy_out[t, p * LX:(p + 1) * LX, :] = swap_ref[p, t * LX:(t + 1) * LX, :]

    def beside(i):
        lines = slice(count * LX + i * nx, count * LX + (i + 1) * nx)
        before = swap_ref[jnp.maximum(me - 1, 0), lines, :]
        after = swap_ref[jnp.minimum(me + 1, spans - 1), lines, :]
        return ends_tile(jnp.where(me > 0, before, 0.0), jnp.where(me < spans - 1, after, 0.0))

    for t in range(count - 1):
        tile = slice(t * SEG, (t + 1) * SEG)
        cx_out[t] = cx_ref[:, tile]
        for f in range(F):
            c0_out[f, t] = c0_ref[f, :, tile]
    cx_out[count - 1] = beside(F)
    cx_out[:, nx - 1:, :] = jnp.zeros((count, 1, SEG), jnp.float32)
    for f in range(F):
        c0_out[f, count - 1] = beside(f)
    make_x_diagonals(x_ref, cx_out)
    make_y_diagonals(y_ref, cy_out)
    sweep_x_into(of_fields(work), of_fields(c0_out), x_ref)
    sweep_y_into(of_fields(u_out), of_fields(work), y_ref)


def diagonals_kernel(_, cx_ref, cy_ref, x_out, y_out):
    make_x_diagonals(x_out, cx_ref)
    make_y_diagonals(y_out, cy_ref)


def join_kernel(spans, *rest):
    parts, out = rest[:spans], rest[spans]
    me = lax.axis_index("px")
    for k, part in enumerate(parts):
        rows = pl.ds(pl.multiple_of((me ^ k) * LX, LX), LX)
        for f in range(F):
            for t in range(out.shape[1]):
                out[f, t, rows, :] = part[f, t]


def solve_kernel(c0_ref, x_ref, y_ref, u_ref, obs_ref, far_ref, r_out, q_out, h_out, dots_out,
                 vec, coef, work):
    for p in range(obs_ref.shape[0]):
        rows = slice(p * LX, (p + 1) * LX)
        for channel in range(2 * F):
            coef[channel, :, rows, :] = obs_ref[p, channel]
        for f in range(F):
            coef[2 * F + f, :, rows, :] = obs_ref[p, 2 * F + f] + far_ref[f, :, rows, :]

    sides = (of_fields(coef), of_fields(coef, F))
    one, two, r, q, s, h = (of_fields(ref) for ref in (
        work.at[0], work.at[1], vec.at[0], vec.at[1], vec.at[2], h_out))
    normal_into(one, of_fields(u_ref), *sides, of_fields(coef, 2 * F))
    sweep_y_into(two, one, y_ref)
    sweep_x_into(r, two, x_ref, of_fields(c0_ref), -1.0)
    sweep_x_into(one, r, x_ref)
    sweep_y_into(two, one, y_ref)
    normal_into(one, two, *sides)
    sweep_y_into(two, one, y_ref)
    sweep_x_into(q, two, x_ref, r)
    sweep_x_into(one, q, x_ref)
    sweep_y_into(s, one, y_ref)
    normal_into(h, s, *sides)

    tiles, nx = vec.shape[2] - 1, vec.shape[3]
    sums = [jnp.zeros((8, SEG), jnp.float32) for _ in range(4)]
    for f in range(F):
        for t in range(tiles):
            r_out[f, :, t * SEG:(t + 1) * SEG] = vec[0, f, t]
            q_out[f, :, t * SEG:(t + 1) * SEG] = vec[1, f, t]
            for low in range(0, nx, 8):
                lines = slice(low, low + 8)
                r, q, s = (vec[i, f, t, lines, :] for i in range(3))
                for i, product in enumerate((r * r, r * q, q * q, s * h_out[f, t, lines, :])):
                    sums[i] = sums[i] + product
    dots = jnp.zeros((1, SEG), jnp.float32)
    for i, total in enumerate(sums):
        line = jnp.sum(total, axis=0, keepdims=True)
        for distance in (64, 32, 16):
            line = line + pltpu.roll(line, distance, 1)
        dots = jnp.where(iota((1, SEG), 1) // SPLIT == i, line, dots)
    dots_out[...] = jnp.broadcast_to(dots, dots_out.shape)


def last_kernel(h_ref, q_ref, x_ref, y_ref, qq_out, work):
    sweep_y_into(of_fields(work.at[0]), of_fields(h_ref), y_ref)
    sweep_x_into(of_fields(work.at[1]), of_fields(work.at[0]), x_ref)
    for f in range(F):
        for t in range(work.shape[2] - 1):
            tile = slice(t * SEG, (t + 1) * SEG)
            qq_out[f, :, tile] = q_ref[f, :, tile] + work[1, f, t]


def finish_kernel(dots_ref, c0_ref, r_ref, q_ref, qq_ref, control_out, residual_out):
    dots = jnp.sum(dots_ref[...], axis=0)
    lane = iota((1, SEG), 1)
    rr, rq, qq2, energy = (pltpu.roll(dots, (SEG - i * SPLIT) % SEG, 1) for i in range(4))

    def total(line):
        return jnp.sum(jnp.where(lane < SPLIT, line, 0.0), axis=1, keepdims=True)

    rr_sum = total(rr)
    alpha = rr_sum / total(rq)
    new_sum = total(rr - 2.0 * alpha * rq + alpha * alpha * qq2)
    more = 1.0 + new_sum / rr_sum
    curve = total(more * more * rq - 2.0 * more * alpha * qq2 + alpha * alpha * (qq2 + energy))
    second = new_sum / curve
    first_weight = alpha + second * more
    both = alpha * second
    for f in range(F):
        r, q = r_ref[f], q_ref[f]
        control_out[f] = c0_ref[f] + first_weight * r - both * q
        residual_out[f] = r - first_weight * q + both * qq_ref[f]


def call(kernel, out_shape, scratch=(), in_specs=None, out_specs=None, limit=VMEM_BYTES,
         weight=1):
    params = {"in_specs": in_specs, "out_specs": out_specs}
    return pl.pallas_call(
        kernel,
        out_shape=out_shape,
        scratch_shapes=list(scratch),
        compiler_params=pltpu.CompilerParams(vmem_limit_bytes=limit),
        cost_estimate=pl.CostEstimate(flops=weight, bytes_accessed=weight, transcendentals=0),
        **{name: value for name, value in params.items() if value is not None},
    )


def f32(*shape):
    return jax.ShapeDtypeStruct(shape, jnp.float32)


def vmem(*shape, kind=jnp.float32):
    return pltpu.VMEM(shape, kind)


def shards(
    control_start, coef_x, coef_y, innovation, obs_weight, interp, obs_owner, cell_key, stencil
):
    groups, spans = lax.axis_size("py"), lax.axis_size("px")
    half = groups // 2
    rows = innovation.shape[0]
    cap = 3 * rows // groups
    blk = SEG if cap % SEG == 0 else HALF
    meta_rows = -(-4 * (cap // blk) // 8) * 8
    block_rows = 2 * cap + meta_rows
    chunks = rows // SEG
    nx, width = control_start.shape[2], control_start.shape[3]
    tiles = width // SEG + 1
    c0, cx = control_start[:, 0], coef_x[0]
    hbm, local, scalars = (
        pl.BlockSpec(memory_space=s) for s in (pltpu.HBM, pltpu.VMEM, pltpu.SMEM))
    ints = vmem(chunks, SEG, kind=jnp.int32)
    dma = pltpu.SemaphoreType.DMA

    def to_half(block, k):
        return lax.ppermute(block, "py", [(i, i ^ k) for i in range(groups)])

    def across(parts):
        return [
            lax.ppermute(parts[k], ("px", "py"), [
                (i * groups + j, (i ^ k) * groups + (j ^ half))
                for i in range(spans) for j in range(groups)])
            for k in range(spans)]

    *w_blocks, slots = call(
        functools.partial(pack_weights_kernel, groups, cap, blk, block_rows),
        (f32(block_rows, SEG),) * half + (jax.ShapeDtypeStruct((chunks, SEG), jnp.int32),),
        [ints, ints, ints, vmem(chunks, SEG), vmem(rows, SEG), vmem(half * block_rows, SEG), ints,
         pltpu.SMEM((chunks, SEG), jnp.int32), dma((5,)), dma((half,)), dma],
        [hbm] * 5,
        (hbm,) * half + (local,),
        limit=PACK_BYTES,
    )(
        obs_owner.reshape(chunks, SEG), cell_key.reshape(chunks, SEG),
        stencil.reshape(chunks, SEG), interp.reshape(chunks, SEG), obs_weight,
    )
    v_blocks = list(call(
        functools.partial(pack_products_kernel, groups, cap),
        (f32(2 * cap, SEG),) * half,
        [vmem(rows, SEG), vmem(rows, SEG), vmem(groups * cap, SEG), dma((2,)), dma((half,))],
        [scalars] + [hbm] * 2,
        (hbm,) * half,
        limit=PACK_BYTES,
    )(slots, obs_weight, innovation))
    w_blocks[1:] = [to_half(w_blocks[k], k) for k in range(1, half)]
    w_blocks[1], *v_blocks[1:] = lax.optimization_barrier((w_blocks[1], *v_blocks[1:]))
    v_blocks[1:] = [to_half(v_blocks[k], k) for k in range(1, half)]

    swap = call(
        pack_swap_kernel,
        f32(spans, LX * tiles + (F + 1) * nx, SEG),
        [vmem(*coef_y.shape[1:]), vmem(F + 1, nx, SEG), vmem(F + 1, nx, SEG), dma((5,))],
        [local] + [hbm] * 3,
        limit=PACK_BYTES,
    )(slots, coef_y[0], c0, cx)
    swap = lax.all_to_all(swap, "px", split_axis=0, concat_axis=0, tiled=True)
    c0_ext, cx_ext, cy_ext, u_ext, token = call(
        start_kernel,
        (f32(F, tiles, nx, SEG), f32(tiles, nx, SEG), f32(tiles, nx, SEG), f32(F, tiles, nx, SEG),
         f32(8, SEG)),
        [vmem(REACH + 1, tiles, nx, SEG), vmem(REACH + 1, tiles, nx, SEG),
         vmem(F, tiles, nx, SEG)],
    )(c0, cx, swap)

    def sum_weights(side, token, weight):
        return call(
            functools.partial(weights_kernel, half, cap, blk, side),
            (f32(half, meta_rows, SEG),) + (f32(ROWS, SEG),) * 2,
            [vmem(ROWS, 3 * SEG)],
            weight=weight,
        )(*w_blocks, token)

    meta, *side_across = sum_weights(1, w_blocks[0], FIRST)
    side_across = [to_half(values, half) for values in side_across]
    meta, *side = sum_weights(0, token, 1)
    parts, token, *sums_across = call(
        functools.partial(products_kernel, half, cap, blk),
        (f32(spans, 3 * F, tiles, LX, SEG), f32(8, SEG)) + (f32(F, tiles, LX, SEG),) * spans,
        [vmem(ROWS, 2 * SEG), vmem(ROWS, SEG), vmem(ROWS, SEG), vmem(2, ROWS, SEG)],
    )(meta, *side, *side_across, *v_blocks)
    far_sums = call(
        functools.partial(join_kernel, spans), f32(F, tiles, nx, SEG), weight=JOIN,
    )(*across(sums_across))
    x_sweep, y_sweep = call(
        diagonals_kernel, (f32(REACH + 1, tiles, nx, SEG),) * 2)(token, cx_ext, cy_ext)
    parts = lax.all_to_all(parts, "px", split_axis=0, concat_axis=0, tiled=True)

    r, q, h, dots = call(
        solve_kernel,
        (f32(F, nx, width),) * 2 + (f32(F, tiles, nx, SEG), f32(groups * spans, 1, SEG)),
        [vmem(3, F, tiles, nx, SEG), vmem(3 * F, tiles, nx, SEG), vmem(2, F, tiles, nx, SEG)],
    )(c0_ext, x_sweep, y_sweep, u_ext, parts, far_sums)
    dots = lax.all_to_all(dots, ("px", "py"), split_axis=0, concat_axis=0, tiled=True)
    qq = call(last_kernel, f32(F, nx, width), [vmem(2, F, tiles, nx, SEG)])(
        h, q, x_sweep, y_sweep)
    control, residual = call(finish_kernel, (f32(F, nx, width),) * 2)(dots, c0, r, q, qq)
    return control[:, None], residual[:, None]


def solution(mesh):
    return jax.shard_map(
        shards,
        mesh=mesh,
        in_specs=(
            P(None, "py", None, "px"),
            P("py", None, "px"),
            P("py", "px", None),
            P(("px", "py"), None),
            P(("px", "py"), None),
            P(("px", "py")),
            P(("px", "py"), None),
            P(("px", "py")),
            P(("px", "py")),
        ),
        out_specs=(P(None, "py", None, "px"), P(None, "py", None, "px")),
        check_vma=False,
    )
```

```python
import functools

import jax
import jax.numpy as jnp
from jax import lax
from jax.experimental import pallas as pl
from jax.experimental.pallas import tpu as pltpu
from jax.sharding import PartitionSpec as P

F = 2
SEG = 128
M = 4
NB = 16
LX = 16
ROWS = F * NB * LX
HALF = SEG // 2
SPLIT = 16
X_TILES = 2
Y_LINES = 16
VMEM_BYTES = 32 * 1024 * 1024
PACK_BYTES = 60 * 1024 * 1024
FIRST = 100_000_000
JOIN = 100_000_000


def iota(shape, axis):
    return lax.broadcasted_iota(jnp.int32, shape, axis)


def flag(condition, kind=jnp.bfloat16):
    return jnp.where(condition, 1.0, 0.0).astype(kind)


def mxu(left, right):
    return jnp.dot(left, right, preferred_element_type=jnp.float32)


def split_parts(values, count):
    parts = []
    for _ in range(count):
        part = values.astype(jnp.bfloat16)
        parts.append(part)
        values = values - part.astype(jnp.float32)
    return parts


def ends_tile(before, after):
    return jnp.where(iota(after.shape, after.ndim - 1) < HALF, after, before)


def start_copies(pairs, sems):
    copies = [pltpu.make_async_copy(*pair, sems.at[i]) for i, pair in enumerate(pairs)]
    for copy in copies:
        copy.start()
    return copies


def pack_weights_kernel(groups, cap, blk, block_rows, own_hbm, key_hbm, sten_hbm, itp_hbm, w_hbm,
                        *rest):
    half = groups // 2
    outs, rest = rest[:half], rest[half:]
    (slot_out, own_ref, key_ref, sten_ref, itp_ref, w_ref, buffer, slot_v, slot_s, sems, out_sems,
     sem) = rest
    loads = start_copies([(own_hbm, own_ref), (key_hbm, key_ref), (sten_hbm, sten_ref),
                          (itp_hbm, itp_ref), (w_hbm, w_ref)], sems)

    def clear(k, carry):
        start = pl.multiple_of(k * block_rows, 8)
        buffer[pl.ds(start, block_rows), :] = jnp.zeros((block_rows, SEG), jnp.float32)
        return carry

    lax.fori_loop(0, half, clear, 0)

    for load in loads[:4]:
        load.wait()
    chunks = own_ref.shape[0]
    nb = cap // blk
    own = own_ref[...]
    high = groups * chunks
    shift = chunks.bit_length() - 1
    masks = [flag(own == o, jnp.float32) for o in range(groups)]
    hits = jnp.concatenate(masks, axis=0).astype(jnp.bfloat16)
    square = (SEG, SEG)
    within = mxu(hits, flag(iota(square, 0) < iota(square, 1)))
    tallies = mxu(hits, jnp.ones(square, jnp.bfloat16)).astype(jnp.bfloat16)
    line, column = iota((high, high), 0), iota((high, high), 1)
    same = (line >> shift) == (column >> shift)
    ranks = within + mxu(flag(same & (column < line)), tallies)
    rank = sum(masks[o] * ranks[o * chunks:(o + 1) * chunks] for o in range(groups))
    rank = rank.astype(jnp.int32)
    relative = own ^ lax.axis_index("py")
    block, across = relative & (half - 1), relative >> (half.bit_length() - 1)
    slot_v[...] = block * block_rows + across * cap + rank
    slot_out[...] = (block * 2 + across) * cap + rank
    copy = pltpu.make_async_copy(slot_v, slot_s, sem)
    copy.start()

    log = blk.bit_length() - 1
    place = relative * nb + (rank >> log)
    lane = rank & (blk - 1)
    key, sten, itp = key_ref[...], sten_ref[...], itp_ref[...]
    tall = groups * nb
    meta = jnp.zeros((5 * tall, SEG), jnp.float32)
    for i in range(chunks):
        chosen = iota((tall, SEG), 0) == place[i:i + 1]
        parts = split_parts(itp[i:i + 1], 3)
        parts += [key[i:i + 1].astype(jnp.bfloat16), (sten[i:i + 1] + 1).astype(jnp.bfloat16)]
        left = [jnp.where(chosen, part.astype(jnp.float32), 0.0) for part in parts]
        right = flag(iota(square, 0) == lane[i:i + 1])
        meta = meta + lax.dot_general(
            jnp.concatenate(left, axis=0).astype(jnp.bfloat16), right,
            (((1,), (1,)), ((), ())), preferred_element_type=jnp.float32)
    shares = meta[:tall] + meta[tall:2 * tall] + meta[2 * tall:3 * tall]
    targets = meta[3 * tall:4 * tall] * LX + meta[4 * tall:]
    for v in range(groups):
        base = (v % half) * block_rows + 2 * cap + (v // half) * 2 * nb
        buffer[base:base + nb, :] = shares[v * nb:(v + 1) * nb]
        buffer[base + nb:base + 2 * nb, :] = targets[v * nb:(v + 1) * nb]

    copy.wait()
    loads[4].wait()

    def place_rows(g, carry):
        weights = w_ref[pl.ds(pl.multiple_of(g * 8, 8), 8), :]
        line, lane = g // 16, (g % 16) * 8
        for i in range(8):
            buffer[pl.ds(slot_s[line, lane + i], 1), :] = weights[i:i + 1]
        return carry

    lax.fori_loop(0, w_ref.shape[0] // 8, place_rows, 0)
    for store in start_copies([(buffer.at[pl.ds(k * block_rows, block_rows)], out)
                               for k, out in enumerate(outs)], out_sems):
        store.wait()


def pack_products_kernel(groups, cap, slot_ref, w_hbm, d_hbm, *rest):
    half = groups // 2
    outs, (w_ref, d_ref, buffer, sems, out_sems) = rest[:half], rest[half:]
    loads = start_copies([(w_hbm, w_ref), (d_hbm, d_ref)], sems)

    def clear(o, carry):
        start = pl.multiple_of(o * cap, 8)
        buffer[pl.ds(start, cap), :] = jnp.zeros((cap, SEG), jnp.float32)
        return carry

    lax.fori_loop(0, groups, clear, 0)

    for load in loads:
        load.wait()

    def place_rows(g, carry):
        start = pl.multiple_of(g * 8, 8)
        products = w_ref[pl.ds(start, 8), :] * d_ref[pl.ds(start, 8), :]
        line, lane = g // 16, (g % 16) * 8
        for i in range(8):
            buffer[pl.ds(slot_ref[line, lane + i], 1), :] = products[i:i + 1]
        return carry

    lax.fori_loop(0, w_ref.shape[0] // 8, place_rows, 0)
    for store in start_copies([(buffer.at[pl.ds(k * 2 * cap, 2 * cap)], out)
                               for k, out in enumerate(outs)], out_sems):
        store.wait()


def pack_swap_kernel(_, cy_hbm, c0_hbm, cx_hbm, swap_out, cy_ref, first, last, sems):
    width = c0_hbm.shape[2]
    for load in start_copies([
        (cy_hbm, cy_ref),
        (c0_hbm.at[:, :, pl.ds(0, SEG)], first.at[pl.ds(0, F)]),
        (cx_hbm.at[:, pl.ds(0, SEG)], first.at[F]),
        (c0_hbm.at[:, :, pl.ds(width - SEG, SEG)], last.at[pl.ds(0, F)]),
        (cx_hbm.at[:, pl.ds(width - SEG, SEG)], last.at[F]),
    ], sems):
        load.wait()
    columns = cy_ref.shape[1]
    cy = cy_ref[...]
    cy = jnp.where(iota(cy.shape, 1) == columns - 1, 0.0, cy)
    empty = jnp.zeros((LX, SEG), jnp.float32)
    me = lax.axis_index("px")
    nx = first.shape[1]
    for q in range(columns // width):
        low, top = q * width, (q + 1) * width
        tiles = [cy[:, t:t + SEG] for t in range(low, top, SEG)]
        before = cy[:, low - SEG:low] if low > 0 else empty
        after = cy[:, top:top + SEG] if top < columns else empty
        tiles.append(ends_tile(before, after))
        for t, tile in enumerate(tiles):
            swap_out[q, t * LX:(t + 1) * LX, :] = tile
        base = len(tiles) * LX
        for i in range(F + 1):
            swap_out[q, base + i * nx:base + (i + 1) * nx, :] = jnp.where(
                q < me, first[i], last[i])


def sum_rows(cap, blk, metas, acc_ref, terms):
    nb = cap // blk
    numbers = 1.0 + iota((ROWS, cap), 0).astype(jnp.float32)
    for source, meta in enumerate(metas):
        upper = jnp.concatenate(
            [jnp.broadcast_to(meta[i:i + 1], (SEG, SEG)).T[:blk] for i in range(nb)], axis=0)
        target = jnp.concatenate([meta[nb + i:nb + i + 1, :blk] for i in range(nb)], axis=1)
        hit = flag(numbers == target)
        values = jnp.concatenate(terms(source, upper), axis=1)
        part = mxu(jnp.concatenate([hit, hit], axis=1),
                   jnp.concatenate(split_parts(values, 2), axis=0))
        if source:
            acc_ref[...] += part
        else:
            acc_ref[...] = part


def cut_part(rows_ref, to, f, q, spans):
    per = to.shape[0] - 1

    def tile(b):
        start = pl.multiple_of((f * NB + b) * LX, LX)
        return rows_ref[pl.ds(start, LX), :]

    for j in range(per):
        to[j] = tile(q * per + j)
    before = tile(jnp.maximum(q * per - 1, 0))
    after = tile(jnp.minimum(q * per + per, NB - 1))
    to[per] = ends_tile(jnp.where(q > 0, before, 0.0), jnp.where(q < spans - 1, after, 0.0))


def weights_kernel(half, cap, blk, across, *rest):
    w_refs, (_, meta_out, diagonal_out, side_out, acc_ref) = rest[:half], rest[half:]
    nb = cap // blk
    for k, w_ref in enumerate(w_refs):
        meta_out[k] = w_ref[2 * cap:, :]
    rows = slice(across * cap, (across + 1) * cap)

    def terms(source, upper):
        lower = 1.0 - upper
        weights = w_refs[source][rows, :]
        lower_w, upper_w = lower * weights, upper * weights
        return [lower * lower_w, upper * lower_w, upper * upper_w]

    low = 2 * cap + across * 2 * nb
    sum_rows(cap, blk, [w_ref[low:low + 2 * nb, :] for w_ref in w_refs], acc_ref, terms)
    diagonal_out[...] = acc_ref[:, :SEG] + pltpu.roll(acc_ref[:, 2 * SEG:], 1, 0)
    side_out[...] = acc_ref[:, SEG:2 * SEG]


def sum_products(half, cap, blk, across, meta_ref, v_refs, acc_ref, sums_ref):
    nb = cap // blk
    rows = slice(across * cap, (across + 1) * cap)

    def terms(source, upper):
        products = v_refs[source][rows, :]
        return [(1.0 - upper) * products, upper * products]

    low = across * 2 * nb
    sum_rows(cap, blk, [meta_ref[k, low:low + 2 * nb, :] for k in range(half)], acc_ref, terms)
    sums_ref[...] = acc_ref[:, :SEG] + pltpu.roll(acc_ref[:, SEG:], 1, 0)


def products_kernel(half, cap, blk, meta_ref, d_ref, e_ref, far_d_ref, far_e_ref, *rest):
    v_refs, (out, *far_outs, acc_ref, sums_ref, far_ref, side) = rest[:half], rest[half:]
    spans = out.shape[0]
    sum_products(half, cap, blk, 1, meta_ref, v_refs, acc_ref, far_ref)
    me = lax.axis_index("px")
    for k, far_out in enumerate(far_outs):
        for f in range(F):
            cut_part(far_ref, far_out.at[f], f, me ^ k, spans)
    sum_products(half, cap, blk, 0, meta_ref, v_refs, acc_ref, sums_ref)
    side[0] = d_ref[...] + far_d_ref[...]
    side[1] = e_ref[...] + far_e_ref[...]
    for q in range(spans):
        for channel, rows_ref in enumerate((side.at[0], side.at[1], sums_ref)):
            for f in range(F):
                cut_part(rows_ref, out.at[q, channel * F + f], f, q, spans)


def x_lines(nx):
    return [pl.ds(i, 8, stride=nx // 8) for i in range(nx // 8)]


def sweep_x_into(to_refs, from_refs, cx_ref, plus_refs=None, sign=1.0):
    tiles, nx, _ = cx_ref.shape
    picks = x_lines(nx)
    for start in range(0, tiles, X_TILES):
        group = range(start, min(start + X_TILES, tiles))
        chains = [(i, t) for t in group for i in range(len(from_refs))]
        coeffs = {t: [cx_ref[t, pick, :] for pick in picks] for t in group}
        wrapped = {t: pltpu.roll(coeffs[t][-1], 1, 0) for t in group}
        fields = {(i, t): [from_refs[i][t, pick, :] for pick in picks] for i, t in chains}
        for _ in range(M):
            for i, t in chains:
                values = fields[i, t]
                after = values[1:] + [pltpu.roll(values[0], 7, 0)]
                low = wrapped[t] * (values[0] - pltpu.roll(values[-1], 1, 0))
                flux = [c * (b - a) for c, a, b in zip(coeffs[t], values, after)]
                fields[i, t] = [a + f - g for a, f, g in zip(values, flux, [low] + flux[:-1])]
        for i, t in chains:
            for pick, value in zip(picks, fields[i, t]):
                if plus_refs is not None:
                    value = value + sign * plus_refs[i][t, pick, :]
                to_refs[i][t, pick, :] = value


def sweep_y_into(to_refs, from_refs, cy_ref):
    tiles, nx, _ = cy_ref.shape
    lane = iota((Y_LINES, SEG), 1)

    def next_cells(values):
        moved = [pltpu.roll(value, SEG - 1, 1) for value in values]
        return [jnp.where(lane == SEG - 1, b, a) for a, b in zip(moved, moved[1:] + moved[:1])]

    def previous_cells(values):
        moved = [pltpu.roll(value, 1, 1) for value in values]
        return [jnp.where(lane == 0, a, b) for a, b in zip(moved[-1:] + moved[:-1], moved)]

    for low in range(0, nx, Y_LINES):
        lines = slice(low, low + Y_LINES)
        coeffs = [cy_ref[t, lines, :] for t in range(tiles)]
        coeffs_low = previous_cells(coeffs)
        fields = [[ref[t, lines, :] for t in range(tiles)] for ref in from_refs]
        for _ in range(M):
            for i, values in enumerate(fields):
                after, before = next_cells(values), previous_cells(values)
                fields[i] = [
                    a + c * (b - a) - d * (a - e)
                    for a, b, c, d, e in zip(values, after, coeffs, coeffs_low, before)]
        for to_ref, values in zip(to_refs, fields):
            for t, value in enumerate(values):
                to_ref[t, lines, :] = value


def normal_into(to_refs, from_refs, diagonal_refs, side_refs, base_refs=None):
    tiles, nx, _ = from_refs[0].shape
    picks = x_lines(nx)
    for t in range(tiles):
        for i, from_ref in enumerate(from_refs):
            values = [from_ref[t, pick, :] for pick in picks]
            sides = [side_refs[i][t, pick, :] for pick in picks]
            low = [e * a for e, a in zip(sides, values)]
            low = [pltpu.roll(low[-1], 1, 0)] + low[:-1]
            after = values[1:] + [pltpu.roll(values[0], 7, 0)]
            for line, pick in enumerate(picks):
                result = (diagonal_refs[i][t, pick, :] * values[line] + sides[line] * after[line]
                          + low[line])
                if base_refs is not None:
                    result = base_refs[i][t, pick, :] - result
                to_refs[i][t, pick, :] = result


def of_fields(ref, start=0):
    return [ref.at[start + f] for f in range(F)]


def start_kernel(c0_ref, cx_ref, swap_ref, c0_out, cx_out, cy_out, u_out, token_out, work):
    token_out[...] = jnp.zeros_like(token_out)
    nx = cx_ref.shape[0]
    spans, count = swap_ref.shape[0], cy_out.shape[0]
    me = lax.axis_index("px")
    for p in range(spans):
        for t in range(count):
            cy_out[t, p * LX:(p + 1) * LX, :] = swap_ref[p, t * LX:(t + 1) * LX, :]

    def beside(i):
        lines = slice(count * LX + i * nx, count * LX + (i + 1) * nx)
        before = swap_ref[jnp.maximum(me - 1, 0), lines, :]
        after = swap_ref[jnp.minimum(me + 1, spans - 1), lines, :]
        return ends_tile(jnp.where(me > 0, before, 0.0), jnp.where(me < spans - 1, after, 0.0))

    for t in range(count - 1):
        tile = slice(t * SEG, (t + 1) * SEG)
        cx_out[t] = cx_ref[:, tile]
        for f in range(F):
            c0_out[f, t] = c0_ref[f, :, tile]
    cx_out[count - 1] = beside(F)
    cx_out[:, nx - 1:, :] = jnp.zeros((count, 1, SEG), jnp.float32)
    for f in range(F):
        c0_out[f, count - 1] = beside(f)
    sweep_x_into(of_fields(work), of_fields(c0_out), cx_out)
    sweep_y_into(of_fields(u_out), of_fields(work), cy_out)


def join_kernel(spans, *rest):
    parts, out = rest[:spans], rest[spans]
    me = lax.axis_index("px")
    for k, part in enumerate(parts):
        rows = pl.ds(pl.multiple_of((me ^ k) * LX, LX), LX)
        for f in range(F):
            for t in range(out.shape[1]):
                out[f, t, rows, :] = part[f, t]


def solve_kernel(c0_ref, cx_ref, cy_ref, u_ref, obs_ref, far_ref, r_out, q_out, h_out, dots_out,
                 vec, coef, work):
    for p in range(obs_ref.shape[0]):
        rows = slice(p * LX, (p + 1) * LX)
        for channel in range(2 * F):
            coef[channel, :, rows, :] = obs_ref[p, channel]
        for f in range(F):
            coef[2 * F + f, :, rows, :] = obs_ref[p, 2 * F + f] + far_ref[f, :, rows, :]

    sides = (of_fields(coef), of_fields(coef, F))
    one, two, r, q, s, h = (of_fields(ref) for ref in (
        work.at[0], work.at[1], vec.at[0], vec.at[1], vec.at[2], h_out))
    normal_into(one, of_fields(u_ref), *sides, of_fields(coef, 2 * F))
    sweep_y_into(two, one, cy_ref)
    sweep_x_into(r, two, cx_ref, of_fields(c0_ref), -1.0)
    sweep_x_into(one, r, cx_ref)
    sweep_y_into(two, one, cy_ref)
    normal_into(one, two, *sides)
    sweep_y_into(two, one, cy_ref)
    sweep_x_into(q, two, cx_ref, r)
    sweep_x_into(one, q, cx_ref)
    sweep_y_into(s, one, cy_ref)
    normal_into(h, s, *sides)

    tiles, nx = vec.shape[2] - 1, vec.shape[3]
    sums = [jnp.zeros((8, SEG), jnp.float32) for _ in range(4)]
    for f in range(F):
        for t in range(tiles):
            r_out[f, :, t * SEG:(t + 1) * SEG] = vec[0, f, t]
            q_out[f, :, t * SEG:(t + 1) * SEG] = vec[1, f, t]
            for low in range(0, nx, 8):
                lines = slice(low, low + 8)
                r, q, s = (vec[i, f, t, lines, :] for i in range(3))
                for i, product in enumerate((r * r, r * q, q * q, s * h_out[f, t, lines, :])):
                    sums[i] = sums[i] + product
    dots = jnp.zeros((1, SEG), jnp.float32)
    for i, total in enumerate(sums):
        line = jnp.sum(total, axis=0, keepdims=True)
        for distance in (64, 32, 16):
            line = line + pltpu.roll(line, distance, 1)
        dots = jnp.where(iota((1, SEG), 1) // SPLIT == i, line, dots)
    dots_out[...] = jnp.broadcast_to(dots, dots_out.shape)


def last_kernel(h_ref, q_ref, cx_ref, cy_ref, qq_out, work):
    sweep_y_into(of_fields(work.at[0]), of_fields(h_ref), cy_ref)
    sweep_x_into(of_fields(work.at[1]), of_fields(work.at[0]), cx_ref)
    for f in range(F):
        for t in range(work.shape[2] - 1):
            tile = slice(t * SEG, (t + 1) * SEG)
            qq_out[f, :, tile] = q_ref[f, :, tile] + work[1, f, t]


def finish_kernel(dots_ref, c0_ref, r_ref, q_ref, qq_ref, control_out, residual_out):
    dots = jnp.sum(dots_ref[...], axis=0)
    lane = iota((1, SEG), 1)
    rr, rq, qq2, energy = (pltpu.roll(dots, (SEG - i * SPLIT) % SEG, 1) for i in range(4))

    def total(line):
        return jnp.sum(jnp.where(lane < SPLIT, line, 0.0), axis=1, keepdims=True)

    rr_sum = total(rr)
    alpha = rr_sum / total(rq)
    new_sum = total(rr - 2.0 * alpha * rq + alpha * alpha * qq2)
    more = 1.0 + new_sum / rr_sum
    curve = total(more * more * rq - 2.0 * more * alpha * qq2 + alpha * alpha * (qq2 + energy))
    second = new_sum / curve
    first_weight = alpha + second * more
    both = alpha * second
    for f in range(F):
        r, q = r_ref[f], q_ref[f]
        control_out[f] = c0_ref[f] + first_weight * r - both * q
        residual_out[f] = r - first_weight * q + both * qq_ref[f]


def call(kernel, out_shape, scratch=(), in_specs=None, out_specs=None, limit=VMEM_BYTES,
         weight=1):
    params = {"in_specs": in_specs, "out_specs": out_specs}
    return pl.pallas_call(
        kernel,
        out_shape=out_shape,
        scratch_shapes=list(scratch),
        compiler_params=pltpu.CompilerParams(vmem_limit_bytes=limit),
        cost_estimate=pl.CostEstimate(flops=weight, bytes_accessed=weight, transcendentals=0),
        **{name: value for name, value in params.items() if value is not None},
    )


def f32(*shape):
    return jax.ShapeDtypeStruct(shape, jnp.float32)


def vmem(*shape, kind=jnp.float32):
    return pltpu.VMEM(shape, kind)


def shards(
    control_start, coef_x, coef_y, innovation, obs_weight, interp, obs_owner, cell_key, stencil
):
    groups, spans = lax.axis_size("py"), lax.axis_size("px")
    half = groups // 2
    rows = innovation.shape[0]
    cap = 3 * rows // groups
    blk = SEG if cap % SEG == 0 else HALF
    meta_rows = -(-4 * (cap // blk) // 8) * 8
    block_rows = 2 * cap + meta_rows
    chunks = rows // SEG
    nx, width = control_start.shape[2], control_start.shape[3]
    tiles = width // SEG + 1
    c0, cx = control_start[:, 0], coef_x[0]
    hbm, local, scalars = (
        pl.BlockSpec(memory_space=s) for s in (pltpu.HBM, pltpu.VMEM, pltpu.SMEM))
    ints = vmem(chunks, SEG, kind=jnp.int32)
    dma = pltpu.SemaphoreType.DMA

    def to_half(block, k):
        return lax.ppermute(block, "py", [(i, i ^ k) for i in range(groups)])

    def across(parts):
        return [
            lax.ppermute(parts[k], ("px", "py"), [
                (i * groups + j, (i ^ k) * groups + (j ^ half))
                for i in range(spans) for j in range(groups)])
            for k in range(spans)]

    *w_blocks, slots = call(
        functools.partial(pack_weights_kernel, groups, cap, blk, block_rows),
        (f32(block_rows, SEG),) * half + (jax.ShapeDtypeStruct((chunks, SEG), jnp.int32),),
        [ints, ints, ints, vmem(chunks, SEG), vmem(rows, SEG), vmem(half * block_rows, SEG), ints,
         pltpu.SMEM((chunks, SEG), jnp.int32), dma((5,)), dma((half,)), dma],
        [hbm] * 5,
        (hbm,) * half + (local,),
        limit=PACK_BYTES,
    )(
        obs_owner.reshape(chunks, SEG), cell_key.reshape(chunks, SEG),
        stencil.reshape(chunks, SEG), interp.reshape(chunks, SEG), obs_weight,
    )
    v_blocks = list(call(
        functools.partial(pack_products_kernel, groups, cap),
        (f32(2 * cap, SEG),) * half,
        [vmem(rows, SEG), vmem(rows, SEG), vmem(groups * cap, SEG), dma((2,)), dma((half,))],
        [scalars] + [hbm] * 2,
        (hbm,) * half,
        limit=PACK_BYTES,
    )(slots, obs_weight, innovation))
    w_blocks[1:] = [to_half(w_blocks[k], k) for k in range(1, half)]
    lead = half // 2
    w_blocks[lead], *v_blocks[1:] = lax.optimization_barrier((w_blocks[lead], *v_blocks[1:]))
    v_blocks[1:] = [to_half(v_blocks[k], k) for k in range(1, half)]

    swap = call(
        pack_swap_kernel,
        f32(spans, LX * tiles + (F + 1) * nx, SEG),
        [vmem(*coef_y.shape[1:]), vmem(F + 1, nx, SEG), vmem(F + 1, nx, SEG), dma((5,))],
        [local] + [hbm] * 3,
        limit=PACK_BYTES,
    )(slots, coef_y[0], c0, cx)
    swap = lax.all_to_all(swap, "px", split_axis=0, concat_axis=0, tiled=True)
    c0_ext, cx_ext, cy_ext, u_ext, token = call(
        start_kernel,
        (f32(F, tiles, nx, SEG), f32(tiles, nx, SEG), f32(tiles, nx, SEG), f32(F, tiles, nx, SEG),
         f32(8, SEG)),
        [vmem(F, tiles, nx, SEG)],
    )(c0, cx, swap)

    def sum_weights(side, token, weight):
        return call(
            functools.partial(weights_kernel, half, cap, blk, side),
            (f32(half, meta_rows, SEG),) + (f32(ROWS, SEG),) * 2,
            [vmem(ROWS, 3 * SEG)],
            weight=weight,
        )(*w_blocks, token)

    meta, *side_across = sum_weights(1, w_blocks[0], FIRST)
    side_across = [to_half(values, half) for values in side_across]
    meta, *side = sum_weights(0, token, 1)
    parts, *sums_across = call(
        functools.partial(products_kernel, half, cap, blk),
        (f32(spans, 3 * F, tiles, LX, SEG),) + (f32(F, tiles, LX, SEG),) * spans,
        [vmem(ROWS, 2 * SEG), vmem(ROWS, SEG), vmem(ROWS, SEG), vmem(2, ROWS, SEG)],
    )(meta, *side, *side_across, *v_blocks)
    far_sums = call(
        functools.partial(join_kernel, spans), f32(F, tiles, nx, SEG), weight=JOIN,
    )(*across(sums_across))
    parts = lax.all_to_all(parts, "px", split_axis=0, concat_axis=0, tiled=True)

    r, q, h, dots = call(
        solve_kernel,
        (f32(F, nx, width),) * 2 + (f32(F, tiles, nx, SEG), f32(groups * spans, 1, SEG)),
        [vmem(3, F, tiles, nx, SEG), vmem(3 * F, tiles, nx, SEG), vmem(2, F, tiles, nx, SEG)],
    )(c0_ext, cx_ext, cy_ext, u_ext, parts, far_sums)
    dots = lax.all_to_all(dots, ("px", "py"), split_axis=0, concat_axis=0, tiled=True)
    qq = call(last_kernel, f32(F, nx, width), [vmem(2, F, tiles, nx, SEG)])(
        h, q, cx_ext, cy_ext)
    control, residual = call(finish_kernel, (f32(F, nx, width),) * 2)(dots, c0, r, q, qq)
    return control[:, None], residual[:, None]


def solution(mesh):
    return jax.shard_map(
        shards,
        mesh=mesh,
        in_specs=(
            P(None, "py", None, "px"),
            P("py", None, "px"),
            P("py", "px", None),
            P(("px", "py"), None),
            P(("px", "py"), None),
            P(("px", "py")),
            P(("px", "py"), None),
            P(("px", "py")),
            P(("px", "py")),
        ),
        out_specs=(P(None, "py", None, "px"), P(None, "py", None, "px")),
        check_vma=False,
    )
```

```python
import functools

import jax
import jax.numpy as jnp
from jax import lax
from jax.experimental import pallas as pl
from jax.experimental.pallas import tpu as pltpu
from jax.sharding import PartitionSpec as P

F = 2
SEG = 128
M = 4
NB = 16
LX = 16
ROWS = F * NB * LX
HALF = SEG // 2
QUARTER = SEG // 4
SPLIT = 16
X_TILES = 2
Y_LINES = 16
VMEM_BYTES = 32 * 1024 * 1024
PACK_BYTES = 60 * 1024 * 1024
FIRST = 100_000_000
JOIN = 100_000_000


def iota(shape, axis):
    return lax.broadcasted_iota(jnp.int32, shape, axis)


def flag(condition, kind=jnp.bfloat16):
    return jnp.where(condition, 1.0, 0.0).astype(kind)


def mxu(left, right):
    return jnp.dot(left, right, preferred_element_type=jnp.float32)


def split_parts(values, count):
    parts = []
    for _ in range(count):
        part = values.astype(jnp.bfloat16)
        parts.append(part)
        values = values - part.astype(jnp.float32)
    return parts


def ends_tile(before, after):
    return jnp.where(iota(after.shape, after.ndim - 1) < HALF, after, before)


def start_copies(pairs, sems):
    copies = [pltpu.make_async_copy(*pair, sems.at[i]) for i, pair in enumerate(pairs)]
    for copy in copies:
        copy.start()
    return copies


def pack_weights_kernel(groups, cap, blk, block_rows, own_hbm, key_hbm, sten_hbm, itp_hbm, w_hbm,
                        *rest):
    half = groups // 2
    outs, rest = rest[:half], rest[half:]
    (slot_out, own_ref, key_ref, sten_ref, itp_ref, w_ref, buffer, slot_v, slot_s, sems, out_sems,
     sem) = rest
    loads = start_copies([(own_hbm, own_ref), (key_hbm, key_ref), (sten_hbm, sten_ref),
                          (itp_hbm, itp_ref), (w_hbm, w_ref)], sems)

    def clear(k, carry):
        start = pl.multiple_of(k * block_rows, 8)
        buffer[pl.ds(start, block_rows), :] = jnp.zeros((block_rows, SEG), jnp.float32)
        return carry

    lax.fori_loop(0, half, clear, 0)

    for load in loads[:4]:
        load.wait()
    chunks = own_ref.shape[0]
    nb = cap // blk
    own = own_ref[...]
    high = groups * chunks
    shift = chunks.bit_length() - 1
    masks = [flag(own == o, jnp.float32) for o in range(groups)]
    hits = jnp.concatenate(masks, axis=0).astype(jnp.bfloat16)
    square = (SEG, SEG)
    within = mxu(hits, flag(iota(square, 0) < iota(square, 1)))
    tallies = mxu(hits, jnp.ones(square, jnp.bfloat16)).astype(jnp.bfloat16)
    line, column = iota((high, high), 0), iota((high, high), 1)
    same = (line >> shift) == (column >> shift)
    ranks = within + mxu(flag(same & (column < line)), tallies)
    rank = sum(masks[o] * ranks[o * chunks:(o + 1) * chunks] for o in range(groups))
    rank = rank.astype(jnp.int32)
    relative = own ^ lax.axis_index("py")
    block, across = relative & (half - 1), relative >> (half.bit_length() - 1)
    slot_v[...] = block * block_rows + across * cap + rank
    slot_out[...] = (block * 2 + across) * cap + rank
    copy = pltpu.make_async_copy(slot_v, slot_s, sem)
    copy.start()

    log = blk.bit_length() - 1
    place = relative * nb + (rank >> log)
    lane = rank & (blk - 1)
    key, sten, itp = key_ref[...], sten_ref[...], itp_ref[...]
    tall = groups * nb
    meta = jnp.zeros((5 * tall, SEG), jnp.float32)
    for i in range(chunks):
        chosen = iota((tall, SEG), 0) == place[i:i + 1]
        parts = split_parts(itp[i:i + 1], 3)
        parts += [key[i:i + 1].astype(jnp.bfloat16), (sten[i:i + 1] + 1).astype(jnp.bfloat16)]
        left = [jnp.where(chosen, part.astype(jnp.float32), 0.0) for part in parts]
        right = flag(iota(square, 0) == lane[i:i + 1])
        meta = meta + lax.dot_general(
            jnp.concatenate(left, axis=0).astype(jnp.bfloat16), right,
            (((1,), (1,)), ((), ())), preferred_element_type=jnp.float32)
    shares = meta[:tall] + meta[tall:2 * tall] + meta[2 * tall:3 * tall]
    targets = meta[3 * tall:4 * tall] * LX + meta[4 * tall:]
    for v in range(groups):
        base = (v % half) * block_rows + 2 * cap + (v // half) * 2 * nb
        buffer[base:base + nb, :] = shares[v * nb:(v + 1) * nb]
        buffer[base + nb:base + 2 * nb, :] = targets[v * nb:(v + 1) * nb]

    copy.wait()
    loads[4].wait()

    def place_rows(g, carry):
        weights = w_ref[pl.ds(pl.multiple_of(g * 8, 8), 8), :]
        line, lane = g // 16, (g % 16) * 8
        for i in range(8):
            buffer[pl.ds(slot_s[line, lane + i], 1), :] = weights[i:i + 1]
        return carry

    lax.fori_loop(0, w_ref.shape[0] // 8, place_rows, 0)
    for store in start_copies([(buffer.at[pl.ds(k * block_rows, block_rows)], out)
                               for k, out in enumerate(outs)], out_sems):
        store.wait()


def pack_products_kernel(groups, cap, slot_ref, w_hbm, d_hbm, *rest):
    half = groups // 2
    outs, (w_ref, d_ref, buffer, sems, out_sems) = rest[:half], rest[half:]
    loads = start_copies([(w_hbm, w_ref), (d_hbm, d_ref)], sems)

    def clear(o, carry):
        start = pl.multiple_of(o * cap, 8)
        buffer[pl.ds(start, cap), :] = jnp.zeros((cap, SEG), jnp.float32)
        return carry

    lax.fori_loop(0, groups, clear, 0)

    for load in loads:
        load.wait()

    def place_rows(g, carry):
        start = pl.multiple_of(g * 8, 8)
        products = w_ref[pl.ds(start, 8), :] * d_ref[pl.ds(start, 8), :]
        line, lane = g // 16, (g % 16) * 8
        for i in range(8):
            buffer[pl.ds(slot_ref[line, lane + i], 1), :] = products[i:i + 1]
        return carry

    lax.fori_loop(0, w_ref.shape[0] // 8, place_rows, 0)
    for store in start_copies([(buffer.at[pl.ds(k * 2 * cap, 2 * cap)], out)
                               for k, out in enumerate(outs)], out_sems):
        store.wait()


def pack_swap_kernel(_, cy_hbm, c0_hbm, cx_hbm, swap_out, cy_ref, first, last, sems):
    width = c0_hbm.shape[2]
    for load in start_copies([
        (cy_hbm, cy_ref),
        (c0_hbm.at[:, :, pl.ds(0, SEG)], first.at[pl.ds(0, F)]),
        (cx_hbm.at[:, pl.ds(0, SEG)], first.at[F]),
        (c0_hbm.at[:, :, pl.ds(width - SEG, SEG)], last.at[pl.ds(0, F)]),
        (cx_hbm.at[:, pl.ds(width - SEG, SEG)], last.at[F]),
    ], sems):
        load.wait()
    columns = cy_ref.shape[1]
    cy = cy_ref[...]
    cy = jnp.where(iota(cy.shape, 1) == columns - 1, 0.0, cy)
    empty = jnp.zeros((LX, SEG), jnp.float32)
    me = lax.axis_index("px")
    nx = first.shape[1]
    for q in range(columns // width):
        low, top = q * width, (q + 1) * width
        tiles = [cy[:, t:t + SEG] for t in range(low, top, SEG)]
        before = cy[:, low - SEG:low] if low > 0 else empty
        after = cy[:, top:top + SEG] if top < columns else empty
        tiles.append(ends_tile(before, after))
        for t, tile in enumerate(tiles):
            swap_out[q, t * LX:(t + 1) * LX, :] = tile
        base = len(tiles) * LX
        for i in range(F + 1):
            swap_out[q, base + i * nx:base + (i + 1) * nx, :] = jnp.where(
                q < me, first[i], last[i])


def sum_rows(cap, blk, metas, acc_ref, terms):
    nb = cap // blk
    numbers = 1.0 + iota((ROWS, cap), 0).astype(jnp.float32)
    for source, meta in enumerate(metas):
        upper = jnp.concatenate(
            [jnp.broadcast_to(meta[i:i + 1], (SEG, SEG)).T[:blk] for i in range(nb)], axis=0)
        target = jnp.concatenate([meta[nb + i:nb + i + 1, :blk] for i in range(nb)], axis=1)
        hit = flag(numbers == target)
        values = jnp.concatenate(terms(source, upper), axis=1)
        part = mxu(jnp.concatenate([hit, hit], axis=1),
                   jnp.concatenate(split_parts(values, 2), axis=0))
        if source:
            acc_ref[...] += part
        else:
            acc_ref[...] = part


def cut_part(rows_ref, to, f, q, spans):
    per = to.shape[0] - 1

    def tile(b):
        start = pl.multiple_of((f * NB + b) * LX, LX)
        return rows_ref[pl.ds(start, LX), :]

    for j in range(per):
        to[j] = tile(q * per + j)
    before = tile(jnp.maximum(q * per - 1, 0))
    after = tile(jnp.minimum(q * per + per, NB - 1))
    to[per] = ends_tile(jnp.where(q > 0, before, 0.0), jnp.where(q < spans - 1, after, 0.0))


def cut_far_part(rows_ref, to, q, spans):
    per = (to.shape[0] - 1) // F

    def tile(f, b):
        start = pl.multiple_of((f * NB + b) * LX, LX)
        return rows_ref[pl.ds(start, LX), :]

    beside = []
    for f in range(F):
        for j in range(per):
            to[f * per + j] = tile(f, q * per + j)
        before = tile(f, jnp.maximum(q * per - 1, 0))
        after = tile(f, jnp.minimum(q * per + per, NB - 1))
        beside.append(ends_tile(jnp.where(q > 0, before, 0.0),
                                jnp.where(q < spans - 1, after, 0.0)))
    lane = iota((LX, SEG), 1)
    inner = jnp.where(lane < HALF, pltpu.roll(beside[1], QUARTER, 1),
                      pltpu.roll(beside[1], SEG - QUARTER, 1))
    to[F * per] = jnp.where((lane >= QUARTER) & (lane < SEG - QUARTER), inner, beside[0])


def weights_kernel(half, cap, blk, across, *rest):
    w_refs, (_, meta_out, diagonal_out, side_out, acc_ref) = rest[:half], rest[half:]
    nb = cap // blk
    for k, w_ref in enumerate(w_refs):
        meta_out[k] = w_ref[2 * cap:, :]
    rows = slice(across * cap, (across + 1) * cap)

    def terms(source, upper):
        lower = 1.0 - upper
        weights = w_refs[source][rows, :]
        lower_w, upper_w = lower * weights, upper * weights
        return [lower * lower_w, upper * lower_w, upper * upper_w]

    low = 2 * cap + across * 2 * nb
    sum_rows(cap, blk, [w_ref[low:low + 2 * nb, :] for w_ref in w_refs], acc_ref, terms)
    diagonal_out[...] = acc_ref[:, :SEG] + pltpu.roll(acc_ref[:, 2 * SEG:], 1, 0)
    side_out[...] = acc_ref[:, SEG:2 * SEG]


def sum_products(half, cap, blk, across, meta_ref, v_refs, acc_ref, sums_ref):
    nb = cap // blk
    rows = slice(across * cap, (across + 1) * cap)

    def terms(source, upper):
        products = v_refs[source][rows, :]
        return [(1.0 - upper) * products, upper * products]

    low = across * 2 * nb
    sum_rows(cap, blk, [meta_ref[k, low:low + 2 * nb, :] for k in range(half)], acc_ref, terms)
    sums_ref[...] = acc_ref[:, :SEG] + pltpu.roll(acc_ref[:, SEG:], 1, 0)


def products_kernel(half, cap, blk, meta_ref, d_ref, e_ref, far_d_ref, far_e_ref, *rest):
    v_refs, (out, *far_outs, acc_ref, sums_ref, far_ref, side) = rest[:half], rest[half:]
    spans = out.shape[0]
    sum_products(half, cap, blk, 1, meta_ref, v_refs, acc_ref, far_ref)
    me = lax.axis_index("px")
    for k, far_out in enumerate(far_outs):
        cut_far_part(far_ref, far_out, me ^ k, spans)
    sum_products(half, cap, blk, 0, meta_ref, v_refs, acc_ref, sums_ref)
    side[0] = d_ref[...] + far_d_ref[...]
    side[1] = e_ref[...] + far_e_ref[...]
    for q in range(spans):
        for channel, rows_ref in enumerate((side.at[0], side.at[1], sums_ref)):
            for f in range(F):
                cut_part(rows_ref, out.at[q, channel * F + f], f, q, spans)


def x_lines(nx):
    return [pl.ds(i, 8, stride=nx // 8) for i in range(nx // 8)]


def sweep_x_into(to_refs, from_refs, cx_ref, plus_refs=None, sign=1.0):
    tiles, nx, _ = cx_ref.shape
    picks = x_lines(nx)
    for start in range(0, tiles, X_TILES):
        group = range(start, min(start + X_TILES, tiles))
        chains = [(i, t) for t in group for i in range(len(from_refs))]
        coeffs = {t: [cx_ref[t, pick, :] for pick in picks] for t in group}
        wrapped = {t: pltpu.roll(coeffs[t][-1], 1, 0) for t in group}
        fields = {(i, t): [from_refs[i][t, pick, :] for pick in picks] for i, t in chains}
        for _ in range(M):
            for i, t in chains:
                values = fields[i, t]
                after = values[1:] + [pltpu.roll(values[0], 7, 0)]
                low = wrapped[t] * (values[0] - pltpu.roll(values[-1], 1, 0))
                flux = [c * (b - a) for c, a, b in zip(coeffs[t], values, after)]
                fields[i, t] = [a + f - g for a, f, g in zip(values, flux, [low] + flux[:-1])]
        for i, t in chains:
            for pick, value in zip(picks, fields[i, t]):
                if plus_refs is not None:
                    value = value + sign * plus_refs[i][t, pick, :]
                to_refs[i][t, pick, :] = value


def sweep_y_into(to_refs, from_refs, cy_ref):
    tiles, nx, _ = cy_ref.shape
    lane = iota((Y_LINES, SEG), 1)

    def next_cells(values):
        moved = [pltpu.roll(value, SEG - 1, 1) for value in values]
        return [jnp.where(lane == SEG - 1, b, a) for a, b in zip(moved, moved[1:] + moved[:1])]

    def previous_cells(values):
        moved = [pltpu.roll(value, 1, 1) for value in values]
        return [jnp.where(lane == 0, a, b) for a, b in zip(moved[-1:] + moved[:-1], moved)]

    for low in range(0, nx, Y_LINES):
        lines = slice(low, low + Y_LINES)
        coeffs = [cy_ref[t, lines, :] for t in range(tiles)]
        coeffs_low = previous_cells(coeffs)
        fields = [[ref[t, lines, :] for t in range(tiles)] for ref in from_refs]
        for _ in range(M):
            for i, values in enumerate(fields):
                after, before = next_cells(values), previous_cells(values)
                fields[i] = [
                    a + c * (b - a) - d * (a - e)
                    for a, b, c, d, e in zip(values, after, coeffs, coeffs_low, before)]
        for to_ref, values in zip(to_refs, fields):
            for t, value in enumerate(values):
                to_ref[t, lines, :] = value


def normal_into(to_refs, from_refs, diagonal_refs, side_refs, base_refs=None):
    tiles, nx, _ = from_refs[0].shape
    picks = x_lines(nx)
    for t in range(tiles):
        for i, from_ref in enumerate(from_refs):
            values = [from_ref[t, pick, :] for pick in picks]
            sides = [side_refs[i][t, pick, :] for pick in picks]
            low = [e * a for e, a in zip(sides, values)]
            low = [pltpu.roll(low[-1], 1, 0)] + low[:-1]
            after = values[1:] + [pltpu.roll(values[0], 7, 0)]
            for line, pick in enumerate(picks):
                result = (diagonal_refs[i][t, pick, :] * values[line] + sides[line] * after[line]
                          + low[line])
                if base_refs is not None:
                    result = base_refs[i][t, pick, :] - result
                to_refs[i][t, pick, :] = result


def of_fields(ref, start=0):
    return [ref.at[start + f] for f in range(F)]


def start_kernel(c0_ref, cx_ref, swap_ref, c0_out, cx_out, cy_out, u_out, token_out, work):
    token_out[...] = jnp.zeros_like(token_out)
    nx = cx_ref.shape[0]
    spans, count = swap_ref.shape[0], cy_out.shape[0]
    me = lax.axis_index("px")
    for p in range(spans):
        for t in range(count):
            cy_out[t, p * LX:(p + 1) * LX, :] = swap_ref[p, t * LX:(t + 1) * LX, :]

    def beside(i):
        lines = slice(count * LX + i * nx, count * LX + (i + 1) * nx)
        before = swap_ref[jnp.maximum(me - 1, 0), lines, :]
        after = swap_ref[jnp.minimum(me + 1, spans - 1), lines, :]
        return ends_tile(jnp.where(me > 0, before, 0.0), jnp.where(me < spans - 1, after, 0.0))

    for t in range(count - 1):
        tile = slice(t * SEG, (t + 1) * SEG)
        cx_out[t] = cx_ref[:, tile]
        for f in range(F):
            c0_out[f, t] = c0_ref[f, :, tile]
    cx_out[count - 1] = beside(F)
    cx_out[:, nx - 1:, :] = jnp.zeros((count, 1, SEG), jnp.float32)
    for f in range(F):
        c0_out[f, count - 1] = beside(f)
    sweep_x_into(of_fields(work), of_fields(c0_out), cx_out)
    sweep_y_into(of_fields(u_out), of_fields(work), cy_out)


def join_kernel(spans, *rest):
    parts, out = rest[:spans], rest[spans]
    per = out.shape[1] - 1
    lane = iota((LX, SEG), 1)
    me = lax.axis_index("px")
    for k, part in enumerate(parts):
        rows = pl.ds(pl.multiple_of((me ^ k) * LX, LX), LX)
        for f in range(F):
            for t in range(per):
                out[f, t, rows, :] = part[f * per + t]
        beside = part[F * per]
        out[0, per, rows, :] = beside
        out[1, per, rows, :] = jnp.where(lane < HALF, pltpu.roll(beside, SEG - QUARTER, 1),
                                         pltpu.roll(beside, QUARTER, 1))


def solve_kernel(c0_ref, cx_ref, cy_ref, u_ref, obs_ref, far_ref, r_out, q_out, h_out, dots_out,
                 vec, coef, work):
    for p in range(obs_ref.shape[0]):
        rows = slice(p * LX, (p + 1) * LX)
        for channel in range(2 * F):
            coef[channel, :, rows, :] = obs_ref[p, channel]
        for f in range(F):
            coef[2 * F + f, :, rows, :] = obs_ref[p, 2 * F + f] + far_ref[f, :, rows, :]

    sides = (of_fields(coef), of_fields(coef, F))
    one, two, r, q, s, h = (of_fields(ref) for ref in (
        work.at[0], work.at[1], vec.at[0], vec.at[1], vec.at[2], h_out))
    normal_into(one, of_fields(u_ref), *sides, of_fields(coef, 2 * F))
    sweep_y_into(two, one, cy_ref)
    sweep_x_into(r, two, cx_ref, of_fields(c0_ref), -1.0)
    sweep_x_into(one, r, cx_ref)
    sweep_y_into(two, one, cy_ref)
    normal_into(one, two, *sides)
    sweep_y_into(two, one, cy_ref)
    sweep_x_into(q, two, cx_ref, r)
    sweep_x_into(one, q, cx_ref)
    sweep_y_into(s, one, cy_ref)
    normal_into(h, s, *sides)

    tiles, nx = vec.shape[2] - 1, vec.shape[3]
    sums = [jnp.zeros((8, SEG), jnp.float32) for _ in range(4)]
    for f in range(F):
        for t in range(tiles):
            r_out[f, :, t * SEG:(t + 1) * SEG] = vec[0, f, t]
            q_out[f, :, t * SEG:(t + 1) * SEG] = vec[1, f, t]
            for low in range(0, nx, 8):
                lines = slice(low, low + 8)
                r, q, s = (vec[i, f, t, lines, :] for i in range(3))
                for i, product in enumerate((r * r, r * q, q * q, s * h_out[f, t, lines, :])):
                    sums[i] = sums[i] + product
    dots = jnp.zeros((1, SEG), jnp.float32)
    for i, total in enumerate(sums):
        line = jnp.sum(total, axis=0, keepdims=True)
        for distance in (64, 32, 16):
            line = line + pltpu.roll(line, distance, 1)
        dots = jnp.where(iota((1, SEG), 1) // SPLIT == i, line, dots)
    dots_out[...] = jnp.broadcast_to(dots, dots_out.shape)


def last_kernel(h_ref, q_ref, cx_ref, cy_ref, qq_out, work):
    sweep_y_into(of_fields(work.at[0]), of_fields(h_ref), cy_ref)
    sweep_x_into(of_fields(work.at[1]), of_fields(work.at[0]), cx_ref)
    for f in range(F):
        for t in range(work.shape[2] - 1):
            tile = slice(t * SEG, (t + 1) * SEG)
            qq_out[f, :, tile] = q_ref[f, :, tile] + work[1, f, t]


def finish_kernel(dots_ref, c0_ref, r_ref, q_ref, qq_ref, control_out, residual_out):
    dots = jnp.sum(dots_ref[...], axis=0)
    lane = iota((1, SEG), 1)
    rr, rq, qq2, energy = (pltpu.roll(dots, (SEG - i * SPLIT) % SEG, 1) for i in range(4))

    def total(line):
        return jnp.sum(jnp.where(lane < SPLIT, line, 0.0), axis=1, keepdims=True)

    rr_sum = total(rr)
    alpha = rr_sum / total(rq)
    new_sum = total(rr - 2.0 * alpha * rq + alpha * alpha * qq2)
    more = 1.0 + new_sum / rr_sum
    curve = total(more * more * rq - 2.0 * more * alpha * qq2 + alpha * alpha * (qq2 + energy))
    second = new_sum / curve
    first_weight = alpha + second * more
    both = alpha * second
    for f in range(F):
        r, q = r_ref[f], q_ref[f]
        control_out[f] = c0_ref[f] + first_weight * r - both * q
        residual_out[f] = r - first_weight * q + both * qq_ref[f]


def call(kernel, out_shape, scratch=(), in_specs=None, out_specs=None, limit=VMEM_BYTES,
         weight=1):
    params = {"in_specs": in_specs, "out_specs": out_specs}
    return pl.pallas_call(
        kernel,
        out_shape=out_shape,
        scratch_shapes=list(scratch),
        compiler_params=pltpu.CompilerParams(vmem_limit_bytes=limit),
        cost_estimate=pl.CostEstimate(flops=weight, bytes_accessed=weight, transcendentals=0),
        **{name: value for name, value in params.items() if value is not None},
    )


def f32(*shape):
    return jax.ShapeDtypeStruct(shape, jnp.float32)


def vmem(*shape, kind=jnp.float32):
    return pltpu.VMEM(shape, kind)


def shards(
    control_start, coef_x, coef_y, innovation, obs_weight, interp, obs_owner, cell_key, stencil
):
    groups, spans = lax.axis_size("py"), lax.axis_size("px")
    half = groups // 2
    rows = innovation.shape[0]
    cap = 3 * rows // groups
    blk = SEG if cap % SEG == 0 else HALF
    meta_rows = -(-4 * (cap // blk) // 8) * 8
    block_rows = 2 * cap + meta_rows
    chunks = rows // SEG
    nx, width = control_start.shape[2], control_start.shape[3]
    tiles = width // SEG + 1
    c0, cx = control_start[:, 0], coef_x[0]
    hbm, local, scalars = (
        pl.BlockSpec(memory_space=s) for s in (pltpu.HBM, pltpu.VMEM, pltpu.SMEM))
    ints = vmem(chunks, SEG, kind=jnp.int32)
    dma = pltpu.SemaphoreType.DMA

    def to_half(block, k):
        return lax.ppermute(block, "py", [(i, i ^ k) for i in range(groups)])

    def across(parts):
        return [
            lax.ppermute(parts[k], ("px", "py"), [
                (i * groups + j, (i ^ k) * groups + (j ^ half))
                for i in range(spans) for j in range(groups)])
            for k in range(spans)]

    *w_blocks, slots = call(
        functools.partial(pack_weights_kernel, groups, cap, blk, block_rows),
        (f32(block_rows, SEG),) * half + (jax.ShapeDtypeStruct((chunks, SEG), jnp.int32),),
        [ints, ints, ints, vmem(chunks, SEG), vmem(rows, SEG), vmem(half * block_rows, SEG), ints,
         pltpu.SMEM((chunks, SEG), jnp.int32), dma((5,)), dma((half,)), dma],
        [hbm] * 5,
        (hbm,) * half + (local,),
        limit=PACK_BYTES,
    )(
        obs_owner.reshape(chunks, SEG), cell_key.reshape(chunks, SEG),
        stencil.reshape(chunks, SEG), interp.reshape(chunks, SEG), obs_weight,
    )
    v_blocks = list(call(
        functools.partial(pack_products_kernel, groups, cap),
        (f32(2 * cap, SEG),) * half,
        [vmem(rows, SEG), vmem(rows, SEG), vmem(groups * cap, SEG), dma((2,)), dma((half,))],
        [scalars] + [hbm] * 2,
        (hbm,) * half,
        limit=PACK_BYTES,
    )(slots, obs_weight, innovation))
    w_blocks[1:] = [to_half(w_blocks[k], k) for k in range(1, half)]
    lead = half // 2
    w_blocks[lead], *v_blocks[1:] = lax.optimization_barrier((w_blocks[lead], *v_blocks[1:]))
    v_blocks[1:] = [to_half(v_blocks[k], k) for k in range(1, half)]

    swap = call(
        pack_swap_kernel,
        f32(spans, LX * tiles + (F + 1) * nx, SEG),
        [vmem(*coef_y.shape[1:]), vmem(F + 1, nx, SEG), vmem(F + 1, nx, SEG), dma((5,))],
        [local] + [hbm] * 3,
        limit=PACK_BYTES,
    )(slots, coef_y[0], c0, cx)
    swap = lax.all_to_all(swap, "px", split_axis=0, concat_axis=0, tiled=True)
    c0_ext, cx_ext, cy_ext, u_ext, token = call(
        start_kernel,
        (f32(F, tiles, nx, SEG), f32(tiles, nx, SEG), f32(tiles, nx, SEG), f32(F, tiles, nx, SEG),
         f32(8, SEG)),
        [vmem(F, tiles, nx, SEG)],
    )(c0, cx, swap)

    def sum_weights(side, token, weight):
        return call(
            functools.partial(weights_kernel, half, cap, blk, side),
            (f32(half, meta_rows, SEG),) + (f32(ROWS, SEG),) * 2,
            [vmem(ROWS, 3 * SEG)],
            weight=weight,
        )(*w_blocks, token)

    meta, *side_across = sum_weights(1, w_blocks[0], FIRST)
    side_across = [to_half(values, half) for values in side_across]
    meta, *side = sum_weights(0, token, 1)
    parts, *sums_across = call(
        functools.partial(products_kernel, half, cap, blk),
        (f32(spans, 3 * F, tiles, LX, SEG),)
        + (f32(F * (tiles - 1) + 1, LX, SEG),) * spans,
        [vmem(ROWS, 2 * SEG), vmem(ROWS, SEG), vmem(ROWS, SEG), vmem(2, ROWS, SEG)],
    )(meta, *side, *side_across, *v_blocks)
    far_sums = call(
        functools.partial(join_kernel, spans), f32(F, tiles, nx, SEG), weight=JOIN,
    )(*across(sums_across))
    parts = lax.all_to_all(parts, "px", split_axis=0, concat_axis=0, tiled=True)

    r, q, h, dots = call(
        solve_kernel,
        (f32(F, nx, width),) * 2 + (f32(F, tiles, nx, SEG), f32(groups * spans, 1, SEG)),
        [vmem(3, F, tiles, nx, SEG), vmem(3 * F, tiles, nx, SEG), vmem(2, F, tiles, nx, SEG)],
    )(c0_ext, cx_ext, cy_ext, u_ext, parts, far_sums)
    dots = lax.all_to_all(dots, ("px", "py"), split_axis=0, concat_axis=0, tiled=True)
    qq = call(last_kernel, f32(F, nx, width), [vmem(2, F, tiles, nx, SEG)])(
        h, q, cx_ext, cy_ext)
    control, residual = call(finish_kernel, (f32(F, nx, width),) * 2)(dots, c0, r, q, qq)
    return control[:, None], residual[:, None]


def solution(mesh):
    return jax.shard_map(
        shards,
        mesh=mesh,
        in_specs=(
            P(None, "py", None, "px"),
            P("py", None, "px"),
            P("py", "px", None),
            P(("px", "py"), None),
            P(("px", "py"), None),
            P(("px", "py")),
            P(("px", "py"), None),
            P(("px", "py")),
            P(("px", "py")),
        ),
        out_specs=(P(None, "py", None, "px"), P(None, "py", None, "px")),
        check_vma=False,
    )
```

```python
import functools

import jax
import jax.numpy as jnp
from jax import lax
from jax.experimental import pallas as pl
from jax.experimental.pallas import tpu as pltpu
from jax.sharding import PartitionSpec as P

F = 2
SEG = 128
M = 4
NB = 16
LX = 16
ROWS = F * NB * LX
HALF = SEG // 2
QUARTER = SEG // 4
SPLIT = 16
X_TILES = 1
Y_LINES = 8
VMEM_BYTES = 32 * 1024 * 1024
PACK_BYTES = 60 * 1024 * 1024
FIRST = 100_000_000
JOIN = 100_000_000


def iota(shape, axis):
    return lax.broadcasted_iota(jnp.int32, shape, axis)


def flag(condition, kind=jnp.bfloat16):
    return jnp.where(condition, 1.0, 0.0).astype(kind)


def mxu(left, right):
    return jnp.dot(left, right, preferred_element_type=jnp.float32)


def split_parts(values, count):
    parts = []
    for _ in range(count):
        part = values.astype(jnp.bfloat16)
        parts.append(part)
        values = values - part.astype(jnp.float32)
    return parts


def ends_tile(before, after):
    return jnp.where(iota(after.shape, after.ndim - 1) < HALF, after, before)


def start_copies(pairs, sems):
    copies = [pltpu.make_async_copy(*pair, sems.at[i]) for i, pair in enumerate(pairs)]
    for copy in copies:
        copy.start()
    return copies


def pack_weights_kernel(groups, cap, blk, block_rows, own_hbm, key_hbm, sten_hbm, itp_hbm, w_hbm,
                        *rest):
    half = groups // 2
    outs, rest = rest[:half], rest[half:]
    (slot_out, own_ref, key_ref, sten_ref, itp_ref, w_ref, buffer, slot_v, slot_s, sems, out_sems,
     sem) = rest
    loads = start_copies([(own_hbm, own_ref), (key_hbm, key_ref), (sten_hbm, sten_ref),
                          (itp_hbm, itp_ref), (w_hbm, w_ref)], sems)

    def clear(k, carry):
        start = pl.multiple_of(k * block_rows, 8)
        buffer[pl.ds(start, block_rows), :] = jnp.zeros((block_rows, SEG), jnp.float32)
        return carry

    lax.fori_loop(0, half, clear, 0)

    for load in loads[:4]:
        load.wait()
    chunks = own_ref.shape[0]
    nb = cap // blk
    own = own_ref[...]
    high = groups * chunks
    shift = chunks.bit_length() - 1
    masks = [flag(own == o, jnp.float32) for o in range(groups)]
    hits = jnp.concatenate(masks, axis=0).astype(jnp.bfloat16)
    square = (SEG, SEG)
    within = mxu(hits, flag(iota(square, 0) < iota(square, 1)))
    tallies = mxu(hits, jnp.ones(square, jnp.bfloat16)).astype(jnp.bfloat16)
    line, column = iota((high, high), 0), iota((high, high), 1)
    same = (line >> shift) == (column >> shift)
    ranks = within + mxu(flag(same & (column < line)), tallies)
    rank = sum(masks[o] * ranks[o * chunks:(o + 1) * chunks] for o in range(groups))
    rank = rank.astype(jnp.int32)
    relative = own ^ lax.axis_index("py")
    block, across = relative & (half - 1), relative >> (half.bit_length() - 1)
    slot_v[...] = block * block_rows + across * cap + rank
    slot_out[...] = (block * 2 + across) * cap + rank
    copy = pltpu.make_async_copy(slot_v, slot_s, sem)
    copy.start()

    log = blk.bit_length() - 1
    place = relative * nb + (rank >> log)
    lane = rank & (blk - 1)
    key, sten, itp = key_ref[...], sten_ref[...], itp_ref[...]
    tall = groups * nb
    meta = jnp.zeros((5 * tall, SEG), jnp.float32)
    for i in range(chunks):
        chosen = iota((tall, SEG), 0) == place[i:i + 1]
        parts = split_parts(itp[i:i + 1], 3)
        parts += [key[i:i + 1].astype(jnp.bfloat16), (sten[i:i + 1] + 1).astype(jnp.bfloat16)]
        left = [jnp.where(chosen, part.astype(jnp.float32), 0.0) for part in parts]
        right = flag(iota(square, 0) == lane[i:i + 1])
        meta = meta + lax.dot_general(
            jnp.concatenate(left, axis=0).astype(jnp.bfloat16), right,
            (((1,), (1,)), ((), ())), preferred_element_type=jnp.float32)
    shares = meta[:tall] + meta[tall:2 * tall] + meta[2 * tall:3 * tall]
    targets = meta[3 * tall:4 * tall] * LX + meta[4 * tall:]
    for v in range(groups):
        base = (v % half) * block_rows + 2 * cap + (v // half) * 2 * nb
        buffer[base:base + nb, :] = shares[v * nb:(v + 1) * nb]
        buffer[base + nb:base + 2 * nb, :] = targets[v * nb:(v + 1) * nb]

    copy.wait()
    loads[4].wait()

    def place_rows(g, carry):
        weights = w_ref[pl.ds(pl.multiple_of(g * 8, 8), 8), :]
        line, lane = g // 16, (g % 16) * 8
        for i in range(8):
            buffer[pl.ds(slot_s[line, lane + i], 1), :] = weights[i:i + 1]
        return carry

    lax.fori_loop(0, w_ref.shape[0] // 8, place_rows, 0)
    for store in start_copies([(buffer.at[pl.ds(k * block_rows, block_rows)], out)
                               for k, out in enumerate(outs)], out_sems):
        store.wait()


def pack_products_kernel(groups, cap, slot_ref, w_hbm, d_hbm, *rest):
    half = groups // 2
    outs, (w_ref, d_ref, buffer, sems, out_sems) = rest[:half], rest[half:]
    loads = start_copies([(w_hbm, w_ref), (d_hbm, d_ref)], sems)

    def clear(o, carry):
        start = pl.multiple_of(o * cap, 8)
        buffer[pl.ds(start, cap), :] = jnp.zeros((cap, SEG), jnp.float32)
        return carry

    lax.fori_loop(0, groups, clear, 0)

    for load in loads:
        load.wait()

    def place_rows(g, carry):
        start = pl.multiple_of(g * 8, 8)
        products = w_ref[pl.ds(start, 8), :] * d_ref[pl.ds(start, 8), :]
        line, lane = g // 16, (g % 16) * 8
        for i in range(8):
            buffer[pl.ds(slot_ref[line, lane + i], 1), :] = products[i:i + 1]
        return carry

    lax.fori_loop(0, w_ref.shape[0] // 8, place_rows, 0)
    for store in start_copies([(buffer.at[pl.ds(k * 2 * cap, 2 * cap)], out)
                               for k, out in enumerate(outs)], out_sems):
        store.wait()


def pack_swap_kernel(_, cy_hbm, c0_hbm, cx_hbm, swap_out, cy_ref, first, last, sems):
    width = c0_hbm.shape[2]
    for load in start_copies([
        (cy_hbm, cy_ref),
        (c0_hbm.at[:, :, pl.ds(0, SEG)], first.at[pl.ds(0, F)]),
        (cx_hbm.at[:, pl.ds(0, SEG)], first.at[F]),
        (c0_hbm.at[:, :, pl.ds(width - SEG, SEG)], last.at[pl.ds(0, F)]),
        (cx_hbm.at[:, pl.ds(width - SEG, SEG)], last.at[F]),
    ], sems):
        load.wait()
    columns = cy_ref.shape[1]
    cy = cy_ref[...]
    cy = jnp.where(iota(cy.shape, 1) == columns - 1, 0.0, cy)
    empty = jnp.zeros((LX, SEG), jnp.float32)
    me = lax.axis_index("px")
    nx = first.shape[1]
    for q in range(columns // width):
        low, top = q * width, (q + 1) * width
        tiles = [cy[:, t:t + SEG] for t in range(low, top, SEG)]
        before = cy[:, low - SEG:low] if low > 0 else empty
        after = cy[:, top:top + SEG] if top < columns else empty
        tiles.append(ends_tile(before, after))
        for t, tile in enumerate(tiles):
            swap_out[q, t * LX:(t + 1) * LX, :] = tile
        base = len(tiles) * LX
        for i in range(F + 1):
            swap_out[q, base + i * nx:base + (i + 1) * nx, :] = jnp.where(
                q < me, first[i], last[i])


def sum_rows(cap, blk, metas, acc_ref, terms):
    nb = cap // blk
    numbers = 1.0 + iota((ROWS, cap), 0).astype(jnp.float32)
    for source, meta in enumerate(metas):
        upper = jnp.concatenate(
            [jnp.broadcast_to(meta[i:i + 1], (SEG, SEG)).T[:blk] for i in range(nb)], axis=0)
        target = jnp.concatenate([meta[nb + i:nb + i + 1, :blk] for i in range(nb)], axis=1)
        hit = flag(numbers == target)
        values = jnp.concatenate(terms(source, upper), axis=1)
        part = mxu(jnp.concatenate([hit, hit], axis=1),
                   jnp.concatenate(split_parts(values, 2), axis=0))
        if source:
            acc_ref[...] += part
        else:
            acc_ref[...] = part


def cut_part(rows_ref, to, f, q, spans):
    per = to.shape[0] - 1

    def tile(b):
        start = pl.multiple_of((f * NB + b) * LX, LX)
        return rows_ref[pl.ds(start, LX), :]

    for j in range(per):
        to[j] = tile(q * per + j)
    before = tile(jnp.maximum(q * per - 1, 0))
    after = tile(jnp.minimum(q * per + per, NB - 1))
    to[per] = ends_tile(jnp.where(q > 0, before, 0.0), jnp.where(q < spans - 1, after, 0.0))


def cut_far_part(rows_ref, to, q, spans):
    per = (to.shape[0] - 1) // F

    def tile(f, b):
        start = pl.multiple_of((f * NB + b) * LX, LX)
        return rows_ref[pl.ds(start, LX), :]

    beside = []
    for f in range(F):
        for j in range(per):
            to[f * per + j] = tile(f, q * per + j)
        before = tile(f, jnp.maximum(q * per - 1, 0))
        after = tile(f, jnp.minimum(q * per + per, NB - 1))
        beside.append(ends_tile(jnp.where(q > 0, before, 0.0),
                                jnp.where(q < spans - 1, after, 0.0)))
    lane = iota((LX, SEG), 1)
    inner = jnp.where(lane < HALF, pltpu.roll(beside[1], QUARTER, 1),
                      pltpu.roll(beside[1], SEG - QUARTER, 1))
    to[F * per] = jnp.where((lane >= QUARTER) & (lane < SEG - QUARTER), inner, beside[0])


def weights_kernel(half, cap, blk, across, *rest):
    w_refs, (_, meta_out, diagonal_out, side_out, acc_ref) = rest[:half], rest[half:]
    nb = cap // blk
    for k, w_ref in enumerate(w_refs):
        meta_out[k] = w_ref[2 * cap:, :]
    rows = slice(across * cap, (across + 1) * cap)

    def terms(source, upper):
        lower = 1.0 - upper
        weights = w_refs[source][rows, :]
        lower_w, upper_w = lower * weights, upper * weights
        return [lower * lower_w, upper * lower_w, upper * upper_w]

    low = 2 * cap + across * 2 * nb
    sum_rows(cap, blk, [w_ref[low:low + 2 * nb, :] for w_ref in w_refs], acc_ref, terms)
    diagonal_out[...] = acc_ref[:, :SEG] + pltpu.roll(acc_ref[:, 2 * SEG:], 1, 0)
    side_out[...] = acc_ref[:, SEG:2 * SEG]


def sum_products(half, cap, blk, across, meta_ref, v_refs, acc_ref, sums_ref):
    nb = cap // blk
    rows = slice(across * cap, (across + 1) * cap)

    def terms(source, upper):
        products = v_refs[source][rows, :]
        return [(1.0 - upper) * products, upper * products]

    low = across * 2 * nb
    sum_rows(cap, blk, [meta_ref[k, low:low + 2 * nb, :] for k in range(half)], acc_ref, terms)
    sums_ref[...] = acc_ref[:, :SEG] + pltpu.roll(acc_ref[:, SEG:], 1, 0)


def products_kernel(half, cap, blk, meta_ref, d_ref, e_ref, far_d_ref, far_e_ref, *rest):
    v_refs, (out, *far_outs, acc_ref, sums_ref, far_ref, side) = rest[:half], rest[half:]
    spans = out.shape[0]
    sum_products(half, cap, blk, 1, meta_ref, v_refs, acc_ref, far_ref)
    me = lax.axis_index("px")
    for k, far_out in enumerate(far_outs):
        cut_far_part(far_ref, far_out, me ^ k, spans)
    sum_products(half, cap, blk, 0, meta_ref, v_refs, acc_ref, sums_ref)
    side[0] = d_ref[...] + far_d_ref[...]
    side[1] = e_ref[...] + far_e_ref[...]
    for q in range(spans):
        for channel, rows_ref in enumerate((side.at[0], side.at[1], sums_ref)):
            for f in range(F):
                cut_part(rows_ref, out.at[q, channel * F + f], f, q, spans)


def x_lines(nx):
    return [pl.ds(i, 8, stride=nx // 8) for i in range(nx // 8)]


def sweep_x_into(to_refs, from_refs, cx_ref, plus_refs=None, sign=1.0):
    tiles, nx, _ = cx_ref.shape
    picks = x_lines(nx)
    for start in range(0, tiles, X_TILES):
        group = range(start, min(start + X_TILES, tiles))
        chains = [(i, t) for t in group for i in range(len(from_refs))]
        coeffs = {t: [cx_ref[t, pick, :] for pick in picks] for t in group}
        wrapped = {t: pltpu.roll(coeffs[t][-1], 1, 0) for t in group}
        fields = {(i, t): [from_refs[i][t, pick, :] for pick in picks] for i, t in chains}
        for _ in range(M):
            for i, t in chains:
                values = fields[i, t]
                after = values[1:] + [pltpu.roll(values[0], 7, 0)]
                low = wrapped[t] * (values[0] - pltpu.roll(values[-1], 1, 0))
                flux = [c * (b - a) for c, a, b in zip(coeffs[t], values, after)]
                fields[i, t] = [a + f - g for a, f, g in zip(values, flux, [low] + flux[:-1])]
        for i, t in chains:
            for pick, value in zip(picks, fields[i, t]):
                if plus_refs is not None:
                    value = value + sign * plus_refs[i][t, pick, :]
                to_refs[i][t, pick, :] = value


def sweep_y_into(to_refs, from_refs, cy_ref):
    tiles, nx, _ = cy_ref.shape
    lane = iota((Y_LINES, SEG), 1)

    def next_cells(values):
        moved = [pltpu.roll(value, SEG - 1, 1) for value in values]
        return [jnp.where(lane == SEG - 1, b, a) for a, b in zip(moved, moved[1:] + moved[:1])]

    def previous_cells(values):
        moved = [pltpu.roll(value, 1, 1) for value in values]
        return [jnp.where(lane == 0, a, b) for a, b in zip(moved[-1:] + moved[:-1], moved)]

    for low in range(0, nx, Y_LINES):
        lines = slice(low, low + Y_LINES)
        coeffs = [cy_ref[t, lines, :] for t in range(tiles)]
        coeffs_low = previous_cells(coeffs)
        fields = [[ref[t, lines, :] for t in range(tiles)] for ref in from_refs]
        for _ in range(M):
            for i, values in enumerate(fields):
                after, before = next_cells(values), previous_cells(values)
                fields[i] = [
                    a + c * (b - a) - d * (a - e)
                    for a, b, c, d, e in zip(values, after, coeffs, coeffs_low, before)]
        for to_ref, values in zip(to_refs, fields):
            for t, value in enumerate(values):
                to_ref[t, lines, :] = value


def normal_into(to_refs, from_refs, diagonal_refs, side_refs, base_refs=None):
    tiles, nx, _ = from_refs[0].shape
    picks = x_lines(nx)
    for t in range(tiles):
        for i, from_ref in enumerate(from_refs):
            values = [from_ref[t, pick, :] for pick in picks]
            sides = [side_refs[i][t, pick, :] for pick in picks]
            low = [e * a for e, a in zip(sides, values)]
            low = [pltpu.roll(low[-1], 1, 0)] + low[:-1]
            after = values[1:] + [pltpu.roll(values[0], 7, 0)]
            for line, pick in enumerate(picks):
                result = (diagonal_refs[i][t, pick, :] * values[line] + sides[line] * after[line]
                          + low[line])
                if base_refs is not None:
                    result = base_refs[i][t, pick, :] - result
                to_refs[i][t, pick, :] = result


def of_fields(ref, start=0):
    return [ref.at[start + f] for f in range(F)]


def start_kernel(c0_ref, cx_ref, swap_ref, c0_out, cx_out, cy_out, u_out, token_out, work):
    token_out[...] = jnp.zeros_like(token_out)
    nx = cx_ref.shape[0]
    spans, count = swap_ref.shape[0], cy_out.shape[0]
    me = lax.axis_index("px")
    for p in range(spans):
        for t in range(count):
            cy_out[t, p * LX:(p + 1) * LX, :] = swap_ref[p, t * LX:(t + 1) * LX, :]

    def beside(i):
        lines = slice(count * LX + i * nx, count * LX + (i + 1) * nx)
        before = swap_ref[jnp.maximum(me - 1, 0), lines, :]
        after = swap_ref[jnp.minimum(me + 1, spans - 1), lines, :]
        return ends_tile(jnp.where(me > 0, before, 0.0), jnp.where(me < spans - 1, after, 0.0))

    for t in range(count - 1):
        tile = slice(t * SEG, (t + 1) * SEG)
        cx_out[t] = cx_ref[:, tile]
        for f in range(F):
            c0_out[f, t] = c0_ref[f, :, tile]
    cx_out[count - 1] = beside(F)
    cx_out[:, nx - 1:, :] = jnp.zeros((count, 1, SEG), jnp.float32)
    for f in range(F):
        c0_out[f, count - 1] = beside(f)
    sweep_x_into(of_fields(work), of_fields(c0_out), cx_out)
    sweep_y_into(of_fields(u_out), of_fields(work), cy_out)


def join_kernel(spans, *rest):
    parts, out = rest[:spans], rest[spans]
    per = out.shape[1] - 1
    lane = iota((LX, SEG), 1)
    me = lax.axis_index("px")
    for k, part in enumerate(parts):
        rows = pl.ds(pl.multiple_of((me ^ k) * LX, LX), LX)
        for f in range(F):
            for t in range(per):
                out[f, t, rows, :] = part[f * per + t]
        beside = part[F * per]
        out[0, per, rows, :] = beside
        out[1, per, rows, :] = jnp.where(lane < HALF, pltpu.roll(beside, SEG - QUARTER, 1),
                                         pltpu.roll(beside, QUARTER, 1))


def solve_kernel(c0_ref, cx_ref, cy_ref, u_ref, obs_ref, far_ref, r_out, q_out, h_out, dots_out,
                 vec, coef, work):
    for p in range(obs_ref.shape[0]):
        rows = slice(p * LX, (p + 1) * LX)
        for channel in range(2 * F):
            coef[channel, :, rows, :] = obs_ref[p, channel]
        for f in range(F):
            coef[2 * F + f, :, rows, :] = obs_ref[p, 2 * F + f] + far_ref[f, :, rows, :]

    sides = (of_fields(coef), of_fields(coef, F))
    one, two, r, q, s, h = (of_fields(ref) for ref in (
        work.at[0], work.at[1], vec.at[0], vec.at[1], vec.at[2], h_out))
    normal_into(one, of_fields(u_ref), *sides, of_fields(coef, 2 * F))
    sweep_y_into(two, one, cy_ref)
    sweep_x_into(r, two, cx_ref, of_fields(c0_ref), -1.0)
    sweep_x_into(one, r, cx_ref)
    sweep_y_into(two, one, cy_ref)
    normal_into(one, two, *sides)
    sweep_y_into(two, one, cy_ref)
    sweep_x_into(q, two, cx_ref, r)
    sweep_x_into(one, q, cx_ref)
    sweep_y_into(s, one, cy_ref)
    normal_into(h, s, *sides)

    tiles, nx = vec.shape[2] - 1, vec.shape[3]
    sums = [jnp.zeros((8, SEG), jnp.float32) for _ in range(4)]
    for f in range(F):
        for t in range(tiles):
            r_out[f, :, t * SEG:(t + 1) * SEG] = vec[0, f, t]
            q_out[f, :, t * SEG:(t + 1) * SEG] = vec[1, f, t]
            for low in range(0, nx, 8):
                lines = slice(low, low + 8)
                r, q, s = (vec[i, f, t, lines, :] for i in range(3))
                for i, product in enumerate((r * r, r * q, q * q, s * h_out[f, t, lines, :])):
                    sums[i] = sums[i] + product
    dots = jnp.zeros((1, SEG), jnp.float32)
    for i, total in enumerate(sums):
        line = jnp.sum(total, axis=0, keepdims=True)
        for distance in (64, 32, 16):
            line = line + pltpu.roll(line, distance, 1)
        dots = jnp.where(iota((1, SEG), 1) // SPLIT == i, line, dots)
    dots_out[...] = jnp.broadcast_to(dots, dots_out.shape)


def last_kernel(h_ref, q_ref, cx_ref, cy_ref, qq_out, work):
    sweep_y_into(of_fields(work.at[0]), of_fields(h_ref), cy_ref)
    sweep_x_into(of_fields(work.at[1]), of_fields(work.at[0]), cx_ref)
    for f in range(F):
        for t in range(work.shape[2] - 1):
            tile = slice(t * SEG, (t + 1) * SEG)
            qq_out[f, :, tile] = q_ref[f, :, tile] + work[1, f, t]


def finish_kernel(dots_ref, c0_ref, r_ref, q_ref, qq_ref, control_out, residual_out):
    dots = jnp.sum(dots_ref[...], axis=0)
    lane = iota((1, SEG), 1)
    rr, rq, qq2, energy = (pltpu.roll(dots, (SEG - i * SPLIT) % SEG, 1) for i in range(4))

    def total(line):
        return jnp.sum(jnp.where(lane < SPLIT, line, 0.0), axis=1, keepdims=True)

    rr_sum = total(rr)
    alpha = rr_sum / total(rq)
    new_sum = total(rr - 2.0 * alpha * rq + alpha * alpha * qq2)
    more = 1.0 + new_sum / rr_sum
    curve = total(more * more * rq - 2.0 * more * alpha * qq2 + alpha * alpha * (qq2 + energy))
    second = new_sum / curve
    first_weight = alpha + second * more
    both = alpha * second
    for f in range(F):
        r, q = r_ref[f], q_ref[f]
        control_out[f] = c0_ref[f] + first_weight * r - both * q
        residual_out[f] = r - first_weight * q + both * qq_ref[f]


def call(kernel, out_shape, scratch=(), in_specs=None, out_specs=None, limit=VMEM_BYTES,
         weight=1):
    params = {"in_specs": in_specs, "out_specs": out_specs}
    return pl.pallas_call(
        kernel,
        out_shape=out_shape,
        scratch_shapes=list(scratch),
        compiler_params=pltpu.CompilerParams(vmem_limit_bytes=limit),
        cost_estimate=pl.CostEstimate(flops=weight, bytes_accessed=weight, transcendentals=0),
        **{name: value for name, value in params.items() if value is not None},
    )


def f32(*shape):
    return jax.ShapeDtypeStruct(shape, jnp.float32)


def vmem(*shape, kind=jnp.float32):
    return pltpu.VMEM(shape, kind)


def shards(
    control_start, coef_x, coef_y, innovation, obs_weight, interp, obs_owner, cell_key, stencil
):
    groups, spans = lax.axis_size("py"), lax.axis_size("px")
    half = groups // 2
    rows = innovation.shape[0]
    cap = 3 * rows // groups
    blk = SEG if cap % SEG == 0 else HALF
    meta_rows = -(-4 * (cap // blk) // 8) * 8
    block_rows = 2 * cap + meta_rows
    chunks = rows // SEG
    nx, width = control_start.shape[2], control_start.shape[3]
    tiles = width // SEG + 1
    c0, cx = control_start[:, 0], coef_x[0]
    hbm, local, scalars = (
        pl.BlockSpec(memory_space=s) for s in (pltpu.HBM, pltpu.VMEM, pltpu.SMEM))
    ints = vmem(chunks, SEG, kind=jnp.int32)
    dma = pltpu.SemaphoreType.DMA

    def to_half(block, k):
        return lax.ppermute(block, "py", [(i, i ^ k) for i in range(groups)])

    def across(parts):
        return [
            lax.ppermute(parts[k], ("px", "py"), [
                (i * groups + j, (i ^ k) * groups + (j ^ half))
                for i in range(spans) for j in range(groups)])
            for k in range(spans)]

    *w_blocks, slots = call(
        functools.partial(pack_weights_kernel, groups, cap, blk, block_rows),
        (f32(block_rows, SEG),) * half + (jax.ShapeDtypeStruct((chunks, SEG), jnp.int32),),
        [ints, ints, ints, vmem(chunks, SEG), vmem(rows, SEG), vmem(half * block_rows, SEG), ints,
         pltpu.SMEM((chunks, SEG), jnp.int32), dma((5,)), dma((half,)), dma],
        [hbm] * 5,
        (hbm,) * half + (local,),
        limit=PACK_BYTES,
    )(
        obs_owner.reshape(chunks, SEG), cell_key.reshape(chunks, SEG),
        stencil.reshape(chunks, SEG), interp.reshape(chunks, SEG), obs_weight,
    )
    v_blocks = list(call(
        functools.partial(pack_products_kernel, groups, cap),
        (f32(2 * cap, SEG),) * half,
        [vmem(rows, SEG), vmem(rows, SEG), vmem(groups * cap, SEG), dma((2,)), dma((half,))],
        [scalars] + [hbm] * 2,
        (hbm,) * half,
        limit=PACK_BYTES,
    )(slots, obs_weight, innovation))
    w_blocks[1:] = [to_half(w_blocks[k], k) for k in range(1, half)]
    lead = half // 2
    w_blocks[lead], *v_blocks[1:] = lax.optimization_barrier((w_blocks[lead], *v_blocks[1:]))
    v_blocks[1:] = [to_half(v_blocks[k], k) for k in range(1, half)]

    swap = call(
        pack_swap_kernel,
        f32(spans, LX * tiles + (F + 1) * nx, SEG),
        [vmem(*coef_y.shape[1:]), vmem(F + 1, nx, SEG), vmem(F + 1, nx, SEG), dma((5,))],
        [local] + [hbm] * 3,
        limit=PACK_BYTES,
    )(slots, coef_y[0], c0, cx)
    swap = lax.all_to_all(swap, "px", split_axis=0, concat_axis=0, tiled=True)
    c0_ext, cx_ext, cy_ext, u_ext, token = call(
        start_kernel,
        (f32(F, tiles, nx, SEG), f32(tiles, nx, SEG), f32(tiles, nx, SEG), f32(F, tiles, nx, SEG),
         f32(8, SEG)),
        [vmem(F, tiles, nx, SEG)],
    )(c0, cx, swap)

    def sum_weights(side, token, weight):
        return call(
            functools.partial(weights_kernel, half, cap, blk, side),
            (f32(half, meta_rows, SEG),) + (f32(ROWS, SEG),) * 2,
            [vmem(ROWS, 3 * SEG)],
            weight=weight,
        )(*w_blocks, token)

    meta, *side_across = sum_weights(1, w_blocks[0], FIRST)
    side_across = [to_half(values, half) for values in side_across]
    meta, *side = sum_weights(0, token, 1)
    parts, *sums_across = call(
        functools.partial(products_kernel, half, cap, blk),
        (f32(spans, 3 * F, tiles, LX, SEG),)
        + (f32(F * (tiles - 1) + 1, LX, SEG),) * spans,
        [vmem(ROWS, 2 * SEG), vmem(ROWS, SEG), vmem(ROWS, SEG), vmem(2, ROWS, SEG)],
    )(meta, *side, *side_across, *v_blocks)
    far_sums = call(
        functools.partial(join_kernel, spans), f32(F, tiles, nx, SEG), weight=JOIN,
    )(*across(sums_across))
    parts = lax.all_to_all(parts, "px", split_axis=0, concat_axis=0, tiled=True)

    r, q, h, dots = call(
        solve_kernel,
        (f32(F, nx, width),) * 2 + (f32(F, tiles, nx, SEG), f32(groups * spans, 1, SEG)),
        [vmem(3, F, tiles, nx, SEG), vmem(3 * F, tiles, nx, SEG), vmem(2, F, tiles, nx, SEG)],
    )(c0_ext, cx_ext, cy_ext, u_ext, parts, far_sums)
    dots = lax.all_to_all(dots, ("px", "py"), split_axis=0, concat_axis=0, tiled=True)
    qq = call(last_kernel, f32(F, nx, width), [vmem(2, F, tiles, nx, SEG)])(
        h, q, cx_ext, cy_ext)
    control, residual = call(finish_kernel, (f32(F, nx, width),) * 2)(dots, c0, r, q, qq)
    return control[:, None], residual[:, None]


def solution(mesh):
    return jax.shard_map(
        shards,
        mesh=mesh,
        in_specs=(
            P(None, "py", None, "px"),
            P("py", None, "px"),
            P("py", "px", None),
            P(("px", "py"), None),
            P(("px", "py"), None),
            P(("px", "py")),
            P(("px", "py"), None),
            P(("px", "py")),
            P(("px", "py")),
        ),
        out_specs=(P(None, "py", None, "px"), P(None, "py", None, "px")),
        check_vma=False,
    )
```
